128 devices in a mesh: dp: 4 (over x), seq: 32 (over y, z, core).
Axes of the slice: x: 4, y: 4, z: 4, core: 2. Of those that a mesh axis runs over, the one named last changes fastest.
Arguments:
- block_input: bfloat16 [16384, 2048], P(('dp', 'seq')), may hold values from -6 to 6
- cotangent: bfloat16 [16384, 2048], P(('dp', 'seq')), may hold values from -6 to 6
- lengths: int32 [4, 4], P('dp'), may hold values from 1 to 4093, as said below
- norm_gain: float32 [2048], P('seq'), may hold values from 0.4 to 1.6
- q_down: bfloat16 [2048, 1024], P('seq'), may hold values from -0.125 to 0.125
- q_gain: float32 [1024], P('seq'), may hold values from 0.4 to 1.6
- q_up: bfloat16 [1024, 4096], P('seq'), may hold values from -0.1875 to 0.1875
- key_weight: bfloat16 [2048, 256], P('seq'), may hold values from -0.125 to 0.125
- value_weight: bfloat16 [2048, 256], P('seq'), may hold values from -0.125 to 0.125
- out_weight: bfloat16 [4096, 2048], P('seq'), may hold values from -0.375 to 0.375
- ffn_gain: float32 [2048], P('seq'), may hold values from 0.4 to 1.6
- gate_weight: bfloat16 [2048, 5632], P('seq'), may hold values from -0.125 to 0.125
- up_weight: bfloat16 [2048, 5632], P('seq'), may hold values from -0.125 to 0.125
- down_weight: bfloat16 [5632, 2048], P('seq'), may hold values from -0.078125 to 0.078125
Outputs:
- output: bfloat16 [16384, 2048], P(('dp', 'seq'))
- input_grad: float32 [16384, 2048], P(('dp', 'seq'))
- grad_norm_gain: float32 [2048], P('seq')
- grad_q_down: float32 [2048, 1024], P('seq')
- grad_q_gain: float32 [1024], P('seq')
- grad_q_up: float32 [1024, 4096], P('seq')
- grad_key_weight: float32 [2048, 256], P('seq')
- grad_value_weight: float32 [2048, 256], P('seq')
- grad_out_weight: float32 [4096, 2048], P('seq')
- grad_ffn_gain: float32 [2048], P('seq')
- grad_gate_weight: float32 [2048, 5632], P('seq')
- grad_up_weight: float32 [2048, 5632], P('seq')
- grad_down_weight: float32 [5632, 2048], P('seq')
The draws below stay inside these ranges and needn't reach their ends.
Inputs may be any that keep to these rules, and one draw needn't show every extreme that they name: `lengths`: each row packs its 4 documents from slot 0 in order, padding after them. The second document begins on the first device of its row and ends on the last; the first document, the documents after the second and the padding each take fewer slots than one device holds.
All inputs are finite; a program needn't handle non-finite values.
Results may differ from the reference program's by a relative error of at most 0.04.
Values may be sent and summed in bfloat16 or wider, within the bound.
A program may use at most 320 MiB of HBM per device.

```python
import math
import jax
import jax.numpy as jnp
from jax import lax

D = 2048
QL = 1024
DH = 256
FF = 5632
HD = 4096
SLOTS = 4096
ROWS = 4
TOKENS = 16384
N_DP = 4
N_SEQ = 32


def draw_lengths(key, part):
    key = jax.random.fold_in(key, 7)
    span = SLOTS // N_SEQ
    keys = jax.random.split(key, 5)
    leading = jax.random.randint(keys[0], (N_DP,), 1, span)
    second_tail = jax.random.randint(keys[1], (N_DP,), 1, (span - 1) // 2 + 1)
    third_tail = jax.random.randint(keys[2], (N_DP,), 1, (span - 1) // 2 + 1)
    padding = jax.random.randint(keys[3], (N_DP,), 0, span - second_tail - third_tail)
    chosen = jax.random.randint(keys[4], (), 0, N_DP)
    marked = jnp.arange(N_DP) == chosen
    leading = jnp.where(marked, 1, leading)
    second_tail = jnp.where(marked, 1, second_tail)
    third_tail = jnp.where(marked, 1, third_tail)
    padding = jnp.where(marked, 0, padding)
    longest = SLOTS - leading - second_tail - third_tail - padding
    return jnp.stack([leading, longest, second_tail, third_tail], axis=1).astype(jnp.int32)


def levels(key, dims, cuts, low, largest):
    level = 1.0
    for dim, parts in cuts:
        heights = jax.random.uniform(jax.random.fold_in(jax.random.fold_in(key, 6), dim), (parts,), jnp.float32, low / len(cuts), largest / len(cuts))
        level = level * jnp.repeat(jnp.exp(heights), dims[dim] // parts).reshape((-1,) + (1,) * (len(dims) - 1 - dim))
    return level


def gaussian(key, dims, deviation, reach, cuts=(), kind=jnp.bfloat16):
    level = levels(key, dims, cuts, -0.22, 0.18) if cuts else 1.0
    drawn = jax.random.normal(key, dims, jnp.float32) * deviation * level
    return jnp.minimum(jnp.maximum(drawn, -reach), reach).astype(kind)


def setup_inputs(seed: int = 0) -> dict:
    key_list = jax.random.split(jax.random.key(seed), 15)
    return {
        "block_input": gaussian(key_list[0], (TOKENS, D), 1.0, 6.0, ((0, 128),)),
        "cotangent": gaussian(key_list[1], (TOKENS, D), 1.0, 6.0, ((0, 128),)),
        "lengths": draw_lengths(jax.random.fold_in(key_list[14], 71), 0),
        "norm_gain": jnp.clip(1.0 + 0.12 * jax.random.normal(key_list[3], (D,), jnp.float32), 0.4, 1.6),
        "q_down": gaussian(key_list[4], (D, QL), D ** -0.5, 0.125, ((0, 32),)),
        "q_gain": jnp.clip(1.0 + 0.12 * jax.random.normal(key_list[5], (QL,), jnp.float32), 0.4, 1.6),
        "q_up": gaussian(key_list[6], (QL, HD), QL ** -0.5, 0.1875, ((0, 32),)),
        "key_weight": gaussian(key_list[7], (D, DH), D ** -0.5, 0.125, ((0, 32),)),
        "value_weight": gaussian(key_list[8], (D, DH), D ** -0.5, 0.125, ((0, 32),)),
        "out_weight": gaussian(key_list[9], (HD, D), (HD // 16) ** -0.5, 0.375, ((0, 32),)),
        "ffn_gain": jnp.clip(1.0 + 0.12 * jax.random.normal(key_list[10], (D,), jnp.float32), 0.4, 1.6),
        "gate_weight": gaussian(key_list[11], (D, FF), D ** -0.5, 0.125, ((0, 32),)),
        "up_weight": gaussian(key_list[12], (D, FF), D ** -0.5, 0.125, ((0, 32),)),
        "down_weight": gaussian(key_list[13], (FF, D), FF ** -0.5, 0.078125, ((0, 32),)),
    }


@jax.custom_vjp
def low(v):
    return lax.optimization_barrier(v.astype(jnp.bfloat16)).astype(jnp.float32)

@jax.custom_vjp
def low_back(v):
    return v

def low_keep(v):
    return (low(v), None)

def low_pass(kept, grad):
    return (grad,)

def back_keep(v):
    return (v, None)

def back_low(kept, grad):
    return (low(grad),)
low.defvjp(low_keep, low_pass)
low_back.defvjp(back_keep, back_low)
EPSILON = 1e-06
HIGHEST = lax.Precision.HIGHEST
MASKED = -1e+30

def product(left, right):
    return jnp.dot(left, right, precision=HIGHEST)

def rms_norm(values, gain):
    factor = lax.rsqrt(lax.optimization_barrier(jnp.mean(values * values, axis=-1, keepdims=True)) + EPSILON)
    return values * factor * gain

def layout(lengths_row, slots):
    count = lengths_row.shape[0]
    ends = jnp.cumsum(lengths_row).astype(jnp.int32)
    starts = jnp.concatenate([ends - lengths_row, ends[-1:]]).astype(jnp.int32)
    places = jnp.arange(slots, dtype=jnp.int32)
    segment = lax.optimization_barrier(jnp.sum((places[:, None] >= ends[None, :]).astype(jnp.int32), axis=1))
    picked = segment[:, None] == jnp.arange(count + 1, dtype=jnp.int32)[None, :]
    start_of = lax.optimization_barrier(jnp.sum(jnp.where(picked, starts[None, :], 0), axis=1)).astype(jnp.int32)
    position = places - start_of
    live = (segment < count).astype(jnp.float32)
    return (segment, position, live)

def tables(position, size):
    half = size // 2
    freq = jnp.exp(jnp.arange(half, dtype=jnp.float32) * (-math.log(10000.0) / half))
    angle = position.astype(jnp.float32)[:, None] * freq[None, :]
    return (jnp.cos(angle), jnp.sin(angle))

def rotate(values, cosine, sine):
    half = values.shape[-1] // 2
    lower, upper = (values[..., :half], values[..., half:])
    return jnp.concatenate([lower * cosine - upper * sine, upper * cosine + lower * sine], axis=-1)

def attend(queries, key_rows, value_rows, segment):
    slots = queries.shape[0]
    block = math.gcd(slots, 512)
    places = jnp.arange(slots, dtype=jnp.int32)
    factor = key_rows.shape[-1] ** (-0.5)

    def one_block(inputs):
        query_block, segment_block, place_block = inputs
        raw = jnp.einsum('thd,kd->thk', query_block, key_rows, precision=HIGHEST) * factor
        allowed = (segment_block[:, None] == segment[None, :]) & (place_block[:, None] >= places[None, :])
        scores = low_back(jnp.where(allowed[:, None, :], raw, MASKED))
        peak = lax.optimization_barrier(jnp.max(scores, axis=-1, keepdims=True))
        weights = jnp.exp(scores - peak)
        probs = weights / lax.optimization_barrier(jnp.sum(weights, axis=-1, keepdims=True))
        return jnp.einsum('thk,kd->thd', low(probs), value_rows, precision=HIGHEST)
    count = slots // block
    pieces = lax.map(jax.checkpoint(one_block), (queries.reshape((count, block) + queries.shape[1:]), segment.reshape(count, block), places.reshape(count, block)))
    return pieces.reshape(queries.shape)

def forward_row(params, inputs, segment, position, live):
    norm_gain, q_down, q_gain, q_up, key_weight, value_weight, out_weight, ffn_gain, gate_weight, up_weight, down_weight = params
    slots = inputs.shape[0]
    size = key_weight.shape[1]
    head_count = q_up.shape[1] // size
    cosine, sine = tables(position, size)
    normed = low(rms_norm(inputs, norm_gain))
    latent = low_back(product(normed, q_down))
    latent_normed = low(rms_norm(latent, q_gain))
    queries = low_back(product(latent_normed, q_up)).reshape(slots, head_count, size)
    queries = low(rotate(queries, cosine[:, None, :], sine[:, None, :]))
    key_rows = low(rotate(low_back(product(normed, key_weight)), cosine, sine))
    value_rows = low(low_back(product(normed, value_weight)))
    mixed = attend(queries, key_rows, value_rows, segment).reshape(slots, head_count * size)
    mixed = low(low_back(mixed * live[:, None]))
    branch = low_back(product(mixed, out_weight))
    middle = inputs + branch
    normed_two = low(rms_norm(middle, ffn_gain))
    gate_pre = low_back(product(normed_two, gate_weight))
    up_pre = low_back(product(normed_two, up_weight))
    hidden = low(jax.nn.silu(gate_pre) * up_pre)
    return middle + low_back(product(hidden, down_weight))

def reference(block_input, cotangent, lengths, norm_gain, q_down, q_gain, q_up, key_weight, value_weight, out_weight, ffn_gain, gate_weight, up_weight, down_weight):
    params = tuple((w.astype(jnp.float32) for w in (norm_gain, q_down, q_gain, q_up, key_weight, value_weight, out_weight, ffn_gain, gate_weight, up_weight, down_weight)))
    input_rows = block_input.astype(jnp.float32).reshape(ROWS, SLOTS, D)
    grad_rows = cotangent.astype(jnp.float32).reshape(ROWS, SLOTS, D)

    def row_pass(totals, row):
        inputs, incoming, lengths_row = row
        segment, position, live = layout(lengths_row, SLOTS)

        def forward(weights, values):
            return forward_row(weights, values, segment, position, live)
        result, pull = jax.vjp(forward, params, inputs)
        grad_params, grad_inputs = pull(incoming)
        totals = jax.tree.map(jnp.add, totals, grad_params)
        return (totals, (result.astype(jnp.bfloat16), grad_inputs))
    zeros = tuple((jnp.zeros_like(w) for w in params))
    totals, (output, input_grad) = lax.scan(row_pass, zeros, (input_rows, grad_rows, lengths))
    return (output.reshape(TOKENS, D), input_grad.reshape(TOKENS, D), totals[0], totals[1], totals[2], totals[3], totals[4], totals[5], totals[6], totals[7], totals[8], totals[9], totals[10])
```

```python
import functools
import math

import jax
import jax.numpy as jnp
from jax import lax
from jax.experimental import pallas as pl
from jax.experimental.pallas import tpu as pltpu
from jax.sharding import Mesh
from jax.sharding import PartitionSpec as P

EPSILON = 1e-06
MASKED = -1e30
BF = jnp.bfloat16
F32 = jnp.float32
SIZE = 256
HALF = 128
BLOCK = 256
ROW = ("y", "z", "c")
HEADS = ("y", "c")
FEED = ("x", "c")


def dot(left, right):
    return jnp.dot(left, right, preferred_element_type=F32)


def dot_tn(left, right):
    return lax.dot_general(left, right, (((0,), (0,)), ((), ())), preferred_element_type=F32)


def dot_nt(left, right):
    return lax.dot_general(left, right, (((1,), (1,)), ((), ())), preferred_element_type=F32)


def norm_back(values, inverse, gain, grad):
    scaled = grad * gain
    grad_values = inverse * scaled - values * inverse * inverse * inverse * jnp.mean(
        scaled * values, axis=-1, keepdims=True
    )
    return grad_values, jnp.sum(grad * values * inverse, axis=0)


def places_of(lengths_row, slots):
    ends = jnp.cumsum(lengths_row)
    begins = jnp.concatenate([ends - lengths_row, ends[-1:]])
    begin = jnp.max(jnp.where(slots[:, None] >= begins[None, :], begins[None, :], 0), axis=1)
    live = (slots < ends[-1]).astype(F32)
    return begin, live


def tables(position):
    freq = jnp.exp(jnp.arange(HALF, dtype=F32) * (-math.log(10000.0) / HALF))
    angle = position.astype(F32)[:, None] * freq[None, :]
    return jnp.cos(angle), jnp.sin(angle)


def rotate(values, cosine, sine):
    lower, upper = values[..., :HALF], values[..., HALF:]
    return jnp.concatenate([lower * cosine - upper * sine, upper * cosine + lower * sine], axis=-1)


def unrotate(grad, cosine, sine):
    lower, upper = grad[..., :HALF], grad[..., HALF:]
    return jnp.concatenate([lower * cosine + upper * sine, upper * cosine - lower * sine], axis=-1)


def attend_kernel(q_ref, k_ref, vt_ref, begin_ref, slot_ref, out_ref, lse_ref, peak, total, accum):
    depth = lax.axis_index("z")
    segments = slot_ref.shape[0]
    rows = slot_ref.shape[2]
    tokens = rows // 2
    for seg in range(segments):
        query = q_ref[pl.ds(seg * tokens, tokens), :]
        query = jnp.concatenate([query[:, :SIZE], query[:, SIZE:]], axis=0).T
        begin = begin_ref[seg]
        slot = slot_ref[seg]
        peak[...] = jnp.full_like(peak, MASKED)
        total[...] = jnp.zeros_like(total)
        accum[...] = jnp.zeros_like(accum)
        count = segments * seg + depth + 1

        @pl.loop(0, count)
        def _(block):
            at = pl.multiple_of(block * BLOCK, BLOCK)
            scores = dot(k_ref[pl.ds(at, BLOCK), :], query)
            key = lax.broadcasted_iota(jnp.int32, scores.shape, 0) + at
            scores = jnp.where((key >= begin) & (key <= slot), scores, MASKED)
            before = peak[...]
            now = jnp.maximum(before, jnp.max(scores, axis=0, keepdims=True))
            weights = jnp.exp(scores - now)
            shrink = jnp.exp(before - now)
            peak[...] = now
            total[...] = total[...] * shrink + jnp.sum(weights, axis=0, keepdims=True)
            accum[...] = accum[...] * shrink + dot(vt_ref[:, pl.ds(at, BLOCK)], weights.astype(BF))

        lse_ref[seg] = peak[...] + jnp.log(total[...])
        result = (accum[...] / total[...]).T
        out_ref[pl.ds(seg * tokens, tokens), :] = jnp.concatenate(
            [result[:tokens], result[tokens:]], axis=1
        )


def attend(q, k, vt, begin, slot):
    segments, _, rows = slot.shape
    return pl.pallas_call(
        attend_kernel,
        name="attend",
        out_shape=(
            jax.ShapeDtypeStruct(q.shape, F32),
            jax.ShapeDtypeStruct((segments, 1, rows), F32),
        ),
        in_specs=[pl.BlockSpec(memory_space=pltpu.VMEM)] * 5,
        out_specs=[pl.BlockSpec(memory_space=pltpu.VMEM)] * 2,
        scratch_shapes=[
            pltpu.VMEM((1, rows), F32),
            pltpu.VMEM((1, rows), F32),
            pltpu.VMEM((SIZE, rows), F32),
        ],
        compiler_params=pltpu.CompilerParams(vmem_limit_bytes=48 << 20),
    )(q, k, vt, begin, slot)


def attend_back_kernel(
    q_ref, do_ref, o_ref, k_ref, kt_ref, v_ref, begin_ref, slot_ref, lse_ref,
    dq_ref, dk_ref, dv_ref, accum,
):
    depth = lax.axis_index("z")
    segments = slot_ref.shape[0]
    rows = slot_ref.shape[2]
    tokens = rows // 2
    dk_ref[...] = jnp.zeros_like(dk_ref)
    dv_ref[...] = jnp.zeros_like(dv_ref)
    for seg in range(segments):
        here = pl.ds(seg * tokens, tokens)

        def stacked(ref):
            value = ref[here, :]
            return jnp.concatenate([value[:, :SIZE], value[:, SIZE:]], axis=0)

        query = stacked(q_ref)
        grad = stacked(do_ref)
        query_t = query.T
        grad_t = grad.T
        delta = jnp.sum(
            grad_t.astype(F32) * stacked(o_ref).T.astype(F32), axis=0, keepdims=True
        )
        begin = begin_ref[seg]
        slot = slot_ref[seg]
        lse = lse_ref[seg]
        accum[...] = jnp.zeros_like(accum)
        count = segments * seg + depth + 1

        @pl.loop(0, count)
        def _(block):
            at = pl.multiple_of(block * BLOCK, BLOCK)
            keys = pl.ds(at, BLOCK)
            scores = dot(k_ref[keys, :], query_t)
            key = lax.broadcasted_iota(jnp.int32, scores.shape, 0) + at
            allowed = (key >= begin) & (key <= slot)
            probs = jnp.where(allowed, jnp.exp(scores - lse), 0.0)
            grad_probs = dot(v_ref[keys, :], grad_t)
            grad_scores = (probs * (grad_probs - delta)).astype(BF)
            dv_ref[keys, :] += dot(probs.astype(BF), grad)
            dk_ref[keys, :] += dot(grad_scores, query)
            accum[...] += dot(kt_ref[:, keys], grad_scores)

        result = accum[...].T * (SIZE ** -0.5)
        dq_ref[here, :] = jnp.concatenate([result[:tokens], result[tokens:]], axis=1)


def attend_back(q, do, o, k, kt, v, begin, slot, lse):
    segments, _, rows = slot.shape
    return pl.pallas_call(
        attend_back_kernel,
        name="attend_back",
        out_shape=(
            jax.ShapeDtypeStruct(q.shape, F32),
            jax.ShapeDtypeStruct(k.shape, F32),
            jax.ShapeDtypeStruct(k.shape, F32),
        ),
        in_specs=[pl.BlockSpec(memory_space=pltpu.VMEM)] * 9,
        out_specs=[pl.BlockSpec(memory_space=pltpu.VMEM)] * 3,
        scratch_shapes=[pltpu.VMEM((SIZE, rows), F32)],
        compiler_params=pltpu.CompilerParams(vmem_limit_bytes=48 << 20),
    )(q, do, o, k, kt, v, begin, slot, lse)


def gather(value, axes):
    return lax.all_gather(value, axes, axis=0, tiled=True)


def scatter_sum(value, axes):
    return lax.psum_scatter(value, axes, scatter_dimension=0, tiled=True)


def swap(value, axes):
    return lax.all_to_all(value, axes, 0, 0, tiled=True)


def on_device(
    block_input, cotangent, lengths, norm_gain, q_down, q_gain, q_up, key_weight, value_weight,
    out_weight, ffn_gain, gate_weight, up_weight, down_weight,
):
    rows, width = block_input.shape
    latent_width = q_down.shape[1]
    n_x, n_y, n_z, n_c = (lax.axis_size(a) for a in ("x", "y", "z", "c"))
    x, y, z, c = (lax.axis_index(a) for a in ("x", "y", "z", "c"))
    span = n_y * n_z * n_c
    members = n_y * n_c
    lengths_row = lengths[0]

    mine = (y * n_z + z) * n_c + c
    slots_mine = mine * rows + jnp.arange(rows, dtype=jnp.int32)
    begin_mine, _ = places_of(lengths_row, slots_mine)
    cosine, sine = tables(slots_mine - begin_mine)
    strip = n_c * rows
    slots_group = (
        (jnp.arange(n_y, dtype=jnp.int32)[:, None] * n_z + z) * strip
        + jnp.arange(strip, dtype=jnp.int32)[None, :]
    ).reshape(-1)
    begin_group, live_group = places_of(lengths_row, slots_group)
    cosine_group, sine_group = tables(slots_group - begin_group)
    begin_lanes = jnp.tile(begin_group.reshape(n_y, 1, strip), (1, 1, 2))
    slot_lanes = jnp.tile(slots_group.reshape(n_y, 1, strip), (1, 1, 2))

    shard = norm_gain.shape[0]
    extra = jnp.stack(
        [norm_gain, ffn_gain, jnp.pad(q_gain, (0, shard - q_gain.shape[0]))], axis=1
    ).astype(BF)
    first_width = latent_width + 2 * SIZE
    first = jnp.concatenate(
        [q_down, key_weight, value_weight, jnp.pad(extra, ((0, 0), (0, 125)))], axis=1
    )
    first_full = gather(first, ROW)
    extra_full = first_full[:, first_width : first_width + 3].astype(F32)
    first_full = first_full[:, :first_width]
    gain_one = extra_full[:, 0]
    gain_two = extra_full[:, 1]
    gain_latent = extra_full[:, 2].reshape(span, shard)[:, : q_gain.shape[0]].reshape(-1)

    per_heads = q_up.shape[1] // members
    q_rows = q_up.shape[0]
    up_part = swap(q_up.reshape(q_rows, members, per_heads).transpose(1, 0, 2), HEADS)
    up_heads = gather(up_part[None], "z")
    up_heads = (
        up_heads.reshape(n_z, n_y, n_c, q_rows, per_heads)
        .transpose(1, 0, 2, 3, 4)
        .reshape(span * q_rows, per_heads)
    )
    out_chip = gather(out_weight, ("z", "c"))
    out_heads = lax.dynamic_slice_in_dim(out_chip, c * per_heads, per_heads)

    wide = gate_weight.shape[1]
    down_rows = down_weight.shape[0]
    share = down_rows // n_x
    padded = -(-share // 16) * 16
    source = lax.broadcasted_iota(jnp.int32, (wide // 2, n_c * (span // 4) * padded), 0)
    target = lax.broadcasted_iota(jnp.int32, source.shape, 1)
    block_at = target // (padded * (span // 4)) + n_c * ((target // padded) % (span // 4))
    inside = target % padded
    picks = (
        (source == block_at * down_rows + x * share + inside) & (inside < share)
    ).astype(BF)

    def spread(weight):
        stacked = jnp.concatenate([weight[:, : wide // 2], weight[:, wide // 2 :]], axis=0)
        part = dot(stacked, picks).astype(BF)
        part = part.reshape(2, shard, n_c, -1).transpose(2, 1, 0, 3)
        return part.reshape(n_c, shard, -1)

    both = jnp.stack([spread(gate_weight), spread(up_weight)], axis=1)
    both = swap(both, "c")
    units = both.shape[-1]
    both = both.transpose(0, 2, 1, 3).reshape(n_c * shard, 2 * units)
    both_full = gather(both, ("y", "z"))
    gate_use, up_use = both_full[:, :units], both_full[:, units:]
    down_part = lax.dynamic_slice_in_dim(down_weight, x * share, share)
    down_part = jnp.pad(down_part, ((0, padded - share), (0, 0)))
    down_use = gather(down_part, ("y", "z"))

    inputs = block_input.astype(F32)
    inverse_one = lax.rsqrt(jnp.mean(inputs * inputs, axis=-1, keepdims=True) + EPSILON)
    normed = (inputs * inverse_one * gain_one).astype(BF)
    firsts = dot(normed, first_full)
    latent = firsts[:, :latent_width]
    inverse_latent = lax.rsqrt(jnp.mean(latent * latent, axis=-1, keepdims=True) + EPSILON)
    latent_normed = (latent * inverse_latent * gain_latent).astype(BF)
    key_mine = rotate(firsts[:, latent_width : latent_width + SIZE], cosine, sine).astype(BF)
    value_mine = firsts[:, latent_width + SIZE :].astype(BF)
    key_value = gather(jnp.concatenate([key_mine, value_mine], axis=1), ROW)
    keys, values = key_value[:, :SIZE], key_value[:, SIZE:]
    latent_group = gather(latent_normed, HEADS)
    group = latent_group.shape[0]
    queries = rotate(
        dot(latent_group, up_heads).reshape(group, 2, SIZE),
        cosine_group[:, None, :], sine_group[:, None, :],
    ).astype(BF) * (SIZE ** -0.5)
    queries = queries.astype(BF).reshape(group, per_heads)
    attended, lse = attend(queries, keys, values.T, begin_lanes, slot_lanes)
    mixed = (attended * live_group[:, None]).astype(BF)
    middle = inputs + scatter_sum(dot(mixed, out_heads).astype(BF), HEADS).astype(F32)

    inverse_two = lax.rsqrt(jnp.mean(middle * middle, axis=-1, keepdims=True) + EPSILON)
    normed_two = gather((middle * inverse_two * gain_two).astype(BF), FEED)
    grad_feed = gather(cotangent, FEED)
    gate_pre = dot(normed_two, gate_use)
    up_pre = dot(normed_two, up_use)
    sigma = jax.nn.sigmoid(gate_pre)
    hidden = (gate_pre * sigma * up_pre).astype(BF)
    grad_hidden = dot_nt(grad_feed, down_use)
    grad_gate_pre = (grad_hidden * up_pre * sigma * (1.0 + gate_pre * (1.0 - sigma))).astype(BF)
    grad_up_pre = (grad_hidden * gate_pre * sigma).astype(BF)
    grad_normed_two = scatter_sum(
        (dot_nt(grad_gate_pre, gate_use) + dot_nt(grad_up_pre, up_use)).astype(BF), FEED
    ).astype(F32)
    branch_two = scatter_sum(dot(hidden, down_use).astype(BF), FEED).astype(F32)
    output = (middle + branch_two).astype(BF)
    grad_result = cotangent.astype(F32)
    grad_mid_norm, grad_gain_two = norm_back(middle, inverse_two, gain_two, grad_normed_two)
    grad_middle = grad_result + grad_mid_norm
    grad_both = jnp.concatenate(
        [dot_tn(normed_two, grad_gate_pre), dot_tn(normed_two, grad_up_pre)], axis=1
    ).astype(BF)
    grad_both = scatter_sum(grad_both, ("y", "z"))
    grad_down = scatter_sum(dot_tn(hidden, grad_feed).astype(BF), ("y", "z"))
    grad_both = grad_both.reshape(n_c, shard, 2, units).transpose(0, 2, 1, 3)
    grad_both = swap(grad_both, "c")
    grad_both = gather(grad_both.reshape(1, n_c, 2, shard, units), "x")
    grad_down = gather(grad_down[None], "x")

    def collect(grads):
        parts = grads.reshape(n_x, n_c, shard, 2, units // 2).transpose(0, 3, 2, 1, 4)
        parts = parts.reshape(n_x, 2 * shard, n_c * units // 2)
        whole = 0.0
        for i in range(n_x):
            picked = (
                (source == block_at * down_rows + i * share + inside) & (inside < share)
            ).astype(BF)
            whole = whole + dot_nt(parts[i], picked)
        return jnp.concatenate([whole[:shard], whole[shard:]], axis=1)

    grad_gate = collect(grad_both[:, :, 0])
    grad_up = collect(grad_both[:, :, 1])
    grad_down = grad_down[:, :share].reshape(down_rows, width).astype(F32)

    grad_branch = gather(grad_middle.astype(BF), HEADS)
    grad_mixed = dot_nt(grad_branch, out_heads).astype(BF)
    grad_attended = grad_mixed * live_group[:, None].astype(BF)
    grad_out = dot_tn(mixed, grad_branch).astype(BF)
    grad_queries, grad_keys, grad_values = attend_back(
        queries, grad_attended, mixed, keys, keys.T, values, begin_lanes, slot_lanes, lse
    )
    grad_kv = scatter_sum(
        jnp.concatenate([grad_keys, grad_values], axis=1).astype(BF), ROW
    ).astype(F32)
    grad_query_raw = (
        unrotate(
            grad_queries.reshape(group, 2, SIZE),
            cosine_group[:, None, :], sine_group[:, None, :],
        )
        .reshape(group, per_heads)
        .astype(BF)
    )
    grad_key_raw = unrotate(grad_kv[:, :SIZE], cosine, sine).astype(BF)
    grad_value_raw = grad_kv[:, SIZE:].astype(BF)
    grad_up_heads = dot_tn(latent_group, grad_query_raw).astype(BF)
    grad_latent_normed = scatter_sum(dot_nt(grad_query_raw, up_heads).astype(BF), HEADS).astype(F32)
    grad_latent_f, grad_gain_latent = norm_back(
        latent, inverse_latent, gain_latent, grad_latent_normed
    )
    grad_firsts = jnp.concatenate(
        [grad_latent_f.astype(BF), grad_key_raw, grad_value_raw], axis=1
    )
    grad_normed = dot_nt(grad_firsts, first_full)
    grad_input_norm, grad_gain_one = norm_back(inputs, inverse_one, gain_one, grad_normed)
    input_grad = grad_middle + grad_input_norm

    normed_group = gather(normed, HEADS)
    tall = width // n_y
    normed_part = lax.dynamic_slice_in_dim(normed_group, y * tall, tall, axis=1)
    grad_firsts_group = gather(grad_firsts, HEADS)
    half_first = first_width // n_c
    first_part = lax.dynamic_slice_in_dim(grad_firsts_group, c * half_first, half_first, axis=1)
    grad_first = dot_tn(normed_part, first_part).astype(BF)

    out_rows = out_weight.shape[0]
    grad_out = grad_out.reshape(n_z // n_c, n_c, out_rows, width).transpose(1, 0, 2, 3)
    grad_out = swap(grad_out, "c").reshape(n_z, out_rows * width)
    grad_first = grad_first.reshape(n_z, n_c, shard, half_first).transpose(1, 0, 2, 3)
    grad_first = swap(grad_first, "c").transpose(1, 2, 0, 3).reshape(n_z, shard * first_width)
    grad_up_heads = grad_up_heads.reshape(n_y, n_z, n_c, q_rows, per_heads)
    grad_up_heads = grad_up_heads.transpose(0, 2, 1, 3, 4).reshape(members, n_z, q_rows, per_heads)
    grad_up_heads = swap(grad_up_heads, HEADS).transpose(1, 2, 0, 3).reshape(n_z, -1)
    pieces = jnp.concatenate([grad_out, grad_first, grad_up_heads], axis=1)
    pieces = lax.psum(scatter_sum(pieces, "z"), "x").astype(F32)[0]
    at_first = out_rows * width
    at_up = at_first + shard * first_width
    grad_out = pieces[:at_first].reshape(out_rows, width)
    grad_first = pieces[at_first:at_up].reshape(shard, first_width)
    grad_q_up = pieces[at_up:].reshape(q_rows, -1)

    gains = jnp.concatenate(
        [
            grad_gain_one.reshape(span, shard),
            grad_gain_two.reshape(span, shard),
            grad_gain_latent.reshape(span, -1),
        ],
        axis=1,
    )
    gains = lax.psum(scatter_sum(gains, ROW), "x")[0]
    return (
        output,
        input_grad,
        gains[:shard],
        grad_first[:, :latent_width],
        gains[2 * shard :],
        grad_q_up,
        grad_first[:, latent_width : latent_width + SIZE],
        grad_first[:, latent_width + SIZE :],
        grad_out,
        gains[shard : 2 * shard],
        grad_gate,
        grad_up,
        grad_down,
    )


def solution(mesh):
    sizes = (4, 4, 4, 2)
    grid = Mesh(mesh.devices.reshape(sizes), ("x", "y", "z", "c"))
    tokens = P(("x", "y", "z", "c"), None)
    wide, thin = P(ROW, None), P(ROW)
    in_specs = (
        tokens, tokens, P("x", None), thin, wide, thin, wide, wide, wide, wide, thin, wide, wide,
        wide,
    )
    out_specs = (
        tokens, tokens, thin, wide, thin, wide, wide, wide, wide, thin, wide, wide, wide,
    )
    return jax.shard_map(
        on_device, mesh=grid, in_specs=in_specs, out_specs=out_specs, check_vma=False
    )
```

```python
import functools
import math

import jax
import jax.numpy as jnp
from jax import lax
from jax.experimental import pallas as pl
from jax.experimental.pallas import tpu as pltpu
from jax.sharding import Mesh
from jax.sharding import PartitionSpec as P

EPSILON = 1e-06
MASKED = -1e30
BF = jnp.bfloat16
F32 = jnp.float32
SIZE = 256
HALF = 128
BLOCK = 256
ROW = ("y", "z", "c")
HEADS = ("y", "c")
FEED = ("x", "c")


def dot(left, right):
    return jnp.dot(left, right, preferred_element_type=F32)


def dot_tn(left, right):
    return lax.dot_general(left, right, (((0,), (0,)), ((), ())), preferred_element_type=F32)


def dot_nt(left, right):
    return lax.dot_general(left, right, (((1,), (1,)), ((), ())), preferred_element_type=F32)


def norm_back(values, inverse, gain, grad):
    scaled = grad * gain
    grad_values = inverse * scaled - values * inverse * inverse * inverse * jnp.mean(
        scaled * values, axis=-1, keepdims=True
    )
    return grad_values, jnp.sum(grad * values * inverse, axis=0)


def places_of(lengths_row, slots):
    ends = jnp.cumsum(lengths_row)
    begins = jnp.concatenate([ends - lengths_row, ends[-1:]])
    begin = jnp.max(jnp.where(slots[:, None] >= begins[None, :], begins[None, :], 0), axis=1)
    live = (slots < ends[-1]).astype(F32)
    return begin, live


def tables(position):
    freq = jnp.exp(jnp.arange(HALF, dtype=F32) * (-math.log(10000.0) / HALF))
    angle = position.astype(F32)[:, None] * freq[None, :]
    return jnp.cos(angle), jnp.sin(angle)


def tables_across(position):
    freq = jnp.exp(jnp.arange(HALF, dtype=F32) * (-math.log(10000.0) / HALF))
    angle = position.astype(F32)[..., None, :] * freq[:, None]
    return jnp.cos(angle), jnp.sin(angle)


def rotate(values, cosine, sine):
    lower, upper = values[..., :HALF], values[..., HALF:]
    return jnp.concatenate([lower * cosine - upper * sine, upper * cosine + lower * sine], axis=-1)


def unrotate(grad, cosine, sine):
    lower, upper = grad[..., :HALF], grad[..., HALF:]
    return jnp.concatenate([lower * cosine + upper * sine, upper * cosine - lower * sine], axis=-1)


def turned(source, target, count, columns):
    @pl.loop(0, count)
    def _(block):
        at = pl.ds(pl.multiple_of(block * BLOCK, BLOCK), BLOCK)
        target[:, at] = source[at, columns].T


KEYS, VALUES = slice(0, SIZE), slice(SIZE, 2 * SIZE)


def attend_kernel(
    q_ref, kv_ref, begin_ref, slot_ref, live_ref, cos_ref, sin_ref,
    out_ref, qt_ref, lse_ref, vt, peak, total, accum,
):
    depth = lax.axis_index("z")
    segments = slot_ref.shape[0]
    rows = slot_ref.shape[2]
    tokens = rows // 2
    turned(kv_ref, vt, segments * (segments - 1) + depth + 1, VALUES)
    for seg in range(segments):
        here = pl.ds(seg * tokens, tokens)
        cosine, sine = cos_ref[seg], sin_ref[seg]
        for head in range(2):
            raw = q_ref[here, head * SIZE : (head + 1) * SIZE].T
            lower, upper = raw[:HALF], raw[HALF:]
            turn = jnp.concatenate(
                [lower * cosine - upper * sine, upper * cosine + lower * sine], axis=0
            )
            qt_ref[seg, :, head * tokens : (head + 1) * tokens] = (
                turn.astype(BF) * (SIZE ** -0.5)
            ).astype(BF)
        query = qt_ref[seg]
        begin = begin_ref[seg]
        slot = slot_ref[seg]
        peak[...] = jnp.full_like(peak, MASKED)
        total[...] = jnp.zeros_like(total)
        accum[...] = jnp.zeros_like(accum)

        @pl.loop(0, segments * seg + depth + 1)
        def _(block):
            at = pl.multiple_of(block * BLOCK, BLOCK)
            scores = dot(kv_ref[pl.ds(at, BLOCK), KEYS], query)
            key = lax.broadcasted_iota(jnp.int32, scores.shape, 0) + at
            scores = jnp.where((key >= begin) & (key <= slot), scores, MASKED)
            before = peak[...]
            now = jnp.maximum(before, jnp.max(scores, axis=0, keepdims=True))
            weights = jnp.exp(scores - now)
            shrink = jnp.exp(before - now)
            peak[...] = now
            total[...] = total[...] * shrink + jnp.sum(weights, axis=0, keepdims=True)
            accum[...] = accum[...] * shrink + dot(vt[:, pl.ds(at, BLOCK)], weights.astype(BF))

        lse_ref[seg] = peak[...] + jnp.log(total[...])
        result = accum[...] * (live_ref[seg] / total[...])
        for head in range(2):
            out_ref[here, head * SIZE : (head + 1) * SIZE] = (
                result[:, head * tokens : (head + 1) * tokens].T.astype(BF)
            )


def attend(q, kv, begin, slot, live, cosine, sine):
    segments, _, rows = slot.shape
    return pl.pallas_call(
        attend_kernel,
        name="attend",
        out_shape=(
            jax.ShapeDtypeStruct(q.shape, BF),
            jax.ShapeDtypeStruct((segments, SIZE, rows), BF),
            jax.ShapeDtypeStruct((segments, 1, rows), F32),
        ),
        in_specs=[pl.BlockSpec(memory_space=pltpu.VMEM)] * 7,
        out_specs=[pl.BlockSpec(memory_space=pltpu.VMEM)] * 3,
        scratch_shapes=[
            pltpu.VMEM((SIZE, kv.shape[0]), BF),
            pltpu.VMEM((1, rows), F32),
            pltpu.VMEM((1, rows), F32),
            pltpu.VMEM((SIZE, rows), F32),
        ],
        compiler_params=pltpu.CompilerParams(vmem_limit_bytes=48 << 20),
    )(q, kv, begin, slot, live, cosine, sine)


def attend_back_kernel(
    qt_ref, do_ref, o_ref, kv_ref, begin_ref, slot_ref, lse_ref, cos_ref, sin_ref,
    dq_ref, dkv_ref, kt, sums, accum,
):
    depth = lax.axis_index("z")
    segments = slot_ref.shape[0]
    rows = slot_ref.shape[2]
    tokens = rows // 2
    sums[...] = jnp.zeros_like(sums)
    turned(kv_ref, kt, segments * (segments - 1) + depth + 1, KEYS)
    for seg in range(segments):
        here = pl.ds(seg * tokens, tokens)

        def stacked(ref):
            value = ref[here, :]
            return jnp.concatenate([value[:, :SIZE], value[:, SIZE:]], axis=0)

        query_t = qt_ref[seg]
        query = query_t.T
        grad = stacked(do_ref)
        grad_t = grad.T
        delta = jnp.sum(
            grad_t.astype(F32) * stacked(o_ref).T.astype(F32), axis=0, keepdims=True
        )
        begin = begin_ref[seg]
        slot = slot_ref[seg]
        lse = lse_ref[seg]
        accum[...] = jnp.zeros_like(accum)

        @pl.loop(0, segments * seg + depth + 1)
        def _(block):
            at = pl.multiple_of(block * BLOCK, BLOCK)
            keys = pl.ds(at, BLOCK)
            scores = dot(kv_ref[keys, KEYS], query_t)
            key = lax.broadcasted_iota(jnp.int32, scores.shape, 0) + at
            allowed = (key >= begin) & (key <= slot)
            probs = jnp.where(allowed, jnp.exp(scores - lse), 0.0)
            grad_probs = dot(kv_ref[keys, VALUES], grad_t)
            grad_scores = (probs * (grad_probs - delta)).astype(BF)
            sums[keys, VALUES] += dot(probs.astype(BF), grad)
            sums[keys, KEYS] += dot(grad_scores, query)
            accum[...] += dot(kt[:, keys], grad_scores)

        cosine, sine = cos_ref[seg], sin_ref[seg]
        for head in range(2):
            part = accum[:, head * tokens : (head + 1) * tokens] * (SIZE ** -0.5)
            lower, upper = part[:HALF], part[HALF:]
            turn = jnp.concatenate(
                [lower * cosine + upper * sine, upper * cosine - lower * sine], axis=0
            )
            dq_ref[here, head * SIZE : (head + 1) * SIZE] = turn.T.astype(BF)

    dkv_ref[...] = sums[...].astype(BF)


def attend_back(qt, do, o, kv, begin, slot, lse, cosine, sine):
    segments, _, rows = slot.shape
    return pl.pallas_call(
        attend_back_kernel,
        name="attend_back",
        out_shape=(
            jax.ShapeDtypeStruct(do.shape, BF),
            jax.ShapeDtypeStruct(kv.shape, BF),
        ),
        in_specs=[pl.BlockSpec(memory_space=pltpu.VMEM)] * 9,
        out_specs=[pl.BlockSpec(memory_space=pltpu.VMEM)] * 2,
        scratch_shapes=[
            pltpu.VMEM((SIZE, kv.shape[0]), BF),
            pltpu.VMEM(kv.shape, F32),
            pltpu.VMEM((SIZE, rows), F32),
        ],
        compiler_params=pltpu.CompilerParams(vmem_limit_bytes=48 << 20),
    )(qt, do, o, kv, begin, slot, lse, cosine, sine)


MESH_IDS = pl.DeviceIdType.MESH
AXES = ("x", "y", "z", "c")
ANYWHERE = pl.BlockSpec(memory_space=pl.ANY)
IN_VMEM = pl.BlockSpec(memory_space=pltpu.VMEM)


def place():
    return {a: lax.axis_index(a) for a in AXES}


def along(axis, step):
    size = lax.axis_size(axis)
    return lax.rem(lax.axis_index(axis) + (step + size), size)


def device(axis, step):
    here = place()
    here[axis] = along(axis, step)
    return tuple(here[a] for a in AXES)


class Net:
    def __init__(self, sends, arrivals, locals_):
        self.sends, self.arrivals, self.locals_ = sends, arrivals, locals_
        self.used = 0
        self.near = 0
        self.open = []

    def send(self, source, target, axis, step):
        copy = pltpu.make_async_remote_copy(
            src_ref=source, dst_ref=target, send_sem=self.sends.at[self.used],
            recv_sem=self.arrivals.at[self.used], device_id=device(axis, step),
            device_id_type=MESH_IDS,
        )
        copy.start()
        self.used += 1
        self.open.append(copy)
        return copy

    def keep(self, source, target):
        copy = pltpu.make_async_copy(source, target, self.locals_.at[self.near])
        copy.start()
        self.near += 1
        return copy

    def close(self):
        for copy in self.open:
            copy.wait_send()


def greet(partners):
    barrier = pltpu.get_barrier_semaphore()
    for axis, step in partners:
        pl.semaphore_signal(barrier, 1, device_id=device(axis, step), device_id_type=MESH_IDS)
    pl.semaphore_wait(barrier, len(partners))


def semaphores(sends, locals_):
    return [
        pltpu.SemaphoreType.DMA((sends,)),
        pltpu.SemaphoreType.DMA((sends,)),
        pltpu.SemaphoreType.DMA((max(locals_, 1),)),
    ]


def comm_call(body, name, number, outs, ins, scratch, sends, locals_, spaces, out_spaces):
    return pl.pallas_call(
        body,
        name=name,
        out_shape=outs,
        in_specs=spaces,
        out_specs=out_spaces,
        scratch_shapes=list(scratch) + semaphores(sends, locals_),
        compiler_params=pltpu.CompilerParams(
            collective_id=number, has_side_effects=True, vmem_limit_bytes=56 << 20
        ),
    )(*ins)


LINE = (1, 2, 3)


class RowGather:
    def __init__(self, net, value, out):
        self.net, self.out = net, out
        h = value.shape[0] // 2
        self.parts = (pl.ds(0, h), pl.ds(h, h))
        y, z, c = (lax.axis_index(a) for a in ROW)
        self.mine = net.keep(value, out.at[y, z, c])
        self.own = net.send(value, out.at[y, z, c], "c", 1)
        self.first = [
            [net.send(value.at[part], out.at[y, z, c, part], axis, d) for d in LINE]
            for part, axis in zip(self.parts, ("z", "y"))
        ]

    def spread(self):
        net, out = self.net, self.out
        y, z, c = (lax.axis_index(a) for a in ROW)
        self.mine.wait()
        (a, b) = self.parts
        for copy in self.first[0]:
            copy.wait_recv()
        self.second = [
            [net.send(out.at[y, :, c, a], out.at[y, :, c, a], "y", d) for d in LINE]
        ]
        for copy in self.first[1]:
            copy.wait_recv()
        self.second.append(
            [net.send(out.at[:, z, c, b], out.at[:, z, c, b], "z", d) for d in LINE]
        )
        self.shared = [self.own]
        for d in LINE:
            spot = out.at[y, along("z", -d), c, a]
            self.shared.append(net.send(spot, spot, "c", 1))
            spot = out.at[along("y", -d), z, c, b]
            self.shared.append(net.send(spot, spot, "c", 1))

    def finish(self):
        net, out = self.net, self.out
        y, z, c = (lax.axis_index(a) for a in ROW)
        (a, b) = self.parts
        for d in LINE:
            self.second[0][d - 1].wait_recv()
            spot = out.at[along("y", -d), :, c, a]
            self.shared.append(net.send(spot, spot, "c", 1))
            self.second[1][d - 1].wait_recv()
            spot = out.at[:, along("z", -d), c, b]
            self.shared.append(net.send(spot, spot, "c", 1))
        for copy in self.shared:
            copy.wait_recv()


class RingGather:
    def __init__(self, net, value, out, axis):
        self.net, self.out, self.axis = net, out, axis
        a, c = lax.axis_index(axis), lax.axis_index("c")
        h = value.shape[0] // 2
        self.parts = one, two = pl.ds(0, h), pl.ds(h, h)
        self.mine = net.keep(value, out.at[a, c])
        self.right = [net.send(value.at[p], out.at[a, c, p], axis, 1) for p in (one, two)]
        self.left = [net.send(value.at[p], out.at[a, c, p], axis, -1) for p in (two, one)]
        self.shared = [net.send(value, out.at[a, c], "c", 1)]

    def spread(self):
        net, out, axis = self.net, self.out, self.axis
        c = lax.axis_index("c")
        one, two = self.parts
        before, after = along(axis, -1), along(axis, 1)
        self.right[0].wait_recv()
        spot = out.at[before, c, one]
        self.far = [net.send(spot, spot, axis, 1)]
        self.left[0].wait_recv()
        spot = out.at[after, c, two]
        self.far.append(net.send(spot, spot, axis, -1))
        for copies, where in ((self.right, before), (self.left, after)):
            copies[1].wait_recv()
            spot = out.at[where, c]
            self.shared.append(net.send(spot, spot, "c", 1))

    def finish(self):
        for copy in self.far:
            copy.wait_recv()
        spot = self.out.at[along(self.axis, 2), lax.axis_index("c")]
        self.shared.append(self.net.send(spot, spot, "c", 1))
        for copy in self.shared:
            copy.wait_recv()
        self.mine.wait()


STEP = 16


def rows_loop(count, body):
    pl.loop(0, count // STEP)(lambda i: body(pl.ds(pl.multiple_of(i * STEP, STEP), STEP)))


def shifted(rows, first):
    return pl.ds(pl.multiple_of(rows.start + first, STEP), STEP)


class RingSum:
    def __init__(self, net, value, out, axis, near, relay, come, go):
        self.net, self.value, self.out, self.axis = net, value, out, axis
        self.near, self.relay, self.come, self.go = near, relay, come, go
        c = lax.axis_index("c")
        self.size = value.shape[2]
        h = self.size // 2
        self.parts = pl.ds(0, h), pl.ds(h, h)
        self.swaps = {
            s: net.send(value.at[along(axis, s), 1 - c], near.at[s], "c", 1) for s in (2, 1, 3, 0)
        }

    def pair(self, s, part=None):
        value, near, go = self.value, self.near, self.go
        where, c = along(self.axis, s), lax.axis_index("c")
        first = 0 if part is None else part.start
        count = self.size if part is None else part.size

        def add(rows):
            at = shifted(rows, first)
            go[s, at] = (
                value[where, c, at].astype(F32) + near[s, at].astype(F32)
            ).astype(BF)

        rows_loop(count, add)

    def relay_far(self):
        net = self.net
        one, two = self.parts
        self.swaps[2].wait_recv()
        self.pair(2)
        self.relays = [
            net.send(self.go.at[2, one], self.relay.at[0], self.axis, 1),
            net.send(self.go.at[2, two], self.relay.at[1], self.axis, -1),
        ]

    def spread(self):
        net, go, relay, come = self.net, self.go, self.relay, self.come
        one, two = self.parts
        self.swaps[1].wait_recv()
        self.pair(1)
        self.ends = [net.send(go.at[1, two], come.at[0, two], self.axis, 1)]
        self.swaps[3].wait_recv()
        self.pair(3)
        self.ends.append(net.send(go.at[3, one], come.at[1, one], self.axis, -1))
        for i, (s, part, step) in enumerate(((1, one, 1), (3, two, -1))):
            self.relays[i].wait_recv()

            def add(rows, i=i, s=s, part=part):
                at = shifted(rows, part.start)
                go[s, at] = (go[s, at].astype(F32) + relay[i, rows].astype(F32)).astype(BF)

            rows_loop(part.size, add)
            self.ends.append(net.send(go.at[s, part], come.at[i, part], self.axis, step))

    def finish(self):
        value, near, come, out = self.value, self.near, self.come, self.out
        where, c = lax.axis_index(self.axis), lax.axis_index("c")
        self.swaps[0].wait_recv()
        for copy in self.ends:
            copy.wait_recv()

        def add(rows):
            out[rows] = (
                value[where, c, rows].astype(F32) + near[0, rows].astype(F32)
            ) + (come[0, rows].astype(F32) + come[1, rows].astype(F32))

        rows_loop(self.size, add)


def ring_sum_scratch(size, width):
    return [
        pltpu.VMEM((4, size, width), BF),
        pltpu.VMEM((2, size // 2, width), BF),
        pltpu.VMEM((2, size, width), BF),
        pltpu.VMEM((4, size, width), BF),
    ]


class RowSum:
    def __init__(self, net, value, out, near, go, first, mid, last):
        self.net, self.value, self.out = net, value, out
        self.near, self.go, self.first, self.mid, self.last = near, go, first, mid, last
        c = lax.axis_index("c")
        self.size = value.shape[3]
        h = self.size // 2
        self.parts = pl.ds(0, h), pl.ds(h, h)
        self.swaps = [
            net.send(value.at[i, :, 1 - c], near.at[i], "c", 1) for i in range(4)
        ]

    def start(self):
        net, value, near, go = self.net, self.value, self.near, self.go
        c = lax.axis_index("c")
        for i in range(4):
            self.swaps[i].wait_recv()
            for j in range(4):

                def add(rows, i=i, j=j):
                    go[i, j, rows] = (
                        value[i, j, c, rows].astype(F32) + near[i, j, rows].astype(F32)
                    ).astype(BF)

                rows_loop(self.size, add)
        a, b = self.parts
        self.ones = [
            [net.send(go.at[along("y", d), :, a], self.first.at[0, d - 1], "y", d) for d in LINE],
            [net.send(go.at[:, along("z", d), b], self.first.at[1, d - 1], "z", d) for d in LINE],
        ]

    def turn(self):
        net, go, first, mid = self.net, self.go, self.first, self.mid
        y, z = lax.axis_index("y"), lax.axis_index("z")
        self.twos = []
        for k, axis in enumerate(("z", "y")):
            for copy in self.ones[k]:
                copy.wait_recv()
            for j in range(4):

                def add(rows, k=k, j=j):
                    at = shifted(rows, self.parts[k].start)
                    own = go[y, j, at] if k == 0 else go[j, z, at]
                    mid[k, j, rows] = (
                        own.astype(F32) + first[k, 0, j, rows].astype(F32)
                        + (first[k, 1, j, rows].astype(F32) + first[k, 2, j, rows].astype(F32))
                    ).astype(BF)

                rows_loop(self.parts[k].size, add)
            self.twos.append(
                [net.send(mid.at[k, along(axis, d)], self.last.at[k, d - 1], axis, d) for d in LINE]
            )

    def finish(self):
        mid, last, out = self.mid, self.last, self.out
        for k, axis in enumerate(("z", "y")):
            for copy in self.twos[k]:
                copy.wait_recv()
            here = lax.axis_index(axis)

            def add(rows, k=k, here=here):
                at = shifted(rows, self.parts[k].start)
                out[at] = (
                    mid[k, here, rows].astype(F32) + last[k, 0, rows].astype(F32)
                    + (last[k, 1, rows].astype(F32) + last[k, 2, rows].astype(F32))
                )

            rows_loop(self.parts[k].size, add)


def row_sum_scratch(size, width):
    h = size // 2
    return [
        pltpu.VMEM((4, 4, size, width), BF),
        pltpu.VMEM((4, 4, size, width), BF),
        pltpu.VMEM((2, 3, 4, h, width), BF),
        pltpu.VMEM((2, 4, h, width), BF),
        pltpu.VMEM((2, 3, h, width), BF),
    ]


Y_LINE = [("y", d) for d in LINE]
Z_LINE = [("z", d) for d in LINE]
X_RING = [("x", 1), ("x", -1)]
Y_RING = [("y", 1), ("y", -1)]
TWIN = [("c", 1)]


def shape(*dims, kind=BF):
    return jax.ShapeDtypeStruct(dims, kind)


def first_weights(first, up, both):
    def body(first_ref, up_ref, both_ref, first_out, up_out, both_out, transit, sends, arrivals, locals_):
        net = Net(sends, arrivals, locals_)
        y, z, c = (lax.axis_index(a) for a in ROW)
        greet(Y_LINE + Z_LINE + TWIN)
        row = RowGather(net, first_ref, first_out)
        up_mine = net.keep(up_ref.at[y], transit.at[y, z])
        ups = [net.send(up_ref.at[along("y", d)], transit.at[y, z], "y", d) for d in LINE]
        both_mine = net.keep(both_ref.at[c], both_out.at[c])
        both_come = net.send(both_ref.at[1 - c], both_out.at[c], "c", 1)
        row.spread()
        up_mine.wait()
        for copy in ups:
            copy.wait_recv()
        ups = [net.send(transit.at[:, z], transit.at[:, z], "z", d) for d in LINE]
        row.finish()
        for copy in ups:
            copy.wait_recv()
        up_keep = net.keep(transit.at[:, :, c], up_out.at[:, :, c])
        up_come = net.send(transit.at[:, :, 1 - c], up_out.at[:, :, c], "c", 1)
        both_mine.wait()
        both_come.wait_recv()
        up_keep.wait()
        up_come.wait_recv()
        net.close()

    _, per, high, thin = up.shape
    outs = (
        shape(4, 4, 2, *first.shape), shape(4, 4, 2, high, thin), shape(*both.shape),
        shape(4, 4, 2, high, thin),
    )
    return comm_call(
        body, "first_weights", 1, outs, (first, up, both), [], 40, 4, [ANYWHERE] * 3, [ANYWHERE] * 4,
    )[:3]


def keys_and_latents(key_value, latent):
    def body(kv_ref, lat_ref, kv_out, lat_out, sends, arrivals, locals_):
        net = Net(sends, arrivals, locals_)
        greet(Y_LINE + Z_LINE + TWIN)
        row = RowGather(net, kv_ref, kv_out)
        ring = RingGather(net, lat_ref, lat_out, "y")
        row.spread()
        ring.spread()
        row.finish()
        ring.finish()
        net.close()

    outs = (shape(4, 4, 2, *key_value.shape), shape(4, 2, *latent.shape))
    return comm_call(
        body, "keys_and_latents", 2, outs, (key_value, latent), [], 40, 2, [ANYWHERE] * 2, [ANYWHERE] * 2,
    )


def heads_sum_and_cotangent(partial, cotangent):
    def body(part_ref, cot_ref, out_ref, cot_out, near, relay, come, go, sends, arrivals, locals_):
        net = Net(sends, arrivals, locals_)
        greet(X_RING + Y_RING + TWIN)
        ring = RingSum(net, part_ref, out_ref, "y", near, relay, come, go)
        feed = RingGather(net, cot_ref, cot_out, "x")
        ring.relay_far()
        ring.spread()
        feed.spread()
        ring.finish()
        feed.finish()
        net.close()

    size, width = cotangent.shape
    outs = (shape(size, width, kind=F32), shape(4, 2, size, width))
    return comm_call(
        body, "heads_sum_and_cotangent", 3, outs, (partial, cotangent), ring_sum_scratch(size, width), 20, 2,
        [IN_VMEM, ANYWHERE], [IN_VMEM, ANYWHERE],
    )


def feed_gather(normed_two, normed):
    def body(two_ref, one_ref, two_out, one_out, sends, arrivals, locals_):
        net = Net(sends, arrivals, locals_)
        y, c = lax.axis_index("y"), lax.axis_index("c")
        tall = one_ref.shape[1] // 4
        greet(X_RING + Y_LINE + TWIN)
        feed = RingGather(net, two_ref, two_out, "x")
        mine = net.keep(one_ref.at[:, pl.ds(pl.multiple_of(y * tall, tall), tall)], one_out.at[y, c])
        ones = [
            net.send(
                one_ref.at[:, pl.ds(pl.multiple_of(along("y", d) * tall, tall), tall)],
                one_out.at[y, c], "y", d,
            )
            for d in LINE
        ]
        feed.spread()
        mine.wait()
        spot = one_out.at[y, c]
        shared = [net.send(spot, spot, "c", 1)]
        for d in LINE:
            ones[d - 1].wait_recv()
            spot = one_out.at[along("y", -d), c]
            shared.append(net.send(spot, spot, "c", 1))
        feed.finish()
        for copy in shared:
            copy.wait_recv()
        net.close()

    size, width = normed_two.shape
    outs = (shape(4, 2, size, width), shape(4, 2, size, width // 4))
    return comm_call(
        body, "feed_gather", 4, outs, (normed_two, normed), [], 20, 2, [ANYWHERE] * 2, [ANYWHERE] * 2,
    )


def feed_sum(partial, partial_two):
    def body(one_ref, two_ref, one_out, two_out, *rest):
        net = Net(*rest[8:])
        greet(X_RING + TWIN)
        one = RingSum(net, one_ref, one_out, "x", *rest[:4])
        two = RingSum(net, two_ref, two_out, "x", *rest[4:8])
        one.relay_far()
        one.spread()
        two.relay_far()
        two.spread()
        one.finish()
        two.finish()
        net.close()

    _, _, size, width = partial.shape
    outs = (shape(size, width, kind=F32),) * 2
    return comm_call(
        body, "feed_sum", 5, outs, (partial, partial_two), ring_sum_scratch(size, width) * 2, 24, 0,
        [IN_VMEM] * 2, [IN_VMEM] * 2,
    )


def heads_gather(value):
    def body(ref, out, sends, arrivals, locals_):
        net = Net(sends, arrivals, locals_)
        greet(Y_RING + TWIN)
        ring = RingGather(net, ref, out, "y")
        ring.spread()
        ring.finish()
        net.close()

    return comm_call(
        body, "heads_gather", 6, shape(4, 2, *value.shape), (value,), [], 12, 2, [ANYWHERE], ANYWHERE,
    )


def keys_and_latents_sum(grad_kv, partial):
    def body(kv_ref, part_ref, kv_out, part_out, *rest):
        net = Net(*rest[9:])
        greet(Y_LINE + Z_LINE + TWIN)
        row = RowSum(net, kv_ref, kv_out, *rest[:5])
        ring = RingSum(net, part_ref, part_out, "y", *rest[5:9])
        row.start()
        ring.relay_far()
        ring.spread()
        row.turn()
        ring.finish()
        row.finish()
        net.close()

    _, _, _, size, thin = grad_kv.shape
    width = partial.shape[3]
    outs = (shape(size, thin, kind=F32), shape(size, width, kind=F32))
    return comm_call(
        body, "keys_and_latents_sum", 7, outs, (grad_kv, partial),
        row_sum_scratch(size, thin) + ring_sum_scratch(size, width), 28, 0, [IN_VMEM] * 2, [IN_VMEM] * 2,
    )


def firsts_gather(value):
    def body(ref, out, sends, arrivals, locals_):
        net = Net(sends, arrivals, locals_)
        y, c = lax.axis_index("y"), lax.axis_index("c")
        greet(Y_RING + TWIN)
        mine = net.keep(ref.at[c], out.at[y, c])
        come = net.send(ref.at[1 - c], out.at[y, c], "c", 1)
        mine.wait()
        spot = out.at[y, c]
        ahead = [net.send(spot, spot, "y", 1), net.send(spot, spot, "y", -1)]
        come.wait_recv()
        spot = out.at[y, 1 - c]
        ahead += [net.send(spot, spot, "y", 1), net.send(spot, spot, "y", -1)]
        ahead[0].wait_recv()
        spot = out.at[along("y", -1), c]
        ahead.append(net.send(spot, spot, "y", 1))
        ahead[3].wait_recv()
        spot = out.at[along("y", 1), 1 - c]
        ahead.append(net.send(spot, spot, "y", -1))
        for i in (1, 2, 4, 5):
            ahead[i].wait_recv()
        net.close()

    return comm_call(
        body, "firsts_gather", 8, shape(4, *value.shape), (value,), [], 12, 2, [ANYWHERE], ANYWHERE,
    )


def gather(value, axes):
    return lax.all_gather(value, axes, axis=0, tiled=True)


def scatter_sum(value, axes):
    return lax.psum_scatter(value, axes, scatter_dimension=0, tiled=True)


def swap(value, axes):
    return lax.all_to_all(value, axes, 0, 0, tiled=True)


def on_device(
    block_input, cotangent, lengths, norm_gain, q_down, q_gain, q_up, key_weight, value_weight,
    out_weight, ffn_gain, gate_weight, up_weight, down_weight,
):
    rows, width = block_input.shape
    latent_width = q_down.shape[1]
    n_x, n_y, n_z, n_c = (lax.axis_size(a) for a in ("x", "y", "z", "c"))
    x, y, z, c = (lax.axis_index(a) for a in ("x", "y", "z", "c"))
    span = n_y * n_z * n_c
    members = n_y * n_c
    lengths_row = lengths[0]

    mine = (y * n_z + z) * n_c + c
    slots_mine = mine * rows + jnp.arange(rows, dtype=jnp.int32)
    begin_mine, _ = places_of(lengths_row, slots_mine)
    cosine, sine = tables(slots_mine - begin_mine)
    strip = n_c * rows
    slots_group = (
        (jnp.arange(n_y, dtype=jnp.int32)[:, None] * n_z + z) * strip
        + jnp.arange(strip, dtype=jnp.int32)[None, :]
    ).reshape(-1)
    begin_group, live_group = places_of(lengths_row, slots_group)
    cosine_group, sine_group = tables_across((slots_group - begin_group).reshape(n_y, strip))
    begin_lanes = jnp.tile(begin_group.reshape(n_y, 1, strip), (1, 1, 2))
    slot_lanes = jnp.tile(slots_group.reshape(n_y, 1, strip), (1, 1, 2))
    live_lanes = jnp.tile(live_group.reshape(n_y, 1, strip), (1, 1, 2))

    shard = norm_gain.shape[0]
    extra = jnp.stack(
        [norm_gain, ffn_gain, jnp.pad(q_gain, (0, shard - q_gain.shape[0]))], axis=1
    ).astype(BF)
    first_width = latent_width + 2 * SIZE
    first = jnp.concatenate(
        [q_down, key_weight, value_weight, jnp.pad(extra, ((0, 0), (0, 125)))], axis=1
    )
    per_heads = q_up.shape[1] // members
    q_rows = q_up.shape[0]
    out_chip = gather(out_weight, ("z", "c"))
    out_heads = lax.dynamic_slice_in_dim(out_chip, c * per_heads, per_heads)

    wide = gate_weight.shape[1]
    down_rows = down_weight.shape[0]
    share = down_rows // n_x
    padded = -(-share // 16) * 16
    source = lax.broadcasted_iota(jnp.int32, (wide // 2, n_c * (span // 4) * padded), 0)
    target = lax.broadcasted_iota(jnp.int32, source.shape, 1)
    block_at = target // (padded * (span // 4)) + n_c * ((target // padded) % (span // 4))
    inside = target % padded
    picks = (
        (source == block_at * down_rows + x * share + inside) & (inside < share)
    ).astype(BF)

    def spread(weight):
        stacked = jnp.concatenate([weight[:, : wide // 2], weight[:, wide // 2 :]], axis=0)
        part = dot(stacked, picks).astype(BF)
        part = part.reshape(2, shard, n_c, -1).transpose(2, 1, 0, 3)
        return part.reshape(n_c, shard, -1)

    both = jnp.concatenate([spread(gate_weight), spread(up_weight)], axis=2)
    units = both.shape[-1] // 2
    up_sent = q_up.reshape(q_rows, n_y, n_c, per_heads).transpose(1, 2, 0, 3)
    first_full, up_heads, both = first_weights(first, up_sent, both)
    first_full = first_full.reshape(span * shard, -1)
    up_heads = up_heads.reshape(span * q_rows, per_heads)
    both = both.reshape(n_c * shard, 2 * units)
    extra_full = first_full[:, first_width : first_width + 3].astype(F32)
    first_full = first_full[:, :first_width]
    gain_one = extra_full[:, 0]
    gain_two = extra_full[:, 1]
    gain_latent = extra_full[:, 2].reshape(span, shard)[:, : q_gain.shape[0]].reshape(-1)

    both_full = gather(both, ("y", "z"))
    gate_use, up_use = both_full[:, :units], both_full[:, units:]
    down_part = lax.dynamic_slice_in_dim(down_weight, x * share, share)
    down_part = jnp.pad(down_part, ((0, padded - share), (0, 0)))
    down_use = gather(down_part, ("y", "z"))

    inputs = block_input.astype(F32)
    inverse_one = lax.rsqrt(jnp.mean(inputs * inputs, axis=-1, keepdims=True) + EPSILON)
    normed = (inputs * inverse_one * gain_one).astype(BF)
    firsts = dot(normed, first_full)
    latent = firsts[:, :latent_width]
    inverse_latent = lax.rsqrt(jnp.mean(latent * latent, axis=-1, keepdims=True) + EPSILON)
    latent_normed = (latent * inverse_latent * gain_latent).astype(BF)
    key_mine = rotate(firsts[:, latent_width : latent_width + SIZE], cosine, sine).astype(BF)
    value_mine = firsts[:, latent_width + SIZE :].astype(BF)
    key_value, latent_group = keys_and_latents(
        jnp.concatenate([key_mine, value_mine], axis=1), latent_normed
    )
    key_value = key_value.reshape(span * rows, 2 * SIZE)
    group = members * rows
    latent_group = latent_group.reshape(group, latent_width)
    mixed, queries_t, lse = attend(
        dot(latent_group, up_heads), key_value, begin_lanes, slot_lanes, live_lanes,
        cosine_group, sine_group,
    )
    branch, grad_feed = heads_sum_and_cotangent(
        dot(mixed, out_heads).astype(BF).reshape(n_y, n_c, rows, width), cotangent
    )
    grad_feed = grad_feed.reshape(group, width)
    middle = inputs + branch

    inverse_two = lax.rsqrt(jnp.mean(middle * middle, axis=-1, keepdims=True) + EPSILON)
    normed_two, normed_part = feed_gather((middle * inverse_two * gain_two).astype(BF), normed)
    normed_two = normed_two.reshape(group, width)
    normed_part = normed_part.reshape(group, -1)
    gate_pre = dot(normed_two, gate_use)
    up_pre = dot(normed_two, up_use)
    sigma = jax.nn.sigmoid(gate_pre)
    hidden = (gate_pre * sigma * up_pre).astype(BF)
    grad_hidden = dot_nt(grad_feed, down_use)
    grad_gate_pre = (grad_hidden * up_pre * sigma * (1.0 + gate_pre * (1.0 - sigma))).astype(BF)
    grad_up_pre = (grad_hidden * gate_pre * sigma).astype(BF)
    grad_normed_two, branch_two = feed_sum(
        (dot_nt(grad_gate_pre, gate_use) + dot_nt(grad_up_pre, up_use))
        .astype(BF)
        .reshape(n_x, n_c, rows, width),
        dot(hidden, down_use).astype(BF).reshape(n_x, n_c, rows, width),
    )
    output = (middle + branch_two).astype(BF)
    grad_result = cotangent.astype(F32)
    grad_mid_norm, grad_gain_two = norm_back(middle, inverse_two, gain_two, grad_normed_two)
    grad_middle = grad_result + grad_mid_norm
    grad_both = jnp.concatenate(
        [dot_tn(normed_two, grad_gate_pre), dot_tn(normed_two, grad_up_pre)], axis=1
    ).astype(BF)
    grad_both = scatter_sum(grad_both, ("y", "z"))
    grad_down = scatter_sum(dot_tn(hidden, grad_feed).astype(BF), ("y", "z"))
    grad_both = grad_both.reshape(n_c, shard, 2, units).transpose(0, 2, 1, 3)
    grad_both = swap(grad_both, "c")
    grad_both = gather(grad_both.reshape(1, n_c, 2, shard, units), "x")
    grad_down = gather(grad_down[None], "x")

    def collect(grads):
        parts = grads.reshape(n_x, n_c, shard, 2, units // 2).transpose(0, 3, 2, 1, 4)
        parts = parts.reshape(n_x, 2 * shard, n_c * units // 2)
        whole = 0.0
        for i in range(n_x):
            picked = (
                (source == block_at * down_rows + i * share + inside) & (inside < share)
            ).astype(BF)
            whole = whole + dot_nt(parts[i], picked)
        return jnp.concatenate([whole[:shard], whole[shard:]], axis=1)

    grad_gate = collect(grad_both[:, :, 0])
    grad_up = collect(grad_both[:, :, 1])
    grad_down = grad_down[:, :share].reshape(down_rows, width).astype(F32)

    grad_branch = heads_gather(grad_middle.astype(BF)).reshape(group, width)
    grad_mixed = dot_nt(grad_branch, out_heads).astype(BF)
    grad_attended = grad_mixed * live_group[:, None].astype(BF)
    grad_out = dot_tn(mixed, grad_branch).astype(BF)
    grad_query_raw, grad_kv = attend_back(
        queries_t, grad_attended, mixed, key_value, begin_lanes, slot_lanes, lse,
        cosine_group, sine_group,
    )
    grad_kv, grad_latent_normed = keys_and_latents_sum(
        grad_kv.reshape(n_y, n_z, n_c, rows, 2 * SIZE),
        dot_nt(grad_query_raw, up_heads).astype(BF).reshape(n_y, n_c, rows, latent_width),
    )
    grad_key_raw = unrotate(grad_kv[:, :SIZE], cosine, sine).astype(BF)
    grad_value_raw = grad_kv[:, SIZE:].astype(BF)
    grad_up_heads = dot_tn(latent_group, grad_query_raw).astype(BF)
    grad_latent_f, grad_gain_latent = norm_back(
        latent, inverse_latent, gain_latent, grad_latent_normed
    )
    grad_firsts = jnp.concatenate(
        [grad_latent_f.astype(BF), grad_key_raw, grad_value_raw], axis=1
    )
    grad_normed = dot_nt(grad_firsts, first_full)
    grad_input_norm, grad_gain_one = norm_back(inputs, inverse_one, gain_one, grad_normed)
    input_grad = grad_middle + grad_input_norm

    half_first = first_width // n_c
    first_part = firsts_gather(
        grad_firsts.reshape(rows, n_c, half_first).transpose(1, 0, 2)
    ).reshape(group, half_first)
    grad_first = dot_tn(normed_part, first_part).astype(BF)

    out_rows = out_weight.shape[0]
    grad_out = grad_out.reshape(n_z // n_c, n_c, out_rows, width).transpose(1, 0, 2, 3)
    grad_out = swap(grad_out, "c").reshape(n_z, out_rows * width)
    grad_first = grad_first.reshape(n_z, n_c, shard, half_first).transpose(1, 0, 2, 3)
    grad_first = swap(grad_first, "c").transpose(1, 2, 0, 3).reshape(n_z, shard * first_width)
    grad_up_heads = grad_up_heads.reshape(n_y, n_z, n_c, q_rows, per_heads)
    grad_up_heads = grad_up_heads.transpose(0, 2, 1, 3, 4).reshape(members, n_z, q_rows, per_heads)
    grad_up_heads = swap(grad_up_heads, HEADS).transpose(1, 2, 0, 3).reshape(n_z, -1)
    pieces = jnp.concatenate([grad_out, grad_first, grad_up_heads], axis=1)
    pieces = lax.psum(scatter_sum(pieces, "z"), "x").astype(F32)[0]
    at_first = out_rows * width
    at_up = at_first + shard * first_width
    grad_out = pieces[:at_first].reshape(out_rows, width)
    grad_first = pieces[at_first:at_up].reshape(shard, first_width)
    grad_q_up = pieces[at_up:].reshape(q_rows, -1)

    gains = jnp.concatenate(
        [
            grad_gain_one.reshape(span, shard),
            grad_gain_two.reshape(span, shard),
            grad_gain_latent.reshape(span, -1),
        ],
        axis=1,
    )
    gains = lax.psum(scatter_sum(gains, ROW), "x")[0]
    return (
        output,
        input_grad,
        gains[:shard],
        grad_first[:, :latent_width],
        gains[2 * shard :],
        grad_q_up,
        grad_first[:, latent_width : latent_width + SIZE],
        grad_first[:, latent_width + SIZE :],
        grad_out,
        gains[shard : 2 * shard],
        grad_gate,
        grad_up,
        grad_down,
    )


def solution(mesh):
    sizes = (4, 4, 4, 2)
    grid = Mesh(mesh.devices.reshape(sizes), ("x", "y", "z", "c"))
    tokens = P(("x", "y", "z", "c"), None)
    wide, thin = P(ROW, None), P(ROW)
    in_specs = (
        tokens, tokens, P("x", None), thin, wide, thin, wide, wide, wide, wide, thin, wide, wide,
        wide,
    )
    out_specs = (
        tokens, tokens, thin, wide, thin, wide, wide, wide, wide, thin, wide, wide, wide,
    )
    return jax.shard_map(
        on_device, mesh=grid, in_specs=in_specs, out_specs=out_specs, check_vma=False
    )
```

```python
import functools
import math

import jax
import jax.numpy as jnp
from jax import lax
from jax.experimental import pallas as pl
from jax.experimental.pallas import tpu as pltpu
from jax.sharding import Mesh
from jax.sharding import PartitionSpec as P

EPSILON = 1e-06
MASKED = -1e30
BF = jnp.bfloat16
F32 = jnp.float32
SIZE = 256
HALF = 128
BLOCK = 256
ROW = ("y", "z", "c")
HEADS = ("y", "c")
FEED = ("x", "c")


def dot(left, right):
    return jnp.dot(left, right, preferred_element_type=F32)


def dot_tn(left, right):
    return lax.dot_general(left, right, (((0,), (0,)), ((), ())), preferred_element_type=F32)


def dot_nt(left, right):
    return lax.dot_general(left, right, (((1,), (1,)), ((), ())), preferred_element_type=F32)


def norm_back(values, inverse, gain, grad):
    scaled = grad * gain
    grad_values = inverse * scaled - values * inverse * inverse * inverse * jnp.mean(
        scaled * values, axis=-1, keepdims=True
    )
    return grad_values, jnp.sum(grad * values * inverse, axis=0)


def places_of(lengths_row, slots):
    ends = jnp.cumsum(lengths_row)
    begins = jnp.concatenate([ends - lengths_row, ends[-1:]])
    begin = jnp.max(jnp.where(slots[:, None] >= begins[None, :], begins[None, :], 0), axis=1)
    live = (slots < ends[-1]).astype(F32)
    return begin, live


def tables(position):
    freq = jnp.exp(jnp.arange(HALF, dtype=F32) * (-math.log(10000.0) / HALF))
    angle = position.astype(F32)[:, None] * freq[None, :]
    return jnp.cos(angle), jnp.sin(angle)


def tables_across(position):
    freq = jnp.exp(jnp.arange(HALF, dtype=F32) * (-math.log(10000.0) / HALF))
    angle = position.astype(F32)[..., None, :] * freq[:, None]
    return jnp.cos(angle), jnp.sin(angle)


def rotate(values, cosine, sine):
    lower, upper = values[..., :HALF], values[..., HALF:]
    return jnp.concatenate([lower * cosine - upper * sine, upper * cosine + lower * sine], axis=-1)


def unrotate(grad, cosine, sine):
    lower, upper = grad[..., :HALF], grad[..., HALF:]
    return jnp.concatenate([lower * cosine + upper * sine, upper * cosine - lower * sine], axis=-1)


def turned(source, target, count, columns):
    @pl.loop(0, count)
    def _(block):
        at = pl.ds(pl.multiple_of(block * BLOCK, BLOCK), BLOCK)
        target[:, at] = source[at, columns].T


KEYS, VALUES = slice(0, SIZE), slice(SIZE, 2 * SIZE)


def attend_kernel(
    q_ref, kv_ref, begin_ref, slot_ref, live_ref, cos_ref, sin_ref,
    out_ref, qt_ref, lse_ref, vt, peak, total, accum,
):
    depth = lax.axis_index("z")
    segments = slot_ref.shape[0]
    rows = slot_ref.shape[2]
    tokens = rows // 2
    turned(kv_ref, vt, segments * (segments - 1) + depth + 1, VALUES)
    for seg in range(segments):
        here = pl.ds(seg * tokens, tokens)
        cosine, sine = cos_ref[seg], sin_ref[seg]
        for head in range(2):
            raw = q_ref[here, head * SIZE : (head + 1) * SIZE].T
            lower, upper = raw[:HALF], raw[HALF:]
            turn = jnp.concatenate(
                [lower * cosine - upper * sine, upper * cosine + lower * sine], axis=0
            )
            qt_ref[seg, :, head * tokens : (head + 1) * tokens] = (
                turn.astype(BF) * (SIZE ** -0.5)
            ).astype(BF)
        query = qt_ref[seg]
        begin = begin_ref[seg]
        slot = slot_ref[seg]
        peak[...] = jnp.full_like(peak, MASKED)
        total[...] = jnp.zeros_like(total)
        accum[...] = jnp.zeros_like(accum)

        @pl.loop(0, segments * seg + depth + 1)
        def _(block):
            at = pl.multiple_of(block * BLOCK, BLOCK)
            scores = dot(kv_ref[pl.ds(at, BLOCK), KEYS], query)
            key = lax.broadcasted_iota(jnp.int32, scores.shape, 0) + at
            scores = jnp.where((key >= begin) & (key <= slot), scores, MASKED)
            before = peak[...]
            now = jnp.maximum(before, jnp.max(scores, axis=0, keepdims=True))
            weights = jnp.exp(scores - now)
            shrink = jnp.exp(before - now)
            peak[...] = now
            total[...] = total[...] * shrink + jnp.sum(weights, axis=0, keepdims=True)
            accum[...] = accum[...] * shrink + dot(vt[:, pl.ds(at, BLOCK)], weights.astype(BF))

        lse_ref[seg] = peak[...] + jnp.log(total[...])
        result = accum[...] * (live_ref[seg] / total[...])
        for head in range(2):
            out_ref[here, head * SIZE : (head + 1) * SIZE] = (
                result[:, head * tokens : (head + 1) * tokens].T.astype(BF)
            )


def attend(q, kv, begin, slot, live, cosine, sine):
    segments, _, rows = slot.shape
    return pl.pallas_call(
        attend_kernel,
        name="attend",
        out_shape=(
            jax.ShapeDtypeStruct(q.shape, BF),
            jax.ShapeDtypeStruct((segments, SIZE, rows), BF),
            jax.ShapeDtypeStruct((segments, 1, rows), F32),
        ),
        in_specs=[pl.BlockSpec(memory_space=pltpu.VMEM)] * 7,
        out_specs=[pl.BlockSpec(memory_space=pltpu.VMEM)] * 3,
        scratch_shapes=[
            pltpu.VMEM((SIZE, kv.shape[0]), BF),
            pltpu.VMEM((1, rows), F32),
            pltpu.VMEM((1, rows), F32),
            pltpu.VMEM((SIZE, rows), F32),
        ],
        compiler_params=pltpu.CompilerParams(vmem_limit_bytes=48 << 20),
    )(q, kv, begin, slot, live, cosine, sine)


def attend_back_kernel(
    qt_ref, do_ref, o_ref, kv_ref, begin_ref, slot_ref, lse_ref, cos_ref, sin_ref,
    dq_ref, dkv_ref, kt, sums, accum,
):
    depth = lax.axis_index("z")
    segments = slot_ref.shape[0]
    rows = slot_ref.shape[2]
    tokens = rows // 2
    sums[...] = jnp.zeros_like(sums)
    turned(kv_ref, kt, segments * (segments - 1) + depth + 1, KEYS)
    for seg in range(segments):
        here = pl.ds(seg * tokens, tokens)

        def stacked(ref):
            value = ref[here, :]
            return jnp.concatenate([value[:, :SIZE], value[:, SIZE:]], axis=0)

        query_t = qt_ref[seg]
        query = query_t.T
        grad = stacked(do_ref)
        grad_t = grad.T
        delta = jnp.sum(
            grad_t.astype(F32) * stacked(o_ref).T.astype(F32), axis=0, keepdims=True
        )
        begin = begin_ref[seg]
        slot = slot_ref[seg]
        lse = lse_ref[seg]
        accum[...] = jnp.zeros_like(accum)

        @pl.loop(0, segments * seg + depth + 1)
        def _(block):
            at = pl.multiple_of(block * BLOCK, BLOCK)
            keys = pl.ds(at, BLOCK)
            scores = dot(kv_ref[keys, KEYS], query_t)
            key = lax.broadcasted_iota(jnp.int32, scores.shape, 0) + at
            allowed = (key >= begin) & (key <= slot)
            probs = jnp.where(allowed, jnp.exp(scores - lse), 0.0)
            grad_probs = dot(kv_ref[keys, VALUES], grad_t)
            grad_scores = (probs * (grad_probs - delta)).astype(BF)
            sums[keys, VALUES] += dot(probs.astype(BF), grad)
            sums[keys, KEYS] += dot(grad_scores, query)
            accum[...] += dot(kt[:, keys], grad_scores)

        cosine, sine = cos_ref[seg], sin_ref[seg]
        for head in range(2):
            part = accum[:, head * tokens : (head + 1) * tokens] * (SIZE ** -0.5)
            lower, upper = part[:HALF], part[HALF:]
            turn = jnp.concatenate(
                [lower * cosine + upper * sine, upper * cosine - lower * sine], axis=0
            )
            dq_ref[here, head * SIZE : (head + 1) * SIZE] = turn.T.astype(BF)

    dkv_ref[...] = sums[...].astype(BF)


def attend_back(qt, do, o, kv, begin, slot, lse, cosine, sine):
    segments, _, rows = slot.shape
    return pl.pallas_call(
        attend_back_kernel,
        name="attend_back",
        out_shape=(
            jax.ShapeDtypeStruct(do.shape, BF),
            jax.ShapeDtypeStruct(kv.shape, BF),
        ),
        in_specs=[pl.BlockSpec(memory_space=pltpu.VMEM)] * 9,
        out_specs=[pl.BlockSpec(memory_space=pltpu.VMEM)] * 2,
        scratch_shapes=[
            pltpu.VMEM((SIZE, kv.shape[0]), BF),
            pltpu.VMEM(kv.shape, F32),
            pltpu.VMEM((SIZE, rows), F32),
        ],
        compiler_params=pltpu.CompilerParams(vmem_limit_bytes=48 << 20),
    )(qt, do, o, kv, begin, slot, lse, cosine, sine)


MESH_IDS = pl.DeviceIdType.MESH
AXES = ("x", "y", "z", "c")
ANYWHERE = pl.BlockSpec(memory_space=pl.ANY)
IN_VMEM = pl.BlockSpec(memory_space=pltpu.VMEM)


def place():
    return {a: lax.axis_index(a) for a in AXES}


def along(axis, step):
    size = lax.axis_size(axis)
    return lax.rem(lax.axis_index(axis) + (step + size), size)


def device(axis, step):
    here = place()
    here[axis] = along(axis, step)
    return tuple(here[a] for a in AXES)


class Net:
    def __init__(self, sends, arrivals, locals_):
        self.sends, self.arrivals, self.locals_ = sends, arrivals, locals_
        self.used = 0
        self.near = 0
        self.open = []

    def send(self, source, target, axis, step):
        copy = pltpu.make_async_remote_copy(
            src_ref=source, dst_ref=target, send_sem=self.sends.at[self.used],
            recv_sem=self.arrivals.at[self.used], device_id=device(axis, step),
            device_id_type=MESH_IDS,
        )
        copy.start()
        self.used += 1
        self.open.append(copy)
        return copy

    def keep(self, source, target):
        copy = pltpu.make_async_copy(source, target, self.locals_.at[self.near])
        copy.start()
        self.near += 1
        return copy

    def close(self):
        for copy in self.open:
            copy.wait_send()


def greet(partners):
    barrier = pltpu.get_barrier_semaphore()
    for axis, step in partners:
        pl.semaphore_signal(barrier, 1, device_id=device(axis, step), device_id_type=MESH_IDS)
    pl.semaphore_wait(barrier, len(partners))


def semaphores(sends, locals_):
    return [
        pltpu.SemaphoreType.DMA((sends,)),
        pltpu.SemaphoreType.DMA((sends,)),
        pltpu.SemaphoreType.DMA((max(locals_, 1),)),
    ]


def comm_call(body, name, number, outs, ins, scratch, sends, locals_, spaces, out_spaces):
    return pl.pallas_call(
        body,
        name=name,
        out_shape=outs,
        in_specs=spaces,
        out_specs=out_spaces,
        scratch_shapes=list(scratch) + semaphores(sends, locals_),
        compiler_params=pltpu.CompilerParams(
            collective_id=number, has_side_effects=True, vmem_limit_bytes=56 << 20
        ),
    )(*ins)


LINE = (1, 2, 3)


class RowGather:
    def __init__(self, net, value, out):
        self.net, self.out = net, out
        h = value.shape[0] // 2
        self.parts = (pl.ds(0, h), pl.ds(h, h))
        y, z, c = (lax.axis_index(a) for a in ROW)
        self.mine = net.keep(value, out.at[y, z, c])
        self.own = net.send(value, out.at[y, z, c], "c", 1)
        self.first = [
            [net.send(value.at[part], out.at[y, z, c, part], axis, d) for d in LINE]
            for part, axis in zip(self.parts, ("z", "y"))
        ]

    def spread(self):
        net, out = self.net, self.out
        y, z, c = (lax.axis_index(a) for a in ROW)
        self.mine.wait()
        (a, b) = self.parts
        for copy in self.first[0]:
            copy.wait_recv()
        self.second = [
            [net.send(out.at[y, :, c, a], out.at[y, :, c, a], "y", d) for d in LINE]
        ]
        for copy in self.first[1]:
            copy.wait_recv()
        self.second.append(
            [net.send(out.at[:, z, c, b], out.at[:, z, c, b], "z", d) for d in LINE]
        )
        self.shared = [self.own]
        for d in LINE:
            spot = out.at[y, along("z", -d), c, a]
            self.shared.append(net.send(spot, spot, "c", 1))
            spot = out.at[along("y", -d), z, c, b]
            self.shared.append(net.send(spot, spot, "c", 1))

    def finish(self):
        net, out = self.net, self.out
        y, z, c = (lax.axis_index(a) for a in ROW)
        (a, b) = self.parts
        for d in LINE:
            self.second[0][d - 1].wait_recv()
            spot = out.at[along("y", -d), :, c, a]
            self.shared.append(net.send(spot, spot, "c", 1))
            self.second[1][d - 1].wait_recv()
            spot = out.at[:, along("z", -d), c, b]
            self.shared.append(net.send(spot, spot, "c", 1))
        for copy in self.shared:
            copy.wait_recv()


class RingGather:
    def __init__(self, net, value, out, axis):
        self.net, self.out, self.axis = net, out, axis
        a, c = lax.axis_index(axis), lax.axis_index("c")
        h = value.shape[0] // 2
        self.parts = one, two = pl.ds(0, h), pl.ds(h, h)
        self.mine = net.keep(value, out.at[a, c])
        self.right = [net.send(value.at[p], out.at[a, c, p], axis, 1) for p in (one, two)]
        self.left = [net.send(value.at[p], out.at[a, c, p], axis, -1) for p in (two, one)]
        self.shared = [net.send(value, out.at[a, c], "c", 1)]

    def spread(self):
        net, out, axis = self.net, self.out, self.axis
        c = lax.axis_index("c")
        one, two = self.parts
        before, after = along(axis, -1), along(axis, 1)
        self.right[0].wait_recv()
        spot = out.at[before, c, one]
        self.far = [net.send(spot, spot, axis, 1)]
        self.left[0].wait_recv()
        spot = out.at[after, c, two]
        self.far.append(net.send(spot, spot, axis, -1))
        for copies, where in ((self.right, before), (self.left, after)):
            copies[1].wait_recv()
            spot = out.at[where, c]
            self.shared.append(net.send(spot, spot, "c", 1))

    def finish(self):
        for copy in self.far:
            copy.wait_recv()
        spot = self.out.at[along(self.axis, 2), lax.axis_index("c")]
        self.shared.append(self.net.send(spot, spot, "c", 1))
        for copy in self.shared:
            copy.wait_recv()
        self.mine.wait()


STEP = 16


def rows_loop(count, body):
    pl.loop(0, count // STEP)(lambda i: body(pl.ds(pl.multiple_of(i * STEP, STEP), STEP)))


def shifted(rows, first):
    return pl.ds(pl.multiple_of(rows.start + first, STEP), STEP)


class RingSum:
    def __init__(self, net, value, out, axis, near, relay, come, go):
        self.net, self.value, self.out, self.axis = net, value, out, axis
        self.near, self.relay, self.come, self.go = near, relay, come, go
        c = lax.axis_index("c")
        self.size = value.shape[2]
        h = self.size // 2
        self.parts = pl.ds(0, h), pl.ds(h, h)
        self.swaps = {
            s: net.send(value.at[along(axis, s), 1 - c], near.at[s], "c", 1) for s in (2, 1, 3, 0)
        }

    def pair(self, s, part=None):
        value, near, go = self.value, self.near, self.go
        where, c = along(self.axis, s), lax.axis_index("c")
        first = 0 if part is None else part.start
        count = self.size if part is None else part.size

        def add(rows):
            at = shifted(rows, first)
            go[s, at] = (
                value[where, c, at].astype(F32) + near[s, at].astype(F32)
            ).astype(BF)

        rows_loop(count, add)

    def relay_far(self):
        net = self.net
        one, two = self.parts
        self.swaps[2].wait_recv()
        self.pair(2)
        self.relays = [
            net.send(self.go.at[2, one], self.relay.at[0], self.axis, 1),
            net.send(self.go.at[2, two], self.relay.at[1], self.axis, -1),
        ]

    def spread(self):
        net, go, relay, come = self.net, self.go, self.relay, self.come
        one, two = self.parts
        self.swaps[1].wait_recv()
        self.pair(1)
        self.ends = [net.send(go.at[1, two], come.at[0, two], self.axis, 1)]
        self.swaps[3].wait_recv()
        self.pair(3)
        self.ends.append(net.send(go.at[3, one], come.at[1, one], self.axis, -1))
        for i, (s, part, step) in enumerate(((1, one, 1), (3, two, -1))):
            self.relays[i].wait_recv()

            def add(rows, i=i, s=s, part=part):
                at = shifted(rows, part.start)
                go[s, at] = (go[s, at].astype(F32) + relay[i, rows].astype(F32)).astype(BF)

            rows_loop(part.size, add)
            self.ends.append(net.send(go.at[s, part], come.at[i, part], self.axis, step))

    def finish(self):
        value, near, come, out = self.value, self.near, self.come, self.out
        where, c = lax.axis_index(self.axis), lax.axis_index("c")
        self.swaps[0].wait_recv()
        for copy in self.ends:
            copy.wait_recv()

        def add(rows):
            out[rows] = (
                value[where, c, rows].astype(F32) + near[0, rows].astype(F32)
            ) + (come[0, rows].astype(F32) + come[1, rows].astype(F32))

        rows_loop(self.size, add)


def ring_sum_scratch(size, width):
    return [
        pltpu.VMEM((4, size, width), BF),
        pltpu.VMEM((2, size // 2, width), BF),
        pltpu.VMEM((2, size, width), BF),
        pltpu.VMEM((4, size, width), BF),
    ]


class RowSum:
    def __init__(self, net, value, out, near, go, first, mid, last):
        self.net, self.value, self.out = net, value, out
        self.near, self.go, self.first, self.mid, self.last = near, go, first, mid, last
        c = lax.axis_index("c")
        self.size = value.shape[3]
        h = self.size // 2
        self.parts = pl.ds(0, h), pl.ds(h, h)
        self.swaps = [
            net.send(value.at[i, :, 1 - c], near.at[i], "c", 1) for i in range(4)
        ]

    def start(self):
        net, value, near, go = self.net, self.value, self.near, self.go
        c = lax.axis_index("c")
        for i in range(4):
            self.swaps[i].wait_recv()
            for j in range(4):

                def add(rows, i=i, j=j):
                    go[i, j, rows] = (
                        value[i, j, c, rows].astype(F32) + near[i, j, rows].astype(F32)
                    ).astype(BF)

                rows_loop(self.size, add)
        a, b = self.parts
        self.ones = [
            [net.send(go.at[along("y", d), :, a], self.first.at[0, d - 1], "y", d) for d in LINE],
            [net.send(go.at[:, along("z", d), b], self.first.at[1, d - 1], "z", d) for d in LINE],
        ]

    def turn(self):
        net, go, first, mid = self.net, self.go, self.first, self.mid
        y, z = lax.axis_index("y"), lax.axis_index("z")
        self.twos = []
        for k, axis in enumerate(("z", "y")):
            for copy in self.ones[k]:
                copy.wait_recv()
            for j in range(4):

                def add(rows, k=k, j=j):
                    at = shifted(rows, self.parts[k].start)
                    own = go[y, j, at] if k == 0 else go[j, z, at]
                    mid[k, j, rows] = (
                        own.astype(F32) + first[k, 0, j, rows].astype(F32)
                        + (first[k, 1, j, rows].astype(F32) + first[k, 2, j, rows].astype(F32))
                    ).astype(BF)

                rows_loop(self.parts[k].size, add)
            self.twos.append(
                [net.send(mid.at[k, along(axis, d)], self.last.at[k, d - 1], axis, d) for d in LINE]
            )

    def finish(self):
        mid, last, out = self.mid, self.last, self.out
        for k, axis in enumerate(("z", "y")):
            for copy in self.twos[k]:
                copy.wait_recv()
            here = lax.axis_index(axis)

            def add(rows, k=k, here=here):
                at = shifted(rows, self.parts[k].start)
                out[at] = (
                    mid[k, here, rows].astype(F32) + last[k, 0, rows].astype(F32)
                    + (last[k, 1, rows].astype(F32) + last[k, 2, rows].astype(F32))
                )

            rows_loop(self.parts[k].size, add)


def row_sum_scratch(size, width):
    h = size // 2
    return [
        pltpu.VMEM((4, 4, size, width), BF),
        pltpu.VMEM((4, 4, size, width), BF),
        pltpu.VMEM((2, 3, 4, h, width), BF),
        pltpu.VMEM((2, 4, h, width), BF),
        pltpu.VMEM((2, 3, h, width), BF),
    ]


Y_LINE = [("y", d) for d in LINE]
Z_LINE = [("z", d) for d in LINE]
X_LINE = [("x", d) for d in LINE]
X_RING = [("x", 1), ("x", -1)]
Y_RING = [("y", 1), ("y", -1)]
TWIN = [("c", 1)]


def shape(*dims, kind=BF):
    return jax.ShapeDtypeStruct(dims, kind)


def first_weights(first, up, both, out):
    def body(
        first_ref, up_ref, both_ref, out_ref, first_out, up_out, both_out, out_out, transit, strip, sheet,
        sends, arrivals, locals_,
    ):
        net = Net(sends, arrivals, locals_)
        x, y, z, c = (lax.axis_index(a) for a in AXES)
        quarter = out_ref.shape[0] // 4
        greet(X_LINE + Y_LINE + Z_LINE + TWIN)
        row = RowGather(net, first_ref, first_out)
        piece = out_ref.at[pl.ds(pl.multiple_of(x * quarter, quarter), quarter)]
        piece_mine = net.keep(piece, strip.at[z])
        pieces = [net.send(piece, strip.at[z], "z", d) for d in LINE]
        up_mine = net.keep(up_ref.at[y], transit.at[y, z])
        ups = [net.send(up_ref.at[along("y", d)], transit.at[y, z], "y", d) for d in LINE]
        both_mine = net.keep(both_ref.at[c], both_out.at[c])
        both_come = net.send(both_ref.at[1 - c], both_out.at[c], "c", 1)
        row.spread()
        piece_mine.wait()
        for copy in pieces:
            copy.wait_recv()
        strip_mine = net.keep(strip, sheet.at[:, x])
        strips = [net.send(strip, sheet.at[:, x], "x", d) for d in LINE]
        up_mine.wait()
        for copy in ups:
            copy.wait_recv()
        ups = [net.send(transit.at[:, z], transit.at[:, z], "z", d) for d in LINE]
        row.finish()
        strip_mine.wait()
        for copy in strips:
            copy.wait_recv()
        half = sheet.shape[0] // 2
        sheet_keep = net.keep(sheet.at[pl.ds(half * c, half)], out_out.at[:, c])
        sheet_come = net.send(sheet.at[pl.ds(half * (1 - c), half)], out_out.at[:, c], "c", 1)
        for copy in ups:
            copy.wait_recv()
        up_keep = net.keep(transit.at[:, :, c], up_out.at[:, :, c])
        up_come = net.send(transit.at[:, :, 1 - c], up_out.at[:, :, c], "c", 1)
        for copy in (both_mine, up_keep, sheet_keep):
            copy.wait()
        for copy in (both_come, up_come, sheet_come):
            copy.wait_recv()
        net.close()

    _, per, high, thin = up.shape
    rows, width = out.shape
    quarter = rows // 4
    outs = (
        shape(4, 4, 2, *first.shape), shape(4, 4, 2, high, thin), shape(*both.shape),
        shape(2, 2, 4, quarter, width), shape(4, 4, 2, high, thin), shape(4, quarter, width),
        shape(4, 4, quarter, width),
    )
    return comm_call(
        body, "first_weights", 1, outs, (first, up, both, out), [], 44, 8, [ANYWHERE] * 4, [ANYWHERE] * 7,
    )[:4]


def keys_and_latents(key_value, latent):
    def body(kv_ref, lat_ref, kv_out, lat_out, sends, arrivals, locals_):
        net = Net(sends, arrivals, locals_)
        greet(Y_LINE + Z_LINE + TWIN)
        row = RowGather(net, kv_ref, kv_out)
        ring = RingGather(net, lat_ref, lat_out, "y")
        row.spread()
        ring.spread()
        row.finish()
        ring.finish()
        net.close()

    outs = (shape(4, 4, 2, *key_value.shape), shape(4, 2, *latent.shape))
    return comm_call(
        body, "keys_and_latents", 2, outs, (key_value, latent), [], 40, 2, [ANYWHERE] * 2, [ANYWHERE] * 2,
    )


def heads_sum_and_cotangent(partial, cotangent):
    def body(part_ref, cot_ref, out_ref, cot_out, near, relay, come, go, sends, arrivals, locals_):
        net = Net(sends, arrivals, locals_)
        greet(X_RING + Y_RING + TWIN)
        ring = RingSum(net, part_ref, out_ref, "y", near, relay, come, go)
        feed = RingGather(net, cot_ref, cot_out, "x")
        ring.relay_far()
        ring.spread()
        feed.spread()
        ring.finish()
        feed.finish()
        net.close()

    size, width = cotangent.shape
    outs = (shape(size, width, kind=F32), shape(4, 2, size, width))
    return comm_call(
        body, "heads_sum_and_cotangent", 3, outs, (partial, cotangent), ring_sum_scratch(size, width), 20, 2,
        [IN_VMEM, ANYWHERE], [IN_VMEM, ANYWHERE],
    )


def feed_gather(normed_two, normed):
    def body(two_ref, one_ref, two_out, one_out, sends, arrivals, locals_):
        net = Net(sends, arrivals, locals_)
        y, c = lax.axis_index("y"), lax.axis_index("c")
        tall = one_ref.shape[1] // 4
        greet(X_RING + Y_LINE + TWIN)
        feed = RingGather(net, two_ref, two_out, "x")
        mine = net.keep(one_ref.at[:, pl.ds(pl.multiple_of(y * tall, tall), tall)], one_out.at[y, c])
        ones = [
            net.send(
                one_ref.at[:, pl.ds(pl.multiple_of(along("y", d) * tall, tall), tall)],
                one_out.at[y, c], "y", d,
            )
            for d in LINE
        ]
        feed.spread()
        mine.wait()
        spot = one_out.at[y, c]
        shared = [net.send(spot, spot, "c", 1)]
        for d in LINE:
            ones[d - 1].wait_recv()
            spot = one_out.at[along("y", -d), c]
            shared.append(net.send(spot, spot, "c", 1))
        feed.finish()
        for copy in shared:
            copy.wait_recv()
        net.close()

    size, width = normed_two.shape
    outs = (shape(4, 2, size, width), shape(4, 2, size, width // 4))
    return comm_call(
        body, "feed_gather", 4, outs, (normed_two, normed), [], 20, 2, [ANYWHERE] * 2, [ANYWHERE] * 2,
    )


def feed_sum(partial):
    def body(ref, out, *rest):
        net = Net(*rest[4:])
        greet(X_RING + TWIN)
        ring = RingSum(net, ref, out, "x", *rest[:4])
        ring.relay_far()
        ring.spread()
        ring.finish()
        net.close()

    _, _, size, width = partial.shape
    return comm_call(
        body, "feed_sum", 5, shape(size, width, kind=F32), (partial,), ring_sum_scratch(size, width), 12, 0,
        [IN_VMEM], IN_VMEM,
    )


def heads_gather_and_branch(value, partial):
    def body(ref, part_ref, out, part_out, *rest):
        net = Net(*rest[4:])
        greet(X_RING + Y_RING + TWIN)
        gathering = RingGather(net, ref, out, "y")
        ring = RingSum(net, part_ref, part_out, "x", *rest[:4])
        ring.relay_far()
        gathering.spread()
        ring.spread()
        gathering.finish()
        ring.finish()
        net.close()

    size, width = value.shape
    return comm_call(
        body, "heads_gather_and_branch", 6, (shape(4, 2, size, width), shape(size, width, kind=F32)),
        (value, partial), ring_sum_scratch(size, width), 24, 2, [ANYWHERE, IN_VMEM], [ANYWHERE, IN_VMEM],
    )


def add_up(terms, out, rows):
    total = terms[0][rows].astype(F32)
    for term in terms[1:]:
        total = total + term[rows].astype(F32)
    out[rows] = total.astype(out.dtype)


def add_all(terms, out):
    rows_loop(out.shape[0], lambda rows: add_up(terms, out, rows))


def keys_and_latents_sum(grad_kv, partial, grad_out, grad_up):
    def body(kv_ref, part_ref, out_ref, up_ref, kv_out, part_out, out_out, up_out, *rest):
        net = Net(*rest[12:])
        stack, out_come, up_come = rest[9:12]
        x, c = lax.axis_index("x"), lax.axis_index("c")
        half = out_ref.shape[0]
        quarter = out_out.shape[1]
        lanes = up_out.shape[-1]

        def strip(at):
            return pl.ds(pl.multiple_of(at * quarter, quarter), quarter)

        def lane(at):
            return pl.ds(pl.multiple_of(at * lanes, lanes), lanes)

        greet(X_LINE + Y_LINE + Z_LINE + TWIN)
        mine = net.keep(out_ref.at[:, c], stack.at[pl.ds(half * c, half)])
        come = net.send(out_ref.at[:, 1 - c], stack.at[pl.ds(half * c, half)], "c", 1)
        row = RowSum(net, kv_ref, kv_out, *rest[:5])
        ring = RingSum(net, part_ref, part_out, "y", *rest[5:9])
        mine.wait()
        come.wait_recv()
        outs = [net.send(stack.at[:, strip(along("x", d))], out_come.at[d - 1], "x", d) for d in LINE]
        row.start()
        ups = [
            net.send(up_ref.at[:, :, :, :, lane(along("x", d))], up_come.at[d - 1], "x", d) for d in LINE
        ]
        ring.relay_far()
        ring.spread()
        row.turn()
        for copy in outs:
            copy.wait_recv()
        for i in range(4):
            add_all([stack.at[i, strip(x)]] + [out_come.at[d, i] for d in range(3)], out_out.at[i])
        for copy in ups:
            copy.wait_recv()
        for i in range(4):

            @pl.loop(0, 8)
            def _(k, i=i):
                j, core = k // 2, k % 2
                add_all(
                    [up_ref.at[i, j, core, :, lane(x)]] + [up_come.at[d, i, j, core] for d in range(3)],
                    up_out.at[i, j, core],
                )

        ring.finish()
        row.finish()
        net.close()

    _, _, _, size, thin = grad_kv.shape
    width = partial.shape[3]
    half, _, tall, wide = grad_out.shape
    high, lanes = grad_up.shape[3], grad_up.shape[4] // 4
    outs = (
        shape(size, thin, kind=F32), shape(size, width, kind=F32), shape(4, tall // 4, wide),
        shape(4, 4, 2, high, lanes),
    )
    scratch = [
        pltpu.VMEM((2 * half, tall, wide), BF),
        pltpu.VMEM((3, 4, tall // 4, wide), BF),
        pltpu.VMEM((3, 4, 4, 2, high, lanes), BF),
    ]
    return comm_call(
        body, "keys_and_latents_sum", 7, outs, (grad_kv, partial, grad_out, grad_up),
        row_sum_scratch(size, thin) + ring_sum_scratch(size, width) + scratch, 36, 1, [IN_VMEM] * 4,
        [IN_VMEM] * 4,
    )


def firsts_gather(value, both, grad_out, grad_up):
    def body(
        ref, both_ref, out_ref, up_ref, gathered, both_out, out_out, up_out, out_come, up_come, up_sum, up_y,
        sends, arrivals, locals_,
    ):
        net = Net(sends, arrivals, locals_)
        x, y, z, c = (lax.axis_index(a) for a in AXES)
        greet(X_LINE + Y_LINE + Z_LINE + TWIN)
        mine = net.keep(ref.at[c], gathered.at[y, c])
        come = net.send(ref.at[1 - c], gathered.at[y, c], "c", 1)
        both_mine = net.keep(both_ref.at[c], both_out.at[x, c])
        both_come = net.send(both_ref.at[1 - c], both_out.at[x, c], "c", 1)
        ups = [net.send(up_ref.at[:, along("z", d)], up_come.at[d - 1], "z", d) for d in LINE]
        outs = [net.send(out_ref.at[along("z", d)], out_come.at[d - 1], "z", d) for d in LINE]

        mine.wait()
        spot = gathered.at[y, c]
        ahead = [net.send(spot, spot, "y", 1), net.send(spot, spot, "y", -1)]
        come.wait_recv()
        spot = gathered.at[y, 1 - c]
        ahead += [net.send(spot, spot, "y", 1), net.send(spot, spot, "y", -1)]
        both_mine.wait()
        both_come.wait_recv()
        zero, one = both_out.at[x, 0], both_out.at[x, 1]
        right = [net.send(spot, spot, "x", 1) for spot in (zero, one)]
        left = [net.send(spot, spot, "x", -1) for spot in (one, zero)]

        for copy in ups:
            copy.wait_recv()
        for i in range(4):
            for core in range(2):
                add_all(
                    [up_ref.at[i, z, core]] + [up_come.at[d, i, core] for d in range(3)], up_sum.at[i, core]
                )
        ups = [net.send(up_sum.at[along("y", d)], up_y.at[y], "y", d) for d in LINE]
        up_mine = net.keep(up_sum.at[y], up_y.at[y])

        ahead[0].wait_recv()
        spot = gathered.at[along("y", -1), c]
        ahead.append(net.send(spot, spot, "y", 1))
        ahead[3].wait_recv()
        spot = gathered.at[along("y", 1), 1 - c]
        ahead.append(net.send(spot, spot, "y", -1))

        for copy in outs:
            copy.wait_recv()
        add_all([out_ref.at[z]] + [out_come.at[d] for d in range(3)], out_out.at[x])
        spot = out_out.at[x]
        outs = [net.send(spot, spot, "x", d) for d in LINE]

        up_mine.wait()
        for copy in ups:
            copy.wait_recv()
        up_near = net.send(up_y.at[:, 1 - c], up_out.at[x, :, c], "c", 1)
        up_mine = net.keep(up_y.at[:, c], up_out.at[x, :, c])

        right[0].wait_recv()
        spot = both_out.at[along("x", -1), 0]
        far = [net.send(spot, spot, "x", 1)]
        left[0].wait_recv()
        spot = both_out.at[along("x", 1), 1]
        far.append(net.send(spot, spot, "x", -1))

        up_near.wait_recv()
        up_mine.wait()
        spot = up_out.at[x]
        ups = [net.send(spot, spot, "x", d) for d in LINE]
        for copy in [ahead[i] for i in (1, 2, 4, 5)] + [right[1], left[1]] + far + outs + ups:
            copy.wait_recv()
        net.close()

    _, tall, wide = grad_out.shape
    _, _, _, high, lanes = grad_up.shape
    outs = (
        shape(4, *value.shape), shape(4, *both.shape), shape(4, tall, wide), shape(4, 4, 2, high, lanes),
    )
    scratch = [
        pltpu.VMEM((3, tall, wide), BF),
        pltpu.VMEM((3, 4, 2, high, lanes), BF),
        pltpu.VMEM((4, 2, high, lanes), BF),
        pltpu.VMEM((4, 2, high, lanes), BF),
    ]
    return comm_call(
        body, "firsts_gather", 8, outs, (value, both, grad_out, grad_up), scratch, 40, 4,
        [ANYWHERE, ANYWHERE, IN_VMEM, IN_VMEM], [ANYWHERE, ANYWHERE, IN_VMEM, IN_VMEM],
    )


def last_sums(grad_first, gains, grad_down):
    def body(
        first_ref, gain_ref, down_ref, first_out, gain_out, down_out, wide, first_come, first_x,
        gain_near, gain_one, gain_come, gain_two, gain_y, gain_three, gain_x, sends, arrivals, locals_,
    ):
        net = Net(sends, arrivals, locals_)
        x, y, z, c = (lax.axis_index(a) for a in AXES)
        greet(X_LINE + Y_LINE + Z_LINE + TWIN)
        first_near = net.send(first_ref.at[:, 1 - c], wide.at[c], "c", 1)
        first_mine = net.keep(first_ref.at[:, c], wide.at[c])
        near = net.send(gain_ref.at[:, :, 1 - c], gain_near, "c", 1)
        down_mine = net.keep(down_ref, down_out.at[x])
        downs = [net.send(down_ref, down_out.at[x], "x", d) for d in LINE]
        first_mine.wait()
        first_near.wait_recv()
        firsts = [net.send(wide.at[:, along("z", d)], first_come.at[d - 1], "z", d) for d in LINE]
        near.wait_recv()
        gain_one[...] = gain_ref[:, :, c] + gain_near[...]
        comes = [net.send(gain_one.at[:, along("z", d)], gain_come.at[d - 1], "z", d) for d in LINE]
        for copy in firsts:
            copy.wait_recv()
        for core in range(2):
            add_all(
                [wide.at[core, z]] + [first_come.at[d, core] for d in range(3)], first_x.at[x, core]
            )
        spot = first_x.at[x]
        firsts = [net.send(spot, spot, "x", d) for d in LINE]
        for copy in comes:
            copy.wait_recv()
        gain_two[...] = (gain_one[:, z] + gain_come[0]) + (gain_come[1] + gain_come[2])
        comes = [net.send(gain_two.at[along("y", d)], gain_y.at[d - 1], "y", d) for d in LINE]
        for copy in comes:
            copy.wait_recv()
        gain_three[...] = (gain_two[y] + gain_y[0]) + (gain_y[1] + gain_y[2])
        gain_mine = net.keep(gain_three, gain_x.at[x])
        comes = [net.send(gain_three, gain_x.at[x], "x", d) for d in LINE]
        for copy in firsts:
            copy.wait_recv()
        for core in range(2):
            add_all([first_x.at[i, core] for i in range(4)], first_out.at[core])
        gain_mine.wait()
        for copy in comes:
            copy.wait_recv()
        gain_out[...] = (gain_x[0] + gain_x[1]) + (gain_x[2] + gain_x[3])
        down_mine.wait()
        for copy in downs:
            copy.wait_recv()
        net.close()

    _, _, high, lanes = grad_first.shape
    outs = (shape(2, high, lanes, kind=F32), shape(8, 128, kind=F32), shape(4, *grad_down.shape))
    scratch = [
        pltpu.VMEM((2, 4, high, lanes), BF),
        pltpu.VMEM((3, 2, high, lanes), BF),
        pltpu.VMEM((4, 2, high, lanes), BF),
        pltpu.VMEM((4, 4, 8, 128), F32),
        pltpu.VMEM((4, 4, 8, 128), F32),
        pltpu.VMEM((3, 4, 8, 128), F32),
        pltpu.VMEM((4, 8, 128), F32),
        pltpu.VMEM((3, 8, 128), F32),
        pltpu.VMEM((8, 128), F32),
        pltpu.VMEM((4, 8, 128), F32),
    ]
    return comm_call(
        body, "last_sums", 9, outs, (grad_first, gains, grad_down), scratch, 24, 3,
        [IN_VMEM, IN_VMEM, ANYWHERE], [IN_VMEM, IN_VMEM, ANYWHERE],
    )


def gather(value, axes):
    return lax.all_gather(value, axes, axis=0, tiled=True)


def scatter_sum(value, axes):
    return lax.psum_scatter(value, axes, scatter_dimension=0, tiled=True)


def on_device(
    block_input, cotangent, lengths, norm_gain, q_down, q_gain, q_up, key_weight, value_weight,
    out_weight, ffn_gain, gate_weight, up_weight, down_weight,
):
    rows, width = block_input.shape
    latent_width = q_down.shape[1]
    n_x, n_y, n_z, n_c = (lax.axis_size(a) for a in ("x", "y", "z", "c"))
    x, y, z, c = (lax.axis_index(a) for a in ("x", "y", "z", "c"))
    span = n_y * n_z * n_c
    members = n_y * n_c
    lengths_row = lengths[0]

    mine = (y * n_z + z) * n_c + c
    slots_mine = mine * rows + jnp.arange(rows, dtype=jnp.int32)
    begin_mine, _ = places_of(lengths_row, slots_mine)
    cosine, sine = tables(slots_mine - begin_mine)
    strip = n_c * rows
    slots_group = (
        (jnp.arange(n_y, dtype=jnp.int32)[:, None] * n_z + z) * strip
        + jnp.arange(strip, dtype=jnp.int32)[None, :]
    ).reshape(-1)
    begin_group, live_group = places_of(lengths_row, slots_group)
    cosine_group, sine_group = tables_across((slots_group - begin_group).reshape(n_y, strip))
    begin_lanes = jnp.tile(begin_group.reshape(n_y, 1, strip), (1, 1, 2))
    slot_lanes = jnp.tile(slots_group.reshape(n_y, 1, strip), (1, 1, 2))
    live_lanes = jnp.tile(live_group.reshape(n_y, 1, strip), (1, 1, 2))

    shard = norm_gain.shape[0]
    extra = jnp.stack(
        [norm_gain, ffn_gain, jnp.pad(q_gain, (0, shard - q_gain.shape[0]))], axis=1
    ).astype(BF)
    first_width = latent_width + 2 * SIZE
    first = jnp.concatenate(
        [q_down, key_weight, value_weight, jnp.pad(extra, ((0, 0), (0, 125)))], axis=1
    )
    per_heads = q_up.shape[1] // members
    q_rows = q_up.shape[0]

    wide = gate_weight.shape[1]
    down_rows = down_weight.shape[0]
    share = down_rows // n_x
    padded = -(-share // 16) * 16
    source = lax.broadcasted_iota(jnp.int32, (wide // 2, n_c * (span // 4) * padded), 0)
    target = lax.broadcasted_iota(jnp.int32, source.shape, 1)
    block_at = target // (padded * (span // 4)) + n_c * ((target // padded) % (span // 4))
    inside = target % padded
    picks = (
        (source == block_at * down_rows + x * share + inside) & (inside < share)
    ).astype(BF)

    def spread(weight):
        stacked = jnp.concatenate([weight[:, : wide // 2], weight[:, wide // 2 :]], axis=0)
        part = dot(stacked, picks).astype(BF)
        part = part.reshape(2, shard, n_c, -1).transpose(2, 1, 0, 3)
        return part.reshape(n_c, shard, -1)

    both = jnp.concatenate([spread(gate_weight), spread(up_weight)], axis=2)
    units = both.shape[-1] // 2
    up_sent = q_up.reshape(q_rows, n_y, n_c, per_heads).transpose(1, 2, 0, 3)
    first_full, up_heads, both, out_heads = first_weights(first, up_sent, both, out_weight)
    out_heads = out_heads.reshape(per_heads, width)
    first_full = first_full.reshape(span * shard, -1)
    up_heads = up_heads.reshape(span * q_rows, per_heads)
    both = both.reshape(n_c * shard, 2 * units)
    extra_full = first_full[:, first_width : first_width + 3].astype(F32)
    first_full = first_full[:, :first_width]
    gain_one = extra_full[:, 0]
    gain_two = extra_full[:, 1]
    gain_latent = extra_full[:, 2].reshape(span, shard)[:, : q_gain.shape[0]].reshape(-1)

    both_full = gather(both, ("y", "z"))
    gate_use, up_use = both_full[:, :units], both_full[:, units:]
    down_part = lax.dynamic_slice_in_dim(down_weight, x * share, share)
    down_part = jnp.pad(down_part, ((0, padded - share), (0, 0)))
    down_part, _ = lax.optimization_barrier((down_part, both_full[:8, :128]))
    down_use = gather(down_part, ("y", "z"))

    inputs = block_input.astype(F32)
    inverse_one = lax.rsqrt(jnp.mean(inputs * inputs, axis=-1, keepdims=True) + EPSILON)
    normed = (inputs * inverse_one * gain_one).astype(BF)
    firsts = dot(normed, first_full)
    latent = firsts[:, :latent_width]
    inverse_latent = lax.rsqrt(jnp.mean(latent * latent, axis=-1, keepdims=True) + EPSILON)
    latent_normed = (latent * inverse_latent * gain_latent).astype(BF)
    key_mine = rotate(firsts[:, latent_width : latent_width + SIZE], cosine, sine).astype(BF)
    value_mine = firsts[:, latent_width + SIZE :].astype(BF)
    key_value, latent_group = keys_and_latents(
        jnp.concatenate([key_mine, value_mine], axis=1), latent_normed
    )
    key_value = key_value.reshape(span * rows, 2 * SIZE)
    group = members * rows
    latent_group = latent_group.reshape(group, latent_width)
    mixed, queries_t, lse = attend(
        dot(latent_group, up_heads), key_value, begin_lanes, slot_lanes, live_lanes,
        cosine_group, sine_group,
    )
    branch, grad_feed = heads_sum_and_cotangent(
        dot(mixed, out_heads).astype(BF).reshape(n_y, n_c, rows, width), cotangent
    )
    grad_feed = grad_feed.reshape(group, width)
    middle = inputs + branch

    inverse_two = lax.rsqrt(jnp.mean(middle * middle, axis=-1, keepdims=True) + EPSILON)
    normed_two, normed_part = feed_gather((middle * inverse_two * gain_two).astype(BF), normed)
    normed_two = normed_two.reshape(group, width)
    normed_part = normed_part.reshape(group, -1)
    gate_pre = dot(normed_two, gate_use)
    up_pre = dot(normed_two, up_use)
    sigma = jax.nn.sigmoid(gate_pre)
    hidden = (gate_pre * sigma * up_pre).astype(BF)
    grad_hidden = dot_nt(grad_feed, down_use)
    grad_gate_pre = (grad_hidden * up_pre * sigma * (1.0 + gate_pre * (1.0 - sigma))).astype(BF)
    grad_up_pre = (grad_hidden * gate_pre * sigma).astype(BF)
    grad_both = jnp.concatenate(
        [dot_tn(normed_two, grad_gate_pre).astype(BF), dot_tn(normed_two, grad_up_pre).astype(BF)],
        axis=1,
    )
    grad_down = dot_tn(hidden, grad_feed).astype(BF)
    branch_part = dot(hidden, down_use).astype(BF).reshape(n_x, n_c, rows, width)
    partial = (dot_nt(grad_gate_pre, gate_use) + dot_nt(grad_up_pre, up_use)).astype(BF)
    partial, grad_both, grad_down, branch_part = lax.optimization_barrier(
        (partial, grad_both, grad_down, branch_part)
    )
    grad_both = scatter_sum(grad_both, ("y", "z"))
    grad_down = scatter_sum(grad_down, ("y", "z"))
    grad_normed_two = feed_sum(partial.reshape(n_x, n_c, rows, width))
    grad_result = cotangent.astype(F32)
    grad_mid_norm, grad_gain_two = norm_back(middle, inverse_two, gain_two, grad_normed_two)
    grad_middle = grad_result + grad_mid_norm

    def collect(grads):
        parts = grads.reshape(n_x, n_c, shard, 2, units // 2).transpose(0, 3, 2, 1, 4)
        parts = parts.reshape(n_x, 2 * shard, n_c * units // 2)
        whole = 0.0
        for i in range(n_x):
            picked = (
                (source == block_at * down_rows + i * share + inside) & (inside < share)
            ).astype(BF)
            whole = whole + dot_nt(parts[i], picked)
        return jnp.concatenate([whole[:shard], whole[shard:]], axis=1)

    grad_branch, branch_two = heads_gather_and_branch(grad_middle.astype(BF), branch_part)
    grad_branch = grad_branch.reshape(group, width)
    output = (middle + branch_two).astype(BF)
    grad_mixed = dot_nt(grad_branch, out_heads).astype(BF)
    grad_attended = grad_mixed * live_group[:, None].astype(BF)
    grad_out = dot_tn(mixed, grad_branch).astype(BF)
    grad_query_raw, grad_kv = attend_back(
        queries_t, grad_attended, mixed, key_value, begin_lanes, slot_lanes, lse,
        cosine_group, sine_group,
    )
    out_rows = out_weight.shape[0]
    grad_up_heads = dot_tn(latent_group, grad_query_raw).astype(BF)
    grad_kv, grad_latent_normed, grad_out, grad_up_heads = keys_and_latents_sum(
        grad_kv.reshape(n_y, n_z, n_c, rows, 2 * SIZE),
        dot_nt(grad_query_raw, up_heads).astype(BF).reshape(n_y, n_c, rows, latent_width),
        grad_out.reshape(n_z // n_c, n_c, out_rows, width),
        grad_up_heads.reshape(n_y, n_z, n_c, q_rows, per_heads),
    )
    grad_key_raw = unrotate(grad_kv[:, :SIZE], cosine, sine).astype(BF)
    grad_value_raw = grad_kv[:, SIZE:].astype(BF)
    grad_latent_f, grad_gain_latent = norm_back(
        latent, inverse_latent, gain_latent, grad_latent_normed
    )
    grad_firsts = jnp.concatenate(
        [grad_latent_f.astype(BF), grad_key_raw, grad_value_raw], axis=1
    )
    grad_normed = dot_nt(grad_firsts, first_full)
    grad_input_norm, grad_gain_one = norm_back(inputs, inverse_one, gain_one, grad_normed)
    input_grad = grad_middle + grad_input_norm

    half_first = first_width // n_c
    first_part, grad_both, grad_out, grad_up_heads = firsts_gather(
        grad_firsts.reshape(rows, n_c, half_first).transpose(1, 0, 2),
        grad_both.reshape(n_c, shard, 2 * units), grad_out, grad_up_heads,
    )
    first_part = first_part.reshape(group, half_first)
    grad_first = dot_tn(normed_part, first_part).astype(BF)
    gains = jnp.concatenate(
        [
            grad_gain_one.reshape(span, shard),
            grad_gain_two.reshape(span, shard),
            grad_gain_latent.reshape(span, -1),
        ],
        axis=1,
    )
    shares = gains.shape[1]
    gains = jnp.pad(gains, ((0, 0), (0, 8 * 128 - shares))).reshape(n_y, n_z, n_c, 8, 128)
    grad_first, gains, grad_down = last_sums(
        grad_first.reshape(n_z, n_c, shard, half_first), gains, grad_down
    )
    gains = gains.reshape(-1)
    grad_first = jnp.concatenate([grad_first[0], grad_first[1]], axis=1)
    grad_out = grad_out.reshape(out_rows, width).astype(F32)
    grad_q_up = grad_up_heads.transpose(3, 1, 2, 0, 4).reshape(q_rows, -1).astype(F32)
    grad_gate = collect(grad_both[..., :units])
    grad_up = collect(grad_both[..., units:])
    grad_down = grad_down[:, :share].reshape(down_rows, width).astype(F32)
    return (
        output,
        input_grad,
        gains[:shard],
        grad_first[:, :latent_width],
        gains[2 * shard : shares],
        grad_q_up,
        grad_first[:, latent_width : latent_width + SIZE],
        grad_first[:, latent_width + SIZE :],
        grad_out,
        gains[shard : 2 * shard],
        grad_gate,
        grad_up,
        grad_down,
    )


def solution(mesh):
    sizes = (4, 4, 4, 2)
    grid = Mesh(mesh.devices.reshape(sizes), ("x", "y", "z", "c"))
    tokens = P(("x", "y", "z", "c"), None)
    wide, thin = P(ROW, None), P(ROW)
    in_specs = (
        tokens, tokens, P("x", None), thin, wide, thin, wide, wide, wide, wide, thin, wide, wide,
        wide,
    )
    out_specs = (
        tokens, tokens, thin, wide, thin, wide, wide, wide, wide, thin, wide, wide, wide,
    )
    return jax.shard_map(
        on_device, mesh=grid, in_specs=in_specs, out_specs=out_specs, check_vma=False
    )
```

```python
import functools
import math

import jax
import jax.numpy as jnp
from jax import lax
from jax.experimental import pallas as pl
from jax.experimental.pallas import tpu as pltpu
from jax.sharding import Mesh
from jax.sharding import PartitionSpec as P

EPSILON = 1e-06
MASKED = -1e30
BF = jnp.bfloat16
F32 = jnp.float32
SIZE = 256
HALF = 128
BLOCK = 256
ROW = ("y", "z", "c")
HEADS = ("y", "c")
FEED = ("x", "c")


def dot(left, right):
    return jnp.dot(left, right, preferred_element_type=F32)


def dot_tn(left, right):
    return lax.dot_general(left, right, (((0,), (0,)), ((), ())), preferred_element_type=F32)


def dot_nt(left, right):
    return lax.dot_general(left, right, (((1,), (1,)), ((), ())), preferred_element_type=F32)


def norm_back(values, inverse, gain, grad):
    scaled = grad * gain
    grad_values = inverse * scaled - values * inverse * inverse * inverse * jnp.mean(
        scaled * values, axis=-1, keepdims=True
    )
    return grad_values, jnp.sum(grad * values * inverse, axis=0)


def places_of(lengths_row, slots):
    ends = jnp.cumsum(lengths_row)
    begins = jnp.concatenate([ends - lengths_row, ends[-1:]])
    begin = jnp.max(jnp.where(slots[:, None] >= begins[None, :], begins[None, :], 0), axis=1)
    live = (slots < ends[-1]).astype(F32)
    return begin, live


def tables(position):
    freq = jnp.exp(jnp.arange(HALF, dtype=F32) * (-math.log(10000.0) / HALF))
    angle = position.astype(F32)[:, None] * freq[None, :]
    return jnp.cos(angle), jnp.sin(angle)


def tables_across(position):
    freq = jnp.exp(jnp.arange(HALF, dtype=F32) * (-math.log(10000.0) / HALF))
    angle = position.astype(F32)[..., None, :] * freq[:, None]
    return jnp.cos(angle), jnp.sin(angle)


def rotate(values, cosine, sine):
    lower, upper = values[..., :HALF], values[..., HALF:]
    return jnp.concatenate([lower * cosine - upper * sine, upper * cosine + lower * sine], axis=-1)


def unrotate(grad, cosine, sine):
    lower, upper = grad[..., :HALF], grad[..., HALF:]
    return jnp.concatenate([lower * cosine + upper * sine, upper * cosine - lower * sine], axis=-1)


def turned(source, target, count, columns):
    @pl.loop(0, count)
    def _(block):
        at = pl.ds(pl.multiple_of(block * BLOCK, BLOCK), BLOCK)
        target[:, at] = source[at, columns].T


KEYS, VALUES = slice(0, SIZE), slice(SIZE, 2 * SIZE)


def attend_kernel(
    q_ref, kv_ref, begin_ref, slot_ref, live_ref, cos_ref, sin_ref,
    out_ref, qt_ref, lse_ref, vt, peak, total, accum,
):
    depth = lax.axis_index("z")
    segments = slot_ref.shape[0]
    rows = slot_ref.shape[2]
    tokens = rows // 2
    turned(kv_ref, vt, segments * (segments - 1) + depth + 1, VALUES)
    for seg in range(segments):
        here = pl.ds(seg * tokens, tokens)
        cosine, sine = cos_ref[seg], sin_ref[seg]
        for head in range(2):
            raw = q_ref[here, head * SIZE : (head + 1) * SIZE].T
            lower, upper = raw[:HALF], raw[HALF:]
            turn = jnp.concatenate(
                [lower * cosine - upper * sine, upper * cosine + lower * sine], axis=0
            )
            qt_ref[seg, :, head * tokens : (head + 1) * tokens] = (
                turn.astype(BF) * (SIZE ** -0.5)
            ).astype(BF)
        query = qt_ref[seg]
        begin = begin_ref[seg]
        slot = slot_ref[seg]
        peak[...] = jnp.full_like(peak, MASKED)
        total[...] = jnp.zeros_like(total)
        accum[...] = jnp.zeros_like(accum)

        @pl.loop(0, segments * seg + depth + 1)
        def _(block):
            at = pl.multiple_of(block * BLOCK, BLOCK)
            scores = dot(kv_ref[pl.ds(at, BLOCK), KEYS], query)
            key = lax.broadcasted_iota(jnp.int32, scores.shape, 0) + at
            scores = jnp.where((key >= begin) & (key <= slot), scores, MASKED)
            before = peak[...]
            now = jnp.maximum(before, jnp.max(scores, axis=0, keepdims=True))
            weights = jnp.exp(scores - now)
            shrink = jnp.exp(before - now)
            peak[...] = now
            total[...] = total[...] * shrink + jnp.sum(weights, axis=0, keepdims=True)
            accum[...] = accum[...] * shrink + dot(vt[:, pl.ds(at, BLOCK)], weights.astype(BF))

        lse_ref[seg] = peak[...] + jnp.log(total[...])
        result = accum[...] * (live_ref[seg] / total[...])
        for head in range(2):
            out_ref[here, head * SIZE : (head + 1) * SIZE] = (
                result[:, head * tokens : (head + 1) * tokens].T.astype(BF)
            )


def attend(q, kv, begin, slot, live, cosine, sine):
    segments, _, rows = slot.shape
    return pl.pallas_call(
        attend_kernel,
        name="attend",
        out_shape=(
            jax.ShapeDtypeStruct(q.shape, BF),
            jax.ShapeDtypeStruct((segments, SIZE, rows), BF),
            jax.ShapeDtypeStruct((segments, 1, rows), F32),
        ),
        in_specs=[pl.BlockSpec(memory_space=pltpu.VMEM)] * 7,
        out_specs=[pl.BlockSpec(memory_space=pltpu.VMEM)] * 3,
        scratch_shapes=[
            pltpu.VMEM((SIZE, kv.shape[0]), BF),
            pltpu.VMEM((1, rows), F32),
            pltpu.VMEM((1, rows), F32),
            pltpu.VMEM((SIZE, rows), F32),
        ],
        compiler_params=pltpu.CompilerParams(vmem_limit_bytes=48 << 20),
    )(q, kv, begin, slot, live, cosine, sine)


MESH_IDS = pl.DeviceIdType.MESH
AXES = ("x", "y", "z", "c")
ANYWHERE = pl.BlockSpec(memory_space=pl.ANY)
IN_VMEM = pl.BlockSpec(memory_space=pltpu.VMEM)


def place():
    return {a: lax.axis_index(a) for a in AXES}


def along(axis, step):
    size = lax.axis_size(axis)
    return lax.rem(lax.axis_index(axis) + (step + size), size)


def device(axis, step):
    here = place()
    here[axis] = along(axis, step)
    return tuple(here[a] for a in AXES)


class Net:
    def __init__(self, sends, arrivals, locals_):
        self.sends, self.arrivals, self.locals_ = sends, arrivals, locals_
        self.used = 0
        self.near = 0
        self.open = []

    def send(self, source, target, axis, step):
        copy = pltpu.make_async_remote_copy(
            src_ref=source, dst_ref=target, send_sem=self.sends.at[self.used],
            recv_sem=self.arrivals.at[self.used], device_id=device(axis, step),
            device_id_type=MESH_IDS,
        )
        copy.start()
        self.used += 1
        self.open.append(copy)
        return copy

    def keep(self, source, target):
        copy = pltpu.make_async_copy(source, target, self.locals_.at[self.near])
        copy.start()
        self.near += 1
        return copy

    def close(self):
        for copy in self.open:
            copy.wait_send()


def greet(partners):
    barrier = pltpu.get_barrier_semaphore()
    for axis, step in partners:
        pl.semaphore_signal(barrier, 1, device_id=device(axis, step), device_id_type=MESH_IDS)
    pl.semaphore_wait(barrier, len(partners))


def semaphores(sends, locals_):
    return [
        pltpu.SemaphoreType.DMA((sends,)),
        pltpu.SemaphoreType.DMA((sends,)),
        pltpu.SemaphoreType.DMA((max(locals_, 1),)),
    ]


def comm_call(body, name, number, outs, ins, scratch, sends, locals_, spaces, out_spaces):
    return pl.pallas_call(
        body,
        name=name,
        out_shape=outs,
        in_specs=spaces,
        out_specs=out_spaces,
        scratch_shapes=list(scratch) + semaphores(sends, locals_),
        compiler_params=pltpu.CompilerParams(
            collective_id=number, has_side_effects=True, vmem_limit_bytes=60 << 20
        ),
    )(*ins)


LINE = (1, 2, 3)


class RowGather:
    def __init__(self, net, value, out):
        self.net, self.out = net, out
        h = value.shape[0] // 2
        self.parts = (pl.ds(0, h), pl.ds(h, h))
        y, z, c = (lax.axis_index(a) for a in ROW)
        self.mine = net.keep(value, out.at[y, z, c])
        self.own = net.send(value, out.at[y, z, c], "c", 1)
        self.first = [
            [net.send(value.at[part], out.at[y, z, c, part], axis, d) for d in LINE]
            for part, axis in zip(self.parts, ("z", "y"))
        ]

    def spread(self):
        net, out = self.net, self.out
        y, z, c = (lax.axis_index(a) for a in ROW)
        self.mine.wait()
        (a, b) = self.parts
        for copy in self.first[0]:
            copy.wait_recv()
        self.second = [
            [net.send(out.at[y, :, c, a], out.at[y, :, c, a], "y", d) for d in LINE]
        ]
        for copy in self.first[1]:
            copy.wait_recv()
        self.second.append(
            [net.send(out.at[:, z, c, b], out.at[:, z, c, b], "z", d) for d in LINE]
        )
        self.shared = [self.own]
        for d in LINE:
            spot = out.at[y, along("z", -d), c, a]
            self.shared.append(net.send(spot, spot, "c", 1))
            spot = out.at[along("y", -d), z, c, b]
            self.shared.append(net.send(spot, spot, "c", 1))

    def finish(self):
        net, out = self.net, self.out
        y, z, c = (lax.axis_index(a) for a in ROW)
        (a, b) = self.parts
        for d in LINE:
            self.second[0][d - 1].wait_recv()
            spot = out.at[along("y", -d), :, c, a]
            self.shared.append(net.send(spot, spot, "c", 1))
            self.second[1][d - 1].wait_recv()
            spot = out.at[:, along("z", -d), c, b]
            self.shared.append(net.send(spot, spot, "c", 1))
        for copy in self.shared:
            copy.wait_recv()


class RingGather:
    def __init__(self, net, value, out, axis):
        self.net, self.out, self.axis = net, out, axis
        a, c = lax.axis_index(axis), lax.axis_index("c")
        h = value.shape[0] // 2
        self.parts = one, two = pl.ds(0, h), pl.ds(h, h)
        self.mine = net.keep(value, out.at[a, c])
        self.right = [net.send(value.at[p], out.at[a, c, p], axis, 1) for p in (one, two)]
        self.left = [net.send(value.at[p], out.at[a, c, p], axis, -1) for p in (two, one)]
        self.shared = [net.send(value, out.at[a, c], "c", 1)]

    def forward(self):
        net, out, axis = self.net, self.out, self.axis
        c = lax.axis_index("c")
        one, two = self.parts
        before, after = along(axis, -1), along(axis, 1)
        self.right[0].wait_recv()
        spot = out.at[before, c, one]
        self.far = [net.send(spot, spot, axis, 1)]
        self.left[0].wait_recv()
        spot = out.at[after, c, two]
        self.far.append(net.send(spot, spot, axis, -1))

    def share(self):
        c = lax.axis_index("c")
        for copies, step in ((self.right, -1), (self.left, 1)):
            copies[1].wait_recv()
            spot = self.out.at[along(self.axis, step), c]
            self.shared.append(self.net.send(spot, spot, "c", 1))

    def finish(self):
        for copy in self.far:
            copy.wait_recv()
        spot = self.out.at[along(self.axis, 2), lax.axis_index("c")]
        self.shared.append(self.net.send(spot, spot, "c", 1))
        for copy in self.shared:
            copy.wait_recv()
        self.mine.wait()


STEP = 16


def rows_loop(count, body):
    pl.loop(0, count // STEP)(lambda i: body(pl.ds(pl.multiple_of(i * STEP, STEP), STEP)))


def shifted(rows, first):
    return pl.ds(pl.multiple_of(rows.start + first, STEP), STEP)


class RingSum:
    def __init__(self, net, value, out, axis, near, relay, come, go):
        self.net, self.value, self.out, self.axis = net, value, out, axis
        self.near, self.relay, self.come, self.go = near, relay, come, go
        c = lax.axis_index("c")
        self.size = value.shape[2]
        h = self.size // 2
        self.parts = pl.ds(0, h), pl.ds(h, h)
        self.swaps = {
            s: net.send(value.at[along(axis, s), 1 - c], near.at[s], "c", 1) for s in (2, 1, 3, 0)
        }

    def pair(self, s, part=None):
        value, near, go = self.value, self.near, self.go
        where, c = along(self.axis, s), lax.axis_index("c")
        first = 0 if part is None else part.start
        count = self.size if part is None else part.size

        def add(rows):
            at = shifted(rows, first)
            go[s, at] = (
                value[where, c, at].astype(F32) + near[s, at].astype(F32)
            ).astype(BF)

        rows_loop(count, add)

    def relay_far(self):
        net = self.net
        one, two = self.parts
        self.swaps[2].wait_recv()
        self.pair(2)
        self.relays = [
            net.send(self.go.at[2, one], self.relay.at[0], self.axis, 1),
            net.send(self.go.at[2, two], self.relay.at[1], self.axis, -1),
        ]

    def issue(self):
        net, go, come = self.net, self.go, self.come
        one, two = self.parts
        self.swaps[1].wait_recv()
        self.pair(1)
        self.ends = [net.send(go.at[1, two], come.at[0, two], self.axis, 1)]
        self.swaps[3].wait_recv()
        self.pair(3)
        self.ends.append(net.send(go.at[3, one], come.at[1, one], self.axis, -1))

    def pass_on(self):
        net, go, relay, come = self.net, self.go, self.relay, self.come
        one, two = self.parts
        for i, (s, part, step) in enumerate(((1, one, 1), (3, two, -1))):
            self.relays[i].wait_recv()

            def add(rows, i=i, s=s, part=part):
                at = shifted(rows, part.start)
                go[s, at] = (go[s, at].astype(F32) + relay[i, rows].astype(F32)).astype(BF)

            rows_loop(part.size, add)
            self.ends.append(net.send(go.at[s, part], come.at[i, part], self.axis, step))

    def finish(self):
        value, near, come, out = self.value, self.near, self.come, self.out
        where, c = lax.axis_index(self.axis), lax.axis_index("c")
        self.swaps[0].wait_recv()
        for copy in self.ends:
            copy.wait_recv()

        def add(rows):
            out[rows] = (
                value[where, c, rows].astype(F32) + near[0, rows].astype(F32)
            ) + (come[0, rows].astype(F32) + come[1, rows].astype(F32))

        rows_loop(self.size, add)


def ring_sum_scratch(size, width):
    return [
        pltpu.VMEM((4, size, width), BF),
        pltpu.VMEM((2, size // 2, width), BF),
        pltpu.VMEM((2, size, width), BF),
        pltpu.VMEM((4, size, width), BF),
    ]


class RowSum:
    def __init__(self, net, value, out, near, go, first, mid, last):
        self.net, self.value, self.out = net, value, out
        self.near, self.go, self.first, self.mid, self.last = near, go, first, mid, last
        c = lax.axis_index("c")
        self.size = value.shape[3]
        h = self.size // 2
        self.parts = pl.ds(0, h), pl.ds(h, h)
        self.swaps = [
            net.send(value.at[i, :, 1 - c], near.at[i], "c", 1) for i in range(4)
        ]

    def start(self):
        net, value, near, go = self.net, self.value, self.near, self.go
        c = lax.axis_index("c")
        for i in range(4):
            self.swaps[i].wait_recv()
            for j in range(4):

                def add(rows, i=i, j=j):
                    go[i, j, rows] = (
                        value[i, j, c, rows].astype(F32) + near[i, j, rows].astype(F32)
                    ).astype(BF)

                rows_loop(self.size, add)
        a, b = self.parts
        self.ones = [
            [net.send(go.at[along("y", d), :, a], self.first.at[0, d - 1], "y", d) for d in LINE],
            [net.send(go.at[:, along("z", d), b], self.first.at[1, d - 1], "z", d) for d in LINE],
        ]

    def turn(self):
        net, go, first, mid = self.net, self.go, self.first, self.mid
        y, z = lax.axis_index("y"), lax.axis_index("z")
        self.twos = []
        for k, axis in enumerate(("z", "y")):
            for copy in self.ones[k]:
                copy.wait_recv()
            for j in range(4):

                def add(rows, k=k, j=j):
                    at = shifted(rows, self.parts[k].start)
                    own = go[y, j, at] if k == 0 else go[j, z, at]
                    mid[k, j, rows] = (
                        own.astype(F32) + first[k, 0, j, rows].astype(F32)
                        + (first[k, 1, j, rows].astype(F32) + first[k, 2, j, rows].astype(F32))
                    ).astype(BF)

                rows_loop(self.parts[k].size, add)
            self.twos.append(
                [net.send(mid.at[k, along(axis, d)], self.last.at[k, d - 1], axis, d) for d in LINE]
            )

    def finish(self):
        mid, last, out = self.mid, self.last, self.out
        for k, axis in enumerate(("z", "y")):
            for copy in self.twos[k]:
                copy.wait_recv()
            here = lax.axis_index(axis)

            def add(rows, k=k, here=here):
                at = shifted(rows, self.parts[k].start)
                out[at] = (
                    mid[k, here, rows].astype(F32) + last[k, 0, rows].astype(F32)
                    + (last[k, 1, rows].astype(F32) + last[k, 2, rows].astype(F32))
                )

            rows_loop(self.parts[k].size, add)


def row_sum_scratch(size, width):
    h = size // 2
    return [
        pltpu.VMEM((4, 4, size, width), BF),
        pltpu.VMEM((4, 4, size, width), BF),
        pltpu.VMEM((2, 3, 4, h, width), BF),
        pltpu.VMEM((2, 4, h, width), BF),
        pltpu.VMEM((2, 3, h, width), BF),
    ]


Y_LINE = [("y", d) for d in LINE]
Z_LINE = [("z", d) for d in LINE]
X_LINE = [("x", d) for d in LINE]
X_RING = [("x", 1), ("x", -1)]
Y_RING = [("y", 1), ("y", -1)]
TWIN = [("c", 1)]


def shape(*dims, kind=BF):
    return jax.ShapeDtypeStruct(dims, kind)


def first_weights(first, both, out, down):
    def body(
        first_ref, both_ref, out_ref, down_ref, first_out, both_out, out_out, down_out, strip, sheet,
        sends, arrivals, locals_,
    ):
        net = Net(sends, arrivals, locals_)
        x, y, z, c = (lax.axis_index(a) for a in AXES)
        quarter = out_ref.shape[0] // 4
        greet(X_LINE + Y_LINE + Z_LINE + TWIN)
        row = RowGather(net, first_ref, first_out)
        piece = out_ref.at[pl.ds(pl.multiple_of(x * quarter, quarter), quarter)]
        piece_mine = net.keep(piece, strip.at[z])
        pieces = [net.send(piece, strip.at[z], "z", d) for d in LINE]
        both_mine = net.keep(both_ref.at[c], both_out.at[c])
        both_come = net.send(both_ref.at[1 - c], both_out.at[c], "c", 1)
        down_mine = net.keep(down_ref, down_out)
        row.spread()
        piece_mine.wait()
        for copy in pieces:
            copy.wait_recv()
        strip_mine = net.keep(strip, sheet.at[:, x])
        strips = [net.send(strip, sheet.at[:, x], "x", d) for d in LINE]
        row.finish()
        strip_mine.wait()
        for copy in strips:
            copy.wait_recv()
        half = sheet.shape[0] // 2
        sheet_keep = net.keep(sheet.at[pl.ds(half * c, half)], out_out.at[:, c])
        sheet_come = net.send(sheet.at[pl.ds(half * (1 - c), half)], out_out.at[:, c], "c", 1)
        for copy in (both_mine, sheet_keep, down_mine):
            copy.wait()
        for copy in (both_come, sheet_come):
            copy.wait_recv()
        net.close()

    rows, width = out.shape
    quarter = rows // 4
    outs = (
        shape(4, 4, 2, *first.shape), shape(*both.shape), shape(2, 2, 4, quarter, width), shape(*down.shape),
    )
    scratch = [pltpu.VMEM((4, quarter, width), BF), pltpu.VMEM((4, 4, quarter, width), BF)]
    return comm_call(
        body, "first_weights", 1, outs, (first, both, out, down), scratch, 36, 8, [IN_VMEM] * 4, [ANYWHERE] * 4,
    )


def keys_and_latents(key_value, latent, up):
    def body(kv_ref, lat_ref, up_ref, kv_out, lat_out, up_out, transit, sends, arrivals, locals_):
        net = Net(sends, arrivals, locals_)
        y, z, c = (lax.axis_index(a) for a in ROW)
        greet(Y_LINE + Z_LINE + TWIN)
        up_mine = net.keep(up_ref.at[y], transit.at[y, z])
        ups = [net.send(up_ref.at[along("y", d)], transit.at[y, z], "y", d) for d in LINE]
        row = RowGather(net, kv_ref, kv_out)
        ring = RingGather(net, lat_ref, lat_out, "y")
        up_mine.wait()
        for copy in ups:
            copy.wait_recv()
        ups = [net.send(transit.at[:, z], transit.at[:, z], "z", d) for d in LINE]
        row.spread()
        ring.forward()
        ring.share()
        for copy in ups:
            copy.wait_recv()
        up_keep = net.keep(transit.at[:, :, c], up_out.at[:, :, c])
        up_come = net.send(transit.at[:, :, 1 - c], up_out.at[:, :, c], "c", 1)
        row.finish()
        ring.finish()
        up_keep.wait()
        up_come.wait_recv()
        net.close()

    _, _, high, thin = up.shape
    outs = (shape(4, 4, 2, *key_value.shape), shape(4, 2, *latent.shape), shape(4, 4, 2, high, thin))
    return comm_call(
        body, "keys_and_latents", 2, outs, (key_value, latent, up), [pltpu.VMEM((4, 4, 2, high, thin), BF)], 44, 4,
        [IN_VMEM] * 3, [ANYWHERE] * 3,
    )


def heads_sum_and_cotangent(partial, cotangent):
    def body(part_ref, cot_ref, out_ref, cot_out, near, relay, come, go, sends, arrivals, locals_):
        net = Net(sends, arrivals, locals_)
        greet(X_RING + Y_RING + TWIN)
        ring = RingSum(net, part_ref, out_ref, "y", near, relay, come, go)
        feed = RingGather(net, cot_ref, cot_out, "x")
        ring.relay_far()
        ring.issue()
        feed.forward()
        ring.pass_on()
        feed.share()
        ring.finish()
        feed.finish()
        net.close()

    size, width = cotangent.shape
    outs = (shape(size, width, kind=F32), shape(4, 2, size, width))
    return comm_call(
        body, "heads_sum_and_cotangent", 3, outs, (partial, cotangent), ring_sum_scratch(size, width), 20, 2,
        [IN_VMEM, IN_VMEM], [IN_VMEM, ANYWHERE],
    )


def add_up(terms, out, rows):
    total = terms[0][rows].astype(F32)
    for term in terms[1:]:
        total = total + term[rows].astype(F32)
    out[rows] = total.astype(out.dtype)


def add_all(terms, out):
    rows_loop(out.shape[0], lambda rows: add_up(terms, out, rows))


def feed_forward(normed_two, normed, grad_out, both, down):
    size, width = normed_two.shape
    units = down.shape[0]
    tall = width // 4
    lanes = width // 2
    high = units // 16

    def body(
        two_ref, one_ref, cot_hbm, both_hbm, down_hbm, sum_out, one_out, branch_out, gb_out, mid_out,
        two, cot, both, down, hidden, grads, part, near, go, come, gb, gd, down_come,
        sends, arrivals, locals_,
    ):
        net = Net(sends, arrivals, locals_)
        x, y, z, c = (lax.axis_index(a) for a in AXES)
        both_load = net.keep(both_hbm, both)
        down_load = net.keep(down_hbm, down)
        cot_load = net.keep(cot_hbm, cot)
        greet(X_LINE + Y_LINE + Z_LINE + TWIN)
        feed = RingGather(net, two_ref, two, "x")
        one_mine = net.keep(one_ref.at[:, pl.ds(pl.multiple_of(y * tall, tall), tall)], one_out.at[y, c])
        ones = [
            net.send(
                one_ref.at[:, pl.ds(pl.multiple_of(along("y", d) * tall, tall), tall)],
                one_out.at[y, c], "y", d,
            )
            for d in LINE
        ]

        def block(s):
            where = along("x", s)
            at = pl.ds(pl.multiple_of(where * 2 * size, 2 * size), 2 * size)
            value = two[where].reshape(2 * size, width)
            pre = dot(value, both[...])
            grad = dot_nt(cot[where].reshape(2 * size, width), down[...])
            gate, up = pre[:, :units], pre[:, units:]
            sigma = 1.0 / (1.0 + jnp.exp(-gate))
            gated = gate * sigma
            hidden[at, :] = (gated * up).astype(BF)
            grads[at, :units] = (grad * up * (sigma + gated * (1.0 - sigma))).astype(BF)
            grads[at, units:] = (grad * gated).astype(BF)
            part[where] = dot_nt(grads[at, :], both[...]).astype(BF).reshape(2, size, width)
            return net.send(part.at[where, 1 - c], near.at[s], "c", 1)

        def pair(s):
            where = along("x", s)
            swaps[s].wait_recv()
            add_all([part.at[where, c], near.at[s]], go.at[s - 1])
            return net.send(go.at[s - 1], come.at[s - 1], "x", s)

        swaps = {}
        feed.mine.wait()
        feed.shared[0].wait_recv()
        both_load.wait()
        down_load.wait()
        cot_load.wait()
        swaps[0] = block(0)
        feed.forward()
        feed.share()
        one_mine.wait()
        spot = one_out.at[y, c]
        shared = [net.send(spot, spot, "c", 1)]
        for d in LINE:
            ones[d - 1].wait_recv()
            spot = one_out.at[along("y", -d), c]
            shared.append(net.send(spot, spot, "c", 1))
        feed.shared[1].wait_recv()
        feed.shared[2].wait_recv()
        swaps[1] = block(1)
        for copy in feed.far:
            copy.wait_recv()
        spot = two.at[along("x", 2), c]
        last = net.send(spot, spot, "c", 1)
        swaps[3] = block(3)
        ends = [pair(1)]
        last.wait_recv()
        swaps[2] = block(2)
        ends.append(pair(3))
        ends.append(pair(2))
        early, net.open = net.open, []

        first = []
        for k, axis in enumerate(("y", "z")):
            columns = slice(k * lanes, (k + 1) * lanes)
            gd[k] = (
                dot_tn(hidden[...], cot[...].reshape(8 * size, width)[:, columns])
                .astype(BF)
                .reshape(4, 4, high, lanes)
            )
            for d in LINE:
                at = along(axis, d)
                source = gd.at[k, at] if k == 0 else gd.at[k, :, at]
                first.append(net.send(source, down_come.at[k, d - 1], axis, d))

        gb_copies = []
        for i in range(8):
            at = pl.ds(i * 2 * size, 2 * size)
            gb[i] = dot_tn(two[...].reshape(8 * size, width)[:, i * 2 * size : (i + 1) * 2 * size], grads[...]).astype(BF)
            gb_copies.append(net.keep(gb.at[i], gb_out.at[at]))
        for copy in early:
            copy.wait_send()

        @pl.loop(0, 4)
        def _(i):
            at = pl.ds(pl.multiple_of(i * 2 * size, 2 * size), 2 * size)
            two[i] = dot(hidden[at, :], down[...]).astype(BF).reshape(2, size, width)

        branch_copy = net.keep(two, branch_out)
        swaps[0].wait_recv()
        for copy in ends:
            copy.wait_recv()
        add_all([part.at[x, c], near.at[0], come.at[0], come.at[1], come.at[2]], sum_out)
        for copy in shared:
            copy.wait_recv()
        for copy in first:
            copy.wait_recv()
        for k in range(2):
            for i in range(4):
                own = gd.at[k, y, i] if k == 0 else gd.at[k, i, z]
                add_all([own] + [down_come.at[k, d, i] for d in range(3)], mid_out.at[k, i])
        for copy in gb_copies + [branch_copy]:
            copy.wait()
        net.close()

    outs = (
        shape(size, width, kind=F32), shape(4, 2, size, tall), shape(4, 2, size, width), shape(width, 2 * units),
        shape(2, 4, high, lanes),
    )
    scratch = [
        pltpu.VMEM((4, 2, size, width), BF),
        pltpu.VMEM((4, 2, size, width), BF),
        pltpu.VMEM((width, 2 * units), BF),
        pltpu.VMEM((units, width), BF),
        pltpu.VMEM((8 * size, units), BF),
        pltpu.VMEM((8 * size, 2 * units), BF),
        pltpu.VMEM((4, 2, size, width), BF),
        pltpu.VMEM((4, size, width), BF),
        pltpu.VMEM((3, size, width), BF),
        pltpu.VMEM((3, size, width), BF),
        pltpu.VMEM((8, 2 * size, 2 * units), BF),
        pltpu.VMEM((2, 4, 4, high, lanes), BF),
        pltpu.VMEM((2, 3, 4, high, lanes), BF),
    ]
    return comm_call(
        body, "feed_forward", 4, outs, (normed_two, normed, grad_out, both, down), scratch, 32, 14,
        [IN_VMEM] * 2 + [ANYWHERE] * 3, [IN_VMEM, ANYWHERE, ANYWHERE, ANYWHERE, IN_VMEM],
    )


class FirstStep:
    def __init__(self, net, value, columns, axis, own, come, out):
        self.own, self.come, self.out = own, come, out
        self.copies = []
        for d in (1, 2, 3, 0):
            at = along(axis, d)
            source = value.at[at, :, :, columns] if axis == "y" else value.at[:, at, :, columns]
            if d:
                self.copies.append(net.send(source, come.at[d - 1], axis, d))
            else:
                self.mine = net.keep(source, own)

    def finish(self):
        self.mine.wait()
        for copy in self.copies:
            copy.wait_recv()
        for i in range(4):
            add_all([self.own.at[i]] + [self.come.at[d, i] for d in range(3)], self.out.at[i])


class SecondStep:
    def __init__(self, net, mid, axis, come):
        self.mid, self.axis, self.come = mid, axis, come
        self.copies = [net.send(mid.at[along(axis, d)], come.at[d - 1], axis, d) for d in LINE]

    def finish(self, out):
        for copy in self.copies:
            copy.wait_recv()
        here = lax.axis_index(self.axis)
        add_all([self.mid.at[here]] + [self.come.at[d] for d in range(3)], out)


def heads_gather_and_branch(value, partial, mid, gb):
    size, width = value.shape
    _, _, high, lanes = mid.shape
    _, _, tall, wide = gb.shape
    third = wide // 3

    def body(ref, part_ref, mid_ref, gb_ref, out, part_out, mid_out, gb_out, *rest):
        net = Net(*rest[8:])
        greet(X_RING + Y_LINE + Z_LINE + TWIN)
        gathering = RingGather(net, ref, out, "y")
        ring = RingSum(net, part_ref, part_out, "x", *rest[:4])
        halves = [SecondStep(net, mid_ref.at[k], axis, rest[4 + k]) for k, axis in enumerate(("z", "y"))]
        step = FirstStep(net, gb_ref, pl.ds(third, third), "z", rest[6], rest[7], gb_out)
        ring.relay_far()
        ring.issue()
        gathering.forward()
        ring.pass_on()
        gathering.share()
        for k in range(2):
            halves[k].finish(mid_out.at[:, pl.ds(k * lanes, lanes)])
        gathering.finish()
        ring.finish()
        step.finish()
        net.close()

    outs = (
        shape(4, 2, size, width), shape(size, width, kind=F32), shape(high, 2 * lanes), shape(4, tall, third),
    )
    scratch = [
        pltpu.VMEM((3, high, lanes), BF),
        pltpu.VMEM((3, high, lanes), BF),
        pltpu.VMEM((4, tall, third), BF),
        pltpu.VMEM((3, 4, tall, third), BF),
    ]
    return comm_call(
        body, "heads_gather_and_branch", 6, outs, (value, partial, mid, gb),
        ring_sum_scratch(size, width) + scratch, 30, 3,
        [IN_VMEM] * 3 + [ANYWHERE], [ANYWHERE] + [IN_VMEM] * 3,
    )


def keys_and_latents_sum(grad_kv, partial, grad_up, grad_out, mids, grad_down):
    _, _, _, size, thin = grad_kv.shape
    width = partial.shape[3]
    high, lanes = grad_up.shape[3], grad_up.shape[4] // 4
    _, quarter, wide = grad_out.shape
    tall, third = mids[0].shape[1:]

    def body(
        kv_ref, part_ref, up_ref, out_ref, one_ref, two_ref, down_ref, kv_out, part_out, up_out, out_out, mid_out,
        down_out, *rest,
    ):
        net = Net(*rest[13:])
        up_come, out_come = rest[9:11]
        x, z = lax.axis_index("x"), lax.axis_index("z")

        def lane(at):
            return pl.ds(pl.multiple_of(at * lanes, lanes), lanes)

        greet(X_LINE + Y_LINE + Z_LINE + TWIN)
        row = RowSum(net, kv_ref, kv_out, *rest[:5])
        ring = RingSum(net, part_ref, part_out, "y", *rest[5:9])
        ups = [
            net.send(up_ref.at[:, :, :, :, lane(along("x", d))], up_come.at[d - 1], "x", d) for d in LINE
        ]
        outs = [net.send(out_ref.at[along("z", d)], out_come.at[d - 1], "z", d) for d in LINE]
        halves = [
            SecondStep(net, mid, axis, come)
            for mid, axis, come in ((one_ref, "z", rest[11]), (two_ref, "y", rest[12]))
        ]
        down_mine = net.keep(down_ref, down_out.at[x])
        downs = [net.send(down_ref, down_out.at[x], "x", d) for d in LINE]
        row.start()
        ring.relay_far()
        ring.issue()
        row.turn()
        ring.pass_on()
        for copy in outs:
            copy.wait_recv()
        add_all([out_ref.at[z]] + [out_come.at[d] for d in range(3)], out_out)
        for copy in ups:
            copy.wait_recv()
        for i in range(4):

            @pl.loop(0, 8)
            def _(k, i=i):
                j, core = k // 2, k % 2
                add_all(
                    [up_ref.at[i, j, core, :, lane(x)]] + [up_come.at[d, i, j, core] for d in range(3)],
                    up_out.at[i, j, core],
                )

        halves[0].finish(mid_out.at[:, pl.ds(0, third)])
        halves[1].finish(mid_out.at[:, pl.ds(2 * third, third)])
        ring.finish()
        row.finish()
        down_mine.wait()
        for copy in downs:
            copy.wait_recv()
        net.close()

    outs = (
        shape(size, thin, kind=F32), shape(size, width, kind=F32), shape(4, 4, 2, high, lanes),
        shape(quarter, wide), shape(tall, 3 * third), shape(4, *grad_down.shape),
    )
    scratch = [
        pltpu.VMEM((3, 4, 4, 2, high, lanes), BF),
        pltpu.VMEM((3, quarter, wide), BF),
        pltpu.VMEM((3, tall, third), BF),
        pltpu.VMEM((3, tall, third), BF),
    ]
    return comm_call(
        body, "keys_and_latents_sum", 7, outs, (grad_kv, partial, grad_up, grad_out, *mids, grad_down),
        row_sum_scratch(size, thin) + ring_sum_scratch(size, width) + scratch, 46, 2,
        [IN_VMEM] * 7, [IN_VMEM] * 5 + [ANYWHERE],
    )


def firsts_gather(value, both, grad_out, grad_up):
    def body(
        ref, both_ref, out_ref, up_ref, gathered, both_out, out_out, up_out, up_come, up_sum, up_y,
        sends, arrivals, locals_,
    ):
        net = Net(sends, arrivals, locals_)
        x, y, z, c = (lax.axis_index(a) for a in AXES)
        greet(X_LINE + Y_LINE + Z_LINE + TWIN)
        mine = net.keep(ref.at[c], gathered.at[y, c])
        come = net.send(ref.at[1 - c], gathered.at[y, c], "c", 1)
        both_mine = net.keep(both_ref.at[c], both_out.at[x, c])
        both_come = net.send(both_ref.at[1 - c], both_out.at[x, c], "c", 1)
        ups = [net.send(up_ref.at[:, along("z", d)], up_come.at[d - 1], "z", d) for d in LINE]
        outs = [net.send(out_ref, out_out.at[x], "x", d) for d in LINE]
        out_mine = net.keep(out_ref, out_out.at[x])

        mine.wait()
        spot = gathered.at[y, c]
        ahead = [net.send(spot, spot, "y", 1), net.send(spot, spot, "y", -1)]
        come.wait_recv()
        spot = gathered.at[y, 1 - c]
        ahead += [net.send(spot, spot, "y", 1), net.send(spot, spot, "y", -1)]
        both_mine.wait()
        both_come.wait_recv()
        zero, one = both_out.at[x, 0], both_out.at[x, 1]
        right = [net.send(spot, spot, "x", 1) for spot in (zero, one)]
        left = [net.send(spot, spot, "x", -1) for spot in (one, zero)]

        for copy in ups:
            copy.wait_recv()
        for i in range(4):
            for core in range(2):
                add_all(
                    [up_ref.at[i, z, core]] + [up_come.at[d, i, core] for d in range(3)], up_sum.at[i, core]
                )
        ups = [net.send(up_sum.at[along("y", d)], up_y.at[y], "y", d) for d in LINE]
        up_mine = net.keep(up_sum.at[y], up_y.at[y])

        ahead[0].wait_recv()
        spot = gathered.at[along("y", -1), c]
        ahead.append(net.send(spot, spot, "y", 1))
        ahead[3].wait_recv()
        spot = gathered.at[along("y", 1), 1 - c]
        ahead.append(net.send(spot, spot, "y", -1))

        up_mine.wait()
        for copy in ups:
            copy.wait_recv()
        up_near = net.send(up_y.at[:, 1 - c], up_out.at[x, :, c], "c", 1)
        up_mine = net.keep(up_y.at[:, c], up_out.at[x, :, c])

        right[0].wait_recv()
        spot = both_out.at[along("x", -1), 0]
        far = [net.send(spot, spot, "x", 1)]
        left[0].wait_recv()
        spot = both_out.at[along("x", 1), 1]
        far.append(net.send(spot, spot, "x", -1))

        up_near.wait_recv()
        up_mine.wait()
        spot = up_out.at[x]
        ups = [net.send(spot, spot, "x", d) for d in LINE]
        for copy in [ahead[i] for i in (1, 2, 4, 5)] + [right[1], left[1]] + far + outs + ups:
            copy.wait_recv()
        out_mine.wait()
        net.close()

    tall, wide = grad_out.shape
    _, _, _, high, lanes = grad_up.shape
    outs = (
        shape(4, *value.shape), shape(4, *both.shape), shape(4, tall, wide), shape(4, 4, 2, high, lanes),
    )
    scratch = [
        pltpu.VMEM((3, 4, 2, high, lanes), BF),
        pltpu.VMEM((4, 2, high, lanes), BF),
        pltpu.VMEM((4, 2, high, lanes), BF),
    ]
    return comm_call(
        body, "firsts_gather", 8, outs, (value, both, grad_out, grad_up), scratch, 40, 6,
        [IN_VMEM] * 4, [ANYWHERE, ANYWHERE, IN_VMEM, IN_VMEM],
    )


def last_sums(grad_first, gains):
    def body(
        first_ref, gain_ref, first_out, gain_out, wide, first_come, first_x,
        gain_near, gain_one, gain_come, gain_two, gain_y, gain_three, gain_x, sends, arrivals, locals_,
    ):
        net = Net(sends, arrivals, locals_)
        x, y, z, c = (lax.axis_index(a) for a in AXES)
        greet(X_LINE + Y_LINE + Z_LINE + TWIN)
        first_near = net.send(first_ref.at[:, 1 - c], wide.at[c], "c", 1)
        first_mine = net.keep(first_ref.at[:, c], wide.at[c])
        near = net.send(gain_ref.at[:, :, 1 - c], gain_near, "c", 1)
        first_mine.wait()
        first_near.wait_recv()
        firsts = [
            [net.send(wide.at[core, along("z", d)], first_come.at[d - 1, core], "z", d) for d in LINE]
            for core in range(2)
        ]
        near.wait_recv()
        gain_one[...] = gain_ref[:, :, c] + gain_near[...]
        comes = [net.send(gain_one.at[:, along("z", d)], gain_come.at[d - 1], "z", d) for d in LINE]
        def onward(core):
            for copy in firsts[core]:
                copy.wait_recv()
            add_all([wide.at[core, z]] + [first_come.at[d, core] for d in range(3)], first_x.at[x, core])
            spot = first_x.at[x, core]
            return [net.send(spot, spot, "x", d) for d in LINE]

        finals = [onward(0)]
        for copy in comes:
            copy.wait_recv()
        gain_two[...] = (gain_one[:, z] + gain_come[0]) + (gain_come[1] + gain_come[2])
        comes = [net.send(gain_two.at[along("y", d)], gain_y.at[d - 1], "y", d) for d in LINE]
        finals.append(onward(1))
        for copy in comes:
            copy.wait_recv()
        gain_three[...] = (gain_two[y] + gain_y[0]) + (gain_y[1] + gain_y[2])
        gain_mine = net.keep(gain_three, gain_x.at[x])
        comes = [net.send(gain_three, gain_x.at[x], "x", d) for d in LINE]
        for core in range(2):
            for copy in finals[core]:
                copy.wait_recv()
            add_all([first_x.at[i, core] for i in range(4)], first_out.at[core])
        gain_mine.wait()
        for copy in comes:
            copy.wait_recv()
        gain_out[...] = (gain_x[0] + gain_x[1]) + (gain_x[2] + gain_x[3])
        net.close()

    _, _, high, lanes = grad_first.shape
    outs = (shape(2, high, lanes, kind=F32), shape(8, 128, kind=F32))
    scratch = [
        pltpu.VMEM((2, 4, high, lanes), BF),
        pltpu.VMEM((3, 2, high, lanes), BF),
        pltpu.VMEM((4, 2, high, lanes), BF),
        pltpu.VMEM((4, 4, 8, 128), F32),
        pltpu.VMEM((4, 4, 8, 128), F32),
        pltpu.VMEM((3, 4, 8, 128), F32),
        pltpu.VMEM((4, 8, 128), F32),
        pltpu.VMEM((3, 8, 128), F32),
        pltpu.VMEM((8, 128), F32),
        pltpu.VMEM((4, 8, 128), F32),
    ]
    return comm_call(
        body, "last_sums", 9, outs, (grad_first, gains), scratch, 24, 2, [IN_VMEM] * 2, [IN_VMEM] * 2,
    )


def attend_back_kernel(
    qt_ref, do_ref, o_ref, kv_ref, begin_ref, slot_ref, lse_ref, cos_ref, sin_ref, go_ref, mid_ref, gb_ref,
    dq_ref, dkv_ref, go_out, one_out, two_out, mid_out,
    kt, sums, accum, gb_own, gb_come, mid_come, stack, go_come, sends, arrivals, locals_,
):
    net = Net(sends, arrivals, locals_)
    x, c = lax.axis_index("x"), lax.axis_index("c")
    greet(X_LINE + Y_LINE + Z_LINE + TWIN)
    half = go_ref.shape[0]
    third = mid_ref.shape[-1]
    quarter = go_out.shape[1]

    def strip(at):
        return pl.ds(pl.multiple_of(at * quarter, quarter), quarter)

    go_mine = net.keep(go_ref.at[:, c], stack.at[pl.ds(half * c, half)])
    go_near = net.send(go_ref.at[:, 1 - c], stack.at[pl.ds(half * c, half)], "c", 1)
    steps = [
        FirstStep(net, gb_ref, pl.ds(0, third), "y", gb_own.at[0], gb_come.at[0], one_out),
        FirstStep(net, gb_ref, pl.ds(2 * third, third), "z", gb_own.at[1], gb_come.at[1], two_out),
    ]
    second = SecondStep(net, mid_ref, "y", mid_come)
    go_mine.wait()
    go_near.wait_recv()
    go_sends = [net.send(stack.at[:, strip(along("x", d))], go_come.at[d - 1], "x", d) for d in LINE]
    depth = lax.axis_index("z")
    segments = slot_ref.shape[0]
    rows = slot_ref.shape[2]
    tokens = rows // 2
    sums[...] = jnp.zeros_like(sums)
    turned(kv_ref, kt, segments * (segments - 1) + depth + 1, KEYS)
    for seg in range(segments):
        here = pl.ds(seg * tokens, tokens)

        def stacked(ref):
            value = ref[here, :]
            return jnp.concatenate([value[:, :SIZE], value[:, SIZE:]], axis=0)

        query_t = qt_ref[seg]
        query = query_t.T
        grad = stacked(do_ref)
        grad_t = grad.T
        delta = jnp.sum(
            grad_t.astype(F32) * stacked(o_ref).T.astype(F32), axis=0, keepdims=True
        )
        begin = begin_ref[seg]
        slot = slot_ref[seg]
        lse = lse_ref[seg]
        accum[...] = jnp.zeros_like(accum)

        @pl.loop(0, segments * seg + depth + 1)
        def _(block):
            at = pl.multiple_of(block * BLOCK, BLOCK)
            keys = pl.ds(at, BLOCK)
            scores = dot(kv_ref[keys, KEYS], query_t)
            key = lax.broadcasted_iota(jnp.int32, scores.shape, 0) + at
            allowed = (key >= begin) & (key <= slot)
            probs = jnp.where(allowed, jnp.exp(scores - lse), 0.0)
            grad_probs = dot(kv_ref[keys, VALUES], grad_t)
            grad_scores = (probs * (grad_probs - delta)).astype(BF)
            sums[keys, VALUES] += dot(probs.astype(BF), grad)
            sums[keys, KEYS] += dot(grad_scores, query)
            accum[...] += dot(kt[:, keys], grad_scores)

        cosine, sine = cos_ref[seg], sin_ref[seg]
        for head in range(2):
            part = accum[:, head * tokens : (head + 1) * tokens] * (SIZE ** -0.5)
            lower, upper = part[:HALF], part[HALF:]
            turn = jnp.concatenate(
                [lower * cosine + upper * sine, upper * cosine - lower * sine], axis=0
            )
            dq_ref[here, head * SIZE : (head + 1) * SIZE] = turn.T.astype(BF)

    dkv_ref[...] = sums[...].astype(BF)
    second.finish(mid_out)
    for copy in go_sends:
        copy.wait_recv()
    for i in range(2 * half):
        add_all([stack.at[i, strip(x)]] + [go_come.at[d, i] for d in range(3)], go_out.at[i])
    for step in steps:
        step.finish()
    net.close()


def attend_back(qt, do, o, kv, begin, slot, lse, cosine, sine, grad_out, mid, gb):
    segments, _, rows = slot.shape
    half, _, tall, wide = grad_out.shape
    _, high, third = mid.shape
    part = jax.ShapeDtypeStruct((4, high, third), BF)
    return pl.pallas_call(
        attend_back_kernel,
        name="attend_back",
        out_shape=(
            jax.ShapeDtypeStruct(do.shape, BF),
            jax.ShapeDtypeStruct(kv.shape, BF),
            jax.ShapeDtypeStruct((2 * half, tall // 4, wide), BF),
            part,
            part,
            jax.ShapeDtypeStruct((high, third), BF),
        ),
        in_specs=[IN_VMEM] * 11 + [ANYWHERE],
        out_specs=[IN_VMEM] * 6,
        scratch_shapes=[
            pltpu.VMEM((SIZE, kv.shape[0]), BF),
            pltpu.VMEM(kv.shape, F32),
            pltpu.VMEM((SIZE, rows), F32),
            pltpu.VMEM((2, 4, high, third), BF),
            pltpu.VMEM((2, 3, 4, high, third), BF),
            pltpu.VMEM((3, high, third), BF),
            pltpu.VMEM((2 * half, tall, wide), BF),
            pltpu.VMEM((3, 2 * half, tall // 4, wide), BF),
        ] + semaphores(14, 3),
        compiler_params=pltpu.CompilerParams(
            collective_id=10, has_side_effects=True, vmem_limit_bytes=60 << 20
        ),
    )(qt, do, o, kv, begin, slot, lse, cosine, sine, grad_out, mid, gb)


def gather(value, axes):
    return lax.all_gather(value, axes, axis=0, tiled=True)


def on_device(
    block_input, cotangent, lengths, norm_gain, q_down, q_gain, q_up, key_weight, value_weight,
    out_weight, ffn_gain, gate_weight, up_weight, down_weight,
):
    rows, width = block_input.shape
    latent_width = q_down.shape[1]
    n_x, n_y, n_z, n_c = (lax.axis_size(a) for a in ("x", "y", "z", "c"))
    x, y, z, c = (lax.axis_index(a) for a in ("x", "y", "z", "c"))
    span = n_y * n_z * n_c
    members = n_y * n_c
    lengths_row = lengths[0]

    mine = (y * n_z + z) * n_c + c
    slots_mine = mine * rows + jnp.arange(rows, dtype=jnp.int32)
    begin_mine, _ = places_of(lengths_row, slots_mine)
    cosine, sine = tables(slots_mine - begin_mine)
    strip = n_c * rows
    slots_group = (
        (jnp.arange(n_y, dtype=jnp.int32)[:, None] * n_z + z) * strip
        + jnp.arange(strip, dtype=jnp.int32)[None, :]
    ).reshape(-1)
    begin_group, live_group = places_of(lengths_row, slots_group)
    cosine_group, sine_group = tables_across((slots_group - begin_group).reshape(n_y, strip))
    begin_lanes = jnp.tile(begin_group.reshape(n_y, 1, strip), (1, 1, 2))
    slot_lanes = jnp.tile(slots_group.reshape(n_y, 1, strip), (1, 1, 2))
    live_lanes = jnp.tile(live_group.reshape(n_y, 1, strip), (1, 1, 2))

    shard = norm_gain.shape[0]
    extra = jnp.stack(
        [norm_gain, ffn_gain, jnp.pad(q_gain, (0, shard - q_gain.shape[0]))], axis=1
    ).astype(BF)
    first_width = latent_width + 2 * SIZE
    first = jnp.concatenate(
        [q_down, key_weight, value_weight, jnp.pad(extra, ((0, 0), (0, 125)))], axis=1
    )
    per_heads = q_up.shape[1] // members
    q_rows = q_up.shape[0]

    wide = gate_weight.shape[1]
    down_rows = down_weight.shape[0]
    share = down_rows // n_x
    padded = -(-share // 16) * 16
    source = lax.broadcasted_iota(jnp.int32, (wide // 2, n_c * (span // 4) * padded), 0)
    target = lax.broadcasted_iota(jnp.int32, source.shape, 1)
    block_at = target // (padded * (span // 4)) + n_c * ((target // padded) % (span // 4))
    inside = target % padded
    picks = (
        (source == block_at * down_rows + x * share + inside) & (inside < share)
    ).astype(BF)

    def spread(weight):
        stacked = jnp.concatenate([weight[:, : wide // 2], weight[:, wide // 2 :]], axis=0)
        part = dot(stacked, picks).astype(BF)
        part = part.reshape(2, shard, n_c, -1).transpose(2, 1, 0, 3)
        return part.reshape(n_c, shard, -1)

    both = jnp.concatenate([spread(gate_weight), spread(up_weight)], axis=2)
    units = both.shape[-1] // 2
    down_part = lax.dynamic_slice_in_dim(down_weight, x * share, share)
    down_part = jnp.pad(down_part, ((0, padded - share), (0, 0)))
    first_full, both, out_heads, down_part = first_weights(first, both, out_weight, down_part)
    out_heads = out_heads.reshape(per_heads, width)
    first_full = first_full.reshape(span * shard, -1)
    both = both.reshape(n_c * shard, 2 * units)
    extra_full = first_full[:, first_width : first_width + 3].astype(F32)
    first_full = first_full[:, :first_width]
    gain_one = extra_full[:, 0]
    gain_two = extra_full[:, 1]
    gain_latent = extra_full[:, 2].reshape(span, shard)[:, : q_gain.shape[0]].reshape(-1)

    both_full = gather(both, ("y", "z"))
    down_use = gather(down_part, ("y", "z"))

    inputs = block_input.astype(F32)
    inverse_one = lax.rsqrt(jnp.mean(inputs * inputs, axis=-1, keepdims=True) + EPSILON)
    normed = (inputs * inverse_one * gain_one).astype(BF)
    firsts = dot(normed, first_full)
    latent = firsts[:, :latent_width]
    inverse_latent = lax.rsqrt(jnp.mean(latent * latent, axis=-1, keepdims=True) + EPSILON)
    latent_normed = (latent * inverse_latent * gain_latent).astype(BF)
    key_mine = rotate(firsts[:, latent_width : latent_width + SIZE], cosine, sine).astype(BF)
    value_mine = firsts[:, latent_width + SIZE :].astype(BF)
    key_value, latent_group, up_heads = keys_and_latents(
        jnp.concatenate([key_mine, value_mine], axis=1), latent_normed,
        q_up.reshape(q_rows, n_y, n_c, per_heads).transpose(1, 2, 0, 3),
    )
    up_heads = up_heads.reshape(span * q_rows, per_heads)
    key_value = key_value.reshape(span * rows, 2 * SIZE)
    group = members * rows
    latent_group = latent_group.reshape(group, latent_width)
    mixed, queries_t, lse = attend(
        dot(latent_group, up_heads), key_value, begin_lanes, slot_lanes, live_lanes,
        cosine_group, sine_group,
    )
    branch, grad_feed = heads_sum_and_cotangent(
        dot(mixed, out_heads).astype(BF).reshape(n_y, n_c, rows, width), cotangent
    )
    middle = inputs + branch

    inverse_two = lax.rsqrt(jnp.mean(middle * middle, axis=-1, keepdims=True) + EPSILON)
    grad_normed_two, normed_part, branch_part, grad_both, grad_down = feed_forward(
        (middle * inverse_two * gain_two).astype(BF), normed, grad_feed, both_full, down_use
    )
    normed_part = normed_part.reshape(group, -1)
    grad_result = cotangent.astype(F32)
    grad_mid_norm, grad_gain_two = norm_back(middle, inverse_two, gain_two, grad_normed_two)
    grad_middle = grad_result + grad_mid_norm

    def collect(grads):
        parts = grads.reshape(n_x, n_c, shard, 2, units // 2).transpose(0, 3, 2, 1, 4)
        parts = parts.reshape(n_x, 2 * shard, n_c * units // 2)
        whole = 0.0
        for i in range(n_x):
            picked = (
                (source == block_at * down_rows + i * share + inside) & (inside < share)
            ).astype(BF)
            whole = whole + dot_nt(parts[i], picked)
        return jnp.concatenate([whole[:shard], whole[shard:]], axis=1)

    grad_both = grad_both.reshape(n_y, n_z, n_c * shard, 2 * units)
    grad_branch, branch_two, grad_down, grad_mid = heads_gather_and_branch(
        grad_middle.astype(BF), branch_part, grad_down, grad_both
    )
    grad_branch = grad_branch.reshape(group, width)
    output = (middle + branch_two).astype(BF)
    grad_mixed = dot_nt(grad_branch, out_heads).astype(BF)
    grad_attended = grad_mixed * live_group[:, None].astype(BF)
    grad_out = dot_tn(mixed, grad_branch).astype(BF)
    out_rows = out_weight.shape[0]
    grad_query_raw, grad_kv, grad_out, grad_one, grad_two, grad_mid = attend_back(
        queries_t, grad_attended, mixed, key_value, begin_lanes, slot_lanes, lse,
        cosine_group, sine_group, grad_out.reshape(n_z // n_c, n_c, out_rows, width), grad_mid, grad_both,
    )
    grad_up_heads = dot_tn(latent_group, grad_query_raw).astype(BF)
    grad_kv, grad_latent_normed, grad_up_heads, grad_out, grad_both, grad_down = keys_and_latents_sum(
        grad_kv.reshape(n_y, n_z, n_c, rows, 2 * SIZE),
        dot_nt(grad_query_raw, up_heads).astype(BF).reshape(n_y, n_c, rows, latent_width),
        grad_up_heads.reshape(n_y, n_z, n_c, q_rows, per_heads),
        grad_out, (grad_one, grad_two), grad_down,
    )
    third = grad_mid.shape[1]
    grad_both = jnp.concatenate([grad_both[:, :third], grad_mid, grad_both[:, 2 * third :]], axis=1)
    grad_key_raw = unrotate(grad_kv[:, :SIZE], cosine, sine).astype(BF)
    grad_value_raw = grad_kv[:, SIZE:].astype(BF)
    grad_latent_f, grad_gain_latent = norm_back(
        latent, inverse_latent, gain_latent, grad_latent_normed
    )
    grad_firsts = jnp.concatenate(
        [grad_latent_f.astype(BF), grad_key_raw, grad_value_raw], axis=1
    )
    grad_normed = dot_nt(grad_firsts, first_full)
    grad_input_norm, grad_gain_one = norm_back(inputs, inverse_one, gain_one, grad_normed)
    input_grad = grad_middle + grad_input_norm

    half_first = first_width // n_c
    first_part, grad_both, grad_out, grad_up_heads = firsts_gather(
        grad_firsts.reshape(rows, n_c, half_first).transpose(1, 0, 2),
        grad_both.reshape(n_c, shard, 2 * units), grad_out, grad_up_heads,
    )
    first_part = first_part.reshape(group, half_first)
    grad_first = dot_tn(normed_part, first_part).astype(BF)
    gains = jnp.concatenate(
        [
            grad_gain_one.reshape(span, shard),
            grad_gain_two.reshape(span, shard),
            grad_gain_latent.reshape(span, -1),
        ],
        axis=1,
    )
    shares = gains.shape[1]
    gains = jnp.pad(gains, ((0, 0), (0, 8 * 128 - shares))).reshape(n_y, n_z, n_c, 8, 128)
    grad_first, gains = last_sums(grad_first.reshape(n_z, n_c, shard, half_first), gains)
    gains = gains.reshape(-1)
    grad_first = jnp.concatenate([grad_first[0], grad_first[1]], axis=1)
    grad_out = grad_out.reshape(out_rows, width).astype(F32)
    grad_q_up = grad_up_heads.transpose(3, 1, 2, 0, 4).reshape(q_rows, -1).astype(F32)
    grad_gate = collect(grad_both[..., :units])
    grad_up = collect(grad_both[..., units:])
    grad_down = grad_down[:, :share].reshape(down_rows, width).astype(F32)
    return (
        output,
        input_grad,
        gains[:shard],
        grad_first[:, :latent_width],
        gains[2 * shard : shares],
        grad_q_up,
        grad_first[:, latent_width : latent_width + SIZE],
        grad_first[:, latent_width + SIZE :],
        grad_out,
        gains[shard : 2 * shard],
        grad_gate,
        grad_up,
        grad_down,
    )


def solution(mesh):
    sizes = (4, 4, 4, 2)
    grid = Mesh(mesh.devices.reshape(sizes), ("x", "y", "z", "c"))
    tokens = P(("x", "y", "z", "c"), None)
    wide, thin = P(ROW, None), P(ROW)
    in_specs = (
        tokens, tokens, P("x", None), thin, wide, thin, wide, wide, wide, wide, thin, wide, wide,
        wide,
    )
    out_specs = (
        tokens, tokens, thin, wide, thin, wide, wide, wide, wide, thin, wide, wide, wide,
    )
    return jax.shard_map(
        on_device, mesh=grid, in_specs=in_specs, out_specs=out_specs, check_vma=False
    )
```

```python
import functools
import math

import jax
import jax.numpy as jnp
from jax import lax
from jax.experimental import pallas as pl
from jax.experimental.pallas import tpu as pltpu
from jax.sharding import Mesh
from jax.sharding import PartitionSpec as P

EPSILON = 1e-06
MASKED = -1e30
BF = jnp.bfloat16
F32 = jnp.float32
SIZE = 256
HALF = 128
BLOCK = 256
ROW = ("y", "z", "c")
HEADS = ("y", "c")
FEED = ("x", "c")


def dot(left, right):
    return jnp.dot(left, right, preferred_element_type=F32)


def dot_tn(left, right):
    return lax.dot_general(left, right, (((0,), (0,)), ((), ())), preferred_element_type=F32)


def dot_nt(left, right):
    return lax.dot_general(left, right, (((1,), (1,)), ((), ())), preferred_element_type=F32)


def norm_back(values, inverse, gain, grad):
    scaled = grad * gain
    grad_values = inverse * scaled - values * inverse * inverse * inverse * jnp.mean(
        scaled * values, axis=-1, keepdims=True
    )
    return grad_values, jnp.sum(grad * values * inverse, axis=0)


def places_of(lengths_row, slots):
    ends = jnp.cumsum(lengths_row)
    begins = jnp.concatenate([ends - lengths_row, ends[-1:]])
    begin = jnp.max(jnp.where(slots[:, None] >= begins[None, :], begins[None, :], 0), axis=1)
    live = (slots < ends[-1]).astype(F32)
    return begin, live


def tables(position):
    freq = jnp.exp(jnp.arange(HALF, dtype=F32) * (-math.log(10000.0) / HALF))
    angle = position.astype(F32)[:, None] * freq[None, :]
    return jnp.cos(angle), jnp.sin(angle)


def tables_across(position):
    freq = jnp.exp(jnp.arange(HALF, dtype=F32) * (-math.log(10000.0) / HALF))
    angle = position.astype(F32)[..., None, :] * freq[:, None]
    return jnp.cos(angle), jnp.sin(angle)


def rotate(values, cosine, sine):
    lower, upper = values[..., :HALF], values[..., HALF:]
    return jnp.concatenate([lower * cosine - upper * sine, upper * cosine + lower * sine], axis=-1)


def unrotate(grad, cosine, sine):
    lower, upper = grad[..., :HALF], grad[..., HALF:]
    return jnp.concatenate([lower * cosine + upper * sine, upper * cosine - lower * sine], axis=-1)


def turned(source, target, count, columns):
    @pl.loop(0, count)
    def _(block):
        at = pl.ds(pl.multiple_of(block * BLOCK, BLOCK), BLOCK)
        target[:, at] = source[at, columns].T


KEYS, VALUES = slice(0, SIZE), slice(SIZE, 2 * SIZE)


def sweep(segment, segments, depth, tile):
    count = segments * segment + depth
    last = (segment // (segments - 1)) * (depth // (lax.axis_size("z") - 1))
    guarded = jnp.minimum(count, 1) * (1 - last) + count * last
    free = count - guarded

    @pl.loop(0, guarded)
    def _(i):
        tile(pl.multiple_of(i * BLOCK, BLOCK), BLOCK, True)

    @pl.loop(0, free // 2)
    def _(i):
        tile(pl.multiple_of((guarded + 2 * i) * BLOCK, BLOCK), 2 * BLOCK, False)

    @pl.loop(0, free % 2)
    def _(i):
        tile(pl.multiple_of((count - 1) * BLOCK, BLOCK), BLOCK, False)

    tile(pl.multiple_of(count * BLOCK, BLOCK), BLOCK, True)


def attend_kernel(
    q_ref, kv_ref, begin_ref, slot_ref, live_ref, cos_ref, sin_ref,
    out_ref, qt_ref, lse_ref, vt, peak, total, accum,
):
    depth = lax.axis_index("z")
    segments = slot_ref.shape[0]
    rows = slot_ref.shape[2]
    tokens = rows // 2
    turned(kv_ref, vt, segments * (segments - 1) + depth + 1, VALUES)

    @pl.loop(0, segments)
    def _(seg):
        here = pl.ds(pl.multiple_of(seg * tokens, tokens), tokens)
        cosine, sine = cos_ref[seg], sin_ref[seg]
        for head in range(2):
            raw = q_ref[here, head * SIZE : (head + 1) * SIZE].T
            lower, upper = raw[:HALF], raw[HALF:]
            turn = jnp.concatenate(
                [lower * cosine - upper * sine, upper * cosine + lower * sine], axis=0
            )
            qt_ref[seg, :, head * tokens : (head + 1) * tokens] = (
                turn.astype(BF) * (SIZE ** -0.5)
            ).astype(BF)
        peak[...] = jnp.full_like(peak, MASKED)
        total[...] = jnp.zeros_like(total)
        accum[...] = jnp.zeros_like(accum)

        def tile(at, size, masked):
            scores = dot(kv_ref[pl.ds(at, size), KEYS], qt_ref[seg])
            if masked:
                key = lax.broadcasted_iota(jnp.int32, scores.shape, 0) + at
                scores = jnp.where((key >= begin_ref[seg]) & (key <= slot_ref[seg]), scores, MASKED)
            before = peak[...]
            now = jnp.maximum(before, jnp.max(scores, axis=0, keepdims=True))
            weights = jnp.exp(scores - now)
            shrink = jnp.exp(before - now)
            peak[...] = now
            total[...] = total[...] * shrink + jnp.sum(weights, axis=0, keepdims=True)
            accum[...] = accum[...] * shrink + dot(vt[:, pl.ds(at, size)], weights.astype(BF))

        sweep(seg, segments, depth, tile)
        lse_ref[seg] = peak[...] + jnp.log(total[...])
        result = accum[...] * (live_ref[seg] / total[...])
        for head in range(2):
            out_ref[here, head * SIZE : (head + 1) * SIZE] = (
                result[:, head * tokens : (head + 1) * tokens].T.astype(BF)
            )


def attend(q, kv, begin, slot, live, cosine, sine):
    segments, _, rows = slot.shape
    return pl.pallas_call(
        attend_kernel,
        name="attend",
        out_shape=(
            jax.ShapeDtypeStruct(q.shape, BF),
            jax.ShapeDtypeStruct((segments, SIZE, rows), BF),
            jax.ShapeDtypeStruct((segments, 1, rows), F32),
        ),
        in_specs=[pl.BlockSpec(memory_space=pltpu.VMEM)] * 7,
        out_specs=[pl.BlockSpec(memory_space=pltpu.VMEM)] * 3,
        scratch_shapes=[
            pltpu.VMEM((SIZE, kv.shape[0]), BF),
            pltpu.VMEM((1, rows), F32),
            pltpu.VMEM((1, rows), F32),
            pltpu.VMEM((SIZE, rows), F32),
        ],
        compiler_params=pltpu.CompilerParams(vmem_limit_bytes=48 << 20),
    )(q, kv, begin, slot, live, cosine, sine)


MESH_IDS = pl.DeviceIdType.MESH
AXES = ("x", "y", "z", "c")
ANYWHERE = pl.BlockSpec(memory_space=pl.ANY)
IN_VMEM = pl.BlockSpec(memory_space=pltpu.VMEM)


def place():
    return {a: lax.axis_index(a) for a in AXES}


def along(axis, step):
    size = lax.axis_size(axis)
    return lax.rem(lax.axis_index(axis) + (step + size), size)


def device(axis, step):
    here = place()
    here[axis] = along(axis, step)
    return tuple(here[a] for a in AXES)


class Net:
    def __init__(self, sends, arrivals, locals_):
        self.sends, self.arrivals, self.locals_ = sends, arrivals, locals_
        self.used = 0
        self.near = 0
        self.open = []

    def send(self, source, target, axis, step):
        copy = pltpu.make_async_remote_copy(
            src_ref=source, dst_ref=target, send_sem=self.sends.at[self.used],
            recv_sem=self.arrivals.at[self.used], device_id=device(axis, step),
            device_id_type=MESH_IDS,
        )
        copy.start()
        self.used += 1
        self.open.append(copy)
        return copy

    def keep(self, source, target):
        copy = pltpu.make_async_copy(source, target, self.locals_.at[self.near])
        copy.start()
        self.near += 1
        return copy

    def close(self):
        for copy in self.open:
            copy.wait_send()


def greet(partners):
    barrier = pltpu.get_barrier_semaphore()
    for axis, step in partners:
        pl.semaphore_signal(barrier, 1, device_id=device(axis, step), device_id_type=MESH_IDS)
    pl.semaphore_wait(barrier, len(partners))


def semaphores(sends, locals_):
    return [
        pltpu.SemaphoreType.DMA((sends,)),
        pltpu.SemaphoreType.DMA((sends,)),
        pltpu.SemaphoreType.DMA((max(locals_, 1),)),
    ]


def comm_call(body, name, number, outs, ins, scratch, sends, locals_, spaces, out_spaces):
    return pl.pallas_call(
        body,
        name=name,
        out_shape=outs,
        in_specs=spaces,
        out_specs=out_spaces,
        scratch_shapes=list(scratch) + semaphores(sends, locals_),
        compiler_params=pltpu.CompilerParams(
            collective_id=number, has_side_effects=True, vmem_limit_bytes=60 << 20
        ),
    )(*ins)


LINE = (1, 2, 3)


class RowGather:
    def __init__(self, net, value, out):
        self.net, self.out = net, out
        h = value.shape[0] // 2
        self.parts = (pl.ds(0, h), pl.ds(h, h))
        y, z, c = (lax.axis_index(a) for a in ROW)
        self.mine = net.keep(value, out.at[y, z, c])
        self.own = net.send(value, out.at[y, z, c], "c", 1)
        self.first = [
            [net.send(value.at[part], out.at[y, z, c, part], axis, d) for d in LINE]
            for part, axis in zip(self.parts, ("z", "y"))
        ]

    def spread(self):
        net, out = self.net, self.out
        y, z, c = (lax.axis_index(a) for a in ROW)
        self.mine.wait()
        (a, b) = self.parts
        for copy in self.first[0]:
            copy.wait_recv()
        self.second = [
            [net.send(out.at[y, :, c, a], out.at[y, :, c, a], "y", d) for d in LINE]
        ]
        for copy in self.first[1]:
            copy.wait_recv()
        self.second.append(
            [net.send(out.at[:, z, c, b], out.at[:, z, c, b], "z", d) for d in LINE]
        )
        self.shared = [self.own]
        for d in LINE:
            spot = out.at[y, along("z", -d), c, a]
            self.shared.append(net.send(spot, spot, "c", 1))
            spot = out.at[along("y", -d), z, c, b]
            self.shared.append(net.send(spot, spot, "c", 1))

    def arrive(self):
        net, out = self.net, self.out
        y, z, c = (lax.axis_index(a) for a in ROW)
        (a, b) = self.parts
        for d in LINE:
            self.second[0][d - 1].wait_recv()
            spot = out.at[along("y", -d), :, c, a]
            self.shared.append(net.send(spot, spot, "c", 1))
            self.second[1][d - 1].wait_recv()
            spot = out.at[:, along("z", -d), c, b]
            self.shared.append(net.send(spot, spot, "c", 1))

    def finish(self):
        for copy in self.shared:
            copy.wait_recv()


class RingGather:
    def __init__(self, net, value, out, axis):
        self.net, self.out, self.axis = net, out, axis
        a, c = lax.axis_index(axis), lax.axis_index("c")
        h = value.shape[0] // 2
        self.parts = one, two = pl.ds(0, h), pl.ds(h, h)
        self.mine = net.keep(value, out.at[a, c])
        self.right = [net.send(value.at[p], out.at[a, c, p], axis, 1) for p in (one, two)]
        self.left = [net.send(value.at[p], out.at[a, c, p], axis, -1) for p in (two, one)]
        self.shared = [net.send(value, out.at[a, c], "c", 1)]

    def forward(self):
        net, out, axis = self.net, self.out, self.axis
        c = lax.axis_index("c")
        one, two = self.parts
        before, after = along(axis, -1), along(axis, 1)
        self.right[0].wait_recv()
        spot = out.at[before, c, one]
        self.far = [net.send(spot, spot, axis, 1)]
        self.left[0].wait_recv()
        spot = out.at[after, c, two]
        self.far.append(net.send(spot, spot, axis, -1))

    def share(self):
        c = lax.axis_index("c")
        for copies, step in ((self.right, -1), (self.left, 1)):
            copies[1].wait_recv()
            spot = self.out.at[along(self.axis, step), c]
            self.shared.append(self.net.send(spot, spot, "c", 1))

    def finish(self):
        for copy in self.far:
            copy.wait_recv()
        spot = self.out.at[along(self.axis, 2), lax.axis_index("c")]
        self.shared.append(self.net.send(spot, spot, "c", 1))
        for copy in self.shared:
            copy.wait_recv()
        self.mine.wait()


STEP = 16
CHUNK = 32 * 1024


def rows_loop(count, width, body):
    step = STEP
    while 2 * step * width <= CHUNK and count % (2 * step) == 0:
        step *= 2
    pl.loop(0, count // step)(lambda i: body(pl.ds(pl.multiple_of(i * step, STEP), step)))


def shifted(rows, first):
    return pl.ds(pl.multiple_of(rows.start + first, STEP), rows.size)


class RingSum:
    def __init__(self, net, value, out, axis, near, relay, come, go):
        self.net, self.value, self.out, self.axis = net, value, out, axis
        self.near, self.relay, self.come, self.go = near, relay, come, go
        c = lax.axis_index("c")
        self.size = value.shape[2]
        h = self.size // 2
        self.parts = pl.ds(0, h), pl.ds(h, h)
        self.swaps = {
            s: net.send(value.at[along(axis, s), 1 - c], near.at[s], "c", 1) for s in (2, 1, 3, 0)
        }

    def pair(self, s, part=None):
        value, near, go = self.value, self.near, self.go
        where, c = along(self.axis, s), lax.axis_index("c")
        first = 0 if part is None else part.start
        count = self.size if part is None else part.size

        def add(rows):
            at = shifted(rows, first)
            go[s, at] = (
                value[where, c, at].astype(F32) + near[s, at].astype(F32)
            ).astype(BF)

        rows_loop(count, value.shape[3], add)

    def relay_far(self):
        net = self.net
        one, two = self.parts
        self.swaps[2].wait_recv()
        self.pair(2)
        self.relays = [
            net.send(self.go.at[2, one], self.relay.at[0], self.axis, 1),
            net.send(self.go.at[2, two], self.relay.at[1], self.axis, -1),
        ]

    def issue(self):
        net, go, come = self.net, self.go, self.come
        one, two = self.parts
        self.swaps[1].wait_recv()
        self.pair(1)
        self.ends = [net.send(go.at[1, two], come.at[0, two], self.axis, 1)]
        self.swaps[3].wait_recv()
        self.pair(3)
        self.ends.append(net.send(go.at[3, one], come.at[1, one], self.axis, -1))

    def pass_on(self):
        net, go, relay, come = self.net, self.go, self.relay, self.come
        one, two = self.parts
        for i, (s, part, step) in enumerate(((1, one, 1), (3, two, -1))):
            self.relays[i].wait_recv()

            def add(rows, i=i, s=s, part=part):
                at = shifted(rows, part.start)
                go[s, at] = (go[s, at].astype(F32) + relay[i, rows].astype(F32)).astype(BF)

            rows_loop(part.size, go.shape[2], add)
            self.ends.append(net.send(go.at[s, part], come.at[i, part], self.axis, step))

    def finish(self):
        value, near, come, out = self.value, self.near, self.come, self.out
        where, c = lax.axis_index(self.axis), lax.axis_index("c")
        self.swaps[0].wait_recv()
        for copy in self.ends:
            copy.wait_recv()

        def add(rows):
            out[rows] = (
                value[where, c, rows].astype(F32) + near[0, rows].astype(F32)
            ) + (come[0, rows].astype(F32) + come[1, rows].astype(F32))

        rows_loop(self.size, out.shape[1], add)


def ring_sum_scratch(size, width):
    return [
        pltpu.VMEM((4, size, width), BF),
        pltpu.VMEM((2, size // 2, width), BF),
        pltpu.VMEM((2, size, width), BF),
        pltpu.VMEM((4, size, width), BF),
    ]


class RowSum:
    def __init__(self, net, value, out, near, go, first, mid, last):
        self.net, self.value, self.out = net, value, out
        self.near, self.go, self.first, self.mid, self.last = near, go, first, mid, last
        c = lax.axis_index("c")
        self.size = value.shape[3]
        h = self.size // 2
        self.parts = pl.ds(0, h), pl.ds(h, h)
        self.swaps = [
            net.send(value.at[i, :, 1 - c], near.at[i], "c", 1) for i in range(4)
        ]

    def start(self):
        net, value, near, go = self.net, self.value, self.near, self.go
        c = lax.axis_index("c")
        for i in range(4):
            self.swaps[i].wait_recv()
            for j in range(4):

                def add(rows, i=i, j=j):
                    go[i, j, rows] = (
                        value[i, j, c, rows].astype(F32) + near[i, j, rows].astype(F32)
                    ).astype(BF)

                rows_loop(self.size, value.shape[4], add)
        a, b = self.parts
        self.ones = [
            [net.send(go.at[along("y", d), :, a], self.first.at[0, d - 1], "y", d) for d in LINE],
            [net.send(go.at[:, along("z", d), b], self.first.at[1, d - 1], "z", d) for d in LINE],
        ]

    def turn(self):
        net, go, first, mid = self.net, self.go, self.first, self.mid
        y, z = lax.axis_index("y"), lax.axis_index("z")
        self.twos = []
        for k, axis in enumerate(("z", "y")):
            for copy in self.ones[k]:
                copy.wait_recv()
            for j in range(4):

                def add(rows, k=k, j=j):
                    at = shifted(rows, self.parts[k].start)
                    own = go[y, j, at] if k == 0 else go[j, z, at]
                    mid[k, j, rows] = (
                        own.astype(F32) + first[k, 0, j, rows].astype(F32)
                        + (first[k, 1, j, rows].astype(F32) + first[k, 2, j, rows].astype(F32))
                    ).astype(BF)

                rows_loop(self.parts[k].size, mid.shape[3], add)
            self.twos.append(
                [net.send(mid.at[k, along(axis, d)], self.last.at[k, d - 1], axis, d) for d in LINE]
            )

    def finish(self):
        mid, last, out = self.mid, self.last, self.out
        for k, axis in enumerate(("z", "y")):
            for copy in self.twos[k]:
                copy.wait_recv()
            here = lax.axis_index(axis)

            def add(rows, k=k, here=here):
                at = shifted(rows, self.parts[k].start)
                out[at] = (
                    mid[k, here, rows].astype(F32) + last[k, 0, rows].astype(F32)
                    + (last[k, 1, rows].astype(F32) + last[k, 2, rows].astype(F32))
                )

            rows_loop(self.parts[k].size, out.shape[1], add)


def row_sum_scratch(size, width):
    h = size // 2
    return [
        pltpu.VMEM((4, 4, size, width), BF),
        pltpu.VMEM((4, 4, size, width), BF),
        pltpu.VMEM((2, 3, 4, h, width), BF),
        pltpu.VMEM((2, 4, h, width), BF),
        pltpu.VMEM((2, 3, h, width), BF),
    ]


Y_LINE = [("y", d) for d in LINE]
Z_LINE = [("z", d) for d in LINE]
X_LINE = [("x", d) for d in LINE]
X_RING = [("x", 1), ("x", -1)]
Y_RING = [("y", 1), ("y", -1)]
TWIN = [("c", 1)]


def shape(*dims, kind=BF):
    return jax.ShapeDtypeStruct(dims, kind)


def unit_places(shape_, axis, x, c, share, padded):
    spot = lax.broadcasted_iota(jnp.int32, shape_, axis)
    block, inside = spot // padded, spot % padded
    return jnp.where(inside < share, (2 * block + c) * (4 * share) + x * share + inside, -1)


OWN_COLUMNS = 640


def first_weights(first, gate, up, out, share, padded):
    rows_in, wide = gate.shape
    half_wide = wide // 2
    half_units = half_wide // (8 * share) * padded
    units = 2 * half_units
    rows, width = out.shape
    quarter = rows // 4
    lanes = (first.shape[1] - OWN_COLUMNS) // 4

    def body(
        first_ref, gate_ref, up_ref, out_ref, first_out, both_out, strip_out, both, sends, arrivals, locals_,
    ):
        net = Net(sends, arrivals, locals_)
        x, y, z, c = (lax.axis_index(a) for a in AXES)

        def columns(step):
            return pl.ds(pl.multiple_of(OWN_COLUMNS + along("x", step) * lanes, 128), lanes)

        def passing(step, h):
            return first_out.at[pl.ds(2 * h, 2), :, c, :, columns(step)]

        greet(X_RING + Y_LINE + Z_LINE + TWIN)
        part = RowGather(net, first_ref.at[:, columns(0)], first_out.at[:, :, :, :, columns(0)])
        every = pl.ds(0, OWN_COLUMNS)
        whole = RowGather(net, first_ref.at[:, every], first_out.at[:, :, :, :, every])
        piece = out_ref.at[pl.ds(pl.multiple_of(x * quarter, quarter), quarter)]
        piece_mine = net.keep(piece, strip_out.at[z])
        pieces = [net.send(piece, strip_out.at[z], "z", d) for d in LINE]
        stacked = jnp.concatenate(
            [ref[:, h * half_wide : (h + 1) * half_wide] for ref in (gate_ref, up_ref) for h in range(2)], axis=0
        )

        def pick(core):
            places = unit_places((1, half_units), 1, x, core, share, padded)
            picks = lax.broadcasted_iota(jnp.int32, (half_wide, half_units), 0) == places
            picked = dot(stacked, picks.astype(BF)).astype(BF)
            for i in range(4):
                both[core, :, i * half_units : (i + 1) * half_units] = (
                    picked[i * rows_in : (i + 1) * rows_in]
                )

        pick(0)
        part.spread()
        whole.spread()
        pick(1)
        both_mine = net.keep(both.at[c], both_out.at[c])
        both_come = net.send(both.at[1 - c], both_out.at[c], "c", 1)
        part.arrive()
        right = [net.send(passing(0, h), passing(0, h), "x", 1) for h in (0, 1)]
        left = [net.send(passing(0, h), passing(0, h), "x", -1) for h in (1, 0)]
        whole.arrive()
        right[0].wait_recv()
        far = [net.send(passing(-1, 0), passing(-1, 0), "x", 1)]
        left[0].wait_recv()
        far.append(net.send(passing(1, 1), passing(1, 1), "x", -1))
        shared = []
        for copies, step in ((right, -1), (left, 1)):
            copies[1].wait_recv()
            spot = first_out.at[:, :, c, :, columns(step)]
            shared.append(net.send(spot, spot, "c", 1))
        for copy in far:
            copy.wait_recv()
        spot = first_out.at[:, :, c, :, columns(2)]
        shared.append(net.send(spot, spot, "c", 1))
        part.finish()
        whole.finish()
        for copy in shared + pieces + [both_come]:
            copy.wait_recv()
        both_mine.wait()
        piece_mine.wait()
        net.close()

    outs = (shape(4, 4, 2, *first.shape), shape(2, rows_in, 2 * units), shape(4, quarter, width))
    return comm_call(
        body, "first_weights", 1, outs, (first, gate, up, out), [pltpu.VMEM((2, rows_in, 2 * units), BF)], 64, 4,
        [IN_VMEM] * 4, [ANYWHERE] * 3,
    )


def keys_and_latents(key_value, latent, up, strip):
    def body(
        kv_ref, lat_ref, up_ref, strip_ref, kv_out, lat_out, up_out, out_out, transit, sheet,
        sends, arrivals, locals_,
    ):
        net = Net(sends, arrivals, locals_)
        x, y, z, c = (lax.axis_index(a) for a in AXES)
        greet(X_LINE + Y_LINE + Z_LINE + TWIN)
        up_mine = net.keep(up_ref.at[y], transit.at[y, z])
        ups = [net.send(up_ref.at[along("y", d)], transit.at[y, z], "y", d) for d in LINE]
        row = RowGather(net, kv_ref, kv_out)
        ring = RingGather(net, lat_ref, lat_out, "y")
        strip_mine = net.keep(strip_ref, sheet.at[:, x])
        strips = [net.send(strip_ref, sheet.at[:, x], "x", d) for d in LINE]
        up_mine.wait()
        for copy in ups:
            copy.wait_recv()
        ups = [net.send(transit.at[:, z], transit.at[:, z], "z", d) for d in LINE]
        row.spread()
        ring.forward()
        ring.share()
        row.arrive()
        strip_mine.wait()
        for copy in strips:
            copy.wait_recv()
        half = sheet.shape[0] // 2
        sheet_keep = net.keep(sheet.at[pl.ds(half * c, half)], out_out.at[:, c])
        sheet_come = net.send(sheet.at[pl.ds(half * (1 - c), half)], out_out.at[:, c], "c", 1)
        for copy in ups:
            copy.wait_recv()
        up_keep = net.keep(transit.at[:, :, c], up_out.at[:, :, c])
        up_come = net.send(transit.at[:, :, 1 - c], up_out.at[:, :, c], "c", 1)
        ring.finish()
        row.finish()
        for copy in (up_keep, sheet_keep):
            copy.wait()
        for copy in (up_come, sheet_come):
            copy.wait_recv()
        net.close()

    _, _, high, thin = up.shape
    _, quarter, width = strip.shape
    outs = (
        shape(4, 4, 2, *key_value.shape), shape(4, 2, *latent.shape), shape(4, 4, 2, high, thin),
        shape(2, 2, 4, quarter, width),
    )
    scratch = [pltpu.VMEM((4, 4, 2, high, thin), BF), pltpu.VMEM((4, 4, quarter, width), BF)]
    return comm_call(
        body, "keys_and_latents", 2, outs, (key_value, latent, up, strip), scratch, 48, 6,
        [IN_VMEM] * 4, [ANYWHERE] * 4,
    )


def heads_sum_and_cotangent(partial, cotangent):
    def body(part_ref, cot_ref, out_ref, cot_out, near, relay, come, go, sends, arrivals, locals_):
        net = Net(sends, arrivals, locals_)
        greet(X_RING + Y_RING + TWIN)
        ring = RingSum(net, part_ref, out_ref, "y", near, relay, come, go)
        feed = RingGather(net, cot_ref, cot_out, "x")
        ring.relay_far()
        ring.issue()
        feed.forward()
        ring.pass_on()
        feed.share()
        ring.finish()
        feed.finish()
        net.close()

    size, width = cotangent.shape
    outs = (shape(size, width, kind=F32), shape(4, 2, size, width))
    return comm_call(
        body, "heads_sum_and_cotangent", 3, outs, (partial, cotangent), ring_sum_scratch(size, width), 20, 2,
        [IN_VMEM, IN_VMEM], [IN_VMEM, ANYWHERE],
    )


def add_up(terms, out, rows):
    total = terms[0][rows].astype(F32)
    for term in terms[1:]:
        total = total + term[rows].astype(F32)
    out[rows] = total.astype(out.dtype)


def add_all(terms, out):
    rows_loop(out.shape[0], out.shape[1], lambda rows: add_up(terms, out, rows))


def feed_forward(normed_two, normed, grad_out, both, down):
    size, width = normed_two.shape
    units = down.shape[0]
    tall = width // 4
    lanes = width // 2
    high = units // 16

    def body(
        two_ref, one_ref, cot_hbm, both_hbm, down_hbm, sum_out, one_out, branch_out, gb_out, mid_out,
        two, cot, both, down, hidden, grads, part, near, go, come, gb, gd, down_come, ahead,
        sends, arrivals, locals_,
    ):
        net = Net(sends, arrivals, locals_)
        x, y, z, c = (lax.axis_index(a) for a in AXES)
        both_load = net.keep(both_hbm, both)
        down_load = net.keep(down_hbm, down)
        cot_load = net.keep(cot_hbm, cot)
        greet(X_LINE + Y_LINE + Z_LINE + TWIN)
        feed = RingGather(net, two_ref, two, "x")
        one_mine = net.keep(one_ref.at[:, pl.ds(pl.multiple_of(y * tall, tall), tall)], one_out.at[y, c])
        ones = [
            net.send(
                one_ref.at[:, pl.ds(pl.multiple_of(along("y", d) * tall, tall), tall)],
                one_out.at[y, c], "y", d,
            )
            for d in LINE
        ]

        def back(s):
            return dot_nt(cot[along("x", s)].reshape(2 * size, width), down[...])

        def block(s):
            where = along("x", s)
            at = pl.ds(pl.multiple_of(where * 2 * size, 2 * size), 2 * size)
            value = two[where].reshape(2 * size, width)
            pre = dot(value, both[...])
            grad = ahead[s - 1] if s else back(0)
            gate, up = pre[:, :units], pre[:, units:]
            sigma = 1.0 / (1.0 + jnp.exp(-gate))
            gated = gate * sigma
            hidden[at, :] = (gated * up).astype(BF)
            grads[at, :units] = (grad * up * (sigma + gated * (1.0 - sigma))).astype(BF)
            grads[at, units:] = (grad * gated).astype(BF)
            part[where] = dot_nt(grads[at, :], both[...]).astype(BF).reshape(2, size, width)
            return net.send(part.at[where, 1 - c], near.at[s], "c", 1)

        def pair(s):
            where = along("x", s)
            swaps[s].wait_recv()
            add_all([part.at[where, c], near.at[s]], go.at[s - 1])
            return net.send(go.at[s - 1], come.at[s - 1], "x", s)

        swaps = {}
        feed.mine.wait()
        feed.shared[0].wait_recv()
        both_load.wait()
        down_load.wait()
        cot_load.wait()
        swaps[0] = block(0)
        feed.forward()
        for s in LINE:
            ahead[s - 1] = back(s)
        feed.share()
        one_mine.wait()
        spot = one_out.at[y, c]
        shared = [net.send(spot, spot, "c", 1)]
        for d in LINE:
            ones[d - 1].wait_recv()
            spot = one_out.at[along("y", -d), c]
            shared.append(net.send(spot, spot, "c", 1))
        feed.shared[1].wait_recv()
        feed.shared[2].wait_recv()
        swaps[1] = block(1)
        for copy in feed.far:
            copy.wait_recv()
        spot = two.at[along("x", 2), c]
        last = net.send(spot, spot, "c", 1)
        swaps[3] = block(3)
        ends = [pair(1)]
        last.wait_recv()
        swaps[2] = block(2)
        ends.append(pair(3))
        ends.append(pair(2))
        early, net.open = net.open, []

        first = []
        for k, axis in enumerate(("y", "z")):
            columns = slice(k * lanes, (k + 1) * lanes)
            gd[k] = (
                dot_tn(hidden[...], cot[...].reshape(8 * size, width)[:, columns])
                .astype(BF)
                .reshape(4, 4, high, lanes)
            )
            for d in LINE:
                at = along(axis, d)
                source = gd.at[k, at] if k == 0 else gd.at[k, :, at]
                first.append(net.send(source, down_come.at[k, d - 1], axis, d))

        gb_copies = []
        for i in range(8):
            at = pl.ds(i * 2 * size, 2 * size)
            gb[i] = dot_tn(two[...].reshape(8 * size, width)[:, i * 2 * size : (i + 1) * 2 * size], grads[...]).astype(BF)
            gb_copies.append(net.keep(gb.at[i], gb_out.at[at]))
        for copy in early:
            copy.wait_send()

        @pl.loop(0, 4)
        def _(i):
            at = pl.ds(pl.multiple_of(i * 2 * size, 2 * size), 2 * size)
            two[i] = dot(hidden[at, :], down[...]).astype(BF).reshape(2, size, width)

        branch_copy = net.keep(two, branch_out)
        swaps[0].wait_recv()
        for copy in ends:
            copy.wait_recv()
        add_all([part.at[x, c], near.at[0], come.at[0], come.at[1], come.at[2]], sum_out)
        for copy in shared:
            copy.wait_recv()
        for copy in first:
            copy.wait_recv()
        for k in range(2):
            for i in range(4):
                own = gd.at[k, y, i] if k == 0 else gd.at[k, i, z]
                add_all([own] + [down_come.at[k, d, i] for d in range(3)], mid_out.at[k, i])
        for copy in gb_copies + [branch_copy]:
            copy.wait()
        net.close()

    outs = (
        shape(size, width, kind=F32), shape(4, 2, size, tall), shape(4, 2, size, width), shape(width, 2 * units),
        shape(2, 4, high, lanes),
    )
    scratch = [
        pltpu.VMEM((4, 2, size, width), BF),
        pltpu.VMEM((4, 2, size, width), BF),
        pltpu.VMEM((width, 2 * units), BF),
        pltpu.VMEM((units, width), BF),
        pltpu.VMEM((8 * size, units), BF),
        pltpu.VMEM((8 * size, 2 * units), BF),
        pltpu.VMEM((4, 2, size, width), BF),
        pltpu.VMEM((4, size, width), BF),
        pltpu.VMEM((3, size, width), BF),
        pltpu.VMEM((3, size, width), BF),
        pltpu.VMEM((8, 2 * size, 2 * units), BF),
        pltpu.VMEM((2, 4, 4, high, lanes), BF),
        pltpu.VMEM((2, 3, 4, high, lanes), BF),
        pltpu.VMEM((3, 2 * size, units), F32),
    ]
    return comm_call(
        body, "feed_forward", 4, outs, (normed_two, normed, grad_out, both, down), scratch, 32, 14,
        [IN_VMEM] * 2 + [ANYWHERE] * 3, [IN_VMEM, ANYWHERE, ANYWHERE, ANYWHERE, IN_VMEM],
    )


GB_PARTS = (640, 384, 512)


class FirstStep:
    def __init__(self, net, value, columns, axis, own, come, out):
        self.own, self.come, self.out = own, come, out
        self.copies = []
        for d in (1, 2, 3, 0):
            at = along(axis, d)
            source = value.at[at, :, :, columns] if axis == "y" else value.at[:, at, :, columns]
            if d:
                self.copies.append(net.send(source, come.at[d - 1], axis, d))
            else:
                self.mine = net.keep(source, own)

    def finish(self):
        self.mine.wait()
        for copy in self.copies:
            copy.wait_recv()
        for i in range(4):
            add_all([self.own.at[i]] + [self.come.at[d, i] for d in range(3)], self.out.at[i])


class SecondStep:
    def __init__(self, net, mid, axis, come):
        self.mid, self.axis, self.come = mid, axis, come
        self.copies = [net.send(mid.at[along(axis, d)], come.at[d - 1], axis, d) for d in LINE]

    def finish(self, out):
        for copy in self.copies:
            copy.wait_recv()
        here = lax.axis_index(self.axis)
        add_all([self.mid.at[here]] + [self.come.at[d] for d in range(3)], out)


def heads_gather_and_branch(value, partial, mid, gb):
    size, width = value.shape
    _, _, high, lanes = mid.shape
    _, _, tall, wide = gb.shape
    skip, third = GB_PARTS[:2]

    def body(ref, part_ref, mid_ref, gb_ref, out, part_out, mid_out, gb_out, *rest):
        net = Net(*rest[8:])
        greet(X_RING + Y_LINE + Z_LINE + TWIN)
        gathering = RingGather(net, ref, out, "y")
        ring = RingSum(net, part_ref, part_out, "x", *rest[:4])
        halves = [SecondStep(net, mid_ref.at[k], axis, rest[4 + k]) for k, axis in enumerate(("z", "y"))]
        step = FirstStep(net, gb_ref, pl.ds(skip, third), "z", rest[6], rest[7], gb_out)
        ring.relay_far()
        ring.issue()
        gathering.forward()
        ring.pass_on()
        gathering.share()
        for k in range(2):
            halves[k].finish(mid_out.at[:, pl.ds(k * lanes, lanes)])
        gathering.finish()
        ring.finish()
        step.finish()
        net.close()

    outs = (
        shape(4, 2, size, width), shape(size, width, kind=F32), shape(high, 2 * lanes), shape(4, tall, third),
    )
    scratch = [
        pltpu.VMEM((3, high, lanes), BF),
        pltpu.VMEM((3, high, lanes), BF),
        pltpu.VMEM((4, tall, third), BF),
        pltpu.VMEM((3, 4, tall, third), BF),
    ]
    return comm_call(
        body, "heads_gather_and_branch", 6, outs, (value, partial, mid, gb),
        ring_sum_scratch(size, width) + scratch, 30, 3,
        [IN_VMEM] * 3 + [ANYWHERE], [ANYWHERE] + [IN_VMEM] * 3,
    )


def keys_and_latents_sum(grad_kv, partial, grad_up, grad_out, mids, grad_down):
    _, _, _, size, thin = grad_kv.shape
    width = partial.shape[3]
    high, lanes = grad_up.shape[3], grad_up.shape[4] // 4
    _, quarter, wide = grad_out.shape
    tall, ahead = mids[0].shape[1:]
    after = mids[1].shape[2]

    def body(
        kv_ref, part_ref, up_ref, out_ref, one_ref, two_ref, down_ref, kv_out, part_out, up_out, out_out, one_out,
        two_out, down_out, *rest,
    ):
        net = Net(*rest[13:])
        up_come, out_come = rest[9:11]
        x, z = lax.axis_index("x"), lax.axis_index("z")

        def lane(at):
            return pl.ds(pl.multiple_of(at * lanes, lanes), lanes)

        greet(X_LINE + Y_LINE + Z_LINE + TWIN)
        row = RowSum(net, kv_ref, kv_out, *rest[:5])
        ring = RingSum(net, part_ref, part_out, "y", *rest[5:9])
        ups = [
            net.send(up_ref.at[:, :, :, :, lane(along("x", d))], up_come.at[d - 1], "x", d) for d in LINE
        ]
        outs = [net.send(out_ref.at[along("z", d)], out_come.at[d - 1], "z", d) for d in LINE]
        halves = [
            SecondStep(net, mid, axis, come)
            for mid, axis, come in ((one_ref, "z", rest[11]), (two_ref, "y", rest[12]))
        ]
        down_mine = net.keep(down_ref, down_out.at[x])
        downs = [net.send(down_ref, down_out.at[x], "x", d) for d in LINE]
        row.start()
        ring.relay_far()
        ring.issue()
        row.turn()
        ring.pass_on()
        for copy in outs:
            copy.wait_recv()
        add_all([out_ref.at[z]] + [out_come.at[d] for d in range(3)], out_out)
        for copy in ups:
            copy.wait_recv()

        @pl.loop(0, 4)
        def _(i):
            up_out[i] = (
                (up_ref[i, :, :, :, lane(x)].astype(F32) + up_come[0, i].astype(F32))
                + (up_come[1, i].astype(F32) + up_come[2, i].astype(F32))
            ).astype(BF)

        halves[0].finish(one_out)
        halves[1].finish(two_out)
        ring.finish()
        row.finish()
        down_mine.wait()
        for copy in downs:
            copy.wait_recv()
        net.close()

    outs = (
        shape(size, thin, kind=F32), shape(size, width, kind=F32), shape(4, 4, 2, high, lanes),
        shape(quarter, wide), shape(tall, ahead), shape(tall, after), shape(4, *grad_down.shape),
    )
    scratch = [
        pltpu.VMEM((3, 4, 4, 2, high, lanes), BF),
        pltpu.VMEM((3, quarter, wide), BF),
        pltpu.VMEM((3, tall, ahead), BF),
        pltpu.VMEM((3, tall, after), BF),
    ]
    return comm_call(
        body, "keys_and_latents_sum", 7, outs, (grad_kv, partial, grad_up, grad_out, *mids, grad_down),
        row_sum_scratch(size, thin) + ring_sum_scratch(size, width) + scratch, 46, 2,
        [IN_VMEM] * 7, [IN_VMEM] * 6 + [ANYWHERE],
    )


def firsts_gather(value, both, grad_out, grad_up, weights):
    _, size, part = value.shape
    tiles = weights.shape[0] // BLOCK
    tall, wide = grad_out.shape
    _, _, _, high, lanes = grad_up.shape

    def body(
        ref, both_ref, out_ref, up_ref, weights_hbm, gathered, both_out, out_out, up_out, back_out,
        up_come, up_sum, up_y, weights_ref, sends, arrivals, locals_,
    ):
        net = Net(sends, arrivals, locals_)
        x, y, z, c = (lax.axis_index(a) for a in AXES)
        load = net.keep(weights_hbm, weights_ref)
        greet(X_LINE + Y_LINE + Z_LINE + TWIN)
        mine = net.keep(ref.at[c], gathered.at[y, c])
        come = net.send(ref.at[1 - c], gathered.at[y, c], "c", 1)
        both_mine = net.keep(both_ref.at[c], both_out.at[x, c])
        both_come = net.send(both_ref.at[1 - c], both_out.at[x, c], "c", 1)
        ups = [net.send(up_ref.at[:, along("z", d)], up_come.at[d - 1], "z", d) for d in LINE]
        outs = [net.send(out_ref, out_out.at[x], "x", d) for d in LINE]
        out_mine = net.keep(out_ref, out_out.at[x])

        mine.wait()
        spot = gathered.at[y, c]
        ahead = [net.send(spot, spot, "y", 1), net.send(spot, spot, "y", -1)]
        come.wait_recv()
        spot = gathered.at[y, 1 - c]
        ahead += [net.send(spot, spot, "y", 1), net.send(spot, spot, "y", -1)]
        both_mine.wait()
        both_come.wait_recv()
        zero, one = both_out.at[x, 0], both_out.at[x, 1]
        right = [net.send(spot, spot, "x", 1) for spot in (zero, one)]
        left = [net.send(spot, spot, "x", -1) for spot in (one, zero)]

        def back(i):
            at = pl.ds(pl.multiple_of(i * BLOCK, BLOCK), BLOCK)
            total = 0.0
            for core in range(2):
                columns = slice(core * part, (core + 1) * part)
                total = total + dot_nt(ref[core], weights_ref[at, columns])
            back_out[:, at] = total

        load.wait()
        pl.loop(0, tiles // 2)(back)
        for copy in ups:
            copy.wait_recv()
        for i in range(4):
            for core in range(2):
                add_all(
                    [up_ref.at[i, z, core]] + [up_come.at[d, i, core] for d in range(3)], up_sum.at[i, core]
                )
        ups = [net.send(up_sum.at[along("y", d)], up_y.at[y], "y", d) for d in LINE]
        up_mine = net.keep(up_sum.at[y], up_y.at[y])

        ahead[0].wait_recv()
        spot = gathered.at[along("y", -1), c]
        ahead.append(net.send(spot, spot, "y", 1))
        ahead[3].wait_recv()
        spot = gathered.at[along("y", 1), 1 - c]
        ahead.append(net.send(spot, spot, "y", -1))

        up_mine.wait()
        for copy in ups:
            copy.wait_recv()
        up_near = net.send(up_y.at[:, 1 - c], up_out.at[x, :, c], "c", 1)
        up_mine = net.keep(up_y.at[:, c], up_out.at[x, :, c])

        right[0].wait_recv()
        spot = both_out.at[along("x", -1), 0]
        far = [net.send(spot, spot, "x", 1)]
        left[0].wait_recv()
        spot = both_out.at[along("x", 1), 1]
        far.append(net.send(spot, spot, "x", -1))
        pl.loop(tiles // 2, tiles)(back)

        up_near.wait_recv()
        up_mine.wait()
        spot = up_out.at[x]
        ups = [net.send(spot, spot, "x", d) for d in LINE]
        for copy in [ahead[i] for i in (1, 2, 4, 5)] + [right[1], left[1]] + far + outs + ups:
            copy.wait_recv()
        out_mine.wait()
        net.close()

    outs = (
        shape(4, *value.shape), shape(4, *both.shape), shape(4, tall, wide), shape(4, 4, 2, high, lanes),
        shape(size, weights.shape[0], kind=F32),
    )
    scratch = [
        pltpu.VMEM((3, 4, 2, high, lanes), BF),
        pltpu.VMEM((4, 2, high, lanes), BF),
        pltpu.VMEM((4, 2, high, lanes), BF),
        pltpu.VMEM(weights.shape, BF),
    ]
    return comm_call(
        body, "firsts_gather", 8, outs, (value, both, grad_out, grad_up, weights), scratch, 40, 6,
        [IN_VMEM] * 4 + [ANYWHERE], [ANYWHERE, ANYWHERE, IN_VMEM, IN_VMEM, IN_VMEM],
    )


def last_sums(grad_first, gains, grad_both, grad_down, grad_up, share):
    rows = grad_both.shape[2]
    half_units = grad_both.shape[3] // 4
    padded, width = grad_down.shape[1:]
    half_wide = 2 * half_units // padded * 4 * share
    up_rows, up_lanes = grad_up.shape[3:]

    def body(
        first_ref, gain_ref, both_ref, down_ref, up_ref, first_out, gain_out, gate_out, up_out, down_out, q_up_out,
        accum, down_rows, wide, first_come, first_x,
        gain_near, gain_one, gain_come, gain_two, gain_y, gain_three, gain_x, sends, arrivals, locals_,
    ):
        net = Net(sends, arrivals, locals_)
        x, y, z, c = (lax.axis_index(a) for a in AXES)
        greet(X_LINE + Y_LINE + Z_LINE + TWIN)
        first_near = net.send(first_ref.at[:, 1 - c], wide.at[c], "c", 1)
        first_mine = net.keep(first_ref.at[:, c], wide.at[c])
        near = net.send(gain_ref.at[:, :, 1 - c], gain_near, "c", 1)
        first_mine.wait()
        first_near.wait_recv()
        firsts = [
            [net.send(wide.at[core, along("z", d)], first_come.at[d - 1, core], "z", d) for d in LINE]
            for core in range(2)
        ]
        accum[...] = jnp.zeros_like(accum)

        def put(i):
            px, pc = i // 2, i % 2
            places = unit_places((half_units, 1), 0, px, pc, share, padded)
            picks = lax.broadcasted_iota(jnp.int32, (half_units, half_wide), 1) == places
            stacked = jnp.concatenate(
                [both_ref[px, pc, :, k * half_units : (k + 1) * half_units] for k in range(4)], axis=0
            )
            accum[...] += dot(stacked, picks.astype(BF))

        near.wait_recv()
        gain_one[...] = gain_ref[:, :, c] + gain_near[...]
        comes = [net.send(gain_one.at[:, along("z", d)], gain_come.at[d - 1], "z", d) for d in LINE]
        def onward(core):
            for copy in firsts[core]:
                copy.wait_recv()
            add_all([wide.at[core, z]] + [first_come.at[d, core] for d in range(3)], first_x.at[x, core])
            spot = first_x.at[x, core]
            return [net.send(spot, spot, "x", d) for d in LINE]

        pl.loop(0, 3)(put)
        finals = [onward(0)]
        for copy in comes:
            copy.wait_recv()
        gain_two[...] = (gain_one[:, z] + gain_come[0]) + (gain_come[1] + gain_come[2])
        comes = [net.send(gain_two.at[along("y", d)], gain_y.at[d - 1], "y", d) for d in LINE]
        finals.append(onward(1))
        pl.loop(3, 8)(put)
        for copy in comes:
            copy.wait_recv()
        gain_three[...] = (gain_two[y] + gain_y[0]) + (gain_y[1] + gain_y[2])
        gain_mine = net.keep(gain_three, gain_x.at[x])
        comes = [net.send(gain_three, gain_x.at[x], "x", d) for d in LINE]
        for k, target in enumerate((gate_out, gate_out, up_out, up_out)):
            target[:, (k % 2) * half_wide : (k % 2 + 1) * half_wide] = accum[k * rows : (k + 1) * rows].astype(BF)
        for px in range(4):
            down_rows[px * share : (px + 1) * share, :] = down_ref[px].astype(F32)[:share]
            for py in range(4):
                for pc in range(2):
                    at = ((2 * py + pc) * 4 + px) * up_lanes
                    q_up_out[:, at : at + up_lanes] = up_ref[px, py, pc]
        down_out[...] = down_rows[...].astype(BF)
        for core in range(2):
            for copy in finals[core]:
                copy.wait_recv()
            add_all([first_x.at[i, core] for i in range(4)], first_out.at[core])
        gain_mine.wait()
        for copy in comes:
            copy.wait_recv()
        gain_out[...] = (gain_x[0] + gain_x[1]) + (gain_x[2] + gain_x[3])
        net.close()

    _, _, high, lanes = grad_first.shape
    outs = (
        shape(2, high, lanes, kind=F32), shape(8, 128, kind=F32), shape(rows, 2 * half_wide),
        shape(rows, 2 * half_wide), shape(4 * share, width), shape(up_rows, 32 * up_lanes),
    )
    scratch = [
        pltpu.VMEM((4 * rows, half_wide), F32),
        pltpu.VMEM((4 * share, width), F32),
        pltpu.VMEM((2, 4, high, lanes), BF),
        pltpu.VMEM((3, 2, high, lanes), BF),
        pltpu.VMEM((4, 2, high, lanes), BF),
        pltpu.VMEM((4, 4, 8, 128), F32),
        pltpu.VMEM((4, 4, 8, 128), F32),
        pltpu.VMEM((3, 4, 8, 128), F32),
        pltpu.VMEM((4, 8, 128), F32),
        pltpu.VMEM((3, 8, 128), F32),
        pltpu.VMEM((8, 128), F32),
        pltpu.VMEM((4, 8, 128), F32),
    ]
    return comm_call(
        body, "last_sums", 9, outs, (grad_first, gains, grad_both, grad_down, grad_up), scratch, 24, 2,
        [IN_VMEM] * 5, [IN_VMEM] * 6,
    )


def attend_back_kernel(
    qt_ref, do_ref, o_ref, kv_ref, begin_ref, slot_ref, lse_ref, cos_ref, sin_ref, go_ref, mid_ref, gb_ref,
    dq_ref, dkv_ref, go_out, one_out, two_out, mid_out,
    kt, sums, accum, query, grad_rows, grad_turned, delta, own_one, come_one, own_two, come_two, mid_come, stack, go_come, sends, arrivals, locals_,
):
    net = Net(sends, arrivals, locals_)
    x, c = lax.axis_index("x"), lax.axis_index("c")
    greet(X_LINE + Y_LINE + Z_LINE + TWIN)
    half = go_ref.shape[0]
    wide = gb_ref.shape[-1]
    ahead, _, after = GB_PARTS
    quarter = go_out.shape[1]

    def strip(at):
        return pl.ds(pl.multiple_of(at * quarter, quarter), quarter)

    go_mine = net.keep(go_ref.at[:, c], stack.at[pl.ds(half * c, half)])
    go_near = net.send(go_ref.at[:, 1 - c], stack.at[pl.ds(half * c, half)], "c", 1)
    steps = [
        FirstStep(net, gb_ref, pl.ds(0, ahead), "y", own_one, come_one, one_out),
        FirstStep(net, gb_ref, pl.ds(wide - after, after), "z", own_two, come_two, two_out),
    ]
    second = SecondStep(net, mid_ref, "y", mid_come)
    go_mine.wait()
    go_near.wait_recv()
    go_sends = [net.send(stack.at[:, strip(along("x", d))], go_come.at[d - 1], "x", d) for d in LINE]
    depth = lax.axis_index("z")
    segments = slot_ref.shape[0]
    rows = slot_ref.shape[2]
    tokens = rows // 2
    sums[...] = jnp.zeros_like(sums)
    turned(kv_ref, kt, segments * (segments - 1) + depth + 1, KEYS)

    @pl.loop(0, segments)
    def _(seg):
        here = pl.ds(pl.multiple_of(seg * tokens, tokens), tokens)

        def stacked(ref):
            value = ref[here, :]
            return jnp.concatenate([value[:, :SIZE], value[:, SIZE:]], axis=0)

        grad = stacked(do_ref)
        query[...] = qt_ref[seg].T
        grad_rows[...] = grad
        grad_turned[...] = grad.T
        delta[...] = jnp.sum(
            grad_turned[...].astype(F32) * stacked(o_ref).T.astype(F32), axis=0, keepdims=True
        )
        accum[...] = jnp.zeros_like(accum)

        def tile(at, size, masked):
            keys = pl.ds(at, size)
            scores = dot(kv_ref[keys, KEYS], qt_ref[seg])
            probs = jnp.exp(scores - lse_ref[seg])
            if masked:
                key = lax.broadcasted_iota(jnp.int32, scores.shape, 0) + at
                probs = jnp.where((key >= begin_ref[seg]) & (key <= slot_ref[seg]), probs, 0.0)
            grad_probs = dot(kv_ref[keys, VALUES], grad_turned[...])
            grad_scores = (probs * (grad_probs - delta[...])).astype(BF)
            sums[keys, VALUES] += dot(probs.astype(BF), grad_rows[...])
            sums[keys, KEYS] += dot(grad_scores, query[...])
            accum[...] += dot(kt[:, keys], grad_scores)

        sweep(seg, segments, depth, tile)
        cosine, sine = cos_ref[seg], sin_ref[seg]
        for head in range(2):
            part = accum[:, head * tokens : (head + 1) * tokens] * (SIZE ** -0.5)
            lower, upper = part[:HALF], part[HALF:]
            turn = jnp.concatenate(
                [lower * cosine + upper * sine, upper * cosine - lower * sine], axis=0
            )
            dq_ref[here, head * SIZE : (head + 1) * SIZE] = turn.T.astype(BF)

    dkv_ref[...] = sums[...].astype(BF)
    second.finish(mid_out)
    for copy in go_sends:
        copy.wait_recv()
    for i in range(2 * half):
        add_all([stack.at[i, strip(x)]] + [go_come.at[d, i] for d in range(3)], go_out.at[i])
    for step in steps:
        step.finish()
    net.close()


def attend_back(qt, do, o, kv, begin, slot, lse, cosine, sine, grad_out, mid, gb):
    segments, _, rows = slot.shape
    half, _, tall, wide = grad_out.shape
    _, high, third = mid.shape
    ahead, _, after = GB_PARTS
    return pl.pallas_call(
        attend_back_kernel,
        name="attend_back",
        out_shape=(
            jax.ShapeDtypeStruct(do.shape, BF),
            jax.ShapeDtypeStruct(kv.shape, BF),
            jax.ShapeDtypeStruct((2 * half, tall // 4, wide), BF),
            jax.ShapeDtypeStruct((4, high, ahead), BF),
            jax.ShapeDtypeStruct((4, high, after), BF),
            jax.ShapeDtypeStruct((high, third), BF),
        ),
        in_specs=[IN_VMEM] * 11 + [ANYWHERE],
        out_specs=[IN_VMEM] * 6,
        scratch_shapes=[
            pltpu.VMEM((SIZE, kv.shape[0]), BF),
            pltpu.VMEM(kv.shape, F32),
            pltpu.VMEM((SIZE, rows), F32),
            pltpu.VMEM((rows, SIZE), BF),
            pltpu.VMEM((rows, SIZE), BF),
            pltpu.VMEM((SIZE, rows), BF),
            pltpu.VMEM((1, rows), F32),
            pltpu.VMEM((4, high, ahead), BF),
            pltpu.VMEM((3, 4, high, ahead), BF),
            pltpu.VMEM((4, high, after), BF),
            pltpu.VMEM((3, 4, high, after), BF),
            pltpu.VMEM((3, high, third), BF),
            pltpu.VMEM((2 * half, tall, wide), BF),
            pltpu.VMEM((3, 2 * half, tall // 4, wide), BF),
        ] + semaphores(14, 3),
        compiler_params=pltpu.CompilerParams(
            collective_id=10, has_side_effects=True, vmem_limit_bytes=60 << 20
        ),
    )(qt, do, o, kv, begin, slot, lse, cosine, sine, grad_out, mid, gb)


def gather(value, axes):
    return lax.all_gather(value, axes, axis=0, tiled=True)


def on_device(
    block_input, cotangent, lengths, norm_gain, q_down, q_gain, q_up, key_weight, value_weight,
    out_weight, ffn_gain, gate_weight, up_weight, down_weight,
):
    rows, width = block_input.shape
    latent_width = q_down.shape[1]
    n_x, n_y, n_z, n_c = (lax.axis_size(a) for a in ("x", "y", "z", "c"))
    x, y, z, c = (lax.axis_index(a) for a in ("x", "y", "z", "c"))
    span = n_y * n_z * n_c
    members = n_y * n_c
    lengths_row = lengths[0]

    mine = (y * n_z + z) * n_c + c
    slots_mine = mine * rows + jnp.arange(rows, dtype=jnp.int32)
    begin_mine, _ = places_of(lengths_row, slots_mine)
    cosine, sine = tables(slots_mine - begin_mine)
    strip = n_c * rows
    slots_group = (
        (jnp.arange(n_y, dtype=jnp.int32)[:, None] * n_z + z) * strip
        + jnp.arange(strip, dtype=jnp.int32)[None, :]
    ).reshape(-1)
    begin_group, live_group = places_of(lengths_row, slots_group)
    cosine_group, sine_group = tables_across((slots_group - begin_group).reshape(n_y, strip))
    begin_lanes = jnp.tile(begin_group.reshape(n_y, 1, strip), (1, 1, 2))
    slot_lanes = jnp.tile(slots_group.reshape(n_y, 1, strip), (1, 1, 2))
    live_lanes = jnp.tile(live_group.reshape(n_y, 1, strip), (1, 1, 2))

    shard = norm_gain.shape[0]
    extra = jnp.stack(
        [norm_gain, ffn_gain, jnp.pad(q_gain, (0, shard - q_gain.shape[0]))], axis=1
    ).astype(BF)
    first_width = latent_width + 2 * SIZE
    first = jnp.concatenate(
        [q_down, key_weight, value_weight, jnp.pad(extra, ((0, 0), (0, 125)))], axis=1
    )
    per_heads = q_up.shape[1] // members
    q_rows = q_up.shape[0]

    down_rows = down_weight.shape[0]
    share = down_rows // n_x
    padded = -(-share // 16) * 16
    down_part = lax.dynamic_slice_in_dim(down_weight, x * share, share)
    down_part = jnp.pad(down_part, ((0, padded - share), (0, 0)))
    first_full, both, out_strip = first_weights(first, gate_weight, up_weight, out_weight, share, padded)
    units = both.shape[2] // 2
    first_full = first_full.reshape(span * shard, -1)
    both = both.reshape(n_c * shard, 2 * units)
    extra_full = first_full[:, first_width : first_width + 3].astype(F32)
    gain_one = extra_full[:, 0]
    gain_two = extra_full[:, 1]
    gain_latent = extra_full[:, 2].reshape(span, shard)[:, : q_gain.shape[0]].reshape(-1)

    both_full = gather(both, ("y", "z"))
    down_use = gather(down_part, ("y", "z"))

    inputs = block_input.astype(F32)
    inverse_one = lax.rsqrt(jnp.mean(inputs * inputs, axis=-1, keepdims=True) + EPSILON)
    normed = (inputs * inverse_one * gain_one).astype(BF)
    firsts = dot(normed, first_full[:, :first_width])
    latent = firsts[:, :latent_width]
    inverse_latent = lax.rsqrt(jnp.mean(latent * latent, axis=-1, keepdims=True) + EPSILON)
    latent_normed = (latent * inverse_latent * gain_latent).astype(BF)
    key_mine = rotate(firsts[:, latent_width : latent_width + SIZE], cosine, sine).astype(BF)
    value_mine = firsts[:, latent_width + SIZE :].astype(BF)
    key_value, latent_group, up_heads, out_heads = keys_and_latents(
        jnp.concatenate([key_mine, value_mine], axis=1), latent_normed,
        q_up.reshape(q_rows, n_y, n_c, per_heads).transpose(1, 2, 0, 3), out_strip,
    )
    up_heads = up_heads.reshape(span * q_rows, per_heads)
    out_heads = out_heads.reshape(per_heads, width)
    key_value = key_value.reshape(span * rows, 2 * SIZE)
    group = members * rows
    latent_group = latent_group.reshape(group, latent_width)
    mixed, queries_t, lse = attend(
        dot(latent_group, up_heads), key_value, begin_lanes, slot_lanes, live_lanes,
        cosine_group, sine_group,
    )
    branch, grad_feed = heads_sum_and_cotangent(
        dot(mixed, out_heads).astype(BF).reshape(n_y, n_c, rows, width), cotangent
    )
    middle = inputs + branch

    inverse_two = lax.rsqrt(jnp.mean(middle * middle, axis=-1, keepdims=True) + EPSILON)
    grad_normed_two, normed_part, branch_part, grad_both, grad_down = feed_forward(
        (middle * inverse_two * gain_two).astype(BF), normed, grad_feed, both_full, down_use
    )
    normed_part = normed_part.reshape(group, -1)
    grad_result = cotangent.astype(F32)
    grad_mid_norm, grad_gain_two = norm_back(middle, inverse_two, gain_two, grad_normed_two)
    grad_middle = grad_result + grad_mid_norm

    grad_both = grad_both.reshape(n_y, n_z, n_c * shard, 2 * units)
    grad_branch, branch_two, grad_down, grad_mid = heads_gather_and_branch(
        grad_middle.astype(BF), branch_part, grad_down, grad_both
    )
    grad_branch = grad_branch.reshape(group, width)
    output = (middle + branch_two).astype(BF)
    grad_mixed = dot_nt(grad_branch, out_heads).astype(BF)
    grad_attended = grad_mixed * live_group[:, None].astype(BF)
    grad_out = dot_tn(mixed, grad_branch).astype(BF)
    out_rows = out_weight.shape[0]
    grad_query_raw, grad_kv, grad_out, grad_one, grad_two, grad_mid = attend_back(
        queries_t, grad_attended, mixed, key_value, begin_lanes, slot_lanes, lse,
        cosine_group, sine_group, grad_out.reshape(n_z // n_c, n_c, out_rows, width), grad_mid, grad_both,
    )
    grad_up_heads = dot_tn(latent_group, grad_query_raw).astype(BF)
    grad_kv, grad_latent_normed, grad_up_heads, grad_out, grad_one, grad_two, grad_down = keys_and_latents_sum(
        grad_kv.reshape(n_y, n_z, n_c, rows, 2 * SIZE),
        dot_nt(grad_query_raw, up_heads).astype(BF).reshape(n_y, n_c, rows, latent_width),
        grad_up_heads.reshape(n_y, n_z, n_c, q_rows, per_heads),
        grad_out, (grad_one, grad_two), grad_down,
    )
    grad_both = jnp.concatenate([grad_one, grad_mid, grad_two], axis=1)
    grad_key_raw = unrotate(grad_kv[:, :SIZE], cosine, sine).astype(BF)
    grad_value_raw = grad_kv[:, SIZE:].astype(BF)
    grad_latent_f, grad_gain_latent = norm_back(
        latent, inverse_latent, gain_latent, grad_latent_normed
    )
    grad_firsts = jnp.concatenate(
        [grad_latent_f.astype(BF), grad_key_raw, grad_value_raw], axis=1
    )
    half_first = first_width // n_c
    first_part, grad_both, grad_out, grad_up_heads, grad_normed = firsts_gather(
        grad_firsts.reshape(rows, n_c, half_first).transpose(1, 0, 2),
        grad_both.reshape(n_c, shard, 2 * units), grad_out, grad_up_heads, first_full,
    )
    first_part = first_part.reshape(group, half_first)
    grad_first = dot_tn(normed_part, first_part).astype(BF)
    grad_input_norm, grad_gain_one = norm_back(inputs, inverse_one, gain_one, grad_normed)
    input_grad = grad_middle + grad_input_norm
    gains = jnp.concatenate(
        [
            grad_gain_one.reshape(span, shard),
            grad_gain_two.reshape(span, shard),
            grad_gain_latent.reshape(span, -1),
        ],
        axis=1,
    )
    shares = gains.shape[1]
    gains = jnp.pad(gains, ((0, 0), (0, 8 * 128 - shares))).reshape(n_y, n_z, n_c, 8, 128)
    grad_first, gains, grad_gate, grad_up, grad_down, grad_q_up = last_sums(
        grad_first.reshape(n_z, n_c, shard, half_first), gains, grad_both, grad_down, grad_up_heads, share
    )
    gains = gains.reshape(-1)
    grad_first = jnp.concatenate([grad_first[0], grad_first[1]], axis=1)
    return (
        output,
        input_grad,
        gains[:shard],
        grad_first[:, :latent_width],
        gains[2 * shard : shares],
        grad_q_up.astype(F32),
        grad_first[:, latent_width : latent_width + SIZE],
        grad_first[:, latent_width + SIZE :],
        grad_out.reshape(out_rows, width).astype(F32),
        gains[shard : 2 * shard],
        grad_gate.astype(F32),
        grad_up.astype(F32),
        grad_down.astype(F32),
    )


def solution(mesh):
    sizes = (4, 4, 4, 2)
    grid = Mesh(mesh.devices.reshape(sizes), ("x", "y", "z", "c"))
    tokens = P(("x", "y", "z", "c"), None)
    wide, thin = P(ROW, None), P(ROW)
    in_specs = (
        tokens, tokens, P("x", None), thin, wide, thin, wide, wide, wide, wide, thin, wide, wide,
        wide,
    )
    out_specs = (
        tokens, tokens, thin, wide, thin, wide, wide, wide, wide, thin, wide, wide, wide,
    )
    return jax.shard_map(
        on_device, mesh=grid, in_specs=in_specs, out_specs=out_specs, check_vma=False
    )
```

```python
import functools
import math

import jax
import jax.numpy as jnp
from jax import lax
from jax.experimental import pallas as pl
from jax.experimental.pallas import tpu as pltpu
from jax.sharding import Mesh
from jax.sharding import PartitionSpec as P

EPSILON = 1e-06
MASKED = -1e30
BF = jnp.bfloat16
F32 = jnp.float32
SIZE = 256
HALF = 128
BLOCK = 256
ROW = ("y", "z", "c")
HEADS = ("y", "c")
FEED = ("x", "c")


def dot(left, right):
    return jnp.dot(left, right, preferred_element_type=F32)


def dot_tn(left, right):
    return lax.dot_general(left, right, (((0,), (0,)), ((), ())), preferred_element_type=F32)


def dot_nt(left, right):
    return lax.dot_general(left, right, (((1,), (1,)), ((), ())), preferred_element_type=F32)


def norm_back(values, inverse, gain, grad):
    scaled = grad * gain
    grad_values = inverse * scaled - values * inverse * inverse * inverse * jnp.mean(
        scaled * values, axis=-1, keepdims=True
    )
    return grad_values, jnp.sum(grad * values * inverse, axis=0)


def places_of(lengths_row, slots):
    ends = jnp.cumsum(lengths_row)
    begins = jnp.concatenate([ends - lengths_row, ends[-1:]])
    begin = jnp.max(jnp.where(slots[:, None] >= begins[None, :], begins[None, :], 0), axis=1)
    live = (slots < ends[-1]).astype(F32)
    return begin, live


def tables(position):
    freq = jnp.exp(jnp.arange(HALF, dtype=F32) * (-math.log(10000.0) / HALF))
    angle = position.astype(F32)[:, None] * freq[None, :]
    return jnp.cos(angle), jnp.sin(angle)


def tables_across(position):
    freq = jnp.exp(jnp.arange(HALF, dtype=F32) * (-math.log(10000.0) / HALF))
    angle = position.astype(F32)[..., None, :] * freq[:, None]
    return jnp.cos(angle), jnp.sin(angle)


def rotate(values, cosine, sine):
    lower, upper = values[..., :HALF], values[..., HALF:]
    return jnp.concatenate([lower * cosine - upper * sine, upper * cosine + lower * sine], axis=-1)


def unrotate(grad, cosine, sine):
    lower, upper = grad[..., :HALF], grad[..., HALF:]
    return jnp.concatenate([lower * cosine + upper * sine, upper * cosine - lower * sine], axis=-1)


def turned(source, target, count, columns):
    @pl.loop(0, count)
    def _(block):
        at = pl.ds(pl.multiple_of(block * BLOCK, BLOCK), BLOCK)
        target[:, at] = source[at, columns].T


KEYS, VALUES = slice(0, SIZE), slice(SIZE, 2 * SIZE)


def sweep(segment, segments, depth, tile):
    count = segments * segment + depth
    last = (segment // (segments - 1)) * (depth // (lax.axis_size("z") - 1))
    guarded = jnp.minimum(count, 1) * (1 - last) + count * last
    free = count - guarded

    @pl.loop(0, guarded)
    def _(i):
        tile(pl.multiple_of(i * BLOCK, BLOCK), BLOCK, True)

    @pl.loop(0, free // 2)
    def _(i):
        tile(pl.multiple_of((guarded + 2 * i) * BLOCK, BLOCK), 2 * BLOCK, False)

    @pl.loop(0, free % 2)
    def _(i):
        tile(pl.multiple_of((count - 1) * BLOCK, BLOCK), BLOCK, False)

    tile(pl.multiple_of(count * BLOCK, BLOCK), BLOCK, True)


def attend_kernel(
    q_ref, kv_ref, begin_ref, slot_ref, live_ref, cos_ref, sin_ref,
    out_ref, qt_ref, lse_ref, vt, peak, total, accum,
):
    depth = lax.axis_index("z")
    segments = slot_ref.shape[0]
    rows = slot_ref.shape[2]
    tokens = rows // 2
    turned(kv_ref, vt, segments * (segments - 1) + depth + 1, VALUES)

    @pl.loop(0, segments)
    def _(seg):
        here = pl.ds(pl.multiple_of(seg * tokens, tokens), tokens)
        cosine, sine = cos_ref[seg], sin_ref[seg]
        for head in range(2):
            raw = q_ref[here, head * SIZE : (head + 1) * SIZE].T
            lower, upper = raw[:HALF], raw[HALF:]
            turn = jnp.concatenate(
                [lower * cosine - upper * sine, upper * cosine + lower * sine], axis=0
            )
            qt_ref[seg, :, head * tokens : (head + 1) * tokens] = (
                turn.astype(BF) * (SIZE ** -0.5)
            ).astype(BF)
        peak[...] = jnp.full_like(peak, MASKED)
        total[...] = jnp.zeros_like(total)
        accum[...] = jnp.zeros_like(accum)

        def tile(at, size, masked):
            scores = dot(kv_ref[pl.ds(at, size), KEYS], qt_ref[seg])
            if masked:
                key = lax.broadcasted_iota(jnp.int32, scores.shape, 0) + at
                scores = jnp.where((key >= begin_ref[seg]) & (key <= slot_ref[seg]), scores, MASKED)
            before = peak[...]
            now = jnp.maximum(before, jnp.max(scores, axis=0, keepdims=True))
            weights = jnp.exp(scores - now)
            shrink = jnp.exp(before - now)
            peak[...] = now
            total[...] = total[...] * shrink + jnp.sum(weights, axis=0, keepdims=True)
            accum[...] = accum[...] * shrink + dot(vt[:, pl.ds(at, size)], weights.astype(BF))

        sweep(seg, segments, depth, tile)
        lse_ref[seg] = peak[...] + jnp.log(total[...])
        result = accum[...] * (live_ref[seg] / total[...])
        for head in range(2):
            out_ref[here, head * SIZE : (head + 1) * SIZE] = (
                result[:, head * tokens : (head + 1) * tokens].T.astype(BF)
            )


def attend(q, kv, begin, slot, live, cosine, sine):
    segments, _, rows = slot.shape
    return pl.pallas_call(
        attend_kernel,
        name="attend",
        out_shape=(
            jax.ShapeDtypeStruct(q.shape, BF),
            jax.ShapeDtypeStruct((segments, SIZE, rows), BF),
            jax.ShapeDtypeStruct((segments, 1, rows), F32),
        ),
        in_specs=[pl.BlockSpec(memory_space=pltpu.VMEM)] * 7,
        out_specs=[pl.BlockSpec(memory_space=pltpu.VMEM)] * 3,
        scratch_shapes=[
            pltpu.VMEM((SIZE, kv.shape[0]), BF),
            pltpu.VMEM((1, rows), F32),
            pltpu.VMEM((1, rows), F32),
            pltpu.VMEM((SIZE, rows), F32),
        ],
        compiler_params=pltpu.CompilerParams(vmem_limit_bytes=48 << 20),
    )(q, kv, begin, slot, live, cosine, sine)


MESH_IDS = pl.DeviceIdType.MESH
AXES = ("x", "y", "z", "c")
ANYWHERE = pl.BlockSpec(memory_space=pl.ANY)
IN_VMEM = pl.BlockSpec(memory_space=pltpu.VMEM)


def place():
    return {a: lax.axis_index(a) for a in AXES}


def along(axis, step):
    size = lax.axis_size(axis)
    return lax.rem(lax.axis_index(axis) + (step + size), size)


def device(axis, step):
    here = place()
    here[axis] = along(axis, step)
    return tuple(here[a] for a in AXES)


class Net:
    def __init__(self, sends, arrivals, locals_):
        self.sends, self.arrivals, self.locals_ = sends, arrivals, locals_
        self.used = 0
        self.near = 0
        self.open = []

    def send(self, source, target, axis, step):
        copy = pltpu.make_async_remote_copy(
            src_ref=source, dst_ref=target, send_sem=self.sends.at[self.used],
            recv_sem=self.arrivals.at[self.used], device_id=device(axis, step),
            device_id_type=MESH_IDS,
        )
        copy.start()
        self.used += 1
        self.open.append(copy)
        return copy

    def keep(self, source, target):
        copy = pltpu.make_async_copy(source, target, self.locals_.at[self.near])
        copy.start()
        self.near += 1
        return copy

    def close(self):
        for copy in self.open:
            copy.wait_send()


def greet(partners):
    barrier = pltpu.get_barrier_semaphore()
    for axis, step in partners:
        pl.semaphore_signal(barrier, 1, device_id=device(axis, step), device_id_type=MESH_IDS)
    pl.semaphore_wait(barrier, len(partners))


def semaphores(sends, locals_):
    return [
        pltpu.SemaphoreType.DMA((sends,)),
        pltpu.SemaphoreType.DMA((sends,)),
        pltpu.SemaphoreType.DMA((max(locals_, 1),)),
    ]


def comm_call(body, name, number, outs, ins, scratch, sends, locals_, spaces, out_spaces):
    return pl.pallas_call(
        body,
        name=name,
        out_shape=outs,
        in_specs=spaces,
        out_specs=out_spaces,
        scratch_shapes=list(scratch) + semaphores(sends, locals_),
        compiler_params=pltpu.CompilerParams(
            collective_id=number, has_side_effects=True, vmem_limit_bytes=60 << 20
        ),
    )(*ins)


LINE = (1, 2, 3)


class RowGather:
    def __init__(self, net, value, out):
        self.net, self.out = net, out
        h = value.shape[0] // 2
        self.parts = (pl.ds(0, h), pl.ds(h, h))
        y, z, c = (lax.axis_index(a) for a in ROW)
        self.mine = net.keep(value, out.at[y, z, c])
        self.own = net.send(value, out.at[y, z, c], "c", 1)
        self.first = [
            [net.send(value.at[part], out.at[y, z, c, part], axis, d) for d in LINE]
            for part, axis in zip(self.parts, ("z", "y"))
        ]

    def spread(self):
        net, out = self.net, self.out
        y, z, c = (lax.axis_index(a) for a in ROW)
        self.mine.wait()
        (a, b) = self.parts
        for copy in self.first[0]:
            copy.wait_recv()
        self.second = [
            [net.send(out.at[y, :, c, a], out.at[y, :, c, a], "y", d) for d in LINE]
        ]
        for copy in self.first[1]:
            copy.wait_recv()
        self.second.append(
            [net.send(out.at[:, z, c, b], out.at[:, z, c, b], "z", d) for d in LINE]
        )
        self.shared = [self.own]
        for d in LINE:
            spot = out.at[y, along("z", -d), c, a]
            self.shared.append(net.send(spot, spot, "c", 1))
            spot = out.at[along("y", -d), z, c, b]
            self.shared.append(net.send(spot, spot, "c", 1))

    def arrive(self):
        net, out = self.net, self.out
        y, z, c = (lax.axis_index(a) for a in ROW)
        (a, b) = self.parts
        for d in LINE:
            self.second[0][d - 1].wait_recv()
            spot = out.at[along("y", -d), :, c, a]
            self.shared.append(net.send(spot, spot, "c", 1))
            self.second[1][d - 1].wait_recv()
            spot = out.at[:, along("z", -d), c, b]
            self.shared.append(net.send(spot, spot, "c", 1))

    def finish(self):
        for copy in self.shared:
            copy.wait_recv()


class RingGather:
    def __init__(self, net, value, out, axis):
        self.net, self.out, self.axis = net, out, axis
        a, c = lax.axis_index(axis), lax.axis_index("c")
        h = value.shape[0] // 2
        self.parts = one, two = pl.ds(0, h), pl.ds(h, h)
        self.mine = net.keep(value, out.at[a, c])
        self.right = [net.send(value.at[p], out.at[a, c, p], axis, 1) for p in (one, two)]
        self.left = [net.send(value.at[p], out.at[a, c, p], axis, -1) for p in (two, one)]
        self.shared = [net.send(value, out.at[a, c], "c", 1)]

    def forward(self):
        net, out, axis = self.net, self.out, self.axis
        c = lax.axis_index("c")
        one, two = self.parts
        before, after = along(axis, -1), along(axis, 1)
        self.right[0].wait_recv()
        spot = out.at[before, c, one]
        self.far = [net.send(spot, spot, axis, 1)]
        self.left[0].wait_recv()
        spot = out.at[after, c, two]
        self.far.append(net.send(spot, spot, axis, -1))

    def share(self):
        c = lax.axis_index("c")
        for copies, step in ((self.right, -1), (self.left, 1)):
            copies[1].wait_recv()
            spot = self.out.at[along(self.axis, step), c]
            self.shared.append(self.net.send(spot, spot, "c", 1))

    def finish(self):
        for copy in self.far:
            copy.wait_recv()
        spot = self.out.at[along(self.axis, 2), lax.axis_index("c")]
        self.shared.append(self.net.send(spot, spot, "c", 1))
        self.arrived()

    def arrived(self):
        if self.mine is not None:
            self.mine.wait()
            self.mine = None
        for copy in self.shared:
            copy.wait_recv()
        self.shared = []


STEP = 16
CHUNK = 32 * 1024


def rows_loop(count, width, body):
    step = STEP
    while 2 * step * width <= CHUNK and count % (2 * step) == 0:
        step *= 2
    pl.loop(0, count // step)(lambda i: body(pl.ds(pl.multiple_of(i * step, STEP), step)))


def shifted(rows, first):
    return pl.ds(pl.multiple_of(rows.start + first, STEP), rows.size)


class RingSum:
    def __init__(self, net, value, out, axis, near, relay, come, go):
        self.net, self.value, self.out, self.axis = net, value, out, axis
        self.near, self.relay, self.come, self.go = near, relay, come, go
        c = lax.axis_index("c")
        self.size = value.shape[2]
        h = self.size // 2
        self.parts = pl.ds(0, h), pl.ds(h, h)
        self.swaps = {
            s: net.send(value.at[along(axis, s), 1 - c], near.at[s], "c", 1) for s in (2, 1, 3, 0)
        }

    def pair(self, s, part=None):
        value, near, go = self.value, self.near, self.go
        where, c = along(self.axis, s), lax.axis_index("c")
        first = 0 if part is None else part.start
        count = self.size if part is None else part.size

        def add(rows):
            at = shifted(rows, first)
            go[s, at] = (
                value[where, c, at].astype(F32) + near[s, at].astype(F32)
            ).astype(BF)

        rows_loop(count, value.shape[3], add)

    def relay_far(self):
        net = self.net
        one, two = self.parts
        self.swaps[2].wait_recv()
        self.pair(2)
        self.relays = [
            net.send(self.go.at[2, one], self.relay.at[0], self.axis, 1),
            net.send(self.go.at[2, two], self.relay.at[1], self.axis, -1),
        ]

    def issue(self):
        net, go, come = self.net, self.go, self.come
        one, two = self.parts
        self.swaps[1].wait_recv()
        self.pair(1)
        self.ends = [net.send(go.at[1, two], come.at[0, two], self.axis, 1)]
        self.swaps[3].wait_recv()
        self.pair(3)
        self.ends.append(net.send(go.at[3, one], come.at[1, one], self.axis, -1))

    def pass_on(self):
        net, go, relay, come = self.net, self.go, self.relay, self.come
        one, two = self.parts
        for i, (s, part, step) in enumerate(((1, one, 1), (3, two, -1))):
            self.relays[i].wait_recv()

            def add(rows, i=i, s=s, part=part):
                at = shifted(rows, part.start)
                go[s, at] = (go[s, at].astype(F32) + relay[i, rows].astype(F32)).astype(BF)

            rows_loop(part.size, go.shape[2], add)
            self.ends.append(net.send(go.at[s, part], come.at[i, part], self.axis, step))

    def finish(self):
        value, near, come, out = self.value, self.near, self.come, self.out
        where, c = lax.axis_index(self.axis), lax.axis_index("c")
        self.swaps[0].wait_recv()
        for copy in self.ends:
            copy.wait_recv()

        def add(rows):
            out[rows] = (
                value[where, c, rows].astype(F32) + near[0, rows].astype(F32)
            ) + (come[0, rows].astype(F32) + come[1, rows].astype(F32))

        rows_loop(self.size, out.shape[1], add)


def ring_sum_scratch(size, width):
    return [
        pltpu.VMEM((4, size, width), BF),
        pltpu.VMEM((2, size // 2, width), BF),
        pltpu.VMEM((2, size, width), BF),
        pltpu.VMEM((4, size, width), BF),
    ]


class RowSum:
    def __init__(self, net, value, out, near, go, first, mid, last):
        self.net, self.value, self.out = net, value, out
        self.near, self.go, self.first, self.mid, self.last = near, go, first, mid, last
        c = lax.axis_index("c")
        self.size = value.shape[3]
        h = self.size // 2
        self.parts = pl.ds(0, h), pl.ds(h, h)
        self.swaps = [
            net.send(value.at[i, :, 1 - c], near.at[i], "c", 1) for i in range(4)
        ]

    def start(self):
        net, value, near, go = self.net, self.value, self.near, self.go
        c = lax.axis_index("c")
        for i in range(4):
            self.swaps[i].wait_recv()
            for j in range(4):

                def add(rows, i=i, j=j):
                    go[i, j, rows] = (
                        value[i, j, c, rows].astype(F32) + near[i, j, rows].astype(F32)
                    ).astype(BF)

                rows_loop(self.size, value.shape[4], add)
        a, b = self.parts
        self.ones = [
            [net.send(go.at[along("y", d), :, a], self.first.at[0, d - 1], "y", d) for d in LINE],
            [net.send(go.at[:, along("z", d), b], self.first.at[1, d - 1], "z", d) for d in LINE],
        ]

    def turn(self):
        net, go, first, mid = self.net, self.go, self.first, self.mid
        y, z = lax.axis_index("y"), lax.axis_index("z")
        self.twos = []
        for k, axis in enumerate(("z", "y")):
            for copy in self.ones[k]:
                copy.wait_recv()
            for j in range(4):

                def add(rows, k=k, j=j):
                    at = shifted(rows, self.parts[k].start)
                    own = go[y, j, at] if k == 0 else go[j, z, at]
                    mid[k, j, rows] = (
                        own.astype(F32) + first[k, 0, j, rows].astype(F32)
                        + (first[k, 1, j, rows].astype(F32) + first[k, 2, j, rows].astype(F32))
                    ).astype(BF)

                rows_loop(self.parts[k].size, mid.shape[3], add)
            self.twos.append(
                [net.send(mid.at[k, along(axis, d)], self.last.at[k, d - 1], axis, d) for d in LINE]
            )

    def finish(self):
        mid, last, out = self.mid, self.last, self.out
        for k, axis in enumerate(("z", "y")):
            for copy in self.twos[k]:
                copy.wait_recv()
            here = lax.axis_index(axis)

            def add(rows, k=k, here=here):
                at = shifted(rows, self.parts[k].start)
                out[at] = (
                    mid[k, here, rows].astype(F32) + last[k, 0, rows].astype(F32)
                    + (last[k, 1, rows].astype(F32) + last[k, 2, rows].astype(F32))
                )

            rows_loop(self.parts[k].size, out.shape[1], add)


def row_sum_scratch(size, width):
    h = size // 2
    return [
        pltpu.VMEM((4, 4, size, width), BF),
        pltpu.VMEM((4, 4, size, width), BF),
        pltpu.VMEM((2, 3, 4, h, width), BF),
        pltpu.VMEM((2, 4, h, width), BF),
        pltpu.VMEM((2, 3, h, width), BF),
    ]


Y_LINE = [("y", d) for d in LINE]
Z_LINE = [("z", d) for d in LINE]
X_LINE = [("x", d) for d in LINE]
X_RING = [("x", 1), ("x", -1)]
Y_RING = [("y", 1), ("y", -1)]
TWIN = [("c", 1)]


def shape(*dims, kind=BF):
    return jax.ShapeDtypeStruct(dims, kind)


def unit_places(shape_, axis, x, c, share, padded):
    spot = lax.broadcasted_iota(jnp.int32, shape_, axis)
    block, inside = spot // padded, spot % padded
    return jnp.where(inside < share, (2 * block + c) * (4 * share) + x * share + inside, -1)


OWN_COLUMNS = 640


def first_weights(first, gate, up, out, share, padded):
    rows_in, wide = gate.shape
    half_wide = wide // 2
    half_units = half_wide // (8 * share) * padded
    units = 2 * half_units
    rows, width = out.shape
    quarter = rows // 4
    lanes = (first.shape[1] - OWN_COLUMNS) // 4

    def body(
        first_ref, gate_ref, up_ref, out_ref, first_out, both_out, strip_out, both, sends, arrivals, locals_,
    ):
        net = Net(sends, arrivals, locals_)
        x, y, z, c = (lax.axis_index(a) for a in AXES)

        def columns(step):
            return pl.ds(pl.multiple_of(OWN_COLUMNS + along("x", step) * lanes, 128), lanes)

        def passing(step, h):
            return first_out.at[pl.ds(2 * h, 2), :, c, :, columns(step)]

        greet(X_RING + Y_LINE + Z_LINE + TWIN)
        part = RowGather(net, first_ref.at[:, columns(0)], first_out.at[:, :, :, :, columns(0)])
        every = pl.ds(0, OWN_COLUMNS)
        whole = RowGather(net, first_ref.at[:, every], first_out.at[:, :, :, :, every])
        piece = out_ref.at[pl.ds(pl.multiple_of(x * quarter, quarter), quarter)]
        piece_mine = net.keep(piece, strip_out.at[z])
        pieces = [net.send(piece, strip_out.at[z], "z", d) for d in LINE]
        stacked = jnp.concatenate(
            [ref[:, h * half_wide : (h + 1) * half_wide] for ref in (gate_ref, up_ref) for h in range(2)], axis=0
        )

        def pick(core):
            places = unit_places((1, half_units), 1, x, core, share, padded)
            picks = lax.broadcasted_iota(jnp.int32, (half_wide, half_units), 0) == places
            picked = dot(stacked, picks.astype(BF)).astype(BF)
            for i in range(4):
                both[core, :, i * half_units : (i + 1) * half_units] = (
                    picked[i * rows_in : (i + 1) * rows_in]
                )

        pick(0)
        part.spread()
        whole.spread()
        pick(1)
        both_mine = net.keep(both.at[c], both_out.at[c])
        both_come = net.send(both.at[1 - c], both_out.at[c], "c", 1)
        part.arrive()
        right = [net.send(passing(0, h), passing(0, h), "x", 1) for h in (0, 1)]
        left = [net.send(passing(0, h), passing(0, h), "x", -1) for h in (1, 0)]
        whole.arrive()
        right[0].wait_recv()
        far = [net.send(passing(-1, 0), passing(-1, 0), "x", 1)]
        left[0].wait_recv()
        far.append(net.send(passing(1, 1), passing(1, 1), "x", -1))
        shared = []
        for copies, step in ((right, -1), (left, 1)):
            copies[1].wait_recv()
            spot = first_out.at[:, :, c, :, columns(step)]
            shared.append(net.send(spot, spot, "c", 1))
        for copy in far:
            copy.wait_recv()
        spot = first_out.at[:, :, c, :, columns(2)]
        shared.append(net.send(spot, spot, "c", 1))
        part.finish()
        whole.finish()
        for copy in shared + pieces + [both_come]:
            copy.wait_recv()
        both_mine.wait()
        piece_mine.wait()
        net.close()

    outs = (shape(4, 4, 2, *first.shape), shape(2, rows_in, 2 * units), shape(4, quarter, width))
    return comm_call(
        body, "first_weights", 1, outs, (first, gate, up, out), [pltpu.VMEM((2, rows_in, 2 * units), BF)], 64, 4,
        [IN_VMEM] * 4, [ANYWHERE] * 3,
    )


def keys_and_latents(key_value, latent, up, strip):
    def body(
        kv_ref, lat_ref, up_ref, strip_ref, kv_out, lat_out, up_out, out_out, transit, sheet,
        sends, arrivals, locals_,
    ):
        net = Net(sends, arrivals, locals_)
        x, y, z, c = (lax.axis_index(a) for a in AXES)
        greet(X_LINE + Y_LINE + Z_LINE + TWIN)
        up_mine = net.keep(up_ref.at[y], transit.at[y, z])
        ups = [net.send(up_ref.at[along("y", d)], transit.at[y, z], "y", d) for d in LINE]
        row = RowGather(net, kv_ref, kv_out)
        ring = RingGather(net, lat_ref, lat_out, "y")
        strip_mine = net.keep(strip_ref, sheet.at[:, x])
        strips = [net.send(strip_ref, sheet.at[:, x], "x", d) for d in LINE]
        up_mine.wait()
        for copy in ups:
            copy.wait_recv()
        ups = [net.send(transit.at[:, z], transit.at[:, z], "z", d) for d in LINE]
        row.spread()
        ring.forward()
        ring.share()
        row.arrive()
        strip_mine.wait()
        for copy in strips:
            copy.wait_recv()
        half = sheet.shape[0] // 2
        sheet_keep = net.keep(sheet.at[pl.ds(half * c, half)], out_out.at[:, c])
        sheet_come = net.send(sheet.at[pl.ds(half * (1 - c), half)], out_out.at[:, c], "c", 1)
        for copy in ups:
            copy.wait_recv()
        up_keep = net.keep(transit.at[:, :, c], up_out.at[:, :, c])
        up_come = net.send(transit.at[:, :, 1 - c], up_out.at[:, :, c], "c", 1)
        ring.finish()
        row.finish()
        for copy in (up_keep, sheet_keep):
            copy.wait()
        for copy in (up_come, sheet_come):
            copy.wait_recv()
        net.close()

    _, _, high, thin = up.shape
    _, quarter, width = strip.shape
    outs = (
        shape(4, 4, 2, *key_value.shape), shape(4, 2, *latent.shape), shape(4, 4, 2, high, thin),
        shape(2, 2, 4, quarter, width),
    )
    scratch = [pltpu.VMEM((4, 4, 2, high, thin), BF), pltpu.VMEM((4, 4, quarter, width), BF)]
    return comm_call(
        body, "keys_and_latents", 2, outs, (key_value, latent, up, strip), scratch, 48, 6,
        [IN_VMEM] * 4, [ANYWHERE] * 4,
    )


def heads_sum_and_cotangent(partial, cotangent):
    def body(part_ref, cot_ref, out_ref, cot_out, near, relay, come, go, sends, arrivals, locals_):
        net = Net(sends, arrivals, locals_)
        greet(X_RING + Y_RING + TWIN)
        ring = RingSum(net, part_ref, out_ref, "y", near, relay, come, go)
        feed = RingGather(net, cot_ref, cot_out, "x")
        ring.relay_far()
        ring.issue()
        feed.forward()
        ring.pass_on()
        feed.share()
        ring.finish()
        feed.finish()
        net.close()

    size, width = cotangent.shape
    outs = (shape(size, width, kind=F32), shape(4, 2, size, width))
    return comm_call(
        body, "heads_sum_and_cotangent", 3, outs, (partial, cotangent), ring_sum_scratch(size, width), 20, 2,
        [IN_VMEM, IN_VMEM], [IN_VMEM, ANYWHERE],
    )


def add_up(terms, out, rows):
    total = terms[0][rows].astype(F32)
    for term in terms[1:]:
        total = total + term[rows].astype(F32)
    out[rows] = total.astype(out.dtype)


def add_all(terms, out):
    rows_loop(out.shape[0], out.shape[1], lambda rows: add_up(terms, out, rows))


def feed_forward(normed_two, normed, grad_out, both, down):
    size, width = normed_two.shape
    units = down.shape[0]
    tall = width // 4
    lanes = width // 2
    high = units // 16

    def body(
        two_ref, one_ref, cot_hbm, both_hbm, down_hbm, sum_out, one_out, branch_out, gb_out, mid_out,
        two, cot, both, down, hidden, grads, part, near, go, come, gb, gd, down_come, ahead,
        sends, arrivals, locals_,
    ):
        net = Net(sends, arrivals, locals_)
        x, y, z, c = (lax.axis_index(a) for a in AXES)
        both_load = net.keep(both_hbm, both)
        down_load = net.keep(down_hbm, down)
        cot_load = net.keep(cot_hbm, cot)
        greet(X_LINE + Y_LINE + Z_LINE + TWIN)
        feed = RingGather(net, two_ref, two, "x")
        one_mine = net.keep(one_ref.at[:, pl.ds(pl.multiple_of(y * tall, tall), tall)], one_out.at[y, c])
        ones = [
            net.send(
                one_ref.at[:, pl.ds(pl.multiple_of(along("y", d) * tall, tall), tall)],
                one_out.at[y, c], "y", d,
            )
            for d in LINE
        ]

        def back(s):
            return dot_nt(cot[along("x", s)].reshape(2 * size, width), down[...])

        def block(s):
            where = along("x", s)
            at = pl.ds(pl.multiple_of(where * 2 * size, 2 * size), 2 * size)
            value = two[where].reshape(2 * size, width)
            pre = dot(value, both[...])
            grad = ahead[s - 1] if s else back(0)
            gate, up = pre[:, :units], pre[:, units:]
            sigma = 1.0 / (1.0 + jnp.exp(-gate))
            gated = gate * sigma
            hidden[at, :] = (gated * up).astype(BF)
            grads[at, :units] = (grad * up * (sigma + gated * (1.0 - sigma))).astype(BF)
            grads[at, units:] = (grad * gated).astype(BF)
            part[where] = dot_nt(grads[at, :], both[...]).astype(BF).reshape(2, size, width)
            return net.send(part.at[where, 1 - c], near.at[s], "c", 1)

        def pair(s):
            where = along("x", s)
            swaps[s].wait_recv()
            add_all([part.at[where, c], near.at[s]], go.at[s - 1])
            return net.send(go.at[s - 1], come.at[s - 1], "x", s)

        swaps = {}
        feed.arrived()
        both_load.wait()
        down_load.wait()
        cot_load.wait()
        swaps[0] = block(0)
        feed.forward()
        for s in LINE:
            ahead[s - 1] = back(s)
        feed.share()
        one_mine.wait()
        spot = one_out.at[y, c]
        shared = [net.send(spot, spot, "c", 1)]
        for d in LINE:
            ones[d - 1].wait_recv()
            spot = one_out.at[along("y", -d), c]
            shared.append(net.send(spot, spot, "c", 1))
        feed.arrived()
        swaps[1] = block(1)
        for copy in feed.far:
            copy.wait_recv()
        spot = two.at[along("x", 2), c]
        last = net.send(spot, spot, "c", 1)
        swaps[3] = block(3)
        ends = [pair(1)]
        last.wait_recv()
        swaps[2] = block(2)
        ends.append(pair(3))
        ends.append(pair(2))
        early, net.open = net.open, []

        first = []
        for k, axis in enumerate(("y", "z")):
            columns = slice(k * lanes, (k + 1) * lanes)
            gd[k] = (
                dot_tn(hidden[...], cot[...].reshape(8 * size, width)[:, columns])
                .astype(BF)
                .reshape(4, 4, high, lanes)
            )
            for d in LINE:
                at = along(axis, d)
                source = gd.at[k, at] if k == 0 else gd.at[k, :, at]
                first.append(net.send(source, down_come.at[k, d - 1], axis, d))

        gb_copies = []
        for i in range(8):
            at = pl.ds(i * 2 * size, 2 * size)
            gb[i] = dot_tn(two[...].reshape(8 * size, width)[:, i * 2 * size : (i + 1) * 2 * size], grads[...]).astype(BF)
            gb_copies.append(net.keep(gb.at[i], gb_out.at[at]))
        for copy in early:
            copy.wait_send()

        @pl.loop(0, 4)
        def _(i):
            at = pl.ds(pl.multiple_of(i * 2 * size, 2 * size), 2 * size)
            two[i] = dot(hidden[at, :], down[...]).astype(BF).reshape(2, size, width)

        branch_copy = net.keep(two, branch_out)
        swaps[0].wait_recv()
        for copy in ends:
            copy.wait_recv()
        add_all([part.at[x, c], near.at[0], come.at[0], come.at[1], come.at[2]], sum_out)
        for copy in shared:
            copy.wait_recv()
        for copy in first:
            copy.wait_recv()
        for k in range(2):
            for i in range(4):
                own = gd.at[k, y, i] if k == 0 else gd.at[k, i, z]
                add_all([own] + [down_come.at[k, d, i] for d in range(3)], mid_out.at[k, i])
        for copy in gb_copies + [branch_copy]:
            copy.wait()
        net.close()

    outs = (
        shape(size, width, kind=F32), shape(4, 2, size, tall), shape(4, 2, size, width), shape(width, 2 * units),
        shape(2, 4, high, lanes),
    )
    scratch = [
        pltpu.VMEM((4, 2, size, width), BF),
        pltpu.VMEM((4, 2, size, width), BF),
        pltpu.VMEM((width, 2 * units), BF),
        pltpu.VMEM((units, width), BF),
        pltpu.VMEM((8 * size, units), BF),
        pltpu.VMEM((8 * size, 2 * units), BF),
        pltpu.VMEM((4, 2, size, width), BF),
        pltpu.VMEM((4, size, width), BF),
        pltpu.VMEM((3, size, width), BF),
        pltpu.VMEM((3, size, width), BF),
        pltpu.VMEM((8, 2 * size, 2 * units), BF),
        pltpu.VMEM((2, 4, 4, high, lanes), BF),
        pltpu.VMEM((2, 3, 4, high, lanes), BF),
        pltpu.VMEM((3, 2 * size, units), F32),
    ]
    return comm_call(
        body, "feed_forward", 4, outs, (normed_two, normed, grad_out, both, down), scratch, 32, 14,
        [IN_VMEM] * 2 + [ANYWHERE] * 3, [IN_VMEM, ANYWHERE, ANYWHERE, ANYWHERE, IN_VMEM],
    )


Y_COLUMNS = 640


class FirstStep:
    def __init__(self, net, value, columns, axis, own, come, out):
        self.own, self.come, self.out = own, come, out
        self.copies = []
        for d in (1, 2, 3, 0):
            at = along(axis, d)
            source = value.at[at, :, :, columns] if axis == "y" else value.at[:, at, :, columns]
            if d:
                self.copies.append(net.send(source, come.at[d - 1], axis, d))
            else:
                self.mine = net.keep(source, own)

    def finish(self):
        self.mine.wait()
        for copy in self.copies:
            copy.wait_recv()
        for i in range(4):
            add_all([self.own.at[i]] + [self.come.at[d, i] for d in range(3)], self.out.at[i])


class SecondStep:
    def __init__(self, net, mid, axis, come):
        self.mid, self.axis, self.come = mid, axis, come
        self.copies = [net.send(mid.at[along(axis, d)], come.at[d - 1], axis, d) for d in LINE]

    def finish(self, out):
        for copy in self.copies:
            copy.wait_recv()
        here = lax.axis_index(self.axis)
        add_all([self.mid.at[here]] + [self.come.at[d] for d in range(3)], out)


def keys_and_latents_sum(
    grad_kv, grad_query, latent_group, up_heads, grad_out, mids, cosine, sine, latent, inverse, gain,
):
    _, _, _, size, thin = grad_kv.shape
    group, width = latent_group.shape
    per = up_heads.shape[1]
    high, lanes = up_heads.shape[0] // 32, per // 4
    _, out_rows, wide = grad_out.shape
    quarter = out_rows // 4
    tall, ahead = mids[0].shape[1:]
    after = mids[1].shape[2]
    part = (width + thin) // 2

    def body(
        kv_ref, query_ref, group_ref, heads_ref, out_ref, one_ref, two_ref, cos_ref, sin_ref, latent_ref, inverse_ref,
        gain_ref, firsts_out, gain_out, up_out, out_out, one_out, two_out, *rest,
    ):
        net = Net(*rest[17:])
        up_come, out_come = rest[9:11]
        partial, ups_here, kv_sum, part_sum = rest[13:17]
        x = lax.axis_index("x")

        def lane(at):
            return pl.ds(pl.multiple_of(at * lanes, lanes), lanes)

        def strip(at):
            return pl.ds(pl.multiple_of(at * quarter, quarter), quarter)

        greet(X_LINE + Y_LINE + Z_LINE + TWIN)
        row = RowSum(net, kv_ref, kv_sum, *rest[:5])
        outs = [net.send(out_ref.at[:, strip(along("x", d))], out_come.at[d - 1], "x", d) for d in LINE]
        for i in range(4):
            at = pl.ds(i * 2 * size, 2 * size)
            partial[i] = dot_nt(query_ref[at, :], heads_ref[...]).astype(BF).reshape(2, size, width)
        ring = RingSum(net, partial, part_sum, "y", *rest[5:9])
        ups_here[...] = dot_tn(group_ref[...], query_ref[...]).astype(BF).reshape(4, 4, 2, high, per)
        ups = [
            net.send(ups_here.at[:, :, :, :, lane(along("x", d))], up_come.at[d - 1], "x", d) for d in LINE
        ]
        row.start()
        halves = [
            SecondStep(net, mid, axis, come)
            for mid, axis, come in ((one_ref, "z", rest[11]), (two_ref, "y", rest[12]))
        ]
        ring.relay_far()
        ring.issue()
        row.turn()
        ring.pass_on()
        for copy in ups:
            copy.wait_recv()

        @pl.loop(0, 4)
        def _(i):
            up_out[i] = (
                (ups_here[i, :, :, :, lane(x)].astype(F32) + up_come[0, i].astype(F32))
                + (up_come[1, i].astype(F32) + up_come[2, i].astype(F32))
            ).astype(BF)

        ring.finish()
        values = latent_ref[...]
        scale = inverse_ref[...]
        scaled = part_sum[...] * gain_ref[...]
        gain_out[...] = jnp.sum(part_sum[...] * values * scale, axis=0, keepdims=True)
        back = scale * scaled - values * (scale * scale * scale) * jnp.mean(scaled * values, axis=-1, keepdims=True)
        firsts_out[0] = back[:, :part].astype(BF)
        firsts_out[1, :, : width - part] = back[:, part:].astype(BF)
        row.finish()
        lower, upper = kv_sum[:, :HALF], kv_sum[:, HALF:SIZE]
        at = width - part
        firsts_out[1, :, at : at + HALF] = (lower * cos_ref[...] + upper * sin_ref[...]).astype(BF)
        firsts_out[1, :, at + HALF : at + SIZE] = (upper * cos_ref[...] - lower * sin_ref[...]).astype(BF)
        firsts_out[1, :, at + SIZE :] = kv_sum[:, SIZE:].astype(BF)
        halves[0].finish(one_out)
        halves[1].finish(two_out)
        for copy in outs:
            copy.wait_recv()
        for i in range(4):
            add_all([out_ref.at[i, strip(x)]] + [out_come.at[d, i] for d in range(3)], out_out.at[i])
        net.close()

    outs = (
        shape(2, size, part), shape(1, width, kind=F32), shape(4, 4, 2, high, lanes), shape(4, quarter, wide),
        shape(tall, ahead), shape(tall, after),
    )
    scratch = [
        pltpu.VMEM((3, 4, 4, 2, high, lanes), BF),
        pltpu.VMEM((3, 4, quarter, wide), BF),
        pltpu.VMEM((3, tall, ahead), BF),
        pltpu.VMEM((3, tall, after), BF),
        pltpu.VMEM((4, 2, size, width), BF),
        pltpu.VMEM((4, 4, 2, high, per), BF),
        pltpu.VMEM((size, thin), F32),
        pltpu.VMEM((size, width), F32),
    ]
    return comm_call(
        body, "keys_and_latents_sum", 7, outs,
        (
            grad_kv, grad_query, latent_group, up_heads, grad_out, *mids, cosine, sine, latent, inverse, gain,
        ),
        row_sum_scratch(size, thin) + ring_sum_scratch(size, width) + scratch, 46, 2,
        [IN_VMEM] * 12, [IN_VMEM] * 6,
    )


def last_sums(
    value, both, grad_out, grad_up, grad_down, normed_part, inputs, inverse, gain_one, gain_two, gain_latent, weights,
    share,
):
    _, size, part = value.shape
    deep = weights.shape[0]
    tiles = deep // BLOCK
    _, tall, wide = grad_out.shape
    _, _, _, high, lanes = grad_up.shape
    rows = both.shape[1]
    half_units = both.shape[2] // 4
    padded, width = grad_down.shape
    half_wide = 2 * half_units // padded * 4 * share

    def body(
        ref, both_ref, out_ref, up_ref, down_ref, normed_ref, input_ref, inverse_ref, gain_ref, two_ref, latent_ref,
        weights_hbm,
        first_out, gain_out, back_out, out_out, gate_out, up_weight_out, down_out, q_up_out,
        gathered, both_all, up_all, down_all, out_come, up_come, up_sum, up_y, weights_ref, accum, down_rows,
        first_here, pair, first_come, first_x, gain_here, gain_near, gain_come, gain_two, gain_y, gain_x,
        sends, arrivals, locals_,
    ):
        net = Net(sends, arrivals, locals_)
        x, y, z, c = (lax.axis_index(a) for a in AXES)
        load = net.keep(weights_hbm, weights_ref)
        greet(X_LINE + Y_LINE + Z_LINE + TWIN)
        mine = net.keep(ref.at[c], gathered.at[y, c])
        come = net.send(ref.at[1 - c], gathered.at[y, c], "c", 1)
        both_mine = net.keep(both_ref.at[c], both_all.at[x, c])
        both_come = net.send(both_ref.at[1 - c], both_all.at[x, c], "c", 1)
        ups = [net.send(up_ref.at[:, along("z", d)], up_come.at[d - 1], "z", d) for d in LINE]
        outs = [net.send(out_ref.at[along("z", d)], out_come.at[d - 1], "z", d) for d in LINE]
        down_mine = net.keep(down_ref, down_all.at[x])

        mine.wait()
        spot = gathered.at[y, c]
        ahead = [net.send(spot, spot, "y", 1), net.send(spot, spot, "y", -1)]
        come.wait_recv()
        spot = gathered.at[y, 1 - c]
        ahead += [net.send(spot, spot, "y", 1), net.send(spot, spot, "y", -1)]
        both_mine.wait()
        both_come.wait_recv()
        zero, one = both_all.at[x, 0], both_all.at[x, 1]
        right = [net.send(spot, spot, "x", 1) for spot in (zero, one)]
        left = [net.send(spot, spot, "x", -1) for spot in (one, zero)]

        def back(i):
            at = pl.ds(pl.multiple_of(i * BLOCK, BLOCK), BLOCK)
            total = 0.0
            for core in range(2):
                columns = slice(core * part, (core + 1) * part)
                total = total + dot_nt(ref[core], weights_ref[at, columns])
            back_out[:, at] = total

        load.wait()
        pl.loop(0, tiles // 2)(back)
        for copy in ups:
            copy.wait_recv()
        for i in range(4):
            up_sum[i] = (
                (up_ref[i, z].astype(F32) + up_come[0, i].astype(F32))
                + (up_come[1, i].astype(F32) + up_come[2, i].astype(F32))
            ).astype(BF)
        ups = [net.send(up_sum.at[along("y", d)], up_y.at[y], "y", d) for d in LINE]
        up_mine = net.keep(up_sum.at[y], up_y.at[y])

        ahead[0].wait_recv()
        spot = gathered.at[along("y", -1), c]
        ahead.append(net.send(spot, spot, "y", 1))
        ahead[3].wait_recv()
        spot = gathered.at[along("y", 1), 1 - c]
        ahead.append(net.send(spot, spot, "y", -1))

        pl.loop(tiles // 2, tiles)(back)
        values = input_ref[...].astype(F32)
        scale = inverse_ref[...]
        grad = back_out[...]
        gain_own = jnp.sum(grad * values * scale, axis=0, keepdims=True)
        scaled = grad * gain_ref[...]
        back_out[...] = scale * scaled - values * (scale * scale * scale) * jnp.mean(
            scaled * values, axis=-1, keepdims=True
        )
        gain_here[...] = jnp.zeros_like(gain_here)
        for i in range(16):
            gain_here[i // 4, i % 4, 0:1, :] = gain_own[:, i * 128 : (i + 1) * 128]
            gain_here[i // 4, i % 4, 1:2, :] = two_ref[:, i * 128 : (i + 1) * 128]
            gain_here[i // 4, i % 4, 2:3, :] = latent_ref[:, i // 2 * 128 : (i // 2 + 1) * 128]
        near = net.send(gain_here, gain_near, "c", 1)

        right[0].wait_recv()
        spot = both_all.at[along("x", -1), 0]
        far = [net.send(spot, spot, "x", 1)]
        left[0].wait_recv()
        spot = both_all.at[along("x", 1), 1]
        far.append(net.send(spot, spot, "x", -1))

        for copy in [ahead[i] for i in (1, 2, 4, 5)]:
            copy.wait_recv()
        first_here[...] = (
            dot_tn(normed_ref[...], gathered[...].reshape(8 * size, part)).astype(BF).reshape(4, 2, rows, part)
        )
        first_near = net.send(first_here.at[:, 1 - c], pair.at[c], "c", 1)
        first_mine = net.keep(first_here.at[:, c], pair.at[c])

        for copy in outs:
            copy.wait_recv()
        add_all([out_ref.at[z]] + [out_come.at[d] for d in range(3)], out_out.at[x])
        spot = out_out.at[x]
        outs = [net.send(spot, spot, "x", d) for d in LINE]
        up_mine.wait()
        for copy in ups:
            copy.wait_recv()
        up_near = net.send(up_y.at[:, 1 - c], up_all.at[x, :, c], "c", 1)
        up_mine = net.keep(up_y.at[:, c], up_all.at[x, :, c])

        first_mine.wait()
        first_near.wait_recv()
        firsts = [
            [net.send(pair.at[core, along("z", d)], first_come.at[d - 1, core], "z", d) for d in LINE]
            for core in range(2)
        ]
        near.wait_recv()
        gain_near[...] = gain_here[...] + gain_near[...]
        comes = [net.send(gain_near.at[:, along("z", d)], gain_come.at[d - 1], "z", d) for d in LINE]
        up_near.wait_recv()
        up_mine.wait()
        spot = up_all.at[x]
        ups = [net.send(spot, spot, "x", d) for d in LINE]
        downs = [net.send(down_ref, down_all.at[x], "x", d) for d in LINE]

        accum[...] = jnp.zeros_like(accum)

        def put(px):
            for pc in range(2):
                places = unit_places((half_units, 1), 0, px, pc, share, padded)
                picks = lax.broadcasted_iota(jnp.int32, (half_units, half_wide), 1) == places
                stacked = jnp.concatenate(
                    [both_all[px, pc, :, k * half_units : (k + 1) * half_units] for k in range(4)], axis=0
                )
                accum[...] += dot(stacked, picks.astype(BF))

        for copy in (right[1], left[1]):
            copy.wait_recv()
        put(x)
        put(along("x", 1))

        def onward(core):
            for copy in firsts[core]:
                copy.wait_recv()
            add_all([pair.at[core, z]] + [first_come.at[d, core] for d in range(3)], first_x.at[x, core])
            spot = first_x.at[x, core]
            return [net.send(spot, spot, "x", d) for d in LINE]

        finals = [onward(0)]
        for copy in comes:
            copy.wait_recv()
        gain_two[...] = (gain_near[:, z] + gain_come[0]) + (gain_come[1] + gain_come[2])
        comes = [net.send(gain_two.at[along("y", d)], gain_y.at[d - 1], "y", d) for d in LINE]
        finals.append(onward(1))
        put(along("x", -1))
        for copy in comes:
            copy.wait_recv()
        gain_x[x] = (gain_two[y] + gain_y[0]) + (gain_y[1] + gain_y[2])
        spot = gain_x.at[x]
        comes = [net.send(spot, spot, "x", d) for d in LINE]
        for copy in far:
            copy.wait_recv()
        put(along("x", 2))
        for k, target in enumerate((gate_out, gate_out, up_weight_out, up_weight_out)):
            target[:, (k % 2) * half_wide : (k % 2 + 1) * half_wide] = accum[k * rows : (k + 1) * rows].astype(BF)
        for copy in outs + ups + downs:
            copy.wait_recv()
        down_mine.wait()
        for px in range(4):
            down_rows[px * share : (px + 1) * share, :] = down_all[px].astype(F32)[:share]
            for py in range(4):
                for pc in range(2):
                    at = ((2 * py + pc) * 4 + px) * lanes
                    q_up_out[:, at : at + lanes] = up_all[px, py, pc]
        down_out[...] = down_rows[...].astype(BF)
        for core in range(2):
            for copy in finals[core]:
                copy.wait_recv()
            add_all([first_x.at[i, core] for i in range(4)], first_out.at[core])
        for copy in comes:
            copy.wait_recv()
        gain_out[...] = (gain_x[0] + gain_x[1]) + (gain_x[2] + gain_x[3])
        net.close()

    outs = (
        shape(2, rows, part, kind=F32), shape(8, 128, kind=F32), shape(size, deep, kind=F32), shape(4, tall, wide),
        shape(rows, 2 * half_wide), shape(rows, 2 * half_wide), shape(4 * share, width), shape(high, 32 * lanes),
    )
    scratch = [
        pltpu.VMEM((4, 2, size, part), BF),
        pltpu.VMEM((4, *both.shape), BF),
        pltpu.VMEM((4, 4, 2, high, lanes), BF),
        pltpu.VMEM((4, padded, width), BF),
        pltpu.VMEM((3, tall, wide), BF),
        pltpu.VMEM((3, 4, 2, high, lanes), BF),
        pltpu.VMEM((4, 2, high, lanes), BF),
        pltpu.VMEM((4, 2, high, lanes), BF),
        pltpu.VMEM(weights.shape, BF),
        pltpu.VMEM((4 * rows, half_wide), F32),
        pltpu.VMEM((4 * share, width), F32),
        pltpu.VMEM((4, 2, rows, part), BF),
        pltpu.VMEM((2, 4, rows, part), BF),
        pltpu.VMEM((3, 2, rows, part), BF),
        pltpu.VMEM((4, 2, rows, part), BF),
        pltpu.VMEM((4, 4, 8, 128), F32),
        pltpu.VMEM((4, 4, 8, 128), F32),
        pltpu.VMEM((3, 4, 8, 128), F32),
        pltpu.VMEM((4, 8, 128), F32),
        pltpu.VMEM((3, 8, 128), F32),
        pltpu.VMEM((4, 8, 128), F32),
    ]
    return comm_call(
        body, "last_sums", 8, outs,
        (
            value, both, grad_out, grad_up, grad_down, normed_part, inputs, inverse, gain_one, gain_two, gain_latent,
            weights,
        ),
        scratch, 64, 8, [IN_VMEM] * 11 + [ANYWHERE], [IN_VMEM] * 8,
    )


def heads_back(
    grad_branch, branch, mixed, qt, kv, out_heads, begin, slot, lse, live, cosine, sine, mid_down, gb,
):
    segments, _, rows = slot.shape
    tokens = rows // 2
    size, width = grad_branch.shape
    _, high, down_lanes = mid_down.shape[1:]
    tall, wide = gb.shape[2:]
    ahead, after = Y_COLUMNS, wide - Y_COLUMNS
    half = out_heads.shape[0] // (2 * size)

    def body(
        grad_ref, branch_ref, mixed_ref, qt_ref, kv_ref, out_ref, begin_ref, slot_ref, lse_ref, live_ref, cos_ref,
        sin_ref, mid_ref, gb_ref,
        dq_ref, dkv_ref, stack, branch_out, down_out, one_out, two_out,
        grads, kt, sums, accum, query, grad_rows, grad_turned, delta, go_send, near, relay, come, go,
        own_one, come_one, own_two, come_two, down_one, down_two, sends, arrivals, locals_,
    ):
        net = Net(sends, arrivals, locals_)
        y, z, c = (lax.axis_index(a) for a in ROW)
        greet(X_RING + Y_LINE + Z_LINE + TWIN)
        gathering = RingGather(net, grad_ref, grads, "y")
        two = FirstStep(net, gb_ref, pl.ds(ahead, after), "z", own_two, come_two, two_out)
        halves = [
            SecondStep(net, mid_ref.at[k], axis, (down_one, down_two)[k]) for k, axis in enumerate(("z", "y"))
        ]
        ring = RingSum(net, branch_ref, branch_out, "x", near, relay, come, go)
        sums[...] = jnp.zeros_like(sums)
        turned(kv_ref, kt, segments * (segments - 1) + z + 1, KEYS)

        def segment(step):
            seg = along("y", step)
            here = pl.ds(pl.multiple_of(seg * tokens, tokens), tokens)
            grad = dot_nt(grads[seg].reshape(tokens, width), out_ref[...]).astype(BF) * live_ref[here, :].astype(BF)
            grad = jnp.concatenate([grad[:, :SIZE], grad[:, SIZE:]], axis=0)
            value = mixed_ref[here, :]
            value = jnp.concatenate([value[:, :SIZE], value[:, SIZE:]], axis=0)
            query[...] = qt_ref[seg].T
            grad_rows[...] = grad
            grad_turned[...] = grad.T
            delta[...] = jnp.sum(grad_turned[...].astype(F32) * value.T.astype(F32), axis=0, keepdims=True)
            accum[...] = jnp.zeros_like(accum)

            def tile(at, count, masked):
                keys = pl.ds(at, count)
                scores = dot(kv_ref[keys, KEYS], qt_ref[seg])
                probs = jnp.exp(scores - lse_ref[seg])
                if masked:
                    key = lax.broadcasted_iota(jnp.int32, scores.shape, 0) + at
                    probs = jnp.where((key >= begin_ref[seg]) & (key <= slot_ref[seg]), probs, 0.0)
                grad_probs = dot(kv_ref[keys, VALUES], grad_turned[...])
                grad_scores = (probs * (grad_probs - delta[...])).astype(BF)
                sums[keys, VALUES] += dot(probs.astype(BF), grad_rows[...])
                sums[keys, KEYS] += dot(grad_scores, query[...])
                accum[...] += dot(kt[:, keys], grad_scores)

            sweep(seg, segments, z, tile)
            cos_here, sin_here = cos_ref[seg], sin_ref[seg]
            for head in range(2):
                part = accum[:, head * tokens : (head + 1) * tokens] * (SIZE ** -0.5)
                lower, upper = part[:HALF], part[HALF:]
                turn = jnp.concatenate(
                    [lower * cos_here + upper * sin_here, upper * cos_here - lower * sin_here], axis=0
                )
                dq_ref[here, head * SIZE : (head + 1) * SIZE] = turn.T.astype(BF)

        gathering.arrived()
        segment(0)
        gathering.forward()
        one = FirstStep(net, gb_ref, pl.ds(0, ahead), "y", own_one, come_one, one_out)
        ring.relay_far()
        ring.issue()
        gathering.share()
        gathering.arrived()
        pl.loop(0, 2)(lambda i: segment(1 + 2 * i))
        ring.pass_on()
        gathering.finish()

        for k in range(4):
            columns = slice(k * width // 4, (k + 1) * width // 4)
            part = dot_tn(mixed_ref[...], grads[...].reshape(segments * tokens, width)[:, columns]).astype(BF)
            part = part.reshape(half, 2, size, width // 4)
            for h in range(half):

                @pl.when(c == 0)
                def _(h=h, part=part, columns=columns):
                    stack[h, :, columns] = part[h, 0]
                    go_send[h, :, columns] = part[h, 1]

                @pl.when(c == 1)
                def _(h=h, part=part, columns=columns):
                    stack[half + h, :, columns] = part[h, 1]
                    go_send[h, :, columns] = part[h, 0]

        go_come = net.send(go_send, stack.at[pl.ds(half * c, half)], "c", 1)
        segment(2)
        dkv_ref[...] = sums[...].astype(BF)
        for k in range(2):
            halves[k].finish(down_out.at[:, pl.ds(k * down_lanes, down_lanes)])
        ring.finish()
        go_come.wait_recv()
        one.finish()
        two.finish()
        net.close()

    outs = (
        shape(*mixed.shape), shape(*kv.shape), shape(2 * half, size, width), shape(size, width, kind=F32),
        shape(high, 2 * down_lanes), shape(4, tall, ahead), shape(4, tall, after),
    )
    scratch = [
        pltpu.VMEM((4, 2, size, width), BF),
        pltpu.VMEM((SIZE, kv.shape[0]), BF),
        pltpu.VMEM(kv.shape, F32),
        pltpu.VMEM((SIZE, rows), F32),
        pltpu.VMEM((rows, SIZE), BF),
        pltpu.VMEM((rows, SIZE), BF),
        pltpu.VMEM((SIZE, rows), BF),
        pltpu.VMEM((1, rows), F32),
        pltpu.VMEM((half, size, width), BF),
    ] + ring_sum_scratch(size, width) + [
        pltpu.VMEM((4, tall, ahead), BF),
        pltpu.VMEM((3, 4, tall, ahead), BF),
        pltpu.VMEM((4, tall, after), BF),
        pltpu.VMEM((3, 4, tall, after), BF),
        pltpu.VMEM((3, high, down_lanes), BF),
        pltpu.VMEM((3, high, down_lanes), BF),
    ]
    return comm_call(
        body, "heads_back", 6, outs,
        (grad_branch, branch, mixed, qt, kv, out_heads, begin, slot, lse, live, cosine, sine, mid_down, gb),
        scratch, 36, 3, [IN_VMEM] * 13 + [ANYWHERE], [IN_VMEM] * 7,
    )


def gather(value, axes):
    return lax.all_gather(value, axes, axis=0, tiled=True)


def on_device(
    block_input, cotangent, lengths, norm_gain, q_down, q_gain, q_up, key_weight, value_weight,
    out_weight, ffn_gain, gate_weight, up_weight, down_weight,
):
    rows, width = block_input.shape
    latent_width = q_down.shape[1]
    n_x, n_y, n_z, n_c = (lax.axis_size(a) for a in ("x", "y", "z", "c"))
    x, y, z, c = (lax.axis_index(a) for a in ("x", "y", "z", "c"))
    span = n_y * n_z * n_c
    members = n_y * n_c
    lengths_row = lengths[0]

    mine = (y * n_z + z) * n_c + c
    slots_mine = mine * rows + jnp.arange(rows, dtype=jnp.int32)
    begin_mine, _ = places_of(lengths_row, slots_mine)
    cosine, sine = tables(slots_mine - begin_mine)
    strip = n_c * rows
    slots_group = (
        (jnp.arange(n_y, dtype=jnp.int32)[:, None] * n_z + z) * strip
        + jnp.arange(strip, dtype=jnp.int32)[None, :]
    ).reshape(-1)
    begin_group, live_group = places_of(lengths_row, slots_group)
    cosine_group, sine_group = tables_across((slots_group - begin_group).reshape(n_y, strip))
    begin_lanes = jnp.tile(begin_group.reshape(n_y, 1, strip), (1, 1, 2))
    slot_lanes = jnp.tile(slots_group.reshape(n_y, 1, strip), (1, 1, 2))
    live_lanes = jnp.tile(live_group.reshape(n_y, 1, strip), (1, 1, 2))

    shard = norm_gain.shape[0]
    extra = jnp.stack(
        [norm_gain, ffn_gain, jnp.pad(q_gain, (0, shard - q_gain.shape[0]))], axis=1
    ).astype(BF)
    first_width = latent_width + 2 * SIZE
    first = jnp.concatenate(
        [q_down, key_weight, value_weight, jnp.pad(extra, ((0, 0), (0, 125)))], axis=1
    )
    per_heads = q_up.shape[1] // members
    q_rows = q_up.shape[0]

    down_rows = down_weight.shape[0]
    share = down_rows // n_x
    padded = -(-share // 16) * 16
    down_part = lax.dynamic_slice_in_dim(down_weight, x * share, share)
    down_part = jnp.pad(down_part, ((0, padded - share), (0, 0)))
    first_full, both, out_strip = first_weights(first, gate_weight, up_weight, out_weight, share, padded)
    units = both.shape[2] // 2
    first_full = first_full.reshape(span * shard, -1)
    both = both.reshape(n_c * shard, 2 * units)
    extra_full = first_full[:, first_width : first_width + 3].astype(F32)
    gain_one = extra_full[:, 0]
    gain_two = extra_full[:, 1]
    gain_latent = extra_full[:, 2].reshape(span, shard)[:, : q_gain.shape[0]].reshape(-1)

    both_full = gather(both, ("y", "z"))
    down_use = gather(down_part, ("y", "z"))

    inputs = block_input.astype(F32)
    inverse_one = lax.rsqrt(jnp.mean(inputs * inputs, axis=-1, keepdims=True) + EPSILON)
    normed = (inputs * inverse_one * gain_one).astype(BF)
    firsts = dot(normed, first_full[:, :first_width])
    latent = firsts[:, :latent_width]
    inverse_latent = lax.rsqrt(jnp.mean(latent * latent, axis=-1, keepdims=True) + EPSILON)
    latent_normed = (latent * inverse_latent * gain_latent).astype(BF)
    key_mine = rotate(firsts[:, latent_width : latent_width + SIZE], cosine, sine).astype(BF)
    value_mine = firsts[:, latent_width + SIZE :].astype(BF)
    key_value, latent_group, up_heads, out_heads = keys_and_latents(
        jnp.concatenate([key_mine, value_mine], axis=1), latent_normed,
        q_up.reshape(q_rows, n_y, n_c, per_heads).transpose(1, 2, 0, 3), out_strip,
    )
    up_heads = up_heads.reshape(span * q_rows, per_heads)
    out_heads = out_heads.reshape(per_heads, width)
    key_value = key_value.reshape(span * rows, 2 * SIZE)
    group = members * rows
    latent_group = latent_group.reshape(group, latent_width)
    mixed, queries_t, lse = attend(
        dot(latent_group, up_heads), key_value, begin_lanes, slot_lanes, live_lanes,
        cosine_group, sine_group,
    )
    branch, grad_feed = heads_sum_and_cotangent(
        dot(mixed, out_heads).astype(BF).reshape(n_y, n_c, rows, width), cotangent
    )
    middle = inputs + branch

    inverse_two = lax.rsqrt(jnp.mean(middle * middle, axis=-1, keepdims=True) + EPSILON)
    grad_normed_two, normed_part, branch_part, grad_both, grad_down = feed_forward(
        (middle * inverse_two * gain_two).astype(BF), normed, grad_feed, both_full, down_use
    )
    normed_part = normed_part.reshape(group, -1)
    grad_result = cotangent.astype(F32)
    grad_mid_norm, grad_gain_two = norm_back(middle, inverse_two, gain_two, grad_normed_two)
    grad_middle = grad_result + grad_mid_norm

    grad_both = grad_both.reshape(n_y, n_z, n_c * shard, 2 * units)
    out_rows = out_weight.shape[0]
    grad_query_raw, grad_kv, grad_out, branch_two, grad_down, grad_one, grad_two = heads_back(
        grad_middle.astype(BF), branch_part, mixed, queries_t, key_value, out_heads, begin_lanes, slot_lanes, lse,
        live_group[:, None], cosine_group, sine_group, grad_down, grad_both,
    )
    output = (middle + branch_two).astype(BF)
    grad_firsts, grad_gain_latent, grad_up_heads, grad_out, grad_one, grad_two = keys_and_latents_sum(
        grad_kv.reshape(n_y, n_z, n_c, rows, 2 * SIZE), grad_query_raw, latent_group, up_heads, grad_out,
        (grad_one, grad_two), cosine, sine, latent, inverse_latent, gain_latent[None, :],
    )
    grad_both = jnp.concatenate([grad_one, grad_two], axis=1)

    grad_first, gains, grad_input_norm, grad_out, grad_gate, grad_up, grad_down, grad_q_up = last_sums(
        grad_firsts, grad_both.reshape(n_c, shard, 2 * units), grad_out, grad_up_heads, grad_down, normed_part,
        block_input, inverse_one, gain_one[None, :], grad_gain_two[None, :], grad_gain_latent, first_full, share,
    )
    input_grad = grad_middle + grad_input_norm
    grad_first = jnp.concatenate([grad_first[0], grad_first[1]], axis=1)
    latent_shard = q_gain.shape[0]
    return (
        output,
        input_grad,
        lax.dynamic_slice(gains[0], (c * shard,), (shard,)),
        grad_first[:, :latent_width],
        lax.dynamic_slice(gains[2], ((z % 2 * n_c + c) * latent_shard,), (latent_shard,)),
        grad_q_up.astype(F32),
        grad_first[:, latent_width : latent_width + SIZE],
        grad_first[:, latent_width + SIZE :],
        grad_out.reshape(out_rows, width).astype(F32),
        lax.dynamic_slice(gains[1], (c * shard,), (shard,)),
        grad_gate.astype(F32),
        grad_up.astype(F32),
        grad_down.astype(F32),
    )


def solution(mesh):
    sizes = (4, 4, 4, 2)
    grid = Mesh(mesh.devices.reshape(sizes), ("x", "y", "z", "c"))
    tokens = P(("x", "y", "z", "c"), None)
    wide, thin = P(ROW, None), P(ROW)
    in_specs = (
        tokens, tokens, P("x", None), thin, wide, thin, wide, wide, wide, wide, thin, wide, wide,
        wide,
    )
    out_specs = (
        tokens, tokens, thin, wide, thin, wide, wide, wide, wide, thin, wide, wide, wide,
    )
    return jax.shard_map(
        on_device, mesh=grid, in_specs=in_specs, out_specs=out_specs, check_vma=False
    )
```

```python
import functools
import math

import jax
import jax.numpy as jnp
from jax import lax
from jax.experimental import pallas as pl
from jax.experimental.pallas import tpu as pltpu
from jax.sharding import Mesh
from jax.sharding import PartitionSpec as P

EPSILON = 1e-06
MASKED = -1e30
BF = jnp.bfloat16
F32 = jnp.float32
SIZE = 256
HALF = 128
BLOCK = 256
ROW = ("y", "z", "c")
HEADS = ("y", "c")
FEED = ("x", "c")


def dot(left, right):
    return jnp.dot(left, right, preferred_element_type=F32)


def dot_tn(left, right):
    return lax.dot_general(left, right, (((0,), (0,)), ((), ())), preferred_element_type=F32)


def dot_nt(left, right):
    return lax.dot_general(left, right, (((1,), (1,)), ((), ())), preferred_element_type=F32)


def turned(source, target, count, columns):
    @pl.loop(0, count)
    def _(block):
        at = pl.ds(pl.multiple_of(block * BLOCK, BLOCK), BLOCK)
        target[:, at] = source[at, columns].T


KEYS, VALUES = slice(0, SIZE), slice(SIZE, 2 * SIZE)


def sweep(segment, segments, depth, tile):
    count = segments * segment + depth
    last = (segment // (segments - 1)) * (depth // (lax.axis_size("z") - 1))
    guarded = jnp.minimum(count, 1) * (1 - last) + count * last
    free = count - guarded

    @pl.loop(0, guarded)
    def _(i):
        tile(pl.multiple_of(i * BLOCK, BLOCK), BLOCK, True)

    @pl.loop(0, free // 2)
    def _(i):
        tile(pl.multiple_of((guarded + 2 * i) * BLOCK, BLOCK), 2 * BLOCK, False)

    @pl.loop(0, free % 2)
    def _(i):
        tile(pl.multiple_of((count - 1) * BLOCK, BLOCK), BLOCK, False)

    tile(pl.multiple_of(count * BLOCK, BLOCK), BLOCK, True)


MESH_IDS = pl.DeviceIdType.MESH
AXES = ("x", "y", "z", "c")
ANYWHERE = pl.BlockSpec(memory_space=pl.ANY)
IN_VMEM = pl.BlockSpec(memory_space=pltpu.VMEM)


def place():
    return {a: lax.axis_index(a) for a in AXES}


def along(axis, step):
    size = lax.axis_size(axis)
    return lax.rem(lax.axis_index(axis) + (step + size), size)


def device(axis, step):
    here = place()
    here[axis] = along(axis, step)
    return tuple(here[a] for a in AXES)


class Net:
    def __init__(self, sends, arrivals, locals_):
        self.sends, self.arrivals, self.locals_ = sends, arrivals, locals_
        self.used = 0
        self.near = 0
        self.open = []

    def send(self, source, target, axis, step):
        copy = pltpu.make_async_remote_copy(
            src_ref=source, dst_ref=target, send_sem=self.sends.at[self.used],
            recv_sem=self.arrivals.at[self.used], device_id=device(axis, step),
            device_id_type=MESH_IDS,
        )
        copy.start()
        self.used += 1
        self.open.append(copy)
        return copy

    def keep(self, source, target):
        copy = pltpu.make_async_copy(source, target, self.locals_.at[self.near])
        copy.start()
        self.near += 1
        return copy

    def close(self):
        for copy in self.open:
            copy.wait_send()


def greet(partners):
    barrier = pltpu.get_barrier_semaphore()
    for axis, step in partners:
        pl.semaphore_signal(barrier, 1, device_id=device(axis, step), device_id_type=MESH_IDS)
    pl.semaphore_wait(barrier, len(partners))


def semaphores(sends, locals_):
    return [
        pltpu.SemaphoreType.DMA((sends,)),
        pltpu.SemaphoreType.DMA((sends,)),
        pltpu.SemaphoreType.DMA((max(locals_, 1),)),
    ]


def comm_call(body, name, number, outs, ins, scratch, sends, locals_, spaces, out_spaces):
    return pl.pallas_call(
        body,
        name=name,
        out_shape=outs,
        in_specs=spaces,
        out_specs=out_spaces,
        scratch_shapes=list(scratch) + semaphores(sends, locals_),
        compiler_params=pltpu.CompilerParams(
            collective_id=number, has_side_effects=True, vmem_limit_bytes=60 << 20
        ),
    )(*ins)


LINE = (1, 2, 3)


class RowGather:
    def __init__(self, net, value, out):
        self.net, self.out = net, out
        h = value.shape[0] // 2
        self.parts = (pl.ds(0, h), pl.ds(h, h))
        y, z, c = (lax.axis_index(a) for a in ROW)
        self.mine = net.keep(value, out.at[y, z, c])
        self.own = net.send(value, out.at[y, z, c], "c", 1)
        self.first = [
            [net.send(value.at[part], out.at[y, z, c, part], axis, d) for d in LINE]
            for part, axis in zip(self.parts, ("z", "y"))
        ]

    def spread(self):
        net, out = self.net, self.out
        y, z, c = (lax.axis_index(a) for a in ROW)
        self.mine.wait()
        (a, b) = self.parts
        for copy in self.first[0]:
            copy.wait_recv()
        self.second = [
            [net.send(out.at[y, :, c, a], out.at[y, :, c, a], "y", d) for d in LINE]
        ]
        for copy in self.first[1]:
            copy.wait_recv()
        self.second.append(
            [net.send(out.at[:, z, c, b], out.at[:, z, c, b], "z", d) for d in LINE]
        )
        self.shared = [self.own]
        for d in LINE:
            spot = out.at[y, along("z", -d), c, a]
            self.shared.append(net.send(spot, spot, "c", 1))
            spot = out.at[along("y", -d), z, c, b]
            self.shared.append(net.send(spot, spot, "c", 1))

    def arrive(self):
        net, out = self.net, self.out
        y, z, c = (lax.axis_index(a) for a in ROW)
        (a, b) = self.parts
        for d in LINE:
            self.second[0][d - 1].wait_recv()
            spot = out.at[along("y", -d), :, c, a]
            self.shared.append(net.send(spot, spot, "c", 1))
            self.second[1][d - 1].wait_recv()
            spot = out.at[:, along("z", -d), c, b]
            self.shared.append(net.send(spot, spot, "c", 1))

    def finish(self):
        for copy in self.shared:
            copy.wait_recv()


class RingGather:
    def __init__(self, net, value, out, axis):
        self.net, self.out, self.axis = net, out, axis
        a, c = lax.axis_index(axis), lax.axis_index("c")
        h = value.shape[0] // 2
        self.parts = one, two = pl.ds(0, h), pl.ds(h, h)
        self.mine = net.keep(value, out.at[a, c])
        self.right = [net.send(value.at[p], out.at[a, c, p], axis, 1) for p in (one, two)]
        self.left = [net.send(value.at[p], out.at[a, c, p], axis, -1) for p in (two, one)]
        self.shared = [net.send(value, out.at[a, c], "c", 1)]

    def forward(self):
        net, out, axis = self.net, self.out, self.axis
        c = lax.axis_index("c")
        one, two = self.parts
        before, after = along(axis, -1), along(axis, 1)
        self.right[0].wait_recv()
        spot = out.at[before, c, one]
        self.far = [net.send(spot, spot, axis, 1)]
        self.left[0].wait_recv()
        spot = out.at[after, c, two]
        self.far.append(net.send(spot, spot, axis, -1))

    def share(self):
        c = lax.axis_index("c")
        for copies, step in ((self.right, -1), (self.left, 1)):
            copies[1].wait_recv()
            spot = self.out.at[along(self.axis, step), c]
            self.shared.append(self.net.send(spot, spot, "c", 1))

    def finish(self):
        for copy in self.far:
            copy.wait_recv()
        spot = self.out.at[along(self.axis, 2), lax.axis_index("c")]
        self.shared.append(self.net.send(spot, spot, "c", 1))
        self.arrived()

    def arrived(self):
        if self.mine is not None:
            self.mine.wait()
            self.mine = None
        for copy in self.shared:
            copy.wait_recv()
        self.shared = []


STEP = 16
CHUNK = 32 * 1024


def rows_loop(count, width, body):
    step = STEP
    while 2 * step * width <= CHUNK and count % (2 * step) == 0:
        step *= 2
    pl.loop(0, count // step)(lambda i: body(pl.ds(pl.multiple_of(i * step, STEP), step)))


def shifted(rows, first):
    return pl.ds(pl.multiple_of(rows.start + first, STEP), rows.size)


class RingSum:
    def __init__(self, net, value, out, axis, near, relay, come, go):
        self.net, self.value, self.out, self.axis = net, value, out, axis
        self.near, self.relay, self.come, self.go = near, relay, come, go
        c = lax.axis_index("c")
        self.size = value.shape[2]
        h = self.size // 2
        self.parts = pl.ds(0, h), pl.ds(h, h)
        self.swaps = {
            s: net.send(value.at[along(axis, s), 1 - c], near.at[s], "c", 1) for s in (2, 1, 3, 0)
        }

    def pair(self, s, part=None):
        value, near, go = self.value, self.near, self.go
        where, c = along(self.axis, s), lax.axis_index("c")
        first = 0 if part is None else part.start
        count = self.size if part is None else part.size

        def add(rows):
            at = shifted(rows, first)
            go[s, at] = (
                value[where, c, at].astype(F32) + near[s, at].astype(F32)
            ).astype(BF)

        rows_loop(count, value.shape[3], add)

    def relay_far(self):
        net = self.net
        one, two = self.parts
        self.swaps[2].wait_recv()
        self.pair(2)
        self.relays = [
            net.send(self.go.at[2, one], self.relay.at[0], self.axis, 1),
            net.send(self.go.at[2, two], self.relay.at[1], self.axis, -1),
        ]

    def issue(self):
        net, go, come = self.net, self.go, self.come
        one, two = self.parts
        self.swaps[1].wait_recv()
        self.pair(1)
        self.ends = [net.send(go.at[1, two], come.at[0, two], self.axis, 1)]
        self.swaps[3].wait_recv()
        self.pair(3)
        self.ends.append(net.send(go.at[3, one], come.at[1, one], self.axis, -1))

    def pass_on(self):
        net, go, relay, come = self.net, self.go, self.relay, self.come
        one, two = self.parts
        for i, (s, part, step) in enumerate(((1, one, 1), (3, two, -1))):
            self.relays[i].wait_recv()

            def add(rows, i=i, s=s, part=part):
                at = shifted(rows, part.start)
                go[s, at] = (go[s, at].astype(F32) + relay[i, rows].astype(F32)).astype(BF)

            rows_loop(part.size, go.shape[2], add)
            self.ends.append(net.send(go.at[s, part], come.at[i, part], self.axis, step))

    def finish(self):
        value, near, come, out = self.value, self.near, self.come, self.out
        where, c = lax.axis_index(self.axis), lax.axis_index("c")
        self.swaps[0].wait_recv()
        for copy in self.ends:
            copy.wait_recv()

        def add(rows):
            out[rows] = (
                value[where, c, rows].astype(F32) + near[0, rows].astype(F32)
            ) + (come[0, rows].astype(F32) + come[1, rows].astype(F32))

        rows_loop(self.size, out.shape[1], add)


def ring_sum_scratch(size, width):
    return [
        pltpu.VMEM((4, size, width), BF),
        pltpu.VMEM((2, size // 2, width), BF),
        pltpu.VMEM((2, size, width), BF),
        pltpu.VMEM((4, size, width), BF),
    ]


class RowSum:
    def __init__(self, net, value, out, near, go, first, mid, last):
        self.net, self.value, self.out = net, value, out
        self.near, self.go, self.first, self.mid, self.last = near, go, first, mid, last
        c = lax.axis_index("c")
        self.size = value.shape[3]
        h = self.size // 2
        self.parts = pl.ds(0, h), pl.ds(h, h)
        self.swaps = [
            net.send(value.at[i, :, 1 - c], near.at[i], "c", 1) for i in range(4)
        ]

    def start(self):
        net, value, near, go = self.net, self.value, self.near, self.go
        c = lax.axis_index("c")
        for i in range(4):
            self.swaps[i].wait_recv()
            for j in range(4):

                def add(rows, i=i, j=j):
                    go[i, j, rows] = (
                        value[i, j, c, rows].astype(F32) + near[i, j, rows].astype(F32)
                    ).astype(BF)

                rows_loop(self.size, value.shape[4], add)
        a, b = self.parts
        self.ones = [
            [net.send(go.at[along("y", d), :, a], self.first.at[0, d - 1], "y", d) for d in LINE],
            [net.send(go.at[:, along("z", d), b], self.first.at[1, d - 1], "z", d) for d in LINE],
        ]

    def turn(self):
        net, go, first, mid = self.net, self.go, self.first, self.mid
        y, z = lax.axis_index("y"), lax.axis_index("z")
        self.twos = []
        for k, axis in enumerate(("z", "y")):
            for copy in self.ones[k]:
                copy.wait_recv()
            for j in range(4):

                def add(rows, k=k, j=j):
                    at = shifted(rows, self.parts[k].start)
                    own = go[y, j, at] if k == 0 else go[j, z, at]
                    mid[k, j, rows] = (
                        own.astype(F32) + first[k, 0, j, rows].astype(F32)
                        + (first[k, 1, j, rows].astype(F32) + first[k, 2, j, rows].astype(F32))
                    ).astype(BF)

                rows_loop(self.parts[k].size, mid.shape[3], add)
            self.twos.append(
                [net.send(mid.at[k, along(axis, d)], self.last.at[k, d - 1], axis, d) for d in LINE]
            )

    def finish(self):
        mid, last, out = self.mid, self.last, self.out
        for k, axis in enumerate(("z", "y")):
            for copy in self.twos[k]:
                copy.wait_recv()
            here = lax.axis_index(axis)

            def add(rows, k=k, here=here):
                at = shifted(rows, self.parts[k].start)
                out[at] = (
                    mid[k, here, rows].astype(F32) + last[k, 0, rows].astype(F32)
                    + (last[k, 1, rows].astype(F32) + last[k, 2, rows].astype(F32))
                )

            rows_loop(self.parts[k].size, out.shape[1], add)


def row_sum_scratch(size, width):
    h = size // 2
    return [
        pltpu.VMEM((4, 4, size, width), BF),
        pltpu.VMEM((4, 4, size, width), BF),
        pltpu.VMEM((2, 3, 4, h, width), BF),
        pltpu.VMEM((2, 4, h, width), BF),
        pltpu.VMEM((2, 3, h, width), BF),
    ]


Y_LINE = [("y", d) for d in LINE]
Z_LINE = [("z", d) for d in LINE]
X_LINE = [("x", d) for d in LINE]
X_RING = [("x", 1), ("x", -1)]
Y_RING = [("y", 1), ("y", -1)]
TWIN = [("c", 1)]


def shape(*dims, kind=BF):
    return jax.ShapeDtypeStruct(dims, kind)


def unit_places(shape_, axis, x, c, share, padded):
    spot = lax.broadcasted_iota(jnp.int32, shape_, axis)
    block, inside = spot // padded, spot % padded
    return jnp.where(inside < share, (2 * block + c) * (4 * share) + x * share + inside, -1)


OWN_COLUMNS = 640


def first_weights(first, gate, up, out, inputs, lengths, latent_width, share, padded):
    rows_in, wide = gate.shape
    half_wide = wide // 2
    half_units = half_wide // (8 * share) * padded
    units = 2 * half_units
    rows, width = out.shape
    quarter = rows // 4
    lanes = (first.shape[1] - OWN_COLUMNS) // 4

    def body(
        first_ref, gate_ref, up_ref, out_ref, input_ref, length_ref,
        first_hbm, both_out, strip_out, normed_out, kv_out, lat_out, latent_out, inverse_out, latent_inverse_out,
        gain_one_out, gain_two_out, gain_latent_out, cos_ref, sin_ref, cos_group, sin_group, begin_out, slot_out,
        live_out, live_rows, first_out, both, sends, arrivals, locals_,
    ):
        net = Net(sends, arrivals, locals_)
        x, y, z, c = (lax.axis_index(a) for a in AXES)

        def columns(step):
            return pl.ds(pl.multiple_of(OWN_COLUMNS + along("x", step) * lanes, 128), lanes)

        def passing(step, h):
            return first_out.at[pl.ds(2 * h, 2), :, c, :, columns(step)]

        stacked = jnp.concatenate(
            [ref[:, h * half_wide : (h + 1) * half_wide] for ref in (gate_ref, up_ref) for h in range(2)], axis=0
        )

        def pick(core):
            places = unit_places((1, half_units), 1, x, core, share, padded)
            picks = lax.broadcasted_iota(jnp.int32, (half_wide, half_units), 0) == places
            picked = dot(stacked, picks.astype(BF)).astype(BF)
            for i in range(4):
                both[core, :, i * half_units : (i + 1) * half_units] = (
                    picked[i * rows_in : (i + 1) * rows_in]
                )

        greet(X_RING + Y_LINE + Z_LINE + TWIN)
        part = RowGather(net, first_ref.at[:, columns(0)], first_out.at[:, :, :, :, columns(0)])
        pick(0)
        part.spread()
        every = pl.ds(0, OWN_COLUMNS)
        whole = RowGather(net, first_ref.at[:, every], first_out.at[:, :, :, :, every])
        piece = out_ref.at[pl.ds(pl.multiple_of(x * quarter, quarter), quarter)]
        piece_mine = net.keep(piece, strip_out.at[z])
        pieces = [net.send(piece, strip_out.at[z], "z", d) for d in LINE]
        pick(1)
        whole.spread()

        begins = [0]
        for i in range(length_ref.shape[1]):
            begins.append(begins[-1] + length_ref[0, i])

        def begin_of(slots):
            begin = jnp.zeros_like(slots)
            for value in begins[1:]:
                begin = jnp.where(slots >= value, value, begin)
            return begin

        def angles(slots, axis):
            feature = lax.broadcasted_iota(jnp.int32, slots.shape, axis).astype(F32)
            return (slots - begin_of(slots)).astype(F32) * jnp.exp(feature * (-math.log(10000.0) / HALF))

        slots = lax.broadcasted_iota(jnp.int32, (size, HALF), 0) + ((y * 4 + z) * 2 + c) * size
        angle = angles(slots, 1)
        cos_ref[...] = jnp.cos(angle)
        sin_ref[...] = jnp.sin(angle)
        both_mine = net.keep(both.at[c], both_out.at[c])
        both_come = net.send(both.at[1 - c], both_out.at[c], "c", 1)
        part.arrive()
        right = [net.send(passing(0, h), passing(0, h), "x", 1) for h in (0, 1)]
        left = [net.send(passing(0, h), passing(0, h), "x", -1) for h in (1, 0)]
        whole.arrive()

        @pl.loop(0, 4)
        def _(seg):
            base = (seg * 4 + z) * 2 * size
            angle = angles(lax.broadcasted_iota(jnp.int32, (HALF, 2 * size), 1) + base, 0)
            cos_group[seg] = jnp.cos(angle)
            sin_group[seg] = jnp.sin(angle)
            slots = lax.broadcasted_iota(jnp.int32, (1, 4 * size), 1) % (2 * size) + base
            slot_out[seg] = slots
            begin_out[seg] = begin_of(slots)
            live_out[seg] = (slots < begins[-1]).astype(F32)
            slots = lax.broadcasted_iota(jnp.int32, (2 * size, 1), 0) + base
            live_rows[pl.ds(pl.multiple_of(seg * 2 * size, 2 * size), 2 * size), :] = (
                (slots < begins[-1]).astype(F32)
            )

        right[0].wait_recv()
        far = [net.send(passing(-1, 0), passing(-1, 0), "x", 1)]
        left[0].wait_recv()
        far.append(net.send(passing(1, 1), passing(1, 1), "x", -1))
        shared = []
        for copies, step in ((right, -1), (left, 1)):
            copies[1].wait_recv()
            spot = first_out.at[:, :, c, :, columns(step)]
            shared.append(net.send(spot, spot, "c", 1))
        for copy in far:
            copy.wait_recv()
        spot = first_out.at[:, :, c, :, columns(2)]
        shared.append(net.send(spot, spot, "c", 1))
        part.finish()
        whole.finish()
        for copy in shared + pieces + [both_come]:
            copy.wait_recv()
        keep = net.keep(first_out, first_hbm)

        gains = pl.ds(first_width, 128)
        for i in range(16):
            for k, target in enumerate((gain_one_out, gain_two_out)):
                target[:, i * 128 : (i + 1) * 128] = (
                    first_out[i // 4, i % 4, 0, k : k + 1, gains].astype(F32)
                    + first_out[i // 4, i % 4, 1, k : k + 1, gains].astype(F32)
                )
        for i in range(8):
            total = 0.0
            for k in range(4):
                total = total + first_out[i // 2, i % 2 * 2 + k // 2, k % 2, 2:3, gains].astype(F32)
            gain_latent_out[:, i * 128 : (i + 1) * 128] = total
        values = input_ref[...].astype(F32)
        inverse = lax.rsqrt(jnp.mean(values * values, axis=-1, keepdims=True) + EPSILON)
        inverse_out[...] = inverse
        normed_out[...] = (values * inverse * gain_one_out[...]).astype(BF)
        firsts = dot(normed_out[...], first_out[...].reshape(32 * rows_in, first_width + 128)[:, :first_width])
        latent = firsts[:, :latent_width]
        latent_out[...] = latent
        inverse = lax.rsqrt(jnp.mean(latent * latent, axis=-1, keepdims=True) + EPSILON)
        latent_inverse_out[...] = inverse
        lat_out[...] = (latent * inverse * gain_latent_out[...]).astype(BF)
        lower, upper = firsts[:, latent_width : latent_width + HALF], firsts[:, latent_width + HALF : latent_width + SIZE]
        kv_out[:, :HALF] = (lower * cos_ref[...] - upper * sin_ref[...]).astype(BF)
        kv_out[:, HALF:SIZE] = (upper * cos_ref[...] + lower * sin_ref[...]).astype(BF)
        kv_out[:, SIZE:] = firsts[:, latent_width + SIZE :].astype(BF)
        both_mine.wait()
        piece_mine.wait()
        keep.wait()
        net.close()

    size, deep = inputs.shape
    first_width = first.shape[1] - 128
    whole = (4, 4, 2, *first.shape)
    outs = (
        shape(*whole), shape(2, rows_in, 2 * units), shape(4, quarter, width), shape(size, deep),
        shape(size, 2 * SIZE), shape(size, latent_width), shape(size, latent_width, kind=F32),
        shape(size, 1, kind=F32), shape(size, 1, kind=F32), shape(1, deep, kind=F32), shape(1, deep, kind=F32),
        shape(1, latent_width, kind=F32), shape(size, HALF, kind=F32), shape(size, HALF, kind=F32),
        shape(4, HALF, 2 * size, kind=F32), shape(4, HALF, 2 * size, kind=F32),
        shape(4, 1, 4 * size, kind=jnp.int32), shape(4, 1, 4 * size, kind=jnp.int32), shape(4, 1, 4 * size, kind=F32),
        shape(8 * size, 1, kind=F32),
    )
    scratch = [pltpu.VMEM(whole, BF), pltpu.VMEM((2, rows_in, 2 * units), BF)]
    return comm_call(
        body, "first_weights", 1, outs, (first, gate, up, out, inputs, lengths), scratch, 64, 5,
        [IN_VMEM] * 5 + [pl.BlockSpec(memory_space=pltpu.SMEM)], [ANYWHERE] * 3 + [IN_VMEM] * 17,
    )


def gain_rows(norm_gain, ffn_gain, q_gain):
    z, c = lax.axis_index("z"), lax.axis_index("c")
    rows = norm_gain.shape[0]

    def spot(values, at):
        count = 128 // values.shape[0]
        return jnp.concatenate([values * (at == i).astype(F32) for i in range(count)])

    block = jnp.stack([spot(norm_gain, c), spot(ffn_gain, c), spot(q_gain, z % 2 * 2 + c)])
    return jnp.pad(block.astype(BF), ((0, rows - 3), (0, 0)))


def keys_and_latents(key_value, latent, up, strip):
    def body(
        kv_ref, lat_ref, up_ref, strip_ref, kv_out, lat_out, up_out, out_out, transit, sheet,
        sends, arrivals, locals_,
    ):
        net = Net(sends, arrivals, locals_)
        x, y, z, c = (lax.axis_index(a) for a in AXES)
        greet(X_LINE + Y_LINE + Z_LINE + TWIN)
        up_mine = net.keep(up_ref.at[y], transit.at[y, z])
        ups = [net.send(up_ref.at[along("y", d)], transit.at[y, z], "y", d) for d in LINE]
        row = RowGather(net, kv_ref, kv_out)
        ring = RingGather(net, lat_ref, lat_out, "y")
        strip_mine = net.keep(strip_ref, sheet.at[:, x])
        strips = [net.send(strip_ref, sheet.at[:, x], "x", d) for d in LINE]
        up_mine.wait()
        for copy in ups:
            copy.wait_recv()
        ups = [net.send(transit.at[:, z], transit.at[:, z], "z", d) for d in LINE]
        row.spread()
        ring.forward()
        ring.share()
        row.arrive()
        strip_mine.wait()
        for copy in strips:
            copy.wait_recv()
        half = sheet.shape[0] // 2
        sheet_keep = net.keep(sheet.at[pl.ds(half * c, half)], out_out.at[:, c])
        sheet_come = net.send(sheet.at[pl.ds(half * (1 - c), half)], out_out.at[:, c], "c", 1)
        for copy in ups:
            copy.wait_recv()
        up_keep = net.keep(transit.at[:, :, c], up_out.at[:, :, c])
        up_come = net.send(transit.at[:, :, 1 - c], up_out.at[:, :, c], "c", 1)
        ring.finish()
        row.finish()
        for copy in (up_keep, sheet_keep):
            copy.wait()
        for copy in (up_come, sheet_come):
            copy.wait_recv()
        net.close()

    _, _, high, thin = up.shape
    _, quarter, width = strip.shape
    outs = (
        shape(4, 4, 2, *key_value.shape), shape(4, 2, *latent.shape), shape(4, 4, 2, high, thin),
        shape(2, 2, 4, quarter, width),
    )
    scratch = [pltpu.VMEM((4, 4, 2, high, thin), BF), pltpu.VMEM((4, 4, quarter, width), BF)]
    return comm_call(
        body, "keys_and_latents", 2, outs, (key_value, latent, up, strip), scratch, 48, 6,
        [IN_VMEM] * 4, [ANYWHERE] * 4,
    )


def add_up(terms, out, rows):
    total = terms[0][rows].astype(F32)
    for term in terms[1:]:
        total = total + term[rows].astype(F32)
    out[rows] = total.astype(out.dtype)


def add_all(terms, out):
    rows_loop(out.shape[0], out.shape[1], lambda rows: add_up(terms, out, rows))


def attend(
    latent, up_heads, kv, begin, slot, live, cosine, sine, out_heads, inputs, gain, cotangent,
):
    segments, _, rows = slot.shape
    tokens = rows // 2
    size, width = inputs.shape

    def body(
        lat_ref, up_ref, kv_ref, begin_ref, slot_ref, live_ref, cos_ref, sin_ref, heads_ref, input_ref, gain_ref,
        cot_ref,
        mixed_out, qt_ref, lse_ref, middle_out, inverse_out, two_out, cot_out,
        vt, peak, total, accum, part, near, go, come, sends, arrivals, locals_,
    ):
        net = Net(sends, arrivals, locals_)
        y, z, c = (lax.axis_index(a) for a in ROW)
        greet(X_RING + Y_LINE + TWIN)
        feed = RingGather(net, cot_ref, cot_out, "x")
        turned(kv_ref, vt, segments * (segments - 1) + z + 1, VALUES)

        def segment(step):
            seg = along("y", step)
            here = pl.ds(pl.multiple_of(seg * tokens, tokens), tokens)
            cos_here, sin_here = cos_ref[seg], sin_ref[seg]
            for head in range(2):
                columns = slice(head * SIZE, (head + 1) * SIZE)
                raw = dot(lat_ref[here, :], up_ref[:, columns]).T
                lower, upper = raw[:HALF], raw[HALF:]
                turn = jnp.concatenate(
                    [lower * cos_here - upper * sin_here, upper * cos_here + lower * sin_here], axis=0
                )
                qt_ref[seg, :, head * tokens : (head + 1) * tokens] = (
                    turn.astype(BF) * (SIZE ** -0.5)
                ).astype(BF)
            peak[...] = jnp.full_like(peak, MASKED)
            total[...] = jnp.zeros_like(total)
            accum[...] = jnp.zeros_like(accum)

            def tile(at, count, masked):
                scores = dot(kv_ref[pl.ds(at, count), KEYS], qt_ref[seg])
                if masked:
                    key = lax.broadcasted_iota(jnp.int32, scores.shape, 0) + at
                    scores = jnp.where((key >= begin_ref[seg]) & (key <= slot_ref[seg]), scores, MASKED)
                before = peak[...]
                now = jnp.maximum(before, jnp.max(scores, axis=0, keepdims=True))
                weights = jnp.exp(scores - now)
                shrink = jnp.exp(before - now)
                peak[...] = now
                total[...] = total[...] * shrink + jnp.sum(weights, axis=0, keepdims=True)
                accum[...] = accum[...] * shrink + dot(vt[:, pl.ds(at, count)], weights.astype(BF))

            sweep(seg, segments, z, tile)
            lse_ref[seg] = peak[...] + jnp.log(total[...])
            result = accum[...] * (live_ref[seg] / total[...])
            for head in range(2):
                mixed_out[here, head * SIZE : (head + 1) * SIZE] = (
                    result[:, head * tokens : (head + 1) * tokens].T.astype(BF)
                )
            part[seg] = dot(mixed_out[here, :], heads_ref[...]).astype(BF).reshape(2, size, width)
            return net.send(part.at[seg, 1 - c], near.at[step], "c", 1)

        def pair(step):
            swaps[step].wait_recv()
            add_all([part.at[along("y", step), c], near.at[step]], go.at[step - 1])
            return net.send(go.at[step - 1], come.at[step - 1], "y", step)

        swaps = {2: segment(2)}
        feed.forward()
        swaps[1] = segment(1)
        ends = [pair(2)]
        feed.share()
        swaps[3] = segment(3)
        ends.append(pair(1))
        ends.append(pair(3))
        feed.finish()
        swaps[0] = segment(0)
        swaps[0].wait_recv()
        for copy in ends:
            copy.wait_recv()
        add_all(
            [input_ref, part.at[y, c], near.at[0], come.at[0], come.at[1], come.at[2]], middle_out
        )
        values = middle_out[...]
        inverse = lax.rsqrt(jnp.mean(values * values, axis=-1, keepdims=True) + EPSILON)
        inverse_out[...] = inverse
        two_out[...] = (values * inverse * gain_ref[...]).astype(BF)
        net.close()

    outs = (
        shape(segments * tokens, 2 * SIZE), shape(segments, SIZE, rows), shape(segments, 1, rows, kind=F32),
        shape(size, width, kind=F32), shape(size, 1, kind=F32), shape(size, width), shape(4, 2, size, width),
    )
    scratch = [
        pltpu.VMEM((SIZE, kv.shape[0]), BF),
        pltpu.VMEM((1, rows), F32),
        pltpu.VMEM((1, rows), F32),
        pltpu.VMEM((SIZE, rows), F32),
        pltpu.VMEM((4, 2, size, width), BF),
        pltpu.VMEM((4, size, width), BF),
        pltpu.VMEM((3, size, width), BF),
        pltpu.VMEM((3, size, width), BF),
    ]
    return comm_call(
        body, "attend", 3, outs,
        (latent, up_heads, kv, begin, slot, live, cosine, sine, out_heads, inputs, gain, cotangent),
        scratch, 20, 2, [IN_VMEM] * 12, [IN_VMEM] * 6 + [ANYWHERE],
    )


def feed_forward(normed_two, normed, grad_out, both, down, middle, inverse, gain):
    size, width = normed_two.shape
    units = down.shape[0]
    tall = width // 4
    lanes = width // 2
    high = units // 16

    def body(
        two_ref, one_ref, middle_ref, inverse_ref, gain_ref, cot_hbm, both_hbm, down_hbm,
        middle_out, grad_out_, gain_out, one_out, branch_out, gb_out, mid_out,
        two, cot, both, down, hidden, grads, part, near, go, come, gb, gd, down_come, ahead,
        sends, arrivals, locals_,
    ):
        net = Net(sends, arrivals, locals_)
        x, y, z, c = (lax.axis_index(a) for a in AXES)
        both_load = net.keep(both_hbm, both)
        down_load = net.keep(down_hbm, down)
        cot_load = net.keep(cot_hbm, cot)
        greet(X_LINE + Y_LINE + Z_LINE + TWIN)
        feed = RingGather(net, two_ref, two, "x")
        one_mine = net.keep(one_ref.at[:, pl.ds(pl.multiple_of(y * tall, tall), tall)], one_out.at[y, c])
        ones = [
            net.send(
                one_ref.at[:, pl.ds(pl.multiple_of(along("y", d) * tall, tall), tall)],
                one_out.at[y, c], "y", d,
            )
            for d in LINE
        ]

        def back(s):
            return dot_nt(cot[along("x", s)].reshape(2 * size, width), down[...])

        def block(s):
            where = along("x", s)
            at = pl.ds(pl.multiple_of(where * 2 * size, 2 * size), 2 * size)
            value = two[where].reshape(2 * size, width)
            pre = dot(value, both[...])
            grad = ahead[s - 1] if s else back(0)
            gate, up = pre[:, :units], pre[:, units:]
            sigma = 1.0 / (1.0 + jnp.exp(-gate))
            gated = gate * sigma
            hidden[at, :] = (gated * up).astype(BF)
            grads[at, :units] = (grad * up * (sigma + gated * (1.0 - sigma))).astype(BF)
            grads[at, units:] = (grad * gated).astype(BF)
            part[where] = dot_nt(grads[at, :], both[...]).astype(BF).reshape(2, size, width)
            return net.send(part.at[where, 1 - c], near.at[s], "c", 1)

        def pair(s):
            where = along("x", s)
            swaps[s].wait_recv()
            add_all([part.at[where, c], near.at[s]], go.at[s - 1])
            return net.send(go.at[s - 1], come.at[s - 1], "x", s)

        swaps = {}
        feed.arrived()
        both_load.wait()
        down_load.wait()
        cot_load.wait()
        swaps[0] = block(0)
        feed.forward()
        for s in LINE:
            ahead[s - 1] = back(s)
        feed.share()
        one_mine.wait()
        spot = one_out.at[y, c]
        shared = [net.send(spot, spot, "c", 1)]
        for d in LINE:
            ones[d - 1].wait_recv()
            spot = one_out.at[along("y", -d), c]
            shared.append(net.send(spot, spot, "c", 1))
        feed.arrived()
        swaps[1] = block(1)
        for copy in feed.far:
            copy.wait_recv()
        spot = two.at[along("x", 2), c]
        last = net.send(spot, spot, "c", 1)
        swaps[3] = block(3)
        ends = [pair(1)]
        last.wait_recv()
        swaps[2] = block(2)
        ends.append(pair(3))
        ends.append(pair(2))
        early, net.open = net.open, []

        first = []
        for k, axis in enumerate(("y", "z")):
            columns = slice(k * lanes, (k + 1) * lanes)
            gd[k] = (
                dot_tn(hidden[...], cot[...].reshape(8 * size, width)[:, columns])
                .astype(BF)
                .reshape(4, 4, high, lanes)
            )
            for d in LINE:
                at = along(axis, d)
                source = gd.at[k, at] if k == 0 else gd.at[k, :, at]
                first.append(net.send(source, down_come.at[k, d - 1], axis, d))

        gb_copies = []
        for i in range(8):
            at = pl.ds(i * 2 * size, 2 * size)
            gb[i] = dot_tn(two[...].reshape(8 * size, width)[:, i * 2 * size : (i + 1) * 2 * size], grads[...]).astype(BF)
            gb_copies.append(net.keep(gb.at[i], gb_out.at[at]))
        for copy in early:
            copy.wait_send()

        @pl.loop(0, 4)
        def _(i):
            at = pl.ds(pl.multiple_of(i * 2 * size, 2 * size), 2 * size)
            two[i] = dot(hidden[at, :], down[...]).astype(BF).reshape(2, size, width)

        branch_copy = net.keep(two, branch_out)
        swaps[0].wait_recv()
        for copy in ends:
            copy.wait_recv()
        add_all([part.at[x, c], near.at[0], come.at[0], come.at[1], come.at[2]], middle_out)
        values, scale, grad = middle_ref[...], inverse_ref[...], middle_out[...]
        gain_out[...] = jnp.sum(grad * values * scale, axis=0, keepdims=True)
        scaled = grad * gain_ref[...]
        grad = cot[x, c].astype(F32) + (
            scale * scaled
            - values * (scale * scale * scale) * jnp.mean(scaled * values, axis=-1, keepdims=True)
        )
        middle_out[...] = grad
        grad_out_[...] = grad.astype(BF)
        for copy in shared:
            copy.wait_recv()
        for copy in first:
            copy.wait_recv()
        for k in range(2):
            for i in range(4):
                own = gd.at[k, y, i] if k == 0 else gd.at[k, i, z]
                add_all([own] + [down_come.at[k, d, i] for d in range(3)], mid_out.at[k, i])
        for copy in gb_copies + [branch_copy]:
            copy.wait()
        net.close()

    outs = (
        shape(size, width, kind=F32), shape(size, width), shape(1, width, kind=F32), shape(4, 2, size, tall),
        shape(4, 2, size, width), shape(width, 2 * units),
        shape(2, 4, high, lanes),
    )
    scratch = [
        pltpu.VMEM((4, 2, size, width), BF),
        pltpu.VMEM((4, 2, size, width), BF),
        pltpu.VMEM((width, 2 * units), BF),
        pltpu.VMEM((units, width), BF),
        pltpu.VMEM((8 * size, units), BF),
        pltpu.VMEM((8 * size, 2 * units), BF),
        pltpu.VMEM((4, 2, size, width), BF),
        pltpu.VMEM((4, size, width), BF),
        pltpu.VMEM((3, size, width), BF),
        pltpu.VMEM((3, size, width), BF),
        pltpu.VMEM((8, 2 * size, 2 * units), BF),
        pltpu.VMEM((2, 4, 4, high, lanes), BF),
        pltpu.VMEM((2, 3, 4, high, lanes), BF),
        pltpu.VMEM((3, 2 * size, units), F32),
    ]
    return comm_call(
        body, "feed_forward", 4, outs, (normed_two, normed, middle, inverse, gain, grad_out, both, down), scratch,
        32, 14, [IN_VMEM] * 5 + [ANYWHERE] * 3, [IN_VMEM] * 3 + [ANYWHERE] * 3 + [IN_VMEM],
    )


Y_COLUMNS = 512


class FirstStep:
    def __init__(self, net, value, columns, axis, own, come, out):
        self.own, self.come, self.out = own, come, out
        self.copies = []
        for d in (1, 2, 3, 0):
            at = along(axis, d)
            source = value.at[at, :, :, columns] if axis == "y" else value.at[:, at, :, columns]
            if d:
                self.copies.append(net.send(source, come.at[d - 1], axis, d))
            else:
                self.mine = net.keep(source, own)

    def finish(self):
        self.mine.wait()
        for copy in self.copies:
            copy.wait_recv()
        for i in range(4):
            add_all([self.own.at[i]] + [self.come.at[d, i] for d in range(3)], self.out.at[i])


class SecondStep:
    def __init__(self, net, mid, axis, come):
        self.mid, self.axis, self.come = mid, axis, come
        self.copies = [net.send(mid.at[along(axis, d)], come.at[d - 1], axis, d) for d in LINE]

    def finish(self, out):
        for copy in self.copies:
            copy.wait_recv()
        here = lax.axis_index(self.axis)
        add_all([self.mid.at[here]] + [self.come.at[d] for d in range(3)], out)


def last_sums(
    grad_kv, grad_query, latent_group, up_heads, grad_out, grad_both, grad_down, cosine, sine, latent,
    latent_inverse, latent_gain, normed_part, inputs, inverse, gain_one, gain_two, weights, share,
):
    _, _, _, size, thin = grad_kv.shape
    group, latent_width = latent_group.shape
    per = up_heads.shape[1]
    high, lanes = up_heads.shape[0] // 32, per // 4
    _, out_rows, wide = grad_out.shape
    quarter = out_rows // 4
    tall, ahead_columns = grad_both[0].shape[1:]
    after_columns = grad_both[1].shape[2]
    both_columns = ahead_columns + after_columns
    rows = tall // 2
    half_units = both_columns // 4
    _, _, padded, down_lanes = grad_down.shape
    width = 2 * down_lanes
    half_wide = 2 * half_units // padded * 4 * share
    part = (latent_width + thin) // 2
    deep = weights.shape[0]
    tiles = deep // BLOCK

    def body(
        kv_ref, query_ref, group_ref, heads_ref, out_ref, one_ref, two_ref, down_ref, cos_ref, sin_ref, latent_ref,
        latent_inverse_ref, latent_gain_ref, normed_ref, input_ref, inverse_ref, gain_ref, gain_two_ref, weights_hbm,
        first_out, gain_out, back_out, out_out, gate_out, up_weight_out, down_out, q_up_out,
        row_near, row_go, row_first, row_mid, row_last, ring_near, ring_relay, ring_come, ring_go,
        partial, ups_here, kv_sum, part_sum, up_come_x, out_come_x, one_come, two_come, down_come, both_here,
        up_kept, out_kept, firsts,
        gathered, both_all, up_all, down_all, out_come, up_come, up_sum, up_y, weights_ref, accum, down_rows,
        first_here, pair, first_come, first_x, gain_here, gain_near, gain_come, gain_z, gain_y, gain_x,
        sends, arrivals, locals_,
    ):
        net = Net(sends, arrivals, locals_)
        x, y, z, c = (lax.axis_index(a) for a in AXES)

        def lane(at):
            return pl.ds(pl.multiple_of(at * lanes, lanes), lanes)

        def strip(at):
            return pl.ds(pl.multiple_of(at * quarter, quarter), quarter)

        load = net.keep(weights_hbm, weights_ref)
        greet(X_LINE + Y_LINE + Z_LINE + TWIN)
        row = RowSum(net, kv_ref, kv_sum, row_near, row_go, row_first, row_mid, row_last)
        outs = [net.send(out_ref.at[:, strip(along("x", d))], out_come_x.at[d - 1], "x", d) for d in LINE]
        for i in range(4):
            at = pl.ds(i * 2 * size, 2 * size)
            partial[i] = dot_nt(query_ref[at, :], heads_ref[...]).astype(BF).reshape(2, size, latent_width)
        ring = RingSum(net, partial, part_sum, "y", ring_near, ring_relay, ring_come, ring_go)
        row.start()
        ring.relay_far()
        ring.issue()
        ups_here[...] = dot_tn(group_ref[...], query_ref[...]).astype(BF).reshape(4, 4, 2, high, per)
        ups = [
            net.send(ups_here.at[:, :, :, :, lane(along("x", d))], up_come_x.at[d - 1], "x", d) for d in LINE
        ]
        row.turn()
        ring.pass_on()
        halves = [
            SecondStep(net, mid, axis, come)
            for mid, axis, come in (
                (one_ref, "z", one_come), (two_ref, "y", two_come), (down_ref.at[0], "z", down_come.at[0]),
                (down_ref.at[1], "y", down_come.at[1]),
            )
        ]

        ring.finish()
        values = latent_ref[...]
        scale = latent_inverse_ref[...]
        scaled = part_sum[...] * latent_gain_ref[...]
        gain_latent = jnp.sum(part_sum[...] * values * scale, axis=0, keepdims=True)
        back = scale * scaled - values * (scale * scale * scale) * jnp.mean(scaled * values, axis=-1, keepdims=True)
        firsts[0] = back[:, :part].astype(BF)
        firsts[1, :, : latent_width - part] = back[:, part:].astype(BF)
        row.finish()
        lower, upper = kv_sum[:, :HALF], kv_sum[:, HALF:SIZE]
        at = latent_width - part
        firsts[1, :, at : at + HALF] = (lower * cos_ref[...] + upper * sin_ref[...]).astype(BF)
        firsts[1, :, at + HALF : at + SIZE] = (upper * cos_ref[...] - lower * sin_ref[...]).astype(BF)
        firsts[1, :, at + SIZE :] = kv_sum[:, SIZE:].astype(BF)

        mine = net.keep(firsts.at[c], gathered.at[y, c])
        come = net.send(firsts.at[1 - c], gathered.at[y, c], "c", 1)
        mine.wait()
        spot = gathered.at[y, c]
        ahead = [net.send(spot, spot, "y", 1), net.send(spot, spot, "y", -1)]
        come.wait_recv()
        spot = gathered.at[y, 1 - c]
        ahead += [net.send(spot, spot, "y", 1), net.send(spot, spot, "y", -1)]
        halves[0].finish(both_here.at[:, pl.ds(0, ahead_columns)])
        halves[1].finish(both_here.at[:, pl.ds(ahead_columns, after_columns)])
        own_rows = pl.ds(pl.multiple_of(c * rows, rows), rows)
        other_rows = pl.ds(pl.multiple_of((1 - c) * rows, rows), rows)
        both_mine = net.keep(both_here.at[own_rows], both_all.at[x, c])
        both_come = net.send(both_here.at[other_rows], both_all.at[x, c], "c", 1)
        both_mine.wait()
        both_come.wait_recv()
        zero, one = both_all.at[x, 0], both_all.at[x, 1]
        right = [net.send(spot, spot, "x", 1) for spot in (zero, one)]
        left = [net.send(spot, spot, "x", -1) for spot in (one, zero)]

        for copy in ups:
            copy.wait_recv()
        for i in range(4):
            up_kept[i] = (
                (ups_here[i, :, :, :, lane(x)].astype(F32) + up_come_x[0, i].astype(F32))
                + (up_come_x[1, i].astype(F32) + up_come_x[2, i].astype(F32))
            ).astype(BF)
        ups = [net.send(up_kept.at[:, along("z", d)], up_come.at[d - 1], "z", d) for d in LINE]
        for copy in outs:
            copy.wait_recv()
        for i in range(4):
            add_all([out_ref.at[i, strip(x)]] + [out_come_x.at[d, i] for d in range(3)], out_kept.at[i])
        outs = [net.send(out_kept.at[along("z", d)], out_come.at[d - 1], "z", d) for d in LINE]

        def back_tile(i):
            at = pl.ds(pl.multiple_of(i * BLOCK, BLOCK), BLOCK)
            total = 0.0
            for core in range(2):
                columns = slice(core * part, (core + 1) * part)
                total = total + dot_nt(firsts[core], weights_ref[at, columns])
            back_out[:, at] = total

        load.wait()
        pl.loop(0, tiles // 2)(back_tile)
        ahead[0].wait_recv()
        spot = gathered.at[along("y", -1), c]
        ahead.append(net.send(spot, spot, "y", 1))
        ahead[3].wait_recv()
        spot = gathered.at[along("y", 1), 1 - c]
        ahead.append(net.send(spot, spot, "y", -1))
        pl.loop(tiles // 2, tiles)(back_tile)

        for copy in ups:
            copy.wait_recv()
        for i in range(4):
            up_sum[i] = (
                (up_kept[i, z].astype(F32) + up_come[0, i].astype(F32))
                + (up_come[1, i].astype(F32) + up_come[2, i].astype(F32))
            ).astype(BF)
        ups = [net.send(up_sum.at[along("y", d)], up_y.at[y], "y", d) for d in LINE]
        up_mine = net.keep(up_sum.at[y], up_y.at[y])

        values = input_ref[...].astype(F32)
        scale = inverse_ref[...]
        grad = back_out[...]
        gain_own = jnp.sum(grad * values * scale, axis=0, keepdims=True)
        scaled = grad * gain_ref[...]
        back_out[...] = scale * scaled - values * (scale * scale * scale) * jnp.mean(
            scaled * values, axis=-1, keepdims=True
        )
        gain_here[...] = jnp.zeros_like(gain_here)
        for i in range(16):
            gain_here[i // 4, i % 4, 0:1, :] = gain_own[:, i * 128 : (i + 1) * 128]
            gain_here[i // 4, i % 4, 1:2, :] = gain_two_ref[:, i * 128 : (i + 1) * 128]
            gain_here[i // 4, i % 4, 2:3, :] = gain_latent[:, i // 2 * 128 : (i // 2 + 1) * 128]
        near = net.send(gain_here, gain_near, "c", 1)

        right[0].wait_recv()
        spot = both_all.at[along("x", -1), 0]
        far = [net.send(spot, spot, "x", 1)]
        left[0].wait_recv()
        spot = both_all.at[along("x", 1), 1]
        far.append(net.send(spot, spot, "x", -1))
        for k in (2, 3):
            halves[k].finish(down_all.at[x, :, pl.ds((k - 2) * down_lanes, down_lanes)])
        spot = down_all.at[x]
        downs = [net.send(spot, spot, "x", d) for d in LINE]

        for copy in [ahead[i] for i in (1, 2, 4, 5)]:
            copy.wait_recv()
        first_here[...] = (
            dot_tn(normed_ref[...], gathered[...].reshape(8 * size, part)).astype(BF).reshape(4, 2, rows, part)
        )
        first_near = net.send(first_here.at[:, 1 - c], pair.at[c], "c", 1)
        first_mine = net.keep(first_here.at[:, c], pair.at[c])

        for copy in outs:
            copy.wait_recv()
        add_all([out_kept.at[z]] + [out_come.at[d] for d in range(3)], out_out.at[x])
        spot = out_out.at[x]
        outs = [net.send(spot, spot, "x", d) for d in LINE]
        up_mine.wait()
        for copy in ups:
            copy.wait_recv()
        up_near = net.send(up_y.at[:, 1 - c], up_all.at[x, :, c], "c", 1)
        up_mine = net.keep(up_y.at[:, c], up_all.at[x, :, c])

        first_mine.wait()
        first_near.wait_recv()
        weight_sends = [
            [net.send(pair.at[core, along("z", d)], first_come.at[d - 1, core], "z", d) for d in LINE]
            for core in range(2)
        ]
        near.wait_recv()
        gain_near[...] = gain_here[...] + gain_near[...]
        comes = [net.send(gain_near.at[:, along("z", d)], gain_come.at[d - 1], "z", d) for d in LINE]
        up_near.wait_recv()
        up_mine.wait()
        spot = up_all.at[x]
        ups = [net.send(spot, spot, "x", d) for d in LINE]

        accum[...] = jnp.zeros_like(accum)

        def put(px):
            for pc in range(2):
                places = unit_places((half_units, 1), 0, px, pc, share, padded)
                picks = lax.broadcasted_iota(jnp.int32, (half_units, half_wide), 1) == places
                stacked = jnp.concatenate(
                    [both_all[px, pc, :, k * half_units : (k + 1) * half_units] for k in range(4)], axis=0
                )
                accum[...] += dot(stacked, picks.astype(BF))

        for copy in (right[1], left[1]):
            copy.wait_recv()
        put(x)
        put(along("x", 1))

        def onward(core):
            for copy in weight_sends[core]:
                copy.wait_recv()
            add_all([pair.at[core, z]] + [first_come.at[d, core] for d in range(3)], first_x.at[x, core])
            spot = first_x.at[x, core]
            return [net.send(spot, spot, "x", d) for d in LINE]

        finals = [onward(0)]
        for copy in comes:
            copy.wait_recv()
        gain_z[...] = (gain_near[:, z] + gain_come[0]) + (gain_come[1] + gain_come[2])
        comes = [net.send(gain_z.at[along("y", d)], gain_y.at[d - 1], "y", d) for d in LINE]
        finals.append(onward(1))
        put(along("x", -1))
        for copy in comes:
            copy.wait_recv()
        gain_x[x] = (gain_z[y] + gain_y[0]) + (gain_y[1] + gain_y[2])
        spot = gain_x.at[x]
        comes = [net.send(spot, spot, "x", d) for d in LINE]
        for copy in far:
            copy.wait_recv()
        put(along("x", 2))
        for k, target in enumerate((gate_out, gate_out, up_weight_out, up_weight_out)):
            target[:, (k % 2) * half_wide : (k % 2 + 1) * half_wide] = accum[k * rows : (k + 1) * rows].astype(BF)
        for copy in outs + ups + downs:
            copy.wait_recv()
        for px in range(4):
            down_rows[px * share : (px + 1) * share, :] = down_all[px].astype(F32)[:share]
            for py in range(4):
                for pc in range(2):
                    at = ((2 * py + pc) * 4 + px) * lanes
                    q_up_out[:, at : at + lanes] = up_all[px, py, pc]
        down_out[...] = down_rows[...].astype(BF)
        for core in range(2):
            for copy in finals[core]:
                copy.wait_recv()
            add_all([first_x.at[i, core] for i in range(4)], first_out.at[core])
        for copy in comes:
            copy.wait_recv()
        gain_out[...] = (gain_x[0] + gain_x[1]) + (gain_x[2] + gain_x[3])
        net.close()

    outs = (
        shape(2, rows, part, kind=F32), shape(8, 128, kind=F32), shape(size, deep, kind=F32),
        shape(4, quarter, wide), shape(rows, 2 * half_wide), shape(rows, 2 * half_wide), shape(4 * share, width),
        shape(high, 32 * lanes),
    )
    scratch = row_sum_scratch(size, thin) + ring_sum_scratch(size, latent_width) + [
        pltpu.VMEM((4, 2, size, latent_width), BF),
        pltpu.VMEM((4, 4, 2, high, per), BF),
        pltpu.VMEM((size, thin), F32),
        pltpu.VMEM((size, latent_width), F32),
        pltpu.VMEM((3, 4, 4, 2, high, lanes), BF),
        pltpu.VMEM((3, 4, quarter, wide), BF),
        pltpu.VMEM((3, tall, ahead_columns), BF),
        pltpu.VMEM((3, tall, after_columns), BF),
        pltpu.VMEM((2, 3, padded, down_lanes), BF),
        pltpu.VMEM((tall, both_columns), BF),
        pltpu.VMEM((4, 4, 2, high, lanes), BF),
        pltpu.VMEM((4, quarter, wide), BF),
        pltpu.VMEM((2, size, part), BF),
        pltpu.VMEM((4, 2, size, part), BF),
        pltpu.VMEM((4, 2, rows, both_columns), BF),
        pltpu.VMEM((4, 4, 2, high, lanes), BF),
        pltpu.VMEM((4, padded, width), BF),
        pltpu.VMEM((3, quarter, wide), BF),
        pltpu.VMEM((3, 4, 2, high, lanes), BF),
        pltpu.VMEM((4, 2, high, lanes), BF),
        pltpu.VMEM((4, 2, high, lanes), BF),
        pltpu.VMEM(weights.shape, BF),
        pltpu.VMEM((4 * rows, half_wide), F32),
        pltpu.VMEM((4 * share, width), F32),
        pltpu.VMEM((4, 2, rows, part), BF),
        pltpu.VMEM((2, 4, rows, part), BF),
        pltpu.VMEM((3, 2, rows, part), BF),
        pltpu.VMEM((4, 2, rows, part), BF),
        pltpu.VMEM((4, 4, 8, 128), F32),
        pltpu.VMEM((4, 4, 8, 128), F32),
        pltpu.VMEM((3, 4, 8, 128), F32),
        pltpu.VMEM((4, 8, 128), F32),
        pltpu.VMEM((3, 8, 128), F32),
        pltpu.VMEM((4, 8, 128), F32),
    ]
    return comm_call(
        body, "last_sums", 7, outs,
        (
            grad_kv, grad_query, latent_group, up_heads, grad_out, *grad_both, grad_down, cosine, sine, latent,
            latent_inverse, latent_gain, normed_part, inputs, inverse, gain_one, gain_two, weights,
        ),
        scratch, 104, 8, [IN_VMEM] * 18 + [ANYWHERE], [IN_VMEM] * 8,
    )


def heads_back(
    grad_branch, branch, mixed, qt, kv, out_heads, begin, slot, lse, live, cosine, sine, gb,
):
    segments, _, rows = slot.shape
    tokens = rows // 2
    size, width = grad_branch.shape
    tall, wide = gb.shape[2:]
    ahead, after = Y_COLUMNS, wide - Y_COLUMNS
    half = out_heads.shape[0] // (2 * size)

    def body(
        grad_ref, branch_ref, mixed_ref, qt_ref, kv_ref, out_ref, begin_ref, slot_ref, lse_ref, live_ref, cos_ref,
        sin_ref, gb_ref,
        dq_ref, dkv_ref, stack, branch_out, one_out, two_out,
        grads, kt, sums, accum, query, grad_rows, grad_turned, delta, go_send, near, relay, come, go,
        own_one, come_one, own_two, come_two, sends, arrivals, locals_,
    ):
        net = Net(sends, arrivals, locals_)
        y, z, c = (lax.axis_index(a) for a in ROW)
        greet(X_RING + Y_LINE + Z_LINE + TWIN)
        gathering = RingGather(net, grad_ref, grads, "y")
        two = FirstStep(net, gb_ref, pl.ds(ahead, after), "z", own_two, come_two, two_out)
        ring = RingSum(net, branch_ref, branch_out, "x", near, relay, come, go)
        sums[...] = jnp.zeros_like(sums)
        turned(kv_ref, kt, segments * (segments - 1) + z + 1, KEYS)

        def segment(step):
            seg = along("y", step)
            here = pl.ds(pl.multiple_of(seg * tokens, tokens), tokens)
            grad = dot_nt(grads[seg].reshape(tokens, width), out_ref[...]).astype(BF) * live_ref[here, :].astype(BF)
            grad = jnp.concatenate([grad[:, :SIZE], grad[:, SIZE:]], axis=0)
            value = mixed_ref[here, :]
            value = jnp.concatenate([value[:, :SIZE], value[:, SIZE:]], axis=0)
            query[...] = qt_ref[seg].T
            grad_rows[...] = grad
            grad_turned[...] = grad.T
            delta[...] = jnp.sum(grad_turned[...].astype(F32) * value.T.astype(F32), axis=0, keepdims=True)
            accum[...] = jnp.zeros_like(accum)

            def tile(at, count, masked):
                keys = pl.ds(at, count)
                scores = dot(kv_ref[keys, KEYS], qt_ref[seg])
                probs = jnp.exp(scores - lse_ref[seg])
                if masked:
                    key = lax.broadcasted_iota(jnp.int32, scores.shape, 0) + at
                    probs = jnp.where((key >= begin_ref[seg]) & (key <= slot_ref[seg]), probs, 0.0)
                grad_probs = dot(kv_ref[keys, VALUES], grad_turned[...])
                grad_scores = (probs * (grad_probs - delta[...])).astype(BF)
                sums[keys, VALUES] += dot(probs.astype(BF), grad_rows[...])
                sums[keys, KEYS] += dot(grad_scores, query[...])
                accum[...] += dot(kt[:, keys], grad_scores)

            sweep(seg, segments, z, tile)
            cos_here, sin_here = cos_ref[seg], sin_ref[seg]
            for head in range(2):
                part = accum[:, head * tokens : (head + 1) * tokens] * (SIZE ** -0.5)
                lower, upper = part[:HALF], part[HALF:]
                turn = jnp.concatenate(
                    [lower * cos_here + upper * sin_here, upper * cos_here - lower * sin_here], axis=0
                )
                dq_ref[here, head * SIZE : (head + 1) * SIZE] = turn.T.astype(BF)

        gathering.arrived()
        segment(0)
        gathering.forward()
        one = FirstStep(net, gb_ref, pl.ds(0, ahead), "y", own_one, come_one, one_out)
        ring.relay_far()
        ring.issue()
        gathering.share()
        gathering.arrived()
        pl.loop(0, 2)(lambda i: segment(1 + 2 * i))
        ring.pass_on()
        gathering.finish()

        for k in range(4):
            columns = slice(k * width // 4, (k + 1) * width // 4)
            part = dot_tn(mixed_ref[...], grads[...].reshape(segments * tokens, width)[:, columns]).astype(BF)
            part = part.reshape(half, 2, size, width // 4)
            for h in range(half):

                @pl.when(c == 0)
                def _(h=h, part=part, columns=columns):
                    stack[h, :, columns] = part[h, 0]
                    go_send[h, :, columns] = part[h, 1]

                @pl.when(c == 1)
                def _(h=h, part=part, columns=columns):
                    stack[half + h, :, columns] = part[h, 1]
                    go_send[h, :, columns] = part[h, 0]

        go_come = net.send(go_send, stack.at[pl.ds(half * c, half)], "c", 1)
        segment(2)
        dkv_ref[...] = sums[...].astype(BF)
        ring.finish()
        go_come.wait_recv()
        one.finish()
        two.finish()
        net.close()

    outs = (
        shape(*mixed.shape), shape(*kv.shape), shape(2 * half, size, width), shape(size, width, kind=F32),
        shape(4, tall, ahead), shape(4, tall, after),
    )
    scratch = [
        pltpu.VMEM((4, 2, size, width), BF),
        pltpu.VMEM((SIZE, kv.shape[0]), BF),
        pltpu.VMEM(kv.shape, F32),
        pltpu.VMEM((SIZE, rows), F32),
        pltpu.VMEM((rows, SIZE), BF),
        pltpu.VMEM((rows, SIZE), BF),
        pltpu.VMEM((SIZE, rows), BF),
        pltpu.VMEM((1, rows), F32),
        pltpu.VMEM((half, size, width), BF),
    ] + ring_sum_scratch(size, width) + [
        pltpu.VMEM((4, tall, ahead), BF),
        pltpu.VMEM((3, 4, tall, ahead), BF),
        pltpu.VMEM((4, tall, after), BF),
        pltpu.VMEM((3, 4, tall, after), BF),
    ]
    return comm_call(
        body, "heads_back", 6, outs,
        (grad_branch, branch, mixed, qt, kv, out_heads, begin, slot, lse, live, cosine, sine, gb),
        scratch, 30, 3, [IN_VMEM] * 12 + [ANYWHERE], [IN_VMEM] * 6,
    )


def results(middle, branch, grad_middle, grad_norm, first, gate, up, down, out, q_up, latent_width):
    size, width = middle.shape
    rows, part = first.shape[1:]
    spare = latent_width - part
    kinds = [BF] + [F32] * 9
    shapes = [
        (size, width), (size, width), (rows, latent_width), (rows, SIZE), (rows, SIZE), gate.shape, up.shape,
        down.shape, (4 * out.shape[1], out.shape[2]), q_up.shape,
    ]
    count = len(shapes)

    def body(
        middle_ref, branch_ref, grad_ref, norm_ref, first_ref, gate_ref, up_ref, down_ref, out_ref, q_up_ref, *rest,
    ):
        targets, made, done = rest[:count], rest[count : 2 * count], rest[2 * count]
        copies = []

        def ready(i):
            copy = pltpu.make_async_copy(made[i], targets[i], done.at[i])
            copy.start()
            copies.append(copy)

        made[5][...] = gate_ref[...].astype(F32)
        ready(5)
        made[6][...] = up_ref[...].astype(F32)
        ready(6)
        made[7][...] = down_ref[...].astype(F32)
        ready(7)
        for i in range(4):
            quarter = out_ref.shape[1]
            made[8][i * quarter : (i + 1) * quarter, :] = out_ref[i].astype(F32)
        ready(8)
        made[1][...] = grad_ref[...] + norm_ref[...]
        ready(1)
        made[0][...] = (middle_ref[...] + branch_ref[...]).astype(BF)
        ready(0)
        made[9][...] = q_up_ref[...].astype(F32)
        ready(9)
        made[2][:, :part] = first_ref[0]
        made[2][:, part:] = first_ref[1, :, :spare]
        ready(2)
        made[3][...] = first_ref[1, :, spare : spare + SIZE]
        ready(3)
        made[4][...] = first_ref[1, :, spare + SIZE :]
        ready(4)
        for copy in copies:
            copy.wait()

    return pl.pallas_call(
        body,
        name="results",
        out_shape=tuple(shape(*dims, kind=kind) for dims, kind in zip(shapes, kinds)),
        in_specs=[IN_VMEM] * 10,
        out_specs=[ANYWHERE] * count,
        scratch_shapes=[pltpu.VMEM(dims, kind) for dims, kind in zip(shapes, kinds)]
        + [pltpu.SemaphoreType.DMA((count,))],
        compiler_params=pltpu.CompilerParams(vmem_limit_bytes=56 << 20),
    )(middle, branch, grad_middle, grad_norm, first, gate, up, down, out, q_up)


def gather(value, axes):
    return lax.all_gather(value, axes, axis=0, tiled=True)


def on_device(
    block_input, cotangent, lengths, norm_gain, q_down, q_gain, q_up, key_weight, value_weight,
    out_weight, ffn_gain, gate_weight, up_weight, down_weight,
):
    rows, width = block_input.shape
    latent_width = q_down.shape[1]
    n_x, n_y, n_z, n_c = (lax.axis_size(a) for a in ("x", "y", "z", "c"))
    x, y, z, c = (lax.axis_index(a) for a in ("x", "y", "z", "c"))
    span = n_y * n_z * n_c
    members = n_y * n_c

    shard = norm_gain.shape[0]
    first_width = latent_width + 2 * SIZE
    first = jnp.concatenate(
        [q_down, key_weight, value_weight, gain_rows(norm_gain, ffn_gain, q_gain)], axis=1
    )
    per_heads = q_up.shape[1] // members
    q_rows = q_up.shape[0]

    down_rows = down_weight.shape[0]
    share = down_rows // n_x
    padded = -(-share // 16) * 16
    down_part = lax.dynamic_slice_in_dim(down_weight, x * share, share)
    down_part = jnp.pad(down_part, ((0, padded - share), (0, 0)))
    (
        first_full, both, out_strip, normed, key_value, latent_normed, latent, inverse_one, inverse_latent, gain_one,
        gain_two, gain_latent, cosine, sine, cosine_group, sine_group, begin_lanes, slot_lanes, live_lanes, live_rows,
    ) = first_weights(
        first, gate_weight, up_weight, out_weight, block_input, lengths, latent_width, share, padded
    )
    units = both.shape[2] // 2
    first_full = first_full.reshape(span * shard, -1)
    both = both.reshape(n_c * shard, 2 * units)
    both_full = gather(both, ("y", "z"))
    down_use = gather(down_part, ("y", "z"))

    key_value, latent_group, up_heads, out_heads = keys_and_latents(
        key_value, latent_normed, q_up.reshape(q_rows, n_y, n_c, per_heads).transpose(1, 2, 0, 3), out_strip,
    )
    up_heads = up_heads.reshape(span * q_rows, per_heads)
    out_heads = out_heads.reshape(per_heads, width)
    key_value = key_value.reshape(span * rows, 2 * SIZE)
    group = members * rows
    latent_group = latent_group.reshape(group, latent_width)
    mixed, queries_t, lse, middle, inverse_two, normed_two, grad_feed = attend(
        latent_group, up_heads, key_value, begin_lanes, slot_lanes, live_lanes, cosine_group, sine_group, out_heads,
        block_input, gain_two, cotangent,
    )

    grad_middle, grad_branch, grad_gain_two, normed_part, branch_part, grad_both, grad_down = feed_forward(
        normed_two, normed, grad_feed, both_full, down_use, middle, inverse_two, gain_two
    )
    normed_part = normed_part.reshape(group, -1)

    grad_both = grad_both.reshape(n_y, n_z, n_c * shard, 2 * units)
    out_rows = out_weight.shape[0]
    grad_query_raw, grad_kv, grad_out, branch_two, grad_one, grad_two = heads_back(
        grad_branch, branch_part, mixed, queries_t, key_value, out_heads, begin_lanes, slot_lanes, lse,
        live_rows, cosine_group, sine_group, grad_both,
    )

    grad_first, gains, grad_input_norm, grad_out, grad_gate, grad_up, grad_down, grad_q_up = last_sums(
        grad_kv.reshape(n_y, n_z, n_c, rows, 2 * SIZE), grad_query_raw, latent_group, up_heads, grad_out,
        (grad_one, grad_two), grad_down, cosine, sine, latent, inverse_latent, gain_latent, normed_part, block_input,
        inverse_one, gain_one, grad_gain_two, first_full, share,
    )
    (
        output, input_grad, grad_q_down, grad_key, grad_value, grad_gate, grad_up, grad_down, grad_out, grad_q_up,
    ) = results(
        middle, branch_two, grad_middle, grad_input_norm, grad_first, grad_gate, grad_up, grad_down, grad_out,
        grad_q_up, latent_width,
    )
    latent_shard = q_gain.shape[0]
    return (
        output,
        input_grad,
        lax.dynamic_slice(gains[0], (c * shard,), (shard,)),
        grad_q_down,
        lax.dynamic_slice(gains[2], ((z % 2 * n_c + c) * latent_shard,), (latent_shard,)),
        grad_q_up,
        grad_key,
        grad_value,
        grad_out,
        lax.dynamic_slice(gains[1], (c * shard,), (shard,)),
        grad_gate,
        grad_up,
        grad_down,
    )


def solution(mesh):
    sizes = (4, 4, 4, 2)
    grid = Mesh(mesh.devices.reshape(sizes), ("x", "y", "z", "c"))
    tokens = P(("x", "y", "z", "c"), None)
    wide, thin = P(ROW, None), P(ROW)
    in_specs = (
        tokens, tokens, P("x", None), thin, wide, thin, wide, wide, wide, wide, thin, wide, wide,
        wide,
    )
    out_specs = (
        tokens, tokens, thin, wide, thin, wide, wide, wide, wide, thin, wide, wide, wide,
    )
    return jax.shard_map(
        on_device, mesh=grid, in_specs=in_specs, out_specs=out_specs, check_vma=False
    )
```

```python
import functools
import math

import jax
import jax.numpy as jnp
from jax import lax
from jax.experimental import pallas as pl
from jax.experimental.pallas import tpu as pltpu
from jax.sharding import Mesh
from jax.sharding import PartitionSpec as P

EPSILON = 1e-06
MASKED = -1e30
BF = jnp.bfloat16
F32 = jnp.float32
SIZE = 256
HALF = 128
BLOCK = 256
ROW = ("y", "z", "c")
HEADS = ("y", "c")
FEED = ("x", "c")


def dot(left, right):
    return jnp.dot(left, right, preferred_element_type=F32)


def dot_tn(left, right):
    return lax.dot_general(left, right, (((0,), (0,)), ((), ())), preferred_element_type=F32)


def dot_nt(left, right):
    return lax.dot_general(left, right, (((1,), (1,)), ((), ())), preferred_element_type=F32)


def turned(source, target, count, columns):
    @pl.loop(0, count)
    def _(block):
        at = pl.ds(pl.multiple_of(block * BLOCK, BLOCK), BLOCK)
        target[:, at] = source[at, columns].T


KEYS, VALUES = slice(0, SIZE), slice(SIZE, 2 * SIZE)


def sweep(segment, segments, depth, tile):
    count = segments * segment + depth
    last = (segment // (segments - 1)) * (depth // (lax.axis_size("z") - 1))
    guarded = jnp.minimum(count, 1) * (1 - last) + count * last
    free = count - guarded

    @pl.loop(0, guarded)
    def _(i):
        tile(pl.multiple_of(i * BLOCK, BLOCK), BLOCK, True)

    @pl.loop(0, free // 2)
    def _(i):
        tile(pl.multiple_of((guarded + 2 * i) * BLOCK, BLOCK), 2 * BLOCK, False)

    @pl.loop(0, free % 2)
    def _(i):
        tile(pl.multiple_of((count - 1) * BLOCK, BLOCK), BLOCK, False)

    tile(pl.multiple_of(count * BLOCK, BLOCK), BLOCK, True)


MESH_IDS = pl.DeviceIdType.MESH
AXES = ("x", "y", "z", "c")
ANYWHERE = pl.BlockSpec(memory_space=pl.ANY)
IN_VMEM = pl.BlockSpec(memory_space=pltpu.VMEM)


def place():
    return {a: lax.axis_index(a) for a in AXES}


def along(axis, step):
    size = lax.axis_size(axis)
    return lax.rem(lax.axis_index(axis) + (step + size), size)


def device(axis, step):
    here = place()
    here[axis] = along(axis, step)
    return tuple(here[a] for a in AXES)


class Net:
    def __init__(self, sends, arrivals, locals_):
        self.sends, self.arrivals, self.locals_ = sends, arrivals, locals_
        self.used = 0
        self.near = 0
        self.open = []

    def send(self, source, target, axis, step):
        copy = pltpu.make_async_remote_copy(
            src_ref=source, dst_ref=target, send_sem=self.sends.at[self.used],
            recv_sem=self.arrivals.at[self.used], device_id=device(axis, step),
            device_id_type=MESH_IDS,
        )
        copy.start()
        self.used += 1
        self.open.append(copy)
        return copy

    def keep(self, source, target):
        copy = pltpu.make_async_copy(source, target, self.locals_.at[self.near])
        copy.start()
        self.near += 1
        return copy

    def close(self):
        for copy in self.open:
            copy.wait_send()


def greet(partners):
    barrier = pltpu.get_barrier_semaphore()
    for axis, step in partners:
        pl.semaphore_signal(barrier, 1, device_id=device(axis, step), device_id_type=MESH_IDS)
    pl.semaphore_wait(barrier, len(partners))


def semaphores(sends, locals_):
    return [
        pltpu.SemaphoreType.DMA((sends,)),
        pltpu.SemaphoreType.DMA((sends,)),
        pltpu.SemaphoreType.DMA((max(locals_, 1),)),
    ]


def comm_call(body, name, number, outs, ins, scratch, sends, locals_, spaces, out_spaces):
    return pl.pallas_call(
        body,
        name=name,
        out_shape=outs,
        in_specs=spaces,
        out_specs=out_spaces,
        scratch_shapes=list(scratch) + semaphores(sends, locals_),
        compiler_params=pltpu.CompilerParams(
            collective_id=number, has_side_effects=True, vmem_limit_bytes=60 << 20
        ),
    )(*ins)


LINE = (1, 2, 3)


class RowGather:
    def __init__(self, net, value, out):
        self.net, self.out = net, out
        h = value.shape[0] // 2
        self.parts = (pl.ds(0, h), pl.ds(h, h))
        y, z, c = (lax.axis_index(a) for a in ROW)
        self.mine = net.keep(value, out.at[y, z, c])
        self.own = net.send(value, out.at[y, z, c], "c", 1)
        self.first = [
            [net.send(value.at[part], out.at[y, z, c, part], axis, d) for d in LINE]
            for part, axis in zip(self.parts, ("z", "y"))
        ]

    def spread(self):
        net, out = self.net, self.out
        y, z, c = (lax.axis_index(a) for a in ROW)
        self.mine.wait()
        (a, b) = self.parts
        for copy in self.first[0]:
            copy.wait_recv()
        self.second = [
            [net.send(out.at[y, :, c, a], out.at[y, :, c, a], "y", d) for d in LINE]
        ]
        for copy in self.first[1]:
            copy.wait_recv()
        self.second.append(
            [net.send(out.at[:, z, c, b], out.at[:, z, c, b], "z", d) for d in LINE]
        )
        self.shared = [self.own]
        for d in LINE:
            spot = out.at[y, along("z", -d), c, a]
            self.shared.append(net.send(spot, spot, "c", 1))
            spot = out.at[along("y", -d), z, c, b]
            self.shared.append(net.send(spot, spot, "c", 1))

    def arrive(self):
        net, out = self.net, self.out
        y, z, c = (lax.axis_index(a) for a in ROW)
        (a, b) = self.parts
        for d in LINE:
            self.second[0][d - 1].wait_recv()
            spot = out.at[along("y", -d), :, c, a]
            self.shared.append(net.send(spot, spot, "c", 1))
            self.second[1][d - 1].wait_recv()
            spot = out.at[:, along("z", -d), c, b]
            self.shared.append(net.send(spot, spot, "c", 1))

    def finish(self):
        for copy in self.shared:
            copy.wait_recv()


class RingGather:
    def __init__(self, net, value, out, axis):
        self.net, self.out, self.axis = net, out, axis
        a, c = lax.axis_index(axis), lax.axis_index("c")
        h = value.shape[0] // 2
        self.parts = one, two = pl.ds(0, h), pl.ds(h, h)
        self.mine = net.keep(value, out.at[a, c])
        self.right = [net.send(value.at[p], out.at[a, c, p], axis, 1) for p in (one, two)]
        self.left = [net.send(value.at[p], out.at[a, c, p], axis, -1) for p in (two, one)]
        self.shared = [net.send(value, out.at[a, c], "c", 1)]

    def forward(self):
        net, out, axis = self.net, self.out, self.axis
        c = lax.axis_index("c")
        one, two = self.parts
        before, after = along(axis, -1), along(axis, 1)
        self.right[0].wait_recv()
        spot = out.at[before, c, one]
        self.far = [net.send(spot, spot, axis, 1)]
        self.left[0].wait_recv()
        spot = out.at[after, c, two]
        self.far.append(net.send(spot, spot, axis, -1))

    def share(self):
        c = lax.axis_index("c")
        for copies, step in ((self.right, -1), (self.left, 1)):
            copies[1].wait_recv()
            spot = self.out.at[along(self.axis, step), c]
            self.shared.append(self.net.send(spot, spot, "c", 1))

    def finish(self):
        for copy in self.far:
            copy.wait_recv()
        spot = self.out.at[along(self.axis, 2), lax.axis_index("c")]
        self.shared.append(self.net.send(spot, spot, "c", 1))
        self.arrived()

    def arrived(self):
        if self.mine is not None:
            self.mine.wait()
            self.mine = None
        for copy in self.shared:
            copy.wait_recv()
        self.shared = []


STEP = 16
CHUNK = 32 * 1024


def rows_loop(count, width, body):
    step = STEP
    while 2 * step * width <= CHUNK and count % (2 * step) == 0:
        step *= 2
    pl.loop(0, count // step)(lambda i: body(pl.ds(pl.multiple_of(i * step, STEP), step)))


def shifted(rows, first):
    return pl.ds(pl.multiple_of(rows.start + first, STEP), rows.size)


class RingSum:
    def __init__(self, net, value, out, axis, near, relay, come, go):
        self.net, self.value, self.out, self.axis = net, value, out, axis
        self.near, self.relay, self.come, self.go = near, relay, come, go
        c = lax.axis_index("c")
        self.size = value.shape[2]
        h = self.size // 2
        self.parts = pl.ds(0, h), pl.ds(h, h)
        self.swaps = {
            s: net.send(value.at[along(axis, s), 1 - c], near.at[s], "c", 1) for s in (2, 1, 3, 0)
        }

    def pair(self, s, part=None):
        value, near, go = self.value, self.near, self.go
        where, c = along(self.axis, s), lax.axis_index("c")
        first = 0 if part is None else part.start
        count = self.size if part is None else part.size

        def add(rows):
            at = shifted(rows, first)
            go[s, at] = (
                value[where, c, at].astype(F32) + near[s, at].astype(F32)
            ).astype(BF)

        rows_loop(count, value.shape[3], add)

    def relay_far(self):
        net = self.net
        one, two = self.parts
        self.swaps[2].wait_recv()
        self.pair(2)
        self.relays = [
            net.send(self.go.at[2, one], self.relay.at[0], self.axis, 1),
            net.send(self.go.at[2, two], self.relay.at[1], self.axis, -1),
        ]

    def issue(self):
        net, go, come = self.net, self.go, self.come
        one, two = self.parts
        self.swaps[1].wait_recv()
        self.pair(1)
        self.ends = [net.send(go.at[1, two], come.at[0, two], self.axis, 1)]
        self.swaps[3].wait_recv()
        self.pair(3)
        self.ends.append(net.send(go.at[3, one], come.at[1, one], self.axis, -1))

    def pass_on(self):
        net, go, relay, come = self.net, self.go, self.relay, self.come
        one, two = self.parts
        for i, (s, part, step) in enumerate(((1, one, 1), (3, two, -1))):
            self.relays[i].wait_recv()

            def add(rows, i=i, s=s, part=part):
                at = shifted(rows, part.start)
                go[s, at] = (go[s, at].astype(F32) + relay[i, rows].astype(F32)).astype(BF)

            rows_loop(part.size, go.shape[2], add)
            self.ends.append(net.send(go.at[s, part], come.at[i, part], self.axis, step))

    def finish(self):
        value, near, come, out = self.value, self.near, self.come, self.out
        where, c = lax.axis_index(self.axis), lax.axis_index("c")
        self.swaps[0].wait_recv()
        for copy in self.ends:
            copy.wait_recv()

        def add(rows):
            out[rows] = (
                value[where, c, rows].astype(F32) + near[0, rows].astype(F32)
            ) + (come[0, rows].astype(F32) + come[1, rows].astype(F32))

        rows_loop(self.size, out.shape[1], add)


def ring_sum_scratch(size, width):
    return [
        pltpu.VMEM((4, size, width), BF),
        pltpu.VMEM((2, size // 2, width), BF),
        pltpu.VMEM((2, size, width), BF),
        pltpu.VMEM((4, size, width), BF),
    ]


class RowSum:
    def __init__(self, net, value, out, near, go, first, mid, last):
        self.net, self.value, self.out = net, value, out
        self.near, self.go, self.first, self.mid, self.last = near, go, first, mid, last
        c = lax.axis_index("c")
        self.size = value.shape[3]
        h = self.size // 2
        self.parts = pl.ds(0, h), pl.ds(h, h)
        self.swaps = [
            net.send(value.at[i, :, 1 - c], near.at[i], "c", 1) for i in range(4)
        ]

    def start(self):
        net, value, near, go = self.net, self.value, self.near, self.go
        c = lax.axis_index("c")
        for i in range(4):
            self.swaps[i].wait_recv()
            for j in range(4):

                def add(rows, i=i, j=j):
                    go[i, j, rows] = (
                        value[i, j, c, rows].astype(F32) + near[i, j, rows].astype(F32)
                    ).astype(BF)

                rows_loop(self.size, value.shape[4], add)
        a, b = self.parts
        self.ones = [
            [net.send(go.at[along("y", d), :, a], self.first.at[0, d - 1], "y", d) for d in LINE],
            [net.send(go.at[:, along("z", d), b], self.first.at[1, d - 1], "z", d) for d in LINE],
        ]

    def turn(self):
        net, go, first, mid = self.net, self.go, self.first, self.mid
        y, z = lax.axis_index("y"), lax.axis_index("z")
        self.twos = []
        for k, axis in enumerate(("z", "y")):
            for copy in self.ones[k]:
                copy.wait_recv()
            for j in range(4):

                def add(rows, k=k, j=j):
                    at = shifted(rows, self.parts[k].start)
                    own = go[y, j, at] if k == 0 else go[j, z, at]
                    mid[k, j, rows] = (
                        own.astype(F32) + first[k, 0, j, rows].astype(F32)
                        + (first[k, 1, j, rows].astype(F32) + first[k, 2, j, rows].astype(F32))
                    ).astype(BF)

                rows_loop(self.parts[k].size, mid.shape[3], add)
            self.twos.append(
                [net.send(mid.at[k, along(axis, d)], self.last.at[k, d - 1], axis, d) for d in LINE]
            )

    def finish(self):
        mid, last, out = self.mid, self.last, self.out
        for k, axis in enumerate(("z", "y")):
            for copy in self.twos[k]:
                copy.wait_recv()
            here = lax.axis_index(axis)

            def add(rows, k=k, here=here):
                at = shifted(rows, self.parts[k].start)
                out[at] = (
                    mid[k, here, rows].astype(F32) + last[k, 0, rows].astype(F32)
                    + (last[k, 1, rows].astype(F32) + last[k, 2, rows].astype(F32))
                )

            rows_loop(self.parts[k].size, out.shape[1], add)


def row_sum_scratch(size, width):
    h = size // 2
    return [
        pltpu.VMEM((4, 4, size, width), BF),
        pltpu.VMEM((4, 4, size, width), BF),
        pltpu.VMEM((2, 3, 4, h, width), BF),
        pltpu.VMEM((2, 4, h, width), BF),
        pltpu.VMEM((2, 3, h, width), BF),
    ]


Y_LINE = [("y", d) for d in LINE]
Z_LINE = [("z", d) for d in LINE]
X_LINE = [("x", d) for d in LINE]
X_RING = [("x", 1), ("x", -1)]
Y_RING = [("y", 1), ("y", -1)]
TWIN = [("c", 1)]


def shape(*dims, kind=BF):
    return jax.ShapeDtypeStruct(dims, kind)


def unit_places(shape_, axis, x, c, share, padded):
    spot = lax.broadcasted_iota(jnp.int32, shape_, axis)
    block, inside = spot // padded, spot % padded
    return jnp.where(inside < share, (2 * block + c) * (4 * share) + x * share + inside, -1)


OWN_COLUMNS = 640


def first_weights(first, gate, up, out, inputs, lengths, latent_width, share, padded):
    rows_in, wide = gate.shape
    half_wide = wide // 2
    half_units = half_wide // (8 * share) * padded
    units = 2 * half_units
    rows, width = out.shape
    quarter = rows // 4
    lanes = (first.shape[1] - OWN_COLUMNS) // 4

    def body(
        first_ref, gate_ref, up_ref, out_ref, input_ref, length_ref,
        first_hbm, both_out, strip_out, normed_out, kv_out, lat_out, latent_out, inverse_out, latent_inverse_out,
        gain_one_out, gain_two_out, gain_latent_out, cos_ref, sin_ref, cos_group, sin_group, begin_out, slot_out,
        live_out, live_rows, first_out, both, sends, arrivals, locals_,
    ):
        net = Net(sends, arrivals, locals_)
        x, y, z, c = (lax.axis_index(a) for a in AXES)

        def columns(step):
            return pl.ds(pl.multiple_of(OWN_COLUMNS + along("x", step) * lanes, 128), lanes)

        def passing(step, h):
            return first_out.at[pl.ds(2 * h, 2), :, c, :, columns(step)]

        stacked = jnp.concatenate(
            [ref[:, h * half_wide : (h + 1) * half_wide] for ref in (gate_ref, up_ref) for h in range(2)], axis=0
        )

        def pick(core):
            places = unit_places((1, half_units), 1, x, core, share, padded)
            picks = lax.broadcasted_iota(jnp.int32, (half_wide, half_units), 0) == places
            picked = dot(stacked, picks.astype(BF)).astype(BF)
            for i in range(4):
                both[core, :, i * half_units : (i + 1) * half_units] = (
                    picked[i * rows_in : (i + 1) * rows_in]
                )

        greet(X_RING + Y_LINE + Z_LINE + TWIN)
        part = RowGather(net, first_ref.at[:, columns(0)], first_out.at[:, :, :, :, columns(0)])
        pick(0)
        part.spread()
        every = pl.ds(0, OWN_COLUMNS)
        whole = RowGather(net, first_ref.at[:, every], first_out.at[:, :, :, :, every])
        piece = out_ref.at[pl.ds(pl.multiple_of(x * quarter, quarter), quarter)]
        piece_mine = net.keep(piece, strip_out.at[z])
        pieces = [net.send(piece, strip_out.at[z], "z", d) for d in LINE]
        pick(1)
        whole.spread()

        begins = [0]
        for i in range(length_ref.shape[1]):
            begins.append(begins[-1] + length_ref[0, i])

        def begin_of(slots):
            begin = jnp.zeros_like(slots)
            for value in begins[1:]:
                begin = jnp.where(slots >= value, value, begin)
            return begin

        def angles(slots, axis):
            feature = lax.broadcasted_iota(jnp.int32, slots.shape, axis).astype(F32)
            return (slots - begin_of(slots)).astype(F32) * jnp.exp(feature * (-math.log(10000.0) / HALF))

        slots = lax.broadcasted_iota(jnp.int32, (size, HALF), 0) + ((y * 4 + z) * 2 + c) * size
        angle = angles(slots, 1)
        cos_ref[...] = jnp.cos(angle)
        sin_ref[...] = jnp.sin(angle)
        both_mine = net.keep(both.at[c], both_out.at[c])
        both_come = net.send(both.at[1 - c], both_out.at[c], "c", 1)
        part.arrive()
        right = [net.send(passing(0, h), passing(0, h), "x", 1) for h in (0, 1)]
        left = [net.send(passing(0, h), passing(0, h), "x", -1) for h in (1, 0)]
        whole.arrive()

        @pl.loop(0, 4)
        def _(seg):
            base = (seg * 4 + z) * 2 * size
            angle = angles(lax.broadcasted_iota(jnp.int32, (HALF, 2 * size), 1) + base, 0)
            cos_group[seg] = jnp.cos(angle)
            sin_group[seg] = jnp.sin(angle)
            slots = lax.broadcasted_iota(jnp.int32, (1, 4 * size), 1) % (2 * size) + base
            slot_out[seg] = slots
            begin_out[seg] = begin_of(slots)
            live_out[seg] = (slots < begins[-1]).astype(F32)
            slots = lax.broadcasted_iota(jnp.int32, (2 * size, 1), 0) + base
            live_rows[pl.ds(pl.multiple_of(seg * 2 * size, 2 * size), 2 * size), :] = (
                (slots < begins[-1]).astype(F32)
            )

        right[0].wait_recv()
        far = [net.send(passing(-1, 0), passing(-1, 0), "x", 1)]
        left[0].wait_recv()
        far.append(net.send(passing(1, 1), passing(1, 1), "x", -1))
        shared = []
        for copies, step in ((right, -1), (left, 1)):
            copies[1].wait_recv()
            spot = first_out.at[:, :, c, :, columns(step)]
            shared.append(net.send(spot, spot, "c", 1))
        for copy in far:
            copy.wait_recv()
        spot = first_out.at[:, :, c, :, columns(2)]
        shared.append(net.send(spot, spot, "c", 1))
        part.finish()
        whole.finish()
        for copy in shared + pieces + [both_come]:
            copy.wait_recv()
        keep = net.keep(first_out, first_hbm)

        gains = pl.ds(first_width, 128)
        for i in range(16):
            for k, target in enumerate((gain_one_out, gain_two_out)):
                target[:, i * 128 : (i + 1) * 128] = (
                    first_out[i // 4, i % 4, 0, k : k + 1, gains].astype(F32)
                    + first_out[i // 4, i % 4, 1, k : k + 1, gains].astype(F32)
                )
        for i in range(8):
            total = 0.0
            for k in range(4):
                total = total + first_out[i // 2, i % 2 * 2 + k // 2, k % 2, 2:3, gains].astype(F32)
            gain_latent_out[:, i * 128 : (i + 1) * 128] = total
        values = input_ref[...].astype(F32)
        inverse = lax.rsqrt(jnp.mean(values * values, axis=-1, keepdims=True) + EPSILON)
        inverse_out[...] = inverse
        normed_out[...] = (values * inverse * gain_one_out[...]).astype(BF)
        firsts = dot(normed_out[...], first_out[...].reshape(32 * rows_in, first_width + 128)[:, :first_width])
        latent = firsts[:, :latent_width]
        latent_out[...] = latent
        inverse = lax.rsqrt(jnp.mean(latent * latent, axis=-1, keepdims=True) + EPSILON)
        latent_inverse_out[...] = inverse
        lat_out[...] = (latent * inverse * gain_latent_out[...]).astype(BF)
        lower, upper = firsts[:, latent_width : latent_width + HALF], firsts[:, latent_width + HALF : latent_width + SIZE]
        kv_out[:, :HALF] = (lower * cos_ref[...] - upper * sin_ref[...]).astype(BF)
        kv_out[:, HALF:SIZE] = (upper * cos_ref[...] + lower * sin_ref[...]).astype(BF)
        kv_out[:, SIZE:] = firsts[:, latent_width + SIZE :].astype(BF)
        both_mine.wait()
        piece_mine.wait()
        keep.wait()
        net.close()

    size, deep = inputs.shape
    first_width = first.shape[1] - 128
    whole = (4, 4, 2, *first.shape)
    outs = (
        shape(*whole), shape(2, rows_in, 2 * units), shape(4, quarter, width), shape(size, deep),
        shape(size, 2 * SIZE), shape(size, latent_width), shape(size, latent_width, kind=F32),
        shape(size, 1, kind=F32), shape(size, 1, kind=F32), shape(1, deep, kind=F32), shape(1, deep, kind=F32),
        shape(1, latent_width, kind=F32), shape(size, HALF, kind=F32), shape(size, HALF, kind=F32),
        shape(4, HALF, 2 * size, kind=F32), shape(4, HALF, 2 * size, kind=F32),
        shape(4, 1, 4 * size, kind=jnp.int32), shape(4, 1, 4 * size, kind=jnp.int32), shape(4, 1, 4 * size, kind=F32),
        shape(8 * size, 1, kind=F32),
    )
    scratch = [pltpu.VMEM(whole, BF), pltpu.VMEM((2, rows_in, 2 * units), BF)]
    return comm_call(
        body, "first_weights", 1, outs, (first, gate, up, out, inputs, lengths), scratch, 64, 5,
        [IN_VMEM] * 5 + [pl.BlockSpec(memory_space=pltpu.SMEM)], [ANYWHERE] * 3 + [IN_VMEM] * 17,
    )


def gain_rows(norm_gain, ffn_gain, q_gain):
    z, c = lax.axis_index("z"), lax.axis_index("c")
    rows = norm_gain.shape[0]

    def spot(values, at):
        count = 128 // values.shape[0]
        return jnp.concatenate([values * (at == i).astype(F32) for i in range(count)])

    block = jnp.stack([spot(norm_gain, c), spot(ffn_gain, c), spot(q_gain, z % 2 * 2 + c)])
    return jnp.pad(block.astype(BF), ((0, rows - 3), (0, 0)))


def keys_and_latents(key_value, latent, up, strip):
    def body(
        kv_ref, lat_ref, up_ref, strip_ref, kv_out, lat_out, up_out, out_out, transit, sheet,
        sends, arrivals, locals_,
    ):
        net = Net(sends, arrivals, locals_)
        x, y, z, c = (lax.axis_index(a) for a in AXES)
        greet(X_LINE + Y_LINE + Z_LINE + TWIN)
        up_mine = net.keep(up_ref.at[y], transit.at[y, z])
        ups = [net.send(up_ref.at[along("y", d)], transit.at[y, z], "y", d) for d in LINE]
        row = RowGather(net, kv_ref, kv_out)
        ring = RingGather(net, lat_ref, lat_out, "y")
        strip_mine = net.keep(strip_ref, sheet.at[:, x])
        strips = [net.send(strip_ref, sheet.at[:, x], "x", d) for d in LINE]
        up_mine.wait()
        for copy in ups:
            copy.wait_recv()
        ups = [net.send(transit.at[:, z], transit.at[:, z], "z", d) for d in LINE]
        row.spread()
        ring.forward()
        ring.share()
        row.arrive()
        strip_mine.wait()
        for copy in strips:
            copy.wait_recv()
        half = sheet.shape[0] // 2
        sheet_keep = net.keep(sheet.at[pl.ds(half * c, half)], out_out.at[:, c])
        sheet_come = net.send(sheet.at[pl.ds(half * (1 - c), half)], out_out.at[:, c], "c", 1)
        for copy in ups:
            copy.wait_recv()
        up_keep = net.keep(transit.at[:, :, c], up_out.at[:, :, c])
        up_come = net.send(transit.at[:, :, 1 - c], up_out.at[:, :, c], "c", 1)
        ring.finish()
        row.finish()
        for copy in (up_keep, sheet_keep):
            copy.wait()
        for copy in (up_come, sheet_come):
            copy.wait_recv()
        net.close()

    _, _, high, thin = up.shape
    _, quarter, width = strip.shape
    outs = (
        shape(4, 4, 2, *key_value.shape), shape(4, 2, *latent.shape), shape(4, 4, 2, high, thin),
        shape(2, 2, 4, quarter, width),
    )
    scratch = [pltpu.VMEM((4, 4, 2, high, thin), BF), pltpu.VMEM((4, 4, quarter, width), BF)]
    return comm_call(
        body, "keys_and_latents", 2, outs, (key_value, latent, up, strip), scratch, 48, 6,
        [IN_VMEM] * 4, [ANYWHERE] * 4,
    )


def add_up(terms, out, rows):
    total = terms[0][rows].astype(F32)
    for term in terms[1:]:
        total = total + term[rows].astype(F32)
    out[rows] = total.astype(out.dtype)


def add_all(terms, out):
    rows_loop(out.shape[0], out.shape[1], lambda rows: add_up(terms, out, rows))


def attend(
    latent, up_heads, kv, begin, slot, live, cosine, sine, out_heads, inputs, gain, cotangent,
):
    segments, _, rows = slot.shape
    tokens = rows // 2
    size, width = inputs.shape

    def body(
        lat_ref, up_ref, kv_ref, begin_ref, slot_ref, live_ref, cos_ref, sin_ref, heads_ref, input_ref, gain_ref,
        cot_ref,
        mixed_out, qt_ref, lse_ref, middle_out, inverse_out, two_out, cot_out,
        vt, peak, total, accum, part, near, go, come, sends, arrivals, locals_,
    ):
        net = Net(sends, arrivals, locals_)
        y, z, c = (lax.axis_index(a) for a in ROW)
        greet(X_RING + Y_LINE + TWIN)
        feed = RingGather(net, cot_ref, cot_out, "x")
        turned(kv_ref, vt, segments * (segments - 1) + z + 1, VALUES)

        def segment(step):
            seg = along("y", step)
            here = pl.ds(pl.multiple_of(seg * tokens, tokens), tokens)
            cos_here, sin_here = cos_ref[seg], sin_ref[seg]
            for head in range(2):
                columns = slice(head * SIZE, (head + 1) * SIZE)
                raw = dot(lat_ref[here, :], up_ref[:, columns]).T
                lower, upper = raw[:HALF], raw[HALF:]
                turn = jnp.concatenate(
                    [lower * cos_here - upper * sin_here, upper * cos_here + lower * sin_here], axis=0
                )
                qt_ref[seg, :, head * tokens : (head + 1) * tokens] = (
                    turn.astype(BF) * (SIZE ** -0.5)
                ).astype(BF)
            peak[...] = jnp.full_like(peak, MASKED)
            total[...] = jnp.zeros_like(total)
            accum[...] = jnp.zeros_like(accum)

            def tile(at, count, masked):
                scores = dot(kv_ref[pl.ds(at, count), KEYS], qt_ref[seg])
                if masked:
                    key = lax.broadcasted_iota(jnp.int32, scores.shape, 0) + at
                    scores = jnp.where((key >= begin_ref[seg]) & (key <= slot_ref[seg]), scores, MASKED)
                before = peak[...]
                now = jnp.maximum(before, jnp.max(scores, axis=0, keepdims=True))
                weights = jnp.exp(scores - now)
                shrink = jnp.exp(before - now)
                peak[...] = now
                total[...] = total[...] * shrink + jnp.sum(weights, axis=0, keepdims=True)
                accum[...] = accum[...] * shrink + dot(vt[:, pl.ds(at, count)], weights.astype(BF))

            sweep(seg, segments, z, tile)
            lse_ref[seg] = peak[...] + jnp.log(total[...])
            result = accum[...] * (live_ref[seg] / total[...])
            for head in range(2):
                mixed_out[here, head * SIZE : (head + 1) * SIZE] = (
                    result[:, head * tokens : (head + 1) * tokens].T.astype(BF)
                )
            part[seg] = dot(mixed_out[here, :], heads_ref[...]).astype(BF).reshape(2, size, width)
            return net.send(part.at[seg, 1 - c], near.at[step], "c", 1)

        def pair(step):
            swaps[step].wait_recv()
            add_all([part.at[along("y", step), c], near.at[step]], go.at[step - 1])
            return net.send(go.at[step - 1], come.at[step - 1], "y", step)

        swaps = {2: segment(2)}
        feed.forward()
        swaps[1] = segment(1)
        ends = [pair(2)]
        feed.share()
        swaps[3] = segment(3)
        ends.append(pair(1))
        ends.append(pair(3))
        feed.finish()
        swaps[0] = segment(0)
        swaps[0].wait_recv()
        for copy in ends:
            copy.wait_recv()
        add_all(
            [input_ref, part.at[y, c], near.at[0], come.at[0], come.at[1], come.at[2]], middle_out
        )
        values = middle_out[...]
        inverse = lax.rsqrt(jnp.mean(values * values, axis=-1, keepdims=True) + EPSILON)
        inverse_out[...] = inverse
        two_out[...] = (values * inverse * gain_ref[...]).astype(BF)
        net.close()

    outs = (
        shape(segments * tokens, 2 * SIZE), shape(segments, SIZE, rows), shape(segments, 1, rows, kind=F32),
        shape(size, width, kind=F32), shape(size, 1, kind=F32), shape(size, width), shape(4, 2, size, width),
    )
    scratch = [
        pltpu.VMEM((SIZE, kv.shape[0]), BF),
        pltpu.VMEM((1, rows), F32),
        pltpu.VMEM((1, rows), F32),
        pltpu.VMEM((SIZE, rows), F32),
        pltpu.VMEM((4, 2, size, width), BF),
        pltpu.VMEM((4, size, width), BF),
        pltpu.VMEM((3, size, width), BF),
        pltpu.VMEM((3, size, width), BF),
    ]
    return comm_call(
        body, "attend", 3, outs,
        (latent, up_heads, kv, begin, slot, live, cosine, sine, out_heads, inputs, gain, cotangent),
        scratch, 20, 2, [IN_VMEM] * 12, [IN_VMEM] * 6 + [ANYWHERE],
    )


def feed_forward(normed_two, normed, grad_out, both, down, middle, inverse, gain):
    size, width = normed_two.shape
    units = down.shape[0]
    tall = width // 4
    lanes = width // 2
    high = units // 16

    def body(
        two_ref, one_ref, middle_ref, inverse_ref, gain_ref, cot_hbm, both_hbm, down_hbm,
        middle_out, grad_out_, gain_out, one_out, branch_out, gb_out, mid_out,
        two, cot, both, down, hidden, grads, part, near, go, come, gb, gd, down_come, ahead,
        sends, arrivals, locals_,
    ):
        net = Net(sends, arrivals, locals_)
        x, y, z, c = (lax.axis_index(a) for a in AXES)
        both_load = net.keep(both_hbm, both)
        down_load = net.keep(down_hbm, down)
        cot_load = net.keep(cot_hbm, cot)
        greet(X_LINE + Y_LINE + Z_LINE + TWIN)
        feed = RingGather(net, two_ref, two, "x")
        one_mine = net.keep(one_ref.at[:, pl.ds(pl.multiple_of(y * tall, tall), tall)], one_out.at[y, c])
        ones = [
            net.send(
                one_ref.at[:, pl.ds(pl.multiple_of(along("y", d) * tall, tall), tall)],
                one_out.at[y, c], "y", d,
            )
            for d in LINE
        ]

        def back(s):
            return dot_nt(cot[along("x", s)].reshape(2 * size, width), down[...])

        def block(s):
            where = along("x", s)
            at = pl.ds(pl.multiple_of(where * 2 * size, 2 * size), 2 * size)
            value = two[where].reshape(2 * size, width)
            pre = dot(value, both[...])
            grad = ahead[s - 1] if s else back(0)
            gate, up = pre[:, :units], pre[:, units:]
            sigma = 1.0 / (1.0 + jnp.exp(-gate))
            gated = gate * sigma
            hidden[at, :] = (gated * up).astype(BF)
            grads[at, :units] = (grad * up * (sigma + gated * (1.0 - sigma))).astype(BF)
            grads[at, units:] = (grad * gated).astype(BF)
            part[where] = dot_nt(grads[at, :], both[...]).astype(BF).reshape(2, size, width)
            return net.send(part.at[where, 1 - c], near.at[s], "c", 1)

        def pair(s):
            where = along("x", s)
            swaps[s].wait_recv()
            add_all([part.at[where, c], near.at[s]], go.at[s - 1])
            return net.send(go.at[s - 1], come.at[s - 1], "x", s)

        swaps = {}
        feed.arrived()
        both_load.wait()
        down_load.wait()
        cot_load.wait()
        swaps[0] = block(0)
        feed.forward()
        for s in LINE:
            ahead[s - 1] = back(s)
        feed.share()
        one_mine.wait()
        spot = one_out.at[y, c]
        shared = [net.send(spot, spot, "c", 1)]
        for d in LINE:
            ones[d - 1].wait_recv()
            spot = one_out.at[along("y", -d), c]
            shared.append(net.send(spot, spot, "c", 1))
        feed.arrived()
        swaps[1] = block(1)
        for copy in feed.far:
            copy.wait_recv()
        spot = two.at[along("x", 2), c]
        last = net.send(spot, spot, "c", 1)
        swaps[3] = block(3)
        ends = [pair(1)]
        last.wait_recv()
        swaps[2] = block(2)
        ends.append(pair(3))
        ends.append(pair(2))
        early, net.open = net.open, []

        first = []
        for k, axis in enumerate(("y", "z")):
            columns = slice(k * lanes, (k + 1) * lanes)
            gd[k] = (
                dot_tn(hidden[...], cot[...].reshape(8 * size, width)[:, columns])
                .astype(BF)
                .reshape(4, 4, high, lanes)
            )
            for d in LINE:
                at = along(axis, d)
                source = gd.at[k, at] if k == 0 else gd.at[k, :, at]
                first.append(net.send(source, down_come.at[k, d - 1], axis, d))

        gb_copies = []
        for i in range(8):
            at = pl.ds(i * 2 * size, 2 * size)
            gb[i] = dot_tn(two[...].reshape(8 * size, width)[:, i * 2 * size : (i + 1) * 2 * size], grads[...]).astype(BF)
            gb_copies.append(net.keep(gb.at[i], gb_out.at[at]))
        for copy in early:
            copy.wait_send()

        @pl.loop(0, 4)
        def _(i):
            at = pl.ds(pl.multiple_of(i * 2 * size, 2 * size), 2 * size)
            two[i] = dot(hidden[at, :], down[...]).astype(BF).reshape(2, size, width)

        branch_copy = net.keep(two, branch_out)
        swaps[0].wait_recv()
        for copy in ends:
            copy.wait_recv()
        add_all([part.at[x, c], near.at[0], come.at[0], come.at[1], come.at[2]], middle_out)
        values, scale, grad = middle_ref[...], inverse_ref[...], middle_out[...]
        gain_out[...] = jnp.sum(grad * values * scale, axis=0, keepdims=True)
        scaled = grad * gain_ref[...]
        grad = cot[x, c].astype(F32) + (
            scale * scaled
            - values * (scale * scale * scale) * jnp.mean(scaled * values, axis=-1, keepdims=True)
        )
        middle_out[...] = grad
        grad_out_[...] = grad.astype(BF)
        for copy in shared:
            copy.wait_recv()
        for copy in first:
            copy.wait_recv()
        for k in range(2):
            for i in range(4):
                own = gd.at[k, y, i] if k == 0 else gd.at[k, i, z]
                add_all([own] + [down_come.at[k, d, i] for d in range(3)], mid_out.at[k, i])
        for copy in gb_copies + [branch_copy]:
            copy.wait()
        net.close()

    outs = (
        shape(size, width, kind=F32), shape(size, width), shape(1, width, kind=F32), shape(4, 2, size, tall),
        shape(4, 2, size, width), shape(width, 2 * units),
        shape(2, 4, high, lanes),
    )
    scratch = [
        pltpu.VMEM((4, 2, size, width), BF),
        pltpu.VMEM((4, 2, size, width), BF),
        pltpu.VMEM((width, 2 * units), BF),
        pltpu.VMEM((units, width), BF),
        pltpu.VMEM((8 * size, units), BF),
        pltpu.VMEM((8 * size, 2 * units), BF),
        pltpu.VMEM((4, 2, size, width), BF),
        pltpu.VMEM((4, size, width), BF),
        pltpu.VMEM((3, size, width), BF),
        pltpu.VMEM((3, size, width), BF),
        pltpu.VMEM((8, 2 * size, 2 * units), BF),
        pltpu.VMEM((2, 4, 4, high, lanes), BF),
        pltpu.VMEM((2, 3, 4, high, lanes), BF),
        pltpu.VMEM((3, 2 * size, units), F32),
    ]
    return comm_call(
        body, "feed_forward", 4, outs, (normed_two, normed, middle, inverse, gain, grad_out, both, down), scratch,
        32, 14, [IN_VMEM] * 5 + [ANYWHERE] * 3, [IN_VMEM] * 3 + [ANYWHERE] * 3 + [IN_VMEM],
    )


Y_COLUMNS = 640


class FirstStep:
    def __init__(self, net, value, columns, axis, own, come, out):
        self.own, self.come, self.out = own, come, out
        self.copies = []
        for d in (1, 2, 3, 0):
            at = along(axis, d)
            source = value.at[at, :, :, columns] if axis == "y" else value.at[:, at, :, columns]
            if d:
                self.copies.append(net.send(source, come.at[d - 1], axis, d))
            else:
                self.mine = net.keep(source, own)

    def finish(self):
        self.mine.wait()
        for copy in self.copies:
            copy.wait_recv()
        for i in range(4):
            add_all([self.own.at[i]] + [self.come.at[d, i] for d in range(3)], self.out.at[i])


class SecondStep:
    def __init__(self, net, mid, axis, come):
        self.mid, self.axis, self.come = mid, axis, come
        self.copies = [net.send(mid.at[along(axis, d)], come.at[d - 1], axis, d) for d in LINE]

    def finish(self, out):
        for copy in self.copies:
            copy.wait_recv()
        here = lax.axis_index(self.axis)
        add_all([self.mid.at[here]] + [self.come.at[d] for d in range(3)], out)


def last_sums(
    grad_kv, grad_query, latent_group, up_heads, grad_out, grad_both, grad_down, cosine, sine, latent,
    latent_inverse, latent_gain, normed_part, inputs, inverse, gain_one, gain_two, weights, share,
):
    _, _, _, size, thin = grad_kv.shape
    group, latent_width = latent_group.shape
    per = up_heads.shape[1]
    high, lanes = up_heads.shape[0] // 32, per // 4
    _, out_rows, wide = grad_out.shape
    quarter = out_rows // 4
    tall, ahead_columns = grad_both[0].shape[1:]
    after_columns = grad_both[1].shape[2]
    both_columns = ahead_columns + after_columns
    rows = tall // 2
    half_units = both_columns // 4
    _, _, padded, down_lanes = grad_down.shape
    width = 2 * down_lanes
    half_wide = 2 * half_units // padded * 4 * share
    part = (latent_width + thin) // 2
    deep = weights.shape[0]
    tiles = deep // BLOCK

    def body(
        kv_ref, query_ref, group_ref, heads_ref, out_ref, one_ref, two_ref, down_ref, cos_ref, sin_ref, latent_ref,
        latent_inverse_ref, latent_gain_ref, normed_ref, input_ref, inverse_ref, gain_ref, gain_two_ref, weights_hbm,
        first_out, gain_out, back_out, out_out, gate_out, up_weight_out, down_out, q_up_out,
        row_near, row_go, row_first, row_mid, row_last, ring_near, ring_relay, ring_come, ring_go,
        partial, ups_here, kv_sum, part_sum, up_come_x, out_come_x, one_come, two_come, down_come, both_here,
        up_kept, out_kept, firsts,
        gathered, both_all, up_all, down_all, out_come, up_come, up_sum, up_y, weights_ref, accum, down_rows,
        first_here, pair, first_come, first_x, gain_here, gain_near, gain_come, gain_z, gain_y, gain_x,
        sends, arrivals, locals_,
    ):
        net = Net(sends, arrivals, locals_)
        x, y, z, c = (lax.axis_index(a) for a in AXES)

        def lane(at):
            return pl.ds(pl.multiple_of(at * lanes, lanes), lanes)

        def strip(at):
            return pl.ds(pl.multiple_of(at * quarter, quarter), quarter)

        load = net.keep(weights_hbm, weights_ref)
        greet(X_LINE + Y_LINE + Z_LINE + TWIN)
        row = RowSum(net, kv_ref, kv_sum, row_near, row_go, row_first, row_mid, row_last)
        outs = [net.send(out_ref.at[:, strip(along("x", d))], out_come_x.at[d - 1], "x", d) for d in LINE]
        halves = [
            SecondStep(net, mid, axis, come)
            for mid, axis, come in (
                (one_ref, "z", one_come), (two_ref, "y", two_come), (down_ref.at[0], "z", down_come.at[0]),
                (down_ref.at[1], "y", down_come.at[1]),
            )
        ]
        for i in range(4):
            at = pl.ds(i * 2 * size, 2 * size)
            partial[i] = dot_nt(query_ref[at, :], heads_ref[...]).astype(BF).reshape(2, size, latent_width)
        ring = RingSum(net, partial, part_sum, "y", ring_near, ring_relay, ring_come, ring_go)
        row.start()
        ring.relay_far()
        ring.issue()
        ups_here[...] = dot_tn(group_ref[...], query_ref[...]).astype(BF).reshape(4, 4, 2, high, per)
        ups = [
            net.send(ups_here.at[:, :, :, :, lane(along("x", d))], up_come_x.at[d - 1], "x", d) for d in LINE
        ]
        halves[0].finish(both_here.at[:, pl.ds(0, ahead_columns)])
        halves[1].finish(both_here.at[:, pl.ds(ahead_columns, after_columns)])
        own_rows = pl.ds(pl.multiple_of(c * rows, rows), rows)
        other_rows = pl.ds(pl.multiple_of((1 - c) * rows, rows), rows)
        both_mine = net.keep(both_here.at[own_rows], both_all.at[x, c])
        both_come = net.send(both_here.at[other_rows], both_all.at[x, c], "c", 1)
        row.turn()
        ring.pass_on()
        both_mine.wait()
        both_come.wait_recv()
        zero, one = both_all.at[x, 0], both_all.at[x, 1]
        right = [net.send(spot, spot, "x", 1) for spot in (zero, one)]
        left = [net.send(spot, spot, "x", -1) for spot in (one, zero)]
        accum[...] = jnp.zeros_like(accum)

        def put(px):
            for pc in range(2):
                places = unit_places((half_units, 1), 0, px, pc, share, padded)
                picks = lax.broadcasted_iota(jnp.int32, (half_units, half_wide), 1) == places
                stacked = jnp.concatenate(
                    [both_all[px, pc, :, k * half_units : (k + 1) * half_units] for k in range(4)], axis=0
                )
                accum[...] += dot(stacked, picks.astype(BF))

        put(x)

        ring.finish()
        values = latent_ref[...]
        scale = latent_inverse_ref[...]
        scaled = part_sum[...] * latent_gain_ref[...]
        gain_latent = jnp.sum(part_sum[...] * values * scale, axis=0, keepdims=True)
        back = scale * scaled - values * (scale * scale * scale) * jnp.mean(scaled * values, axis=-1, keepdims=True)
        firsts[0] = back[:, :part].astype(BF)
        firsts[1, :, : latent_width - part] = back[:, part:].astype(BF)
        row.finish()
        lower, upper = kv_sum[:, :HALF], kv_sum[:, HALF:SIZE]
        at = latent_width - part
        firsts[1, :, at : at + HALF] = (lower * cos_ref[...] + upper * sin_ref[...]).astype(BF)
        firsts[1, :, at + HALF : at + SIZE] = (upper * cos_ref[...] - lower * sin_ref[...]).astype(BF)
        firsts[1, :, at + SIZE :] = kv_sum[:, SIZE:].astype(BF)

        mine = net.keep(firsts.at[c], gathered.at[y, c])
        come = net.send(firsts.at[1 - c], gathered.at[y, c], "c", 1)
        mine.wait()
        spot = gathered.at[y, c]
        ahead = [net.send(spot, spot, "y", 1), net.send(spot, spot, "y", -1)]
        come.wait_recv()
        spot = gathered.at[y, 1 - c]
        ahead += [net.send(spot, spot, "y", 1), net.send(spot, spot, "y", -1)]

        right[0].wait_recv()
        spot = both_all.at[along("x", -1), 0]
        far = [net.send(spot, spot, "x", 1)]
        left[0].wait_recv()
        spot = both_all.at[along("x", 1), 1]
        far.append(net.send(spot, spot, "x", -1))

        for copy in ups:
            copy.wait_recv()
        for i in range(4):
            up_kept[i] = (
                (ups_here[i, :, :, :, lane(x)].astype(F32) + up_come_x[0, i].astype(F32))
                + (up_come_x[1, i].astype(F32) + up_come_x[2, i].astype(F32))
            ).astype(BF)
        ups = [net.send(up_kept.at[:, along("z", d)], up_come.at[d - 1], "z", d) for d in LINE]
        for copy in outs:
            copy.wait_recv()
        for i in range(4):
            add_all([out_ref.at[i, strip(x)]] + [out_come_x.at[d, i] for d in range(3)], out_kept.at[i])
        outs = [net.send(out_kept.at[along("z", d)], out_come.at[d - 1], "z", d) for d in LINE]

        def back_tile(i):
            at = pl.ds(pl.multiple_of(i * BLOCK, BLOCK), BLOCK)
            total = 0.0
            for core in range(2):
                columns = slice(core * part, (core + 1) * part)
                total = total + dot_nt(firsts[core], weights_ref[at, columns])
            back_out[:, at] = total

        load.wait()
        pl.loop(0, tiles // 2)(back_tile)
        ahead[0].wait_recv()
        spot = gathered.at[along("y", -1), c]
        ahead.append(net.send(spot, spot, "y", 1))
        ahead[3].wait_recv()
        spot = gathered.at[along("y", 1), 1 - c]
        ahead.append(net.send(spot, spot, "y", -1))
        pl.loop(tiles // 2, tiles)(back_tile)

        for copy in ups:
            copy.wait_recv()
        for i in range(4):
            up_sum[i] = (
                (up_kept[i, z].astype(F32) + up_come[0, i].astype(F32))
                + (up_come[1, i].astype(F32) + up_come[2, i].astype(F32))
            ).astype(BF)
        ups = [net.send(up_sum.at[along("y", d)], up_y.at[y], "y", d) for d in LINE]
        up_mine = net.keep(up_sum.at[y], up_y.at[y])

        values = input_ref[...].astype(F32)
        scale = inverse_ref[...]
        grad = back_out[...]
        gain_own = jnp.sum(grad * values * scale, axis=0, keepdims=True)
        scaled = grad * gain_ref[...]
        back_out[...] = scale * scaled - values * (scale * scale * scale) * jnp.mean(
            scaled * values, axis=-1, keepdims=True
        )
        gain_here[...] = jnp.zeros_like(gain_here)
        for i in range(16):
            gain_here[i // 4, i % 4, 0:1, :] = gain_own[:, i * 128 : (i + 1) * 128]
            gain_here[i // 4, i % 4, 1:2, :] = gain_two_ref[:, i * 128 : (i + 1) * 128]
            gain_here[i // 4, i % 4, 2:3, :] = gain_latent[:, i // 2 * 128 : (i // 2 + 1) * 128]
        near = net.send(gain_here, gain_near, "c", 1)

        for k in (2, 3):
            halves[k].finish(down_all.at[x, :, pl.ds((k - 2) * down_lanes, down_lanes)])
        spot = down_all.at[x]
        downs = [net.send(spot, spot, "x", d) for d in LINE]

        for copy in [ahead[i] for i in (1, 2, 4, 5)]:
            copy.wait_recv()
        first_here[...] = (
            dot_tn(normed_ref[...], gathered[...].reshape(8 * size, part)).astype(BF).reshape(4, 2, rows, part)
        )
        first_near = net.send(first_here.at[:, 1 - c], pair.at[c], "c", 1)
        first_mine = net.keep(first_here.at[:, c], pair.at[c])

        for copy in outs:
            copy.wait_recv()
        add_all([out_kept.at[z]] + [out_come.at[d] for d in range(3)], out_out.at[x])
        spot = out_out.at[x]
        outs = [net.send(spot, spot, "x", d) for d in LINE]
        up_mine.wait()
        for copy in ups:
            copy.wait_recv()
        up_near = net.send(up_y.at[:, 1 - c], up_all.at[x, :, c], "c", 1)
        up_mine = net.keep(up_y.at[:, c], up_all.at[x, :, c])

        first_mine.wait()
        first_near.wait_recv()
        weight_sends = [
            [net.send(pair.at[core, along("z", d)], first_come.at[d - 1, core], "z", d) for d in LINE]
            for core in range(2)
        ]
        near.wait_recv()
        gain_near[...] = gain_here[...] + gain_near[...]
        comes = [net.send(gain_near.at[:, along("z", d)], gain_come.at[d - 1], "z", d) for d in LINE]
        up_near.wait_recv()
        up_mine.wait()
        spot = up_all.at[x]
        ups = [net.send(spot, spot, "x", d) for d in LINE]

        for copy in (right[1], left[1]):
            copy.wait_recv()
        put(along("x", 1))

        def onward(core):
            for copy in weight_sends[core]:
                copy.wait_recv()
            add_all([pair.at[core, z]] + [first_come.at[d, core] for d in range(3)], first_x.at[x, core])
            spot = first_x.at[x, core]
            return [net.send(spot, spot, "x", d) for d in LINE]

        finals = [onward(0)]
        for copy in comes:
            copy.wait_recv()
        gain_z[...] = (gain_near[:, z] + gain_come[0]) + (gain_come[1] + gain_come[2])
        comes = [net.send(gain_z.at[along("y", d)], gain_y.at[d - 1], "y", d) for d in LINE]
        finals.append(onward(1))
        put(along("x", -1))
        for copy in comes:
            copy.wait_recv()
        gain_x[x] = (gain_z[y] + gain_y[0]) + (gain_y[1] + gain_y[2])
        spot = gain_x.at[x]
        comes = [net.send(spot, spot, "x", d) for d in LINE]
        for copy in far:
            copy.wait_recv()
        put(along("x", 2))
        for k, target in enumerate((gate_out, gate_out, up_weight_out, up_weight_out)):
            target[:, (k % 2) * half_wide : (k % 2 + 1) * half_wide] = accum[k * rows : (k + 1) * rows].astype(BF)
        for copy in outs + ups + downs:
            copy.wait_recv()
        for px in range(4):
            down_rows[px * share : (px + 1) * share, :] = down_all[px].astype(F32)[:share]
            for py in range(4):
                for pc in range(2):
                    at = ((2 * py + pc) * 4 + px) * lanes
                    q_up_out[:, at : at + lanes] = up_all[px, py, pc]
        down_out[...] = down_rows[...].astype(BF)
        for core in range(2):
            for copy in finals[core]:
                copy.wait_recv()
            add_all([first_x.at[i, core] for i in range(4)], first_out.at[core])
        for copy in comes:
            copy.wait_recv()
        gain_out[...] = (gain_x[0] + gain_x[1]) + (gain_x[2] + gain_x[3])
        net.close()

    outs = (
        shape(2, rows, part, kind=F32), shape(8, 128, kind=F32), shape(size, deep, kind=F32),
        shape(4, quarter, wide), shape(rows, 2 * half_wide), shape(rows, 2 * half_wide), shape(4 * share, width),
        shape(high, 32 * lanes),
    )
    scratch = row_sum_scratch(size, thin) + ring_sum_scratch(size, latent_width) + [
        pltpu.VMEM((4, 2, size, latent_width), BF),
        pltpu.VMEM((4, 4, 2, high, per), BF),
        pltpu.VMEM((size, thin), F32),
        pltpu.VMEM((size, latent_width), F32),
        pltpu.VMEM((3, 4, 4, 2, high, lanes), BF),
        pltpu.VMEM((3, 4, quarter, wide), BF),
        pltpu.VMEM((3, tall, ahead_columns), BF),
        pltpu.VMEM((3, tall, after_columns), BF),
        pltpu.VMEM((2, 3, padded, down_lanes), BF),
        pltpu.VMEM((tall, both_columns), BF),
        pltpu.VMEM((4, 4, 2, high, lanes), BF),
        pltpu.VMEM((4, quarter, wide), BF),
        pltpu.VMEM((2, size, part), BF),
        pltpu.VMEM((4, 2, size, part), BF),
        pltpu.VMEM((4, 2, rows, both_columns), BF),
        pltpu.VMEM((4, 4, 2, high, lanes), BF),
        pltpu.VMEM((4, padded, width), BF),
        pltpu.VMEM((3, quarter, wide), BF),
        pltpu.VMEM((3, 4, 2, high, lanes), BF),
        pltpu.VMEM((4, 2, high, lanes), BF),
        pltpu.VMEM((4, 2, high, lanes), BF),
        pltpu.VMEM(weights.shape, BF),
        pltpu.VMEM((4 * rows, half_wide), F32),
        pltpu.VMEM((4 * share, width), F32),
        pltpu.VMEM((4, 2, rows, part), BF),
        pltpu.VMEM((2, 4, rows, part), BF),
        pltpu.VMEM((3, 2, rows, part), BF),
        pltpu.VMEM((4, 2, rows, part), BF),
        pltpu.VMEM((4, 4, 8, 128), F32),
        pltpu.VMEM((4, 4, 8, 128), F32),
        pltpu.VMEM((3, 4, 8, 128), F32),
        pltpu.VMEM((4, 8, 128), F32),
        pltpu.VMEM((3, 8, 128), F32),
        pltpu.VMEM((4, 8, 128), F32),
    ]
    return comm_call(
        body, "last_sums", 7, outs,
        (
            grad_kv, grad_query, latent_group, up_heads, grad_out, *grad_both, grad_down, cosine, sine, latent,
            latent_inverse, latent_gain, normed_part, inputs, inverse, gain_one, gain_two, weights,
        ),
        scratch, 104, 8, [IN_VMEM] * 18 + [ANYWHERE], [IN_VMEM] * 8,
    )


def heads_back(
    grad_branch, branch, mixed, qt, kv, out_heads, begin, slot, lse, live, cosine, sine, gb,
):
    segments, _, rows = slot.shape
    tokens = rows // 2
    size, width = grad_branch.shape
    tall, wide = gb.shape[2:]
    ahead, after = Y_COLUMNS, wide - Y_COLUMNS
    half = out_heads.shape[0] // (2 * size)

    def body(
        grad_ref, branch_ref, mixed_ref, qt_ref, kv_ref, out_ref, begin_ref, slot_ref, lse_ref, live_ref, cos_ref,
        sin_ref, gb_ref,
        dq_ref, dkv_ref, stack, branch_out, one_out, two_out,
        grads, kt, sums, accum, query, grad_rows, grad_turned, delta, go_send, near, relay, come, go,
        own_one, come_one, own_two, come_two, sends, arrivals, locals_,
    ):
        net = Net(sends, arrivals, locals_)
        y, z, c = (lax.axis_index(a) for a in ROW)
        greet(X_RING + Y_LINE + Z_LINE + TWIN)
        gathering = RingGather(net, grad_ref, grads, "y")
        two = FirstStep(net, gb_ref, pl.ds(ahead, after), "z", own_two, come_two, two_out)
        ring = RingSum(net, branch_ref, branch_out, "x", near, relay, come, go)
        sums[...] = jnp.zeros_like(sums)
        turned(kv_ref, kt, segments * (segments - 1) + z + 1, KEYS)

        def segment(step):
            seg = along("y", step)
            here = pl.ds(pl.multiple_of(seg * tokens, tokens), tokens)
            grad = dot_nt(grads[seg].reshape(tokens, width), out_ref[...]).astype(BF) * live_ref[here, :].astype(BF)
            grad = jnp.concatenate([grad[:, :SIZE], grad[:, SIZE:]], axis=0)
            value = mixed_ref[here, :]
            value = jnp.concatenate([value[:, :SIZE], value[:, SIZE:]], axis=0)
            query[...] = qt_ref[seg].T
            grad_rows[...] = grad
            grad_turned[...] = grad.T
            delta[...] = jnp.sum(grad_turned[...].astype(F32) * value.T.astype(F32), axis=0, keepdims=True)
            accum[...] = jnp.zeros_like(accum)

            def tile(at, count, masked):
                keys = pl.ds(at, count)
                scores = dot(kv_ref[keys, KEYS], qt_ref[seg])
                probs = jnp.exp(scores - lse_ref[seg])
                if masked:
                    key = lax.broadcasted_iota(jnp.int32, scores.shape, 0) + at
                    probs = jnp.where((key >= begin_ref[seg]) & (key <= slot_ref[seg]), probs, 0.0)
                grad_probs = dot(kv_ref[keys, VALUES], grad_turned[...])
                grad_scores = (probs * (grad_probs - delta[...])).astype(BF)
                sums[keys, VALUES] += dot(probs.astype(BF), grad_rows[...])
                sums[keys, KEYS] += dot(grad_scores, query[...])
                accum[...] += dot(kt[:, keys], grad_scores)

            sweep(seg, segments, z, tile)
            cos_here, sin_here = cos_ref[seg], sin_ref[seg]
            for head in range(2):
                part = accum[:, head * tokens : (head + 1) * tokens] * (SIZE ** -0.5)
                lower, upper = part[:HALF], part[HALF:]
                turn = jnp.concatenate(
                    [lower * cos_here + upper * sin_here, upper * cos_here - lower * sin_here], axis=0
                )
                dq_ref[here, head * SIZE : (head + 1) * SIZE] = turn.T.astype(BF)

        gathering.arrived()
        segment(0)
        gathering.forward()
        one = FirstStep(net, gb_ref, pl.ds(0, ahead), "y", own_one, come_one, one_out)
        ring.relay_far()
        ring.issue()
        gathering.share()
        gathering.arrived()
        pl.loop(0, 2)(lambda i: segment(1 + 2 * i))
        ring.pass_on()
        gathering.finish()

        for k in range(4):
            columns = slice(k * width // 4, (k + 1) * width // 4)
            part = dot_tn(mixed_ref[...], grads[...].reshape(segments * tokens, width)[:, columns]).astype(BF)
            part = part.reshape(half, 2, size, width // 4)
            for h in range(half):

                @pl.when(c == 0)
                def _(h=h, part=part, columns=columns):
                    stack[h, :, columns] = part[h, 0]
                    go_send[h, :, columns] = part[h, 1]

                @pl.when(c == 1)
                def _(h=h, part=part, columns=columns):
                    stack[half + h, :, columns] = part[h, 1]
                    go_send[h, :, columns] = part[h, 0]

        go_come = net.send(go_send, stack.at[pl.ds(half * c, half)], "c", 1)
        segment(2)
        dkv_ref[...] = sums[...].astype(BF)
        ring.finish()
        go_come.wait_recv()
        one.finish()
        two.finish()
        net.close()

    outs = (
        shape(*mixed.shape), shape(*kv.shape), shape(2 * half, size, width), shape(size, width, kind=F32),
        shape(4, tall, ahead), shape(4, tall, after),
    )
    scratch = [
        pltpu.VMEM((4, 2, size, width), BF),
        pltpu.VMEM((SIZE, kv.shape[0]), BF),
        pltpu.VMEM(kv.shape, F32),
        pltpu.VMEM((SIZE, rows), F32),
        pltpu.VMEM((rows, SIZE), BF),
        pltpu.VMEM((rows, SIZE), BF),
        pltpu.VMEM((SIZE, rows), BF),
        pltpu.VMEM((1, rows), F32),
        pltpu.VMEM((half, size, width), BF),
    ] + ring_sum_scratch(size, width) + [
        pltpu.VMEM((4, tall, ahead), BF),
        pltpu.VMEM((3, 4, tall, ahead), BF),
        pltpu.VMEM((4, tall, after), BF),
        pltpu.VMEM((3, 4, tall, after), BF),
    ]
    return comm_call(
        body, "heads_back", 6, outs,
        (grad_branch, branch, mixed, qt, kv, out_heads, begin, slot, lse, live, cosine, sine, gb),
        scratch, 30, 3, [IN_VMEM] * 12 + [ANYWHERE], [IN_VMEM] * 6,
    )


def results(middle, branch, grad_middle, grad_norm, first, gate, up, down, out, q_up, latent_width):
    size, width = middle.shape
    rows, part = first.shape[1:]
    spare = latent_width - part
    kinds = [BF] + [F32] * 9
    shapes = [
        (size, width), (size, width), (rows, latent_width), (rows, SIZE), (rows, SIZE), gate.shape, up.shape,
        down.shape, (4 * out.shape[1], out.shape[2]), q_up.shape,
    ]
    count = len(shapes)

    def body(
        middle_ref, branch_ref, grad_ref, norm_ref, first_ref, gate_ref, up_ref, down_ref, out_ref, q_up_ref, *rest,
    ):
        targets, made, done = rest[:count], rest[count : 2 * count], rest[2 * count]
        copies = []

        def ready(i):
            copy = pltpu.make_async_copy(made[i], targets[i], done.at[i])
            copy.start()
            copies.append(copy)

        made[5][...] = gate_ref[...].astype(F32)
        ready(5)
        made[6][...] = up_ref[...].astype(F32)
        ready(6)
        made[7][...] = down_ref[...].astype(F32)
        ready(7)
        for i in range(4):
            quarter = out_ref.shape[1]
            made[8][i * quarter : (i + 1) * quarter, :] = out_ref[i].astype(F32)
        ready(8)
        made[1][...] = grad_ref[...] + norm_ref[...]
        ready(1)
        made[0][...] = (middle_ref[...] + branch_ref[...]).astype(BF)
        ready(0)
        made[9][...] = q_up_ref[...].astype(F32)
        ready(9)
        made[2][:, :part] = first_ref[0]
        made[2][:, part:] = first_ref[1, :, :spare]
        ready(2)
        made[3][...] = first_ref[1, :, spare : spare + SIZE]
        ready(3)
        made[4][...] = first_ref[1, :, spare + SIZE :]
        ready(4)
        for copy in copies:
            copy.wait()

    return pl.pallas_call(
        body,
        name="results",
        out_shape=tuple(shape(*dims, kind=kind) for dims, kind in zip(shapes, kinds)),
        in_specs=[IN_VMEM] * 10,
        out_specs=[ANYWHERE] * count,
        scratch_shapes=[pltpu.VMEM(dims, kind) for dims, kind in zip(shapes, kinds)]
        + [pltpu.SemaphoreType.DMA((count,))],
        compiler_params=pltpu.CompilerParams(vmem_limit_bytes=56 << 20),
    )(middle, branch, grad_middle, grad_norm, first, gate, up, down, out, q_up)


def gather(value, axes):
    return lax.all_gather(value, axes, axis=0, tiled=True)


def on_device(
    block_input, cotangent, lengths, norm_gain, q_down, q_gain, q_up, key_weight, value_weight,
    out_weight, ffn_gain, gate_weight, up_weight, down_weight,
):
    rows, width = block_input.shape
    latent_width = q_down.shape[1]
    n_x, n_y, n_z, n_c = (lax.axis_size(a) for a in ("x", "y", "z", "c"))
    x, y, z, c = (lax.axis_index(a) for a in ("x", "y", "z", "c"))
    span = n_y * n_z * n_c
    members = n_y * n_c

    shard = norm_gain.shape[0]
    first_width = latent_width + 2 * SIZE
    first = jnp.concatenate(
        [q_down, key_weight, value_weight, gain_rows(norm_gain, ffn_gain, q_gain)], axis=1
    )
    per_heads = q_up.shape[1] // members
    q_rows = q_up.shape[0]

    down_rows = down_weight.shape[0]
    share = down_rows // n_x
    padded = -(-share // 16) * 16
    down_part = lax.dynamic_slice_in_dim(down_weight, x * share, share)
    down_part = jnp.pad(down_part, ((0, padded - share), (0, 0)))
    (
        first_full, both, out_strip, normed, key_value, latent_normed, latent, inverse_one, inverse_latent, gain_one,
        gain_two, gain_latent, cosine, sine, cosine_group, sine_group, begin_lanes, slot_lanes, live_lanes, live_rows,
    ) = first_weights(
        first, gate_weight, up_weight, out_weight, block_input, lengths, latent_width, share, padded
    )
    units = both.shape[2] // 2
    first_full = first_full.reshape(span * shard, -1)
    both = both.reshape(n_c * shard, 2 * units)
    both_full = gather(both, ("y", "z"))
    down_use = gather(down_part, ("y", "z"))

    key_value, latent_group, up_heads, out_heads = keys_and_latents(
        key_value, latent_normed, q_up.reshape(q_rows, n_y, n_c, per_heads).transpose(1, 2, 0, 3), out_strip,
    )
    up_heads = up_heads.reshape(span * q_rows, per_heads)
    out_heads = out_heads.reshape(per_heads, width)
    key_value = key_value.reshape(span * rows, 2 * SIZE)
    group = members * rows
    latent_group = latent_group.reshape(group, latent_width)
    mixed, queries_t, lse, middle, inverse_two, normed_two, grad_feed = attend(
        latent_group, up_heads, key_value, begin_lanes, slot_lanes, live_lanes, cosine_group, sine_group, out_heads,
        block_input, gain_two, cotangent,
    )

    grad_middle, grad_branch, grad_gain_two, normed_part, branch_part, grad_both, grad_down = feed_forward(
        normed_two, normed, grad_feed, both_full, down_use, middle, inverse_two, gain_two
    )
    normed_part = normed_part.reshape(group, -1)

    grad_both = grad_both.reshape(n_y, n_z, n_c * shard, 2 * units)
    out_rows = out_weight.shape[0]
    grad_query_raw, grad_kv, grad_out, branch_two, grad_one, grad_two = heads_back(
        grad_branch, branch_part, mixed, queries_t, key_value, out_heads, begin_lanes, slot_lanes, lse,
        live_rows, cosine_group, sine_group, grad_both,
    )

    grad_first, gains, grad_input_norm, grad_out, grad_gate, grad_up, grad_down, grad_q_up = last_sums(
        grad_kv.reshape(n_y, n_z, n_c, rows, 2 * SIZE), grad_query_raw, latent_group, up_heads, grad_out,
        (grad_one, grad_two), grad_down, cosine, sine, latent, inverse_latent, gain_latent, normed_part, block_input,
        inverse_one, gain_one, grad_gain_two, first_full, share,
    )
    (
        output, input_grad, grad_q_down, grad_key, grad_value, grad_gate, grad_up, grad_down, grad_out, grad_q_up,
    ) = results(
        middle, branch_two, grad_middle, grad_input_norm, grad_first, grad_gate, grad_up, grad_down, grad_out,
        grad_q_up, latent_width,
    )
    latent_shard = q_gain.shape[0]
    return (
        output,
        input_grad,
        lax.dynamic_slice(gains[0], (c * shard,), (shard,)),
        grad_q_down,
        lax.dynamic_slice(gains[2], ((z % 2 * n_c + c) * latent_shard,), (latent_shard,)),
        grad_q_up,
        grad_key,
        grad_value,
        grad_out,
        lax.dynamic_slice(gains[1], (c * shard,), (shard,)),
        grad_gate,
        grad_up,
        grad_down,
    )


def solution(mesh):
    sizes = (4, 4, 4, 2)
    grid = Mesh(mesh.devices.reshape(sizes), ("x", "y", "z", "c"))
    tokens = P(("x", "y", "z", "c"), None)
    wide, thin = P(ROW, None), P(ROW)
    in_specs = (
        tokens, tokens, P("x", None), thin, wide, thin, wide, wide, wide, wide, thin, wide, wide,
        wide,
    )
    out_specs = (
        tokens, tokens, thin, wide, thin, wide, wide, wide, wide, thin, wide, wide, wide,
    )
    return jax.shard_map(
        on_device, mesh=grid, in_specs=in_specs, out_specs=out_specs, check_vma=False
    )
```

```python
import functools
import math

import jax
import jax.numpy as jnp
from jax import lax
from jax.experimental import pallas as pl
from jax.experimental.pallas import tpu as pltpu
from jax.sharding import Mesh
from jax.sharding import PartitionSpec as P

EPSILON = 1e-06
MASKED = -1e30
BF = jnp.bfloat16
F32 = jnp.float32
SIZE = 256
HALF = 128
BLOCK = 256
ROW = ("y", "z", "c")
HEADS = ("y", "c")
FEED = ("x", "c")


def dot(left, right):
    return jnp.dot(left, right, preferred_element_type=F32)


def dot_tn(left, right):
    return lax.dot_general(left, right, (((0,), (0,)), ((), ())), preferred_element_type=F32)


def dot_nt(left, right):
    return lax.dot_general(left, right, (((1,), (1,)), ((), ())), preferred_element_type=F32)


def turned(source, target, count, columns):
    @pl.loop(0, count)
    def _(block):
        at = pl.ds(pl.multiple_of(block * BLOCK, BLOCK), BLOCK)
        target[:, at] = source[at, columns].T


KEYS, VALUES = slice(0, SIZE), slice(SIZE, 2 * SIZE)


def sweep(segment, segments, depth, tile):
    count = segments * segment + depth
    last = (segment // (segments - 1)) * (depth // (lax.axis_size("z") - 1))
    guarded = jnp.minimum(count, 1) * (1 - last) + count * last
    free = count - guarded

    @pl.loop(0, guarded)
    def _(i):
        tile(pl.multiple_of(i * BLOCK, BLOCK), BLOCK, True)

    @pl.loop(0, free // 2)
    def _(i):
        tile(pl.multiple_of((guarded + 2 * i) * BLOCK, BLOCK), 2 * BLOCK, False)

    @pl.loop(0, free % 2)
    def _(i):
        tile(pl.multiple_of((count - 1) * BLOCK, BLOCK), BLOCK, False)

    tile(pl.multiple_of(count * BLOCK, BLOCK), BLOCK, True)


MESH_IDS = pl.DeviceIdType.MESH
AXES = ("x", "y", "z", "c")
ANYWHERE = pl.BlockSpec(memory_space=pl.ANY)
IN_VMEM = pl.BlockSpec(memory_space=pltpu.VMEM)


def place():
    return {a: lax.axis_index(a) for a in AXES}


def along(axis, step):
    size = lax.axis_size(axis)
    return lax.rem(lax.axis_index(axis) + (step + size), size)


def device(axis, step):
    here = place()
    here[axis] = along(axis, step)
    return tuple(here[a] for a in AXES)


class Net:
    def __init__(self, sends, arrivals, locals_):
        self.sends, self.arrivals, self.locals_ = sends, arrivals, locals_
        self.used = 0
        self.near = 0
        self.open = []

    def send(self, source, target, axis, step):
        copy = pltpu.make_async_remote_copy(
            src_ref=source, dst_ref=target, send_sem=self.sends.at[self.used],
            recv_sem=self.arrivals.at[self.used], device_id=device(axis, step),
            device_id_type=MESH_IDS,
        )
        copy.start()
        self.used += 1
        self.open.append(copy)
        return copy

    def keep(self, source, target):
        copy = pltpu.make_async_copy(source, target, self.locals_.at[self.near])
        copy.start()
        self.near += 1
        return copy

    def close(self):
        for copy in self.open:
            copy.wait_send()


def greet(partners):
    barrier = pltpu.get_barrier_semaphore()
    for axis, step in partners:
        pl.semaphore_signal(barrier, 1, device_id=device(axis, step), device_id_type=MESH_IDS)
    pl.semaphore_wait(barrier, len(partners))


def semaphores(sends, locals_):
    return [
        pltpu.SemaphoreType.DMA((sends,)),
        pltpu.SemaphoreType.DMA((sends,)),
        pltpu.SemaphoreType.DMA((max(locals_, 1),)),
    ]


def comm_call(body, name, number, outs, ins, scratch, sends, locals_, spaces, out_spaces):
    return pl.pallas_call(
        body,
        name=name,
        out_shape=outs,
        in_specs=spaces,
        out_specs=out_spaces,
        scratch_shapes=list(scratch) + semaphores(sends, locals_),
        compiler_params=pltpu.CompilerParams(
            collective_id=number, has_side_effects=True, vmem_limit_bytes=60 << 20
        ),
    )(*ins)


LINE = (1, 2, 3)


class RowGather:
    def __init__(self, net, value, out):
        self.net, self.out = net, out
        h = value.shape[0] // 2
        self.parts = (pl.ds(0, h), pl.ds(h, h))
        y, z, c = (lax.axis_index(a) for a in ROW)
        self.mine = net.keep(value, out.at[y, z, c])
        self.own = net.send(value, out.at[y, z, c], "c", 1)
        self.first = [
            [net.send(value.at[part], out.at[y, z, c, part], axis, d) for d in LINE]
            for part, axis in zip(self.parts, ("z", "y"))
        ]

    def spread(self):
        net, out = self.net, self.out
        y, z, c = (lax.axis_index(a) for a in ROW)
        self.mine.wait()
        (a, b) = self.parts
        for copy in self.first[0]:
            copy.wait_recv()
        self.second = [
            [net.send(out.at[y, :, c, a], out.at[y, :, c, a], "y", d) for d in LINE]
        ]
        for copy in self.first[1]:
            copy.wait_recv()
        self.second.append(
            [net.send(out.at[:, z, c, b], out.at[:, z, c, b], "z", d) for d in LINE]
        )
        self.shared = [self.own]
        for d in LINE:
            spot = out.at[y, along("z", -d), c, a]
            self.shared.append(net.send(spot, spot, "c", 1))
            spot = out.at[along("y", -d), z, c, b]
            self.shared.append(net.send(spot, spot, "c", 1))

    def arrive(self):
        net, out = self.net, self.out
        y, z, c = (lax.axis_index(a) for a in ROW)
        (a, b) = self.parts
        for d in LINE:
            self.second[0][d - 1].wait_recv()
            spot = out.at[along("y", -d), :, c, a]
            self.shared.append(net.send(spot, spot, "c", 1))
            self.second[1][d - 1].wait_recv()
            spot = out.at[:, along("z", -d), c, b]
            self.shared.append(net.send(spot, spot, "c", 1))

    def finish(self):
        for copy in self.shared:
            copy.wait_recv()


class RingGather:
    def __init__(self, net, value, out, axis):
        self.net, self.out, self.axis = net, out, axis
        a, c = lax.axis_index(axis), lax.axis_index("c")
        h = value.shape[0] // 2
        self.parts = one, two = pl.ds(0, h), pl.ds(h, h)
        self.mine = net.keep(value, out.at[a, c])
        self.right = [net.send(value.at[p], out.at[a, c, p], axis, 1) for p in (one, two)]
        self.left = [net.send(value.at[p], out.at[a, c, p], axis, -1) for p in (two, one)]
        self.shared = [net.send(value, out.at[a, c], "c", 1)]

    def forward(self):
        net, out, axis = self.net, self.out, self.axis
        c = lax.axis_index("c")
        one, two = self.parts
        before, after = along(axis, -1), along(axis, 1)
        self.right[0].wait_recv()
        spot = out.at[before, c, one]
        self.far = [net.send(spot, spot, axis, 1)]
        self.left[0].wait_recv()
        spot = out.at[after, c, two]
        self.far.append(net.send(spot, spot, axis, -1))

    def share(self):
        c = lax.axis_index("c")
        for copies, step in ((self.right, -1), (self.left, 1)):
            copies[1].wait_recv()
            spot = self.out.at[along(self.axis, step), c]
            self.shared.append(self.net.send(spot, spot, "c", 1))

    def finish(self):
        for copy in self.far:
            copy.wait_recv()
        spot = self.out.at[along(self.axis, 2), lax.axis_index("c")]
        self.shared.append(self.net.send(spot, spot, "c", 1))
        self.arrived()

    def arrived(self):
        if self.mine is not None:
            self.mine.wait()
            self.mine = None
        for copy in self.shared:
            copy.wait_recv()
        self.shared = []


STEP = 16
CHUNK = 32 * 1024


def rows_loop(count, width, body):
    step = STEP
    while 2 * step * width <= CHUNK and count % (2 * step) == 0:
        step *= 2
    pl.loop(0, count // step)(lambda i: body(pl.ds(pl.multiple_of(i * step, STEP), step)))


def shifted(rows, first):
    return pl.ds(pl.multiple_of(rows.start + first, STEP), rows.size)


class RingSum:
    def __init__(self, net, value, out, axis, near, relay, come, go):
        self.net, self.value, self.out, self.axis = net, value, out, axis
        self.near, self.relay, self.come, self.go = near, relay, come, go
        c = lax.axis_index("c")
        self.size = value.shape[2]
        h = self.size // 2
        self.parts = pl.ds(0, h), pl.ds(h, h)
        self.swaps = {
            s: net.send(value.at[along(axis, s), 1 - c], near.at[s], "c", 1) for s in (2, 1, 3, 0)
        }

    def pair(self, s, part=None):
        value, near, go = self.value, self.near, self.go
        where, c = along(self.axis, s), lax.axis_index("c")
        first = 0 if part is None else part.start
        count = self.size if part is None else part.size

        def add(rows):
            at = shifted(rows, first)
            go[s, at] = (
                value[where, c, at].astype(F32) + near[s, at].astype(F32)
            ).astype(BF)

        rows_loop(count, value.shape[3], add)

    def relay_far(self):
        net = self.net
        one, two = self.parts
        self.swaps[2].wait_recv()
        self.pair(2)
        self.relays = [
            net.send(self.go.at[2, one], self.relay.at[0], self.axis, 1),
            net.send(self.go.at[2, two], self.relay.at[1], self.axis, -1),
        ]

    def issue(self):
        net, go, come = self.net, self.go, self.come
        one, two = self.parts
        self.swaps[1].wait_recv()
        self.pair(1)
        self.ends = [net.send(go.at[1, two], come.at[0, two], self.axis, 1)]
        self.swaps[3].wait_recv()
        self.pair(3)
        self.ends.append(net.send(go.at[3, one], come.at[1, one], self.axis, -1))

    def pass_on(self):
        net, go, relay, come = self.net, self.go, self.relay, self.come
        one, two = self.parts
        for i, (s, part, step) in enumerate(((1, one, 1), (3, two, -1))):
            self.relays[i].wait_recv()

            def add(rows, i=i, s=s, part=part):
                at = shifted(rows, part.start)
                go[s, at] = (go[s, at].astype(F32) + relay[i, rows].astype(F32)).astype(BF)

            rows_loop(part.size, go.shape[2], add)
            self.ends.append(net.send(go.at[s, part], come.at[i, part], self.axis, step))

    def finish(self):
        value, near, come, out = self.value, self.near, self.come, self.out
        where, c = lax.axis_index(self.axis), lax.axis_index("c")
        self.swaps[0].wait_recv()
        for copy in self.ends:
            copy.wait_recv()

        def add(rows):
            out[rows] = (
                value[where, c, rows].astype(F32) + near[0, rows].astype(F32)
            ) + (come[0, rows].astype(F32) + come[1, rows].astype(F32))

        rows_loop(self.size, out.shape[1], add)


def ring_sum_scratch(size, width):
    return [
        pltpu.VMEM((4, size, width), BF),
        pltpu.VMEM((2, size // 2, width), BF),
        pltpu.VMEM((2, size, width), BF),
        pltpu.VMEM((4, size, width), BF),
    ]


class RowSum:
    def __init__(self, net, value, out, near, go, first, mid, last):
        self.net, self.value, self.out = net, value, out
        self.near, self.go, self.first, self.mid, self.last = near, go, first, mid, last
        c = lax.axis_index("c")
        self.size = value.shape[3]
        h = self.size // 2
        self.parts = pl.ds(0, h), pl.ds(h, h)
        self.swaps = [
            net.send(value.at[i, :, 1 - c], near.at[i], "c", 1) for i in range(4)
        ]

    def start(self):
        net, value, near, go = self.net, self.value, self.near, self.go
        c = lax.axis_index("c")
        for i in range(4):
            self.swaps[i].wait_recv()
            for j in range(4):

                def add(rows, i=i, j=j):
                    go[i, j, rows] = (
                        value[i, j, c, rows].astype(F32) + near[i, j, rows].astype(F32)
                    ).astype(BF)

                rows_loop(self.size, value.shape[4], add)
        a, b = self.parts
        self.ones = [
            [net.send(go.at[along("y", d), :, a], self.first.at[0, d - 1], "y", d) for d in LINE],
            [net.send(go.at[:, along("z", d), b], self.first.at[1, d - 1], "z", d) for d in LINE],
        ]

    def turn(self):
        net, go, first, mid = self.net, self.go, self.first, self.mid
        y, z = lax.axis_index("y"), lax.axis_index("z")
        self.twos = []
        for k, axis in enumerate(("z", "y")):
            for copy in self.ones[k]:
                copy.wait_recv()
            for j in range(4):

                def add(rows, k=k, j=j):
                    at = shifted(rows, self.parts[k].start)
                    own = go[y, j, at] if k == 0 else go[j, z, at]
                    mid[k, j, rows] = (
                        own.astype(F32) + first[k, 0, j, rows].astype(F32)
                        + (first[k, 1, j, rows].astype(F32) + first[k, 2, j, rows].astype(F32))
                    ).astype(BF)

                rows_loop(self.parts[k].size, mid.shape[3], add)
            self.twos.append(
                [net.send(mid.at[k, along(axis, d)], self.last.at[k, d - 1], axis, d) for d in LINE]
            )

    def finish(self):
        mid, last, out = self.mid, self.last, self.out
        for k, axis in enumerate(("z", "y")):
            for copy in self.twos[k]:
                copy.wait_recv()
            here = lax.axis_index(axis)

            def add(rows, k=k, here=here):
                at = shifted(rows, self.parts[k].start)
                out[at] = (
                    mid[k, here, rows].astype(F32) + last[k, 0, rows].astype(F32)
                    + (last[k, 1, rows].astype(F32) + last[k, 2, rows].astype(F32))
                )

            rows_loop(self.parts[k].size, out.shape[1], add)


def row_sum_scratch(size, width):
    h = size // 2
    return [
        pltpu.VMEM((4, 4, size, width), BF),
        pltpu.VMEM((4, 4, size, width), BF),
        pltpu.VMEM((2, 3, 4, h, width), BF),
        pltpu.VMEM((2, 4, h, width), BF),
        pltpu.VMEM((2, 3, h, width), BF),
    ]


Y_LINE = [("y", d) for d in LINE]
Z_LINE = [("z", d) for d in LINE]
X_LINE = [("x", d) for d in LINE]
X_RING = [("x", 1), ("x", -1)]
Y_RING = [("y", 1), ("y", -1)]
TWIN = [("c", 1)]


def shape(*dims, kind=BF):
    return jax.ShapeDtypeStruct(dims, kind)


def unit_places(shape_, axis, x, c, share, padded):
    spot = lax.broadcasted_iota(jnp.int32, shape_, axis)
    block, inside = spot // padded, spot % padded
    return jnp.where(inside < share, (2 * block + c) * (4 * share) + x * share + inside, -1)


OWN_COLUMNS = 640


def first_weights(weights, gate, up, out, inputs, lengths, share, padded):
    rows_in, wide = gate.shape
    half_wide = wide // 2
    half_units = half_wide // (8 * share) * padded
    units = 2 * half_units
    rows, width = out.shape
    quarter = rows // 4
    first_width = sum(w.shape[1] for w in weights) - 128
    latent_width = weights[0].shape[1]
    lanes = (first_width + 128 - OWN_COLUMNS) // 4
    pieces_in = len(weights)

    def body(*refs):
        kernel(refs[:pieces_in], *refs[pieces_in:])

    def kernel(
        weight_refs, gate_ref, up_ref, out_ref, input_ref, length_ref,
        first_hbm, both_out, strip_out, normed_out, kv_out, lat_out, latent_out, inverse_out, latent_inverse_out,
        gain_one_out, gain_two_out, gain_latent_out, cos_ref, sin_ref, cos_group, sin_group, begin_out, slot_out,
        live_out, live_rows, first_ref, first_out, both, sends, arrivals, locals_,
    ):
        net = Net(sends, arrivals, locals_)
        x, y, z, c = (lax.axis_index(a) for a in AXES)

        at = 0
        for ref in weight_refs:
            first_ref[:, at : at + ref.shape[1]] = ref[...]
            at += ref.shape[1]

        def columns(step):
            return pl.ds(pl.multiple_of(OWN_COLUMNS + along("x", step) * lanes, 128), lanes)

        def passing(step, h):
            return first_out.at[pl.ds(2 * h, 2), :, c, :, columns(step)]

        stacked = jnp.concatenate(
            [ref[:, h * half_wide : (h + 1) * half_wide] for ref in (gate_ref, up_ref) for h in range(2)], axis=0
        )

        def pick(core):
            places = unit_places((1, half_units), 1, x, core, share, padded)
            picks = lax.broadcasted_iota(jnp.int32, (half_wide, half_units), 0) == places
            picked = dot(stacked, picks.astype(BF)).astype(BF)
            for i in range(4):
                both[core, :, i * half_units : (i + 1) * half_units] = (
                    picked[i * rows_in : (i + 1) * rows_in]
                )

        greet(X_RING + Y_LINE + Z_LINE + TWIN)
        part = RowGather(net, first_ref.at[:, columns(0)], first_out.at[:, :, :, :, columns(0)])
        pick(0)
        part.spread()
        every = pl.ds(0, OWN_COLUMNS)
        whole = RowGather(net, first_ref.at[:, every], first_out.at[:, :, :, :, every])
        piece = out_ref.at[pl.ds(pl.multiple_of(x * quarter, quarter), quarter)]
        piece_mine = net.keep(piece, strip_out.at[z])
        pieces = [net.send(piece, strip_out.at[z], "z", d) for d in LINE]
        pick(1)
        whole.spread()

        begins = [0]
        for i in range(length_ref.shape[1]):
            begins.append(begins[-1] + length_ref[0, i])

        def begin_of(slots):
            begin = jnp.zeros_like(slots)
            for value in begins[1:]:
                begin = jnp.where(slots >= value, value, begin)
            return begin

        def angles(slots, axis):
            feature = lax.broadcasted_iota(jnp.int32, slots.shape, axis).astype(F32)
            return (slots - begin_of(slots)).astype(F32) * jnp.exp(feature * (-math.log(10000.0) / HALF))

        slots = lax.broadcasted_iota(jnp.int32, (size, HALF), 0) + ((y * 4 + z) * 2 + c) * size
        angle = angles(slots, 1)
        cos_ref[...] = jnp.cos(angle)
        sin_ref[...] = jnp.sin(angle)
        both_mine = net.keep(both.at[c], both_out.at[c])
        both_come = net.send(both.at[1 - c], both_out.at[c], "c", 1)
        part.arrive()
        right = [net.send(passing(0, h), passing(0, h), "x", 1) for h in (0, 1)]
        left = [net.send(passing(0, h), passing(0, h), "x", -1) for h in (1, 0)]
        whole.arrive()

        @pl.loop(0, 4)
        def _(seg):
            base = (seg * 4 + z) * 2 * size
            angle = angles(lax.broadcasted_iota(jnp.int32, (HALF, 2 * size), 1) + base, 0)
            cos_group[seg] = jnp.cos(angle)
            sin_group[seg] = jnp.sin(angle)
            slots = lax.broadcasted_iota(jnp.int32, (1, 4 * size), 1) % (2 * size) + base
            slot_out[seg] = slots
            begin_out[seg] = begin_of(slots)
            live_out[seg] = (slots < begins[-1]).astype(F32)
            slots = lax.broadcasted_iota(jnp.int32, (2 * size, 1), 0) + base
            live_rows[pl.ds(pl.multiple_of(seg * 2 * size, 2 * size), 2 * size), :] = (
                (slots < begins[-1]).astype(F32)
            )

        right[0].wait_recv()
        far = [net.send(passing(-1, 0), passing(-1, 0), "x", 1)]
        left[0].wait_recv()
        far.append(net.send(passing(1, 1), passing(1, 1), "x", -1))
        shared = []
        for copies, step in ((right, -1), (left, 1)):
            copies[1].wait_recv()
            spot = first_out.at[:, :, c, :, columns(step)]
            shared.append(net.send(spot, spot, "c", 1))
        for copy in far:
            copy.wait_recv()
        spot = first_out.at[:, :, c, :, columns(2)]
        shared.append(net.send(spot, spot, "c", 1))
        part.finish()
        whole.finish()
        for copy in shared + pieces + [both_come]:
            copy.wait_recv()
        keep = net.keep(first_out, first_hbm)

        gains = pl.ds(first_width, 128)
        for i in range(16):
            for k, target in enumerate((gain_one_out, gain_two_out)):
                target[:, i * 128 : (i + 1) * 128] = (
                    first_out[i // 4, i % 4, 0, k : k + 1, gains].astype(F32)
                    + first_out[i // 4, i % 4, 1, k : k + 1, gains].astype(F32)
                )
        for i in range(8):
            total = 0.0
            for k in range(4):
                total = total + first_out[i // 2, i % 2 * 2 + k // 2, k % 2, 2:3, gains].astype(F32)
            gain_latent_out[:, i * 128 : (i + 1) * 128] = total
        values = input_ref[...].astype(F32)
        inverse = lax.rsqrt(jnp.mean(values * values, axis=-1, keepdims=True) + EPSILON)
        inverse_out[...] = inverse
        normed_out[...] = (values * inverse * gain_one_out[...]).astype(BF)
        firsts = dot(normed_out[...], first_out[...].reshape(32 * rows_in, first_width + 128)[:, :first_width])
        latent = firsts[:, :latent_width]
        latent_out[...] = latent
        inverse = lax.rsqrt(jnp.mean(latent * latent, axis=-1, keepdims=True) + EPSILON)
        latent_inverse_out[...] = inverse
        lat_out[...] = (latent * inverse * gain_latent_out[...]).astype(BF)
        lower, upper = firsts[:, latent_width : latent_width + HALF], firsts[:, latent_width + HALF : latent_width + SIZE]
        kv_out[:, :HALF] = (lower * cos_ref[...] - upper * sin_ref[...]).astype(BF)
        kv_out[:, HALF:SIZE] = (upper * cos_ref[...] + lower * sin_ref[...]).astype(BF)
        kv_out[:, SIZE:] = firsts[:, latent_width + SIZE :].astype(BF)
        both_mine.wait()
        piece_mine.wait()
        keep.wait()
        net.close()

    size, deep = inputs.shape
    whole = (4, 4, 2, rows_in, first_width + 128)
    outs = (
        shape(*whole), shape(2, rows_in, 2 * units), shape(4, quarter, width), shape(size, deep),
        shape(size, 2 * SIZE), shape(size, latent_width), shape(size, latent_width, kind=F32),
        shape(size, 1, kind=F32), shape(size, 1, kind=F32), shape(1, deep, kind=F32), shape(1, deep, kind=F32),
        shape(1, latent_width, kind=F32), shape(size, HALF, kind=F32), shape(size, HALF, kind=F32),
        shape(4, HALF, 2 * size, kind=F32), shape(4, HALF, 2 * size, kind=F32),
        shape(4, 1, 4 * size, kind=jnp.int32), shape(4, 1, 4 * size, kind=jnp.int32), shape(4, 1, 4 * size, kind=F32),
        shape(8 * size, 1, kind=F32),
    )
    scratch = [
        pltpu.VMEM((rows_in, first_width + 128), BF), pltpu.VMEM(whole, BF), pltpu.VMEM((2, rows_in, 2 * units), BF),
    ]
    return comm_call(
        body, "first_weights", 1, outs, (*weights, gate, up, out, inputs, lengths), scratch, 64, 5,
        [IN_VMEM] * (pieces_in + 4) + [pl.BlockSpec(memory_space=pltpu.SMEM)], [ANYWHERE] * 3 + [IN_VMEM] * 17,
    )


def gain_rows(norm_gain, ffn_gain, q_gain):
    z, c = lax.axis_index("z"), lax.axis_index("c")
    rows = norm_gain.shape[0]

    def spot(values, at):
        count = 128 // values.shape[0]
        return jnp.concatenate([values * (at == i).astype(F32) for i in range(count)])

    block = jnp.stack([spot(norm_gain, c), spot(ffn_gain, c), spot(q_gain, z % 2 * 2 + c)])
    return jnp.pad(block.astype(BF), ((0, rows - 3), (0, 0)))


def keys_and_latents(key_value, latent, up, strip):
    def body(
        kv_ref, lat_ref, up_ref, strip_ref, kv_out, lat_out, up_out, out_out, transit, sheet,
        sends, arrivals, locals_,
    ):
        net = Net(sends, arrivals, locals_)
        x, y, z, c = (lax.axis_index(a) for a in AXES)
        greet(X_LINE + Y_LINE + Z_LINE + TWIN)
        up_mine = net.keep(up_ref.at[y], transit.at[y, z])
        ups = [net.send(up_ref.at[along("y", d)], transit.at[y, z], "y", d) for d in LINE]
        row = RowGather(net, kv_ref, kv_out)
        ring = RingGather(net, lat_ref, lat_out, "y")
        half = strip_ref.shape[0] // 2
        strip_mine = net.keep(strip_ref.at[pl.ds(half * c, half)], sheet.at[:, c])
        strip_come = net.send(strip_ref.at[pl.ds(half * (1 - c), half)], sheet.at[:, c], "c", 1)
        up_mine.wait()
        for copy in ups:
            copy.wait_recv()
        ups = [net.send(transit.at[:, z], transit.at[:, z], "z", d) for d in LINE]
        strip_mine.wait()
        strip_come.wait_recv()
        sheet_keep = net.keep(sheet, out_out.at[:, :, x])
        right = [net.send(sheet.at[h], out_out.at[h, :, x], "x", 1) for h in (0, 1)]
        left = [net.send(sheet.at[h], out_out.at[h, :, x], "x", -1) for h in (1, 0)]
        row.spread()
        ring.forward()
        right[0].wait_recv()
        spot = out_out.at[0, :, along("x", -1)]
        far = [net.send(spot, spot, "x", 1)]
        left[0].wait_recv()
        spot = out_out.at[1, :, along("x", 1)]
        far.append(net.send(spot, spot, "x", -1))
        ring.share()
        row.arrive()
        for copy in ups:
            copy.wait_recv()
        up_keep = net.keep(transit.at[:, :, c], up_out.at[:, :, c])
        up_come = net.send(transit.at[:, :, 1 - c], up_out.at[:, :, c], "c", 1)
        ring.finish()
        row.finish()
        for copy in (up_keep, sheet_keep):
            copy.wait()
        for copy in [up_come, right[1], left[1]] + far:
            copy.wait_recv()
        net.close()

    _, _, high, thin = up.shape
    _, quarter, width = strip.shape
    outs = (
        shape(4, 4, 2, *key_value.shape), shape(4, 2, *latent.shape), shape(4, 4, 2, high, thin),
        shape(2, 2, 4, quarter, width),
    )
    scratch = [pltpu.VMEM((4, 4, 2, high, thin), BF), pltpu.VMEM((2, 2, quarter, width), BF)]
    return comm_call(
        body, "keys_and_latents", 2, outs, (key_value, latent, up, strip), scratch, 52, 6,
        [IN_VMEM] * 4, [ANYWHERE] * 4,
    )


def add_up(terms, out, rows):
    total = terms[0][rows].astype(F32)
    for term in terms[1:]:
        total = total + term[rows].astype(F32)
    out[rows] = total.astype(out.dtype)


def add_all(terms, out):
    rows_loop(out.shape[0], out.shape[1], lambda rows: add_up(terms, out, rows))


def attend(
    latent, up_heads, kv, begin, slot, live, cosine, sine, out_heads, inputs, gain, cotangent,
):
    segments, _, rows = slot.shape
    tokens = rows // 2
    size, width = inputs.shape

    def body(
        lat_ref, up_ref, kv_ref, begin_ref, slot_ref, live_ref, cos_ref, sin_ref, heads_ref, input_ref, gain_ref,
        cot_ref,
        mixed_out, qt_ref, lse_ref, middle_out, inverse_out, two_out, cot_out,
        vt, peak, total, accum, part, near, go, come, sends, arrivals, locals_,
    ):
        net = Net(sends, arrivals, locals_)
        y, z, c = (lax.axis_index(a) for a in ROW)
        greet(X_RING + Y_LINE + TWIN)
        feed = RingGather(net, cot_ref, cot_out, "x")
        turned(kv_ref, vt, segments * (segments - 1) + z + 1, VALUES)

        def segment(step):
            seg = along("y", step)
            here = pl.ds(pl.multiple_of(seg * tokens, tokens), tokens)
            cos_here, sin_here = cos_ref[seg], sin_ref[seg]
            for head in range(2):
                columns = slice(head * SIZE, (head + 1) * SIZE)
                raw = dot(lat_ref[here, :], up_ref[:, columns]).T
                lower, upper = raw[:HALF], raw[HALF:]
                turn = jnp.concatenate(
                    [lower * cos_here - upper * sin_here, upper * cos_here + lower * sin_here], axis=0
                )
                qt_ref[seg, :, head * tokens : (head + 1) * tokens] = (
                    turn.astype(BF) * (SIZE ** -0.5)
                ).astype(BF)
            peak[...] = jnp.full_like(peak, MASKED)
            total[...] = jnp.zeros_like(total)
            accum[...] = jnp.zeros_like(accum)

            def tile(at, count, masked):
                scores = dot(kv_ref[pl.ds(at, count), KEYS], qt_ref[seg])
                if masked:
                    key = lax.broadcasted_iota(jnp.int32, scores.shape, 0) + at
                    scores = jnp.where((key >= begin_ref[seg]) & (key <= slot_ref[seg]), scores, MASKED)
                before = peak[...]
                now = jnp.maximum(before, jnp.max(scores, axis=0, keepdims=True))
                weights = jnp.exp(scores - now)
                shrink = jnp.exp(before - now)
                peak[...] = now
                total[...] = total[...] * shrink + jnp.sum(weights, axis=0, keepdims=True)
                accum[...] = accum[...] * shrink + dot(vt[:, pl.ds(at, count)], weights.astype(BF))

            sweep(seg, segments, z, tile)
            lse_ref[seg] = peak[...] + jnp.log(total[...])
            result = accum[...] * (live_ref[seg] / total[...])
            for head in range(2):
                mixed_out[here, head * SIZE : (head + 1) * SIZE] = (
                    result[:, head * tokens : (head + 1) * tokens].T.astype(BF)
                )
            part[seg] = dot(mixed_out[here, :], heads_ref[...]).astype(BF).reshape(2, size, width)
            return net.send(part.at[seg, 1 - c], near.at[step], "c", 1)

        def pair(step):
            swaps[step].wait_recv()
            add_all([part.at[along("y", step), c], near.at[step]], go.at[step - 1])
            return net.send(go.at[step - 1], come.at[step - 1], "y", step)

        swaps = {2: segment(2)}
        feed.forward()
        swaps[1] = segment(1)
        ends = [pair(2)]
        feed.share()
        swaps[3] = segment(3)
        ends.append(pair(1))
        ends.append(pair(3))
        feed.finish()
        swaps[0] = segment(0)
        swaps[0].wait_recv()
        for copy in ends:
            copy.wait_recv()
        add_all(
            [input_ref, part.at[y, c], near.at[0], come.at[0], come.at[1], come.at[2]], middle_out
        )
        values = middle_out[...]
        inverse = lax.rsqrt(jnp.mean(values * values, axis=-1, keepdims=True) + EPSILON)
        inverse_out[...] = inverse
        two_out[...] = (values * inverse * gain_ref[...]).astype(BF)
        net.close()

    outs = (
        shape(segments * tokens, 2 * SIZE), shape(segments, SIZE, rows), shape(segments, 1, rows, kind=F32),
        shape(size, width, kind=F32), shape(size, 1, kind=F32), shape(size, width), shape(4, 2, size, width),
    )
    scratch = [
        pltpu.VMEM((SIZE, kv.shape[0]), BF),
        pltpu.VMEM((1, rows), F32),
        pltpu.VMEM((1, rows), F32),
        pltpu.VMEM((SIZE, rows), F32),
        pltpu.VMEM((4, 2, size, width), BF),
        pltpu.VMEM((4, size, width), BF),
        pltpu.VMEM((3, size, width), BF),
        pltpu.VMEM((3, size, width), BF),
    ]
    return comm_call(
        body, "attend", 3, outs,
        (latent, up_heads, kv, begin, slot, live, cosine, sine, out_heads, inputs, gain, cotangent),
        scratch, 20, 2, [IN_VMEM] * 12, [IN_VMEM] * 6 + [ANYWHERE],
    )


def feed_forward(normed_two, normed, grad_out, both, down, middle, inverse, gain):
    size, width = normed_two.shape
    units = down.shape[0]
    tall = width // 4
    lanes = width // 2
    high = units // 16

    def body(
        two_ref, one_ref, middle_ref, inverse_ref, gain_ref, cot_hbm, both_hbm, down_hbm,
        middle_out, grad_out_, gain_out, one_out, branch_out, gb_out, mid_out,
        two, cot, both, down, hidden, grads, part, near, go, come, gb, gd, down_come, ahead,
        sends, arrivals, locals_,
    ):
        net = Net(sends, arrivals, locals_)
        x, y, z, c = (lax.axis_index(a) for a in AXES)
        both_load = net.keep(both_hbm, both)
        down_load = net.keep(down_hbm, down)
        cot_load = net.keep(cot_hbm, cot)
        greet(X_LINE + Y_LINE + Z_LINE + TWIN)
        feed = RingGather(net, two_ref, two, "x")
        one_mine = net.keep(one_ref.at[:, pl.ds(pl.multiple_of(y * tall, tall), tall)], one_out.at[y, c])
        ones = [
            net.send(
                one_ref.at[:, pl.ds(pl.multiple_of(along("y", d) * tall, tall), tall)],
                one_out.at[y, c], "y", d,
            )
            for d in LINE
        ]

        def back(s):
            return dot_nt(cot[along("x", s)].reshape(2 * size, width), down[...])

        def block(s):
            where = along("x", s)
            at = pl.ds(pl.multiple_of(where * 2 * size, 2 * size), 2 * size)
            value = two[where].reshape(2 * size, width)
            pre = dot(value, both[...])
            grad = ahead[s - 1] if s else back(0)
            gate, up = pre[:, :units], pre[:, units:]
            sigma = 1.0 / (1.0 + jnp.exp(-gate))
            gated = gate * sigma
            hidden[at, :] = (gated * up).astype(BF)
            grads[at, :units] = (grad * up * (sigma + gated * (1.0 - sigma))).astype(BF)
            grads[at, units:] = (grad * gated).astype(BF)
            part[where] = dot_nt(grads[at, :], both[...]).astype(BF).reshape(2, size, width)
            return net.send(part.at[where, 1 - c], near.at[s], "c", 1)

        def pair(s):
            where = along("x", s)
            swaps[s].wait_recv()
            add_all([part.at[where, c], near.at[s]], go.at[s - 1])
            return net.send(go.at[s - 1], come.at[s - 1], "x", s)

        swaps = {}
        feed.arrived()
        both_load.wait()
        down_load.wait()
        cot_load.wait()
        swaps[0] = block(0)
        feed.forward()
        for s in LINE:
            ahead[s - 1] = back(s)
        feed.share()
        one_mine.wait()
        spot = one_out.at[y, c]
        shared = [net.send(spot, spot, "c", 1)]
        for d in LINE:
            ones[d - 1].wait_recv()
            spot = one_out.at[along("y", -d), c]
            shared.append(net.send(spot, spot, "c", 1))
        feed.arrived()
        swaps[1] = block(1)
        for copy in feed.far:
            copy.wait_recv()
        spot = two.at[along("x", 2), c]
        last = net.send(spot, spot, "c", 1)
        swaps[3] = block(3)
        ends = [pair(1)]
        last.wait_recv()
        swaps[2] = block(2)
        ends.append(pair(3))
        ends.append(pair(2))
        early, net.open = net.open, []

        first = []
        for k, axis in enumerate(("y", "z")):
            columns = slice(k * lanes, (k + 1) * lanes)
            gd[k] = (
                dot_tn(hidden[...], cot[...].reshape(8 * size, width)[:, columns])
                .astype(BF)
                .reshape(4, 4, high, lanes)
            )
            for d in LINE:
                at = along(axis, d)
                source = gd.at[k, at] if k == 0 else gd.at[k, :, at]
                first.append(net.send(source, down_come.at[k, d - 1], axis, d))

        gb_copies = []
        for i in range(8):
            at = pl.ds(i * 2 * size, 2 * size)
            gb[i] = dot_tn(two[...].reshape(8 * size, width)[:, i * 2 * size : (i + 1) * 2 * size], grads[...]).astype(BF)
            gb_copies.append(net.keep(gb.at[i], gb_out.at[at]))
        for copy in early:
            copy.wait_send()

        @pl.loop(0, 4)
        def _(i):
            at = pl.ds(pl.multiple_of(i * 2 * size, 2 * size), 2 * size)
            two[i] = dot(hidden[at, :], down[...]).astype(BF).reshape(2, size, width)

        branch_copy = net.keep(two, branch_out)
        swaps[0].wait_recv()
        for copy in ends:
            copy.wait_recv()
        add_all([part.at[x, c], near.at[0], come.at[0], come.at[1], come.at[2]], middle_out)
        values, scale, grad = middle_ref[...], inverse_ref[...], middle_out[...]
        gain_out[...] = jnp.sum(grad * values * scale, axis=0, keepdims=True)
        scaled = grad * gain_ref[...]
        grad = cot[x, c].astype(F32) + (
            scale * scaled
            - values * (scale * scale * scale) * jnp.mean(scaled * values, axis=-1, keepdims=True)
        )
        middle_out[...] = grad
        grad_out_[...] = grad.astype(BF)
        for copy in shared:
            copy.wait_recv()
        for copy in first:
            copy.wait_recv()
        for k in range(2):
            for i in range(4):
                own = gd.at[k, y, i] if k == 0 else gd.at[k, i, z]
                add_all([own] + [down_come.at[k, d, i] for d in range(3)], mid_out.at[k, i])
        for copy in gb_copies + [branch_copy]:
            copy.wait()
        net.close()

    outs = (
        shape(size, width, kind=F32), shape(size, width), shape(1, width, kind=F32), shape(4, 2, size, tall),
        shape(4, 2, size, width), shape(width, 2 * units),
        shape(2, 4, high, lanes),
    )
    scratch = [
        pltpu.VMEM((4, 2, size, width), BF),
        pltpu.VMEM((4, 2, size, width), BF),
        pltpu.VMEM((width, 2 * units), BF),
        pltpu.VMEM((units, width), BF),
        pltpu.VMEM((8 * size, units), BF),
        pltpu.VMEM((8 * size, 2 * units), BF),
        pltpu.VMEM((4, 2, size, width), BF),
        pltpu.VMEM((4, size, width), BF),
        pltpu.VMEM((3, size, width), BF),
        pltpu.VMEM((3, size, width), BF),
        pltpu.VMEM((8, 2 * size, 2 * units), BF),
        pltpu.VMEM((2, 4, 4, high, lanes), BF),
        pltpu.VMEM((2, 3, 4, high, lanes), BF),
        pltpu.VMEM((3, 2 * size, units), F32),
    ]
    return comm_call(
        body, "feed_forward", 4, outs, (normed_two, normed, middle, inverse, gain, grad_out, both, down), scratch,
        32, 14, [IN_VMEM] * 5 + [ANYWHERE] * 3, [IN_VMEM] * 3 + [ANYWHERE] * 3 + [IN_VMEM],
    )


Y_COLUMNS = 640


class FirstStep:
    def __init__(self, net, value, columns, axis, own, come, out):
        self.own, self.come, self.out = own, come, out
        self.copies = []
        for d in (1, 2, 3, 0):
            at = along(axis, d)
            source = value.at[at, :, :, columns] if axis == "y" else value.at[:, at, :, columns]
            if d:
                self.copies.append(net.send(source, come.at[d - 1], axis, d))
            else:
                self.mine = net.keep(source, own)

    def finish(self):
        self.mine.wait()
        for copy in self.copies:
            copy.wait_recv()
        for i in range(4):
            add_all([self.own.at[i]] + [self.come.at[d, i] for d in range(3)], self.out.at[i])


class SecondStep:
    def __init__(self, net, mid, axis, come):
        self.mid, self.axis, self.come = mid, axis, come
        self.copies = [net.send(mid.at[along(axis, d)], come.at[d - 1], axis, d) for d in LINE]

    def finish(self, out):
        for copy in self.copies:
            copy.wait_recv()
        here = lax.axis_index(self.axis)
        add_all([self.mid.at[here]] + [self.come.at[d] for d in range(3)], out)


def last_sums(
    grad_kv, grad_query, latent_group, up_heads, grad_out, grad_both, grad_down, cosine, sine, latent,
    latent_inverse, latent_gain, normed_part, inputs, inverse, gain_one, gain_two, weights, share,
):
    _, _, _, size, thin = grad_kv.shape
    group, latent_width = latent_group.shape
    per = up_heads.shape[1]
    high, lanes = up_heads.shape[0] // 32, per // 4
    _, out_rows, wide = grad_out.shape
    quarter = out_rows // 4
    tall, ahead_columns = grad_both[0].shape[1:]
    after_columns = grad_both[1].shape[2]
    both_columns = ahead_columns + after_columns
    rows = tall // 2
    half_units = both_columns // 4
    _, _, padded, down_lanes = grad_down.shape
    width = 2 * down_lanes
    half_wide = 2 * half_units // padded * 4 * share
    part = (latent_width + thin) // 2
    deep = weights.shape[0]
    tiles = deep // BLOCK

    def body(
        kv_ref, query_ref, group_ref, heads_ref, out_ref, one_ref, two_ref, down_ref, cos_ref, sin_ref, latent_ref,
        latent_inverse_ref, latent_gain_ref, normed_ref, input_ref, inverse_ref, gain_ref, gain_two_ref, weights_hbm,
        first_out, gain_out, back_out, out_out, gate_out, up_weight_out, down_out, q_up_out,
        row_near, row_go, row_first, row_mid, row_last, ring_near, ring_relay, ring_come, ring_go,
        partial, ups_here, kv_sum, part_sum, up_come_x, out_come_x, one_come, two_come, down_come, both_here,
        up_kept, out_kept, firsts,
        gathered, both_all, up_all, down_all, out_come, up_come, up_sum, up_y, weights_ref, accum, down_rows,
        first_here, pair, first_come, first_x, gain_here, gain_near, gain_come, gain_z, gain_y, gain_x,
        sends, arrivals, locals_,
    ):
        net = Net(sends, arrivals, locals_)
        x, y, z, c = (lax.axis_index(a) for a in AXES)

        def lane(at):
            return pl.ds(pl.multiple_of(at * lanes, lanes), lanes)

        def strip(at):
            return pl.ds(pl.multiple_of(at * quarter, quarter), quarter)

        load = net.keep(weights_hbm, weights_ref)
        greet(X_LINE + Y_LINE + Z_LINE + TWIN)
        row = RowSum(net, kv_ref, kv_sum, row_near, row_go, row_first, row_mid, row_last)
        outs = [net.send(out_ref.at[:, strip(along("x", d))], out_come_x.at[d - 1], "x", d) for d in LINE]
        halves = [
            SecondStep(net, mid, axis, come)
            for mid, axis, come in (
                (one_ref, "z", one_come), (two_ref, "y", two_come), (down_ref.at[0], "z", down_come.at[0]),
                (down_ref.at[1], "y", down_come.at[1]),
            )
        ]
        for i in range(4):
            at = pl.ds(i * 2 * size, 2 * size)
            partial[i] = dot_nt(query_ref[at, :], heads_ref[...]).astype(BF).reshape(2, size, latent_width)
        ring = RingSum(net, partial, part_sum, "y", ring_near, ring_relay, ring_come, ring_go)
        row.start()
        ring.relay_far()
        ring.issue()
        ups_here[...] = dot_tn(group_ref[...], query_ref[...]).astype(BF).reshape(4, 4, 2, high, per)
        ups = [
            net.send(ups_here.at[:, :, :, :, lane(along("x", d))], up_come_x.at[d - 1], "x", d) for d in LINE
        ]
        halves[0].finish(both_here.at[:, pl.ds(0, ahead_columns)])
        halves[1].finish(both_here.at[:, pl.ds(ahead_columns, after_columns)])
        own_rows = pl.ds(pl.multiple_of(c * rows, rows), rows)
        other_rows = pl.ds(pl.multiple_of((1 - c) * rows, rows), rows)
        both_mine = net.keep(both_here.at[own_rows], both_all.at[x, c])
        both_come = net.send(both_here.at[other_rows], both_all.at[x, c], "c", 1)
        row.turn()
        ring.pass_on()
        both_mine.wait()
        both_come.wait_recv()
        zero, one = both_all.at[x, 0], both_all.at[x, 1]
        right = [net.send(spot, spot, "x", 1) for spot in (zero, one)]
        left = [net.send(spot, spot, "x", -1) for spot in (one, zero)]
        accum[...] = jnp.zeros_like(accum)

        def put(px):
            for pc in range(2):
                places = unit_places((half_units, 1), 0, px, pc, share, padded)
                picks = lax.broadcasted_iota(jnp.int32, (half_units, half_wide), 1) == places
                stacked = jnp.concatenate(
                    [both_all[px, pc, :, k * half_units : (k + 1) * half_units] for k in range(4)], axis=0
                )
                accum[...] += dot(stacked, picks.astype(BF))

        put(x)

        ring.finish()
        values = latent_ref[...]
        scale = latent_inverse_ref[...]
        scaled = part_sum[...] * latent_gain_ref[...]
        gain_latent = jnp.sum(part_sum[...] * values * scale, axis=0, keepdims=True)
        back = scale * scaled - values * (scale * scale * scale) * jnp.mean(scaled * values, axis=-1, keepdims=True)
        firsts[0] = back[:, :part].astype(BF)
        firsts[1, :, : latent_width - part] = back[:, part:].astype(BF)
        row.finish()
        lower, upper = kv_sum[:, :HALF], kv_sum[:, HALF:SIZE]
        at = latent_width - part
        firsts[1, :, at : at + HALF] = (lower * cos_ref[...] + upper * sin_ref[...]).astype(BF)
        firsts[1, :, at + HALF : at + SIZE] = (upper * cos_ref[...] - lower * sin_ref[...]).astype(BF)
        firsts[1, :, at + SIZE :] = kv_sum[:, SIZE:].astype(BF)

        mine = net.keep(firsts.at[c], gathered.at[y, c])
        come = net.send(firsts.at[1 - c], gathered.at[y, c], "c", 1)
        mine.wait()
        spot = gathered.at[y, c]
        ahead = [net.send(spot, spot, "y", 1), net.send(spot, spot, "y", -1)]
        come.wait_recv()
        spot = gathered.at[y, 1 - c]
        ahead += [net.send(spot, spot, "y", 1), net.send(spot, spot, "y", -1)]

        right[0].wait_recv()
        spot = both_all.at[along("x", -1), 0]
        far = [net.send(spot, spot, "x", 1)]
        left[0].wait_recv()
        spot = both_all.at[along("x", 1), 1]
        far.append(net.send(spot, spot, "x", -1))

        for copy in ups:
            copy.wait_recv()
        for i in range(4):
            up_kept[i] = (
                (ups_here[i, :, :, :, lane(x)].astype(F32) + up_come_x[0, i].astype(F32))
                + (up_come_x[1, i].astype(F32) + up_come_x[2, i].astype(F32))
            ).astype(BF)
        ups = [net.send(up_kept.at[:, along("z", d)], up_come.at[d - 1], "z", d) for d in LINE]
        for copy in outs:
            copy.wait_recv()
        for i in range(4):
            add_all([out_ref.at[i, strip(x)]] + [out_come_x.at[d, i] for d in range(3)], out_kept.at[i])
        outs = [net.send(out_kept.at[along("z", d)], out_come.at[d - 1], "z", d) for d in LINE]

        def back_tile(i):
            at = pl.ds(pl.multiple_of(i * BLOCK, BLOCK), BLOCK)
            total = 0.0
            for core in range(2):
                columns = slice(core * part, (core + 1) * part)
                total = total + dot_nt(firsts[core], weights_ref[at, columns])
            back_out[:, at] = total

        load.wait()
        pl.loop(0, tiles // 2)(back_tile)
        ahead[0].wait_recv()
        spot = gathered.at[along("y", -1), c]
        ahead.append(net.send(spot, spot, "y", 1))
        ahead[3].wait_recv()
        spot = gathered.at[along("y", 1), 1 - c]
        ahead.append(net.send(spot, spot, "y", -1))
        pl.loop(tiles // 2, tiles)(back_tile)

        for copy in ups:
            copy.wait_recv()
        for i in range(4):
            up_sum[i] = (
                (up_kept[i, z].astype(F32) + up_come[0, i].astype(F32))
                + (up_come[1, i].astype(F32) + up_come[2, i].astype(F32))
            ).astype(BF)
        ups = [net.send(up_sum.at[along("y", d)], up_y.at[y], "y", d) for d in LINE]
        up_mine = net.keep(up_sum.at[y], up_y.at[y])

        values = input_ref[...].astype(F32)
        scale = inverse_ref[...]
        grad = back_out[...]
        gain_own = jnp.sum(grad * values * scale, axis=0, keepdims=True)
        scaled = grad * gain_ref[...]
        back_out[...] = scale * scaled - values * (scale * scale * scale) * jnp.mean(
            scaled * values, axis=-1, keepdims=True
        )
        gain_here[...] = jnp.zeros_like(gain_here)
        for i in range(16):
            gain_here[i // 4, i % 4, 0:1, :] = gain_own[:, i * 128 : (i + 1) * 128]
            gain_here[i // 4, i % 4, 1:2, :] = gain_two_ref[:, i * 128 : (i + 1) * 128]
            gain_here[i // 4, i % 4, 2:3, :] = gain_latent[:, i // 2 * 128 : (i // 2 + 1) * 128]
        near = net.send(gain_here, gain_near, "c", 1)

        for k in (2, 3):
            halves[k].finish(down_all.at[x, :, pl.ds((k - 2) * down_lanes, down_lanes)])
        spot = down_all.at[x]
        downs = [net.send(spot, spot, "x", d) for d in LINE]

        for copy in [ahead[i] for i in (1, 2, 4, 5)]:
            copy.wait_recv()
        first_here[...] = (
            dot_tn(normed_ref[...], gathered[...].reshape(8 * size, part)).astype(BF).reshape(4, 2, rows, part)
        )
        first_near = net.send(first_here.at[:, 1 - c], pair.at[c], "c", 1)
        first_mine = net.keep(first_here.at[:, c], pair.at[c])

        for copy in outs:
            copy.wait_recv()
        add_all([out_kept.at[z]] + [out_come.at[d] for d in range(3)], out_out.at[x])
        spot = out_out.at[x]
        outs = [net.send(spot, spot, "x", d) for d in LINE]
        up_mine.wait()
        for copy in ups:
            copy.wait_recv()
        up_near = net.send(up_y.at[:, 1 - c], up_all.at[x, :, c], "c", 1)
        up_mine = net.keep(up_y.at[:, c], up_all.at[x, :, c])

        first_mine.wait()
        first_near.wait_recv()
        weight_sends = [
            [net.send(pair.at[core, along("z", d)], first_come.at[d - 1, core], "z", d) for d in LINE]
            for core in range(2)
        ]
        near.wait_recv()
        gain_near[...] = gain_here[...] + gain_near[...]
        comes = [net.send(gain_near.at[:, along("z", d)], gain_come.at[d - 1], "z", d) for d in LINE]
        up_near.wait_recv()
        up_mine.wait()
        spot = up_all.at[x]
        ups = [net.send(spot, spot, "x", d) for d in LINE]

        for copy in (right[1], left[1]):
            copy.wait_recv()
        put(along("x", 1))

        def onward(core):
            for copy in weight_sends[core]:
                copy.wait_recv()
            add_all([pair.at[core, z]] + [first_come.at[d, core] for d in range(3)], first_x.at[x, core])
            spot = first_x.at[x, core]
            return [net.send(spot, spot, "x", d) for d in LINE]

        finals = [onward(0)]
        for copy in comes:
            copy.wait_recv()
        gain_z[...] = (gain_near[:, z] + gain_come[0]) + (gain_come[1] + gain_come[2])
        comes = [net.send(gain_z.at[along("y", d)], gain_y.at[d - 1], "y", d) for d in LINE]
        finals.append(onward(1))
        put(along("x", -1))
        for copy in comes:
            copy.wait_recv()
        gain_x[x] = (gain_z[y] + gain_y[0]) + (gain_y[1] + gain_y[2])
        spot = gain_x.at[x]
        comes = [net.send(spot, spot, "x", d) for d in LINE]
        for copy in far:
            copy.wait_recv()
        put(along("x", 2))
        for k, target in enumerate((gate_out, gate_out, up_weight_out, up_weight_out)):
            target[:, (k % 2) * half_wide : (k % 2 + 1) * half_wide] = accum[k * rows : (k + 1) * rows].astype(BF)
        for copy in outs + ups + downs:
            copy.wait_recv()
        for px in range(4):
            down_rows[px * share : (px + 1) * share, :] = down_all[px].astype(F32)[:share]
            for py in range(4):
                for pc in range(2):
                    at = ((2 * py + pc) * 4 + px) * lanes
                    q_up_out[:, at : at + lanes] = up_all[px, py, pc]
        down_out[...] = down_rows[...].astype(BF)
        for core in range(2):
            for copy in finals[core]:
                copy.wait_recv()
            add_all([first_x.at[i, core] for i in range(4)], first_out.at[core])
        for copy in comes:
            copy.wait_recv()
        gain_out[...] = (gain_x[0] + gain_x[1]) + (gain_x[2] + gain_x[3])
        net.close()

    outs = (
        shape(2, rows, part, kind=F32), shape(8, 128, kind=F32), shape(size, deep, kind=F32),
        shape(4, quarter, wide), shape(rows, 2 * half_wide), shape(rows, 2 * half_wide), shape(4 * share, width),
        shape(high, 32 * lanes),
    )
    scratch = row_sum_scratch(size, thin) + ring_sum_scratch(size, latent_width) + [
        pltpu.VMEM((4, 2, size, latent_width), BF),
        pltpu.VMEM((4, 4, 2, high, per), BF),
        pltpu.VMEM((size, thin), F32),
        pltpu.VMEM((size, latent_width), F32),
        pltpu.VMEM((3, 4, 4, 2, high, lanes), BF),
        pltpu.VMEM((3, 4, quarter, wide), BF),
        pltpu.VMEM((3, tall, ahead_columns), BF),
        pltpu.VMEM((3, tall, after_columns), BF),
        pltpu.VMEM((2, 3, padded, down_lanes), BF),
        pltpu.VMEM((tall, both_columns), BF),
        pltpu.VMEM((4, 4, 2, high, lanes), BF),
        pltpu.VMEM((4, quarter, wide), BF),
        pltpu.VMEM((2, size, part), BF),
        pltpu.VMEM((4, 2, size, part), BF),
        pltpu.VMEM((4, 2, rows, both_columns), BF),
        pltpu.VMEM((4, 4, 2, high, lanes), BF),
        pltpu.VMEM((4, padded, width), BF),
        pltpu.VMEM((3, quarter, wide), BF),
        pltpu.VMEM((3, 4, 2, high, lanes), BF),
        pltpu.VMEM((4, 2, high, lanes), BF),
        pltpu.VMEM((4, 2, high, lanes), BF),
        pltpu.VMEM(weights.shape, BF),
        pltpu.VMEM((4 * rows, half_wide), F32),
        pltpu.VMEM((4 * share, width), F32),
        pltpu.VMEM((4, 2, rows, part), BF),
        pltpu.VMEM((2, 4, rows, part), BF),
        pltpu.VMEM((3, 2, rows, part), BF),
        pltpu.VMEM((4, 2, rows, part), BF),
        pltpu.VMEM((4, 4, 8, 128), F32),
        pltpu.VMEM((4, 4, 8, 128), F32),
        pltpu.VMEM((3, 4, 8, 128), F32),
        pltpu.VMEM((4, 8, 128), F32),
        pltpu.VMEM((3, 8, 128), F32),
        pltpu.VMEM((4, 8, 128), F32),
    ]
    return comm_call(
        body, "last_sums", 7, outs,
        (
            grad_kv, grad_query, latent_group, up_heads, grad_out, *grad_both, grad_down, cosine, sine, latent,
            latent_inverse, latent_gain, normed_part, inputs, inverse, gain_one, gain_two, weights,
        ),
        scratch, 104, 8, [IN_VMEM] * 18 + [ANYWHERE], [IN_VMEM] * 8,
    )


def heads_back(
    grad_branch, branch, mixed, qt, kv, out_heads, begin, slot, lse, live, cosine, sine, gb,
):
    segments, _, rows = slot.shape
    tokens = rows // 2
    size, width = grad_branch.shape
    tall, wide = gb.shape[2:]
    ahead, after = Y_COLUMNS, wide - Y_COLUMNS
    half = out_heads.shape[0] // (2 * size)

    def body(
        grad_ref, branch_ref, mixed_ref, qt_ref, kv_ref, out_ref, begin_ref, slot_ref, lse_ref, live_ref, cos_ref,
        sin_ref, gb_ref,
        dq_ref, dkv_ref, stack, branch_out, one_out, two_out,
        grads, kt, sums, accum, query, grad_rows, grad_turned, delta, go_send, near, relay, come, go,
        own_one, come_one, own_two, come_two, sends, arrivals, locals_,
    ):
        net = Net(sends, arrivals, locals_)
        y, z, c = (lax.axis_index(a) for a in ROW)
        greet(X_RING + Y_LINE + Z_LINE + TWIN)
        gathering = RingGather(net, grad_ref, grads, "y")
        two = FirstStep(net, gb_ref, pl.ds(ahead, after), "z", own_two, come_two, two_out)
        ring = RingSum(net, branch_ref, branch_out, "x", near, relay, come, go)
        sums[...] = jnp.zeros_like(sums)
        turned(kv_ref, kt, segments * (segments - 1) + z + 1, KEYS)

        def segment(step):
            seg = along("y", step)
            here = pl.ds(pl.multiple_of(seg * tokens, tokens), tokens)
            grad = dot_nt(grads[seg].reshape(tokens, width), out_ref[...]).astype(BF) * live_ref[here, :].astype(BF)
            grad = jnp.concatenate([grad[:, :SIZE], grad[:, SIZE:]], axis=0)
            value = mixed_ref[here, :]
            value = jnp.concatenate([value[:, :SIZE], value[:, SIZE:]], axis=0)
            query[...] = qt_ref[seg].T
            grad_rows[...] = grad
            grad_turned[...] = grad.T
            delta[...] = jnp.sum(grad_turned[...].astype(F32) * value.T.astype(F32), axis=0, keepdims=True)
            accum[...] = jnp.zeros_like(accum)

            def tile(at, count, masked):
                keys = pl.ds(at, count)
                scores = dot(kv_ref[keys, KEYS], qt_ref[seg])
                probs = jnp.exp(scores - lse_ref[seg])
                if masked:
                    key = lax.broadcasted_iota(jnp.int32, scores.shape, 0) + at
                    probs = jnp.where((key >= begin_ref[seg]) & (key <= slot_ref[seg]), probs, 0.0)
                grad_probs = dot(kv_ref[keys, VALUES], grad_turned[...])
                grad_scores = (probs * (grad_probs - delta[...])).astype(BF)
                sums[keys, VALUES] += dot(probs.astype(BF), grad_rows[...])
                sums[keys, KEYS] += dot(grad_scores, query[...])
                accum[...] += dot(kt[:, keys], grad_scores)

            sweep(seg, segments, z, tile)
            cos_here, sin_here = cos_ref[seg], sin_ref[seg]
            for head in range(2):
                part = accum[:, head * tokens : (head + 1) * tokens] * (SIZE ** -0.5)
                lower, upper = part[:HALF], part[HALF:]
                turn = jnp.concatenate(
                    [lower * cos_here + upper * sin_here, upper * cos_here - lower * sin_here], axis=0
                )
                dq_ref[here, head * SIZE : (head + 1) * SIZE] = turn.T.astype(BF)

        gathering.arrived()
        segment(0)
        gathering.forward()
        one = FirstStep(net, gb_ref, pl.ds(0, ahead), "y", own_one, come_one, one_out)
        ring.relay_far()
        ring.issue()
        gathering.share()
        gathering.arrived()
        pl.loop(0, 2)(lambda i: segment(1 + 2 * i))
        ring.pass_on()
        gathering.finish()

        for k in range(4):
            columns = slice(k * width // 4, (k + 1) * width // 4)
            part = dot_tn(mixed_ref[...], grads[...].reshape(segments * tokens, width)[:, columns]).astype(BF)
            part = part.reshape(half, 2, size, width // 4)
            for h in range(half):

                @pl.when(c == 0)
                def _(h=h, part=part, columns=columns):
                    stack[h, :, columns] = part[h, 0]
                    go_send[h, :, columns] = part[h, 1]

                @pl.when(c == 1)
                def _(h=h, part=part, columns=columns):
                    stack[half + h, :, columns] = part[h, 1]
                    go_send[h, :, columns] = part[h, 0]

        go_come = net.send(go_send, stack.at[pl.ds(half * c, half)], "c", 1)
        segment(2)
        dkv_ref[...] = sums[...].astype(BF)
        ring.finish()
        go_come.wait_recv()
        one.finish()
        two.finish()
        net.close()

    outs = (
        shape(*mixed.shape), shape(*kv.shape), shape(2 * half, size, width), shape(size, width, kind=F32),
        shape(4, tall, ahead), shape(4, tall, after),
    )
    scratch = [
        pltpu.VMEM((4, 2, size, width), BF),
        pltpu.VMEM((SIZE, kv.shape[0]), BF),
        pltpu.VMEM(kv.shape, F32),
        pltpu.VMEM((SIZE, rows), F32),
        pltpu.VMEM((rows, SIZE), BF),
        pltpu.VMEM((rows, SIZE), BF),
        pltpu.VMEM((SIZE, rows), BF),
        pltpu.VMEM((1, rows), F32),
        pltpu.VMEM((half, size, width), BF),
    ] + ring_sum_scratch(size, width) + [
        pltpu.VMEM((4, tall, ahead), BF),
        pltpu.VMEM((3, 4, tall, ahead), BF),
        pltpu.VMEM((4, tall, after), BF),
        pltpu.VMEM((3, 4, tall, after), BF),
    ]
    return comm_call(
        body, "heads_back", 6, outs,
        (grad_branch, branch, mixed, qt, kv, out_heads, begin, slot, lse, live, cosine, sine, gb),
        scratch, 30, 3, [IN_VMEM] * 12 + [ANYWHERE], [IN_VMEM] * 6,
    )


def results(middle, branch, grad_middle, grad_norm, first, gate, up, down, out, q_up, latent_width):
    size, width = middle.shape
    rows, part = first.shape[1:]
    spare = latent_width - part
    kinds = [BF] + [F32] * 9
    shapes = [
        (size, width), (size, width), (rows, latent_width), (rows, SIZE), (rows, SIZE), gate.shape, up.shape,
        down.shape, (4 * out.shape[1], out.shape[2]), q_up.shape,
    ]
    count = len(shapes)

    def body(
        middle_ref, branch_ref, grad_ref, norm_ref, first_ref, gate_ref, up_ref, down_ref, out_ref, q_up_ref, *rest,
    ):
        targets, made, done = rest[:count], rest[count : 2 * count], rest[2 * count]
        copies = []

        def ready(i):
            copy = pltpu.make_async_copy(made[i], targets[i], done.at[i])
            copy.start()
            copies.append(copy)

        made[5][...] = gate_ref[...].astype(F32)
        ready(5)
        made[6][...] = up_ref[...].astype(F32)
        ready(6)
        made[7][...] = down_ref[...].astype(F32)
        ready(7)
        for i in range(4):
            quarter = out_ref.shape[1]
            made[8][i * quarter : (i + 1) * quarter, :] = out_ref[i].astype(F32)
        ready(8)
        made[1][...] = grad_ref[...] + norm_ref[...]
        ready(1)
        made[0][...] = (middle_ref[...] + branch_ref[...]).astype(BF)
        ready(0)
        made[9][...] = q_up_ref[...].astype(F32)
        ready(9)
        made[2][:, :part] = first_ref[0]
        made[2][:, part:] = first_ref[1, :, :spare]
        ready(2)
        made[3][...] = first_ref[1, :, spare : spare + SIZE]
        ready(3)
        made[4][...] = first_ref[1, :, spare + SIZE :]
        ready(4)
        for copy in copies:
            copy.wait()

    return pl.pallas_call(
        body,
        name="results",
        out_shape=tuple(shape(*dims, kind=kind) for dims, kind in zip(shapes, kinds)),
        in_specs=[IN_VMEM] * 10,
        out_specs=[ANYWHERE] * count,
        scratch_shapes=[pltpu.VMEM(dims, kind) for dims, kind in zip(shapes, kinds)]
        + [pltpu.SemaphoreType.DMA((count,))],
        compiler_params=pltpu.CompilerParams(vmem_limit_bytes=56 << 20),
    )(middle, branch, grad_middle, grad_norm, first, gate, up, down, out, q_up)


def gather(value, axes):
    return lax.all_gather(value, axes, axis=0, tiled=True)


def on_device(
    block_input, cotangent, lengths, norm_gain, q_down, q_gain, q_up, key_weight, value_weight,
    out_weight, ffn_gain, gate_weight, up_weight, down_weight,
):
    rows, width = block_input.shape
    latent_width = q_down.shape[1]
    n_x, n_y, n_z, n_c = (lax.axis_size(a) for a in ("x", "y", "z", "c"))
    x, y, z, c = (lax.axis_index(a) for a in ("x", "y", "z", "c"))
    span = n_y * n_z * n_c
    members = n_y * n_c

    shard = norm_gain.shape[0]
    per_heads = q_up.shape[1] // members
    q_rows = q_up.shape[0]

    down_rows = down_weight.shape[0]
    share = down_rows // n_x
    padded = -(-share // 16) * 16
    down_part = lax.dynamic_slice_in_dim(down_weight, x * share, share)
    down_part = jnp.pad(down_part, ((0, padded - share), (0, 0)))
    (
        first_full, both, out_strip, normed, key_value, latent_normed, latent, inverse_one, inverse_latent, gain_one,
        gain_two, gain_latent, cosine, sine, cosine_group, sine_group, begin_lanes, slot_lanes, live_lanes, live_rows,
    ) = first_weights(
        (q_down, key_weight, value_weight, gain_rows(norm_gain, ffn_gain, q_gain)), gate_weight, up_weight, out_weight,
        block_input, lengths, share, padded
    )
    units = both.shape[2] // 2
    first_full = first_full.reshape(span * shard, -1)
    both = both.reshape(n_c * shard, 2 * units)
    both_full = gather(both, ("y", "z"))
    down_use = gather(down_part, ("y", "z"))

    key_value, latent_group, up_heads, out_heads = keys_and_latents(
        key_value, latent_normed, q_up.reshape(q_rows, n_y, n_c, per_heads).transpose(1, 2, 0, 3), out_strip,
    )
    up_heads = up_heads.reshape(span * q_rows, per_heads)
    out_heads = out_heads.reshape(per_heads, width)
    key_value = key_value.reshape(span * rows, 2 * SIZE)
    group = members * rows
    latent_group = latent_group.reshape(group, latent_width)
    mixed, queries_t, lse, middle, inverse_two, normed_two, grad_feed = attend(
        latent_group, up_heads, key_value, begin_lanes, slot_lanes, live_lanes, cosine_group, sine_group, out_heads,
        block_input, gain_two, cotangent,
    )

    grad_middle, grad_branch, grad_gain_two, normed_part, branch_part, grad_both, grad_down = feed_forward(
        normed_two, normed, grad_feed, both_full, down_use, middle, inverse_two, gain_two
    )
    normed_part = normed_part.reshape(group, -1)

    grad_both = grad_both.reshape(n_y, n_z, n_c * shard, 2 * units)
    out_rows = out_weight.shape[0]
    grad_query_raw, grad_kv, grad_out, branch_two, grad_one, grad_two = heads_back(
        grad_branch, branch_part, mixed, queries_t, key_value, out_heads, begin_lanes, slot_lanes, lse,
        live_rows, cosine_group, sine_group, grad_both,
    )

    grad_first, gains, grad_input_norm, grad_out, grad_gate, grad_up, grad_down, grad_q_up = last_sums(
        grad_kv.reshape(n_y, n_z, n_c, rows, 2 * SIZE), grad_query_raw, latent_group, up_heads, grad_out,
        (grad_one, grad_two), grad_down, cosine, sine, latent, inverse_latent, gain_latent, normed_part, block_input,
        inverse_one, gain_one, grad_gain_two, first_full, share,
    )
    (
        output, input_grad, grad_q_down, grad_key, grad_value, grad_gate, grad_up, grad_down, grad_out, grad_q_up,
    ) = results(
        middle, branch_two, grad_middle, grad_input_norm, grad_first, grad_gate, grad_up, grad_down, grad_out,
        grad_q_up, latent_width,
    )
    latent_shard = q_gain.shape[0]
    return (
        output,
        input_grad,
        lax.dynamic_slice(gains[0], (c * shard,), (shard,)),
        grad_q_down,
        lax.dynamic_slice(gains[2], ((z % 2 * n_c + c) * latent_shard,), (latent_shard,)),
        grad_q_up,
        grad_key,
        grad_value,
        grad_out,
        lax.dynamic_slice(gains[1], (c * shard,), (shard,)),
        grad_gate,
        grad_up,
        grad_down,
    )


def solution(mesh):
    sizes = (4, 4, 4, 2)
    grid = Mesh(mesh.devices.reshape(sizes), ("x", "y", "z", "c"))
    tokens = P(("x", "y", "z", "c"), None)
    wide, thin = P(ROW, None), P(ROW)
    in_specs = (
        tokens, tokens, P("x", None), thin, wide, thin, wide, wide, wide, wide, thin, wide, wide,
        wide,
    )
    out_specs = (
        tokens, tokens, thin, wide, thin, wide, wide, wide, wide, thin, wide, wide, wide,
    )
    return jax.shard_map(
        on_device, mesh=grid, in_specs=in_specs, out_specs=out_specs, check_vma=False
    )
```
